32 devices in a mesh: dp: 8 (over z, y), mp: 4 (over x, core).
Axes of the slice: x: 2, y: 2, z: 4, core: 2. Of those that a mesh axis runs over, the one named last changes fastest.
Arguments:
- tokens: bfloat16 [256, 5120], P('dp'), may hold values from -14 to 14
- parent_keys: bfloat16 [64, 256, 1024], P('dp', None, 'mp'), may hold values from -56 to 56
- parent_values: bfloat16 [64, 256, 1024], P('dp', None, 'mp'), may hold values from -24 to 24
- parent_blocks: int32 [64], replicated, may hold values from 1 to 2
- child_parent: int32 [256], replicated, may hold values from 0 to 63, as said below
- child_count: int32 [8], P('dp'), may hold values from 24 to 32, as said below
- node_shard: int32 [256], replicated, may hold values from 0 to 7, as said below
- attn_gain: float32 [5120], replicated, may hold values from 0.5 to 1.5
- w_query: bfloat16 [5120, 3072], P(None, 'mp'), may hold values from -1 to 1
- w_key: bfloat16 [5120, 1024], P(None, 'mp'), may hold values from -1 to 1
- w_value: bfloat16 [5120, 1024], P(None, 'mp'), may hold values from -0.078125 to 0.078125
- w_out: bfloat16 [3072, 5120], P('mp'), may hold values from -0.109375 to 0.109375
- reward_up: bfloat16 [8, 5120, 512], P('dp', 'mp'), may hold values from -0.078125 to 0.078125
- reward_out: float32 [8, 512], P('dp'), may hold values from -0.25 to 0.25
Outputs:
- rewards: float32 [8, 384], P(None, 'dp')
The draws below stay inside these ranges and needn't reach their ends.
Inputs may be any that keep to these rules, and one draw needn't show every extreme that they name: `child_parent`: the children of one index of dp name parents of one index of dp at most 8 times, and exactly 8 times for some pair at every index. `child_count`: every index of dp holds 24 or more live children, and some index holds 32. `node_shard`: the children of one index of dp name one shard at most 6 times, exactly 6 times for some shard at every index.
All inputs are finite; a program needn't handle non-finite values.
Results may differ from the reference program's by a relative error of at most 0.015.
Values may be sent and summed in bfloat16 or wider, within the bound.
No kernel may reach another device: no remote copies, remote signals or barrier semaphores. Data moves between devices by JAX's collectives and lax.ppermute only.
A program may use at most 128 MiB of HBM per device.

```python
import jax
import jax.numpy as jnp
from jax import lax

D = 5120
HEADS = 24
KVH = 8
HD = 128
STEPS = 8
RH = 512
PLEN = 256
PAR_DEV = 8
CH_DEV = 32
PARENTS = 64
CHILDREN = 256
CAP = 8
RCAP = 6
N_DP = 8


def route_blocks(key, blocks, per_block, targets, capacity):

    def one(block_key):
        key_order, key_forced, key_shuffle = jax.random.split(block_key, 3)
        order = jax.random.permutation(key_order, targets * capacity).astype(jnp.int32)
        forced = jax.random.randint(key_forced, (), 0, targets)
        slot_ids = jnp.arange(targets * capacity, dtype=jnp.int32)
        priority = jnp.where(slot_ids // capacity == forced, -1 - slot_ids % capacity, order)
        chosen = jnp.argsort(priority, stable=True)[:per_block]
        return jax.random.permutation(key_shuffle, (chosen // capacity).astype(jnp.int32))
    keys = jax.random.split(key, blocks)
    return jax.vmap(one)(keys).reshape(-1).astype(jnp.int32)


def draw_tokens(key, part):
    drawn_key = jax.random.fold_in(key, 41)
    rows = jax.random.truncated_normal(drawn_key, -6.0, 6.0, (CHILDREN, D), jnp.float32)
    return rows.astype(jnp.bfloat16)


def draw_w_query(key, part):
    drawn_key = jax.random.fold_in(key, 43)
    values = jax.random.truncated_normal(drawn_key, -6.0, 6.0, (D, HEADS * HD), jnp.float32) * D ** (-0.5)
    return values.astype(jnp.bfloat16)


def draw_w_key(key, part):
    drawn_key = jax.random.fold_in(key, 47)
    values = jax.random.truncated_normal(drawn_key, -6.0, 6.0, (D, KVH * HD), jnp.float32) * D ** (-0.5)
    return values.astype(jnp.bfloat16)


def draw_parent_keys(key, part):
    drawn_key = jax.random.fold_in(key, 53)
    values = jax.random.truncated_normal(drawn_key, -6.0, 6.0, (PARENTS, PLEN, KVH * HD), jnp.float32)
    return values.astype(jnp.bfloat16)


def draw_child_parent(key, part):
    key = jax.random.fold_in(key, 11)
    key_route, key_local = jax.random.split(key)
    source = route_blocks(key_route, N_DP, CH_DEV, N_DP, CAP)
    local = jax.random.randint(key_local, (CH_DEV * N_DP,), 0, PAR_DEV)
    return (source * PAR_DEV + local).astype(jnp.int32)


def draw_child_count(key, part):
    key = jax.random.fold_in(key, 23)
    key_count, key_full = jax.random.split(key)
    counts = jax.random.randint(key_count, (N_DP,), 3 * CH_DEV // 4, CH_DEV + 1)
    full = jax.random.randint(key_full, (), 0, N_DP)
    return jnp.where(jnp.arange(N_DP) == full, CH_DEV, counts).astype(jnp.int32)


def draw_node_shard(key, part):
    key = jax.random.fold_in(key, 37)
    return route_blocks(key, N_DP, CH_DEV, N_DP, RCAP)


def plant(drawn, rng, low, largest):
    spot = [jax.random.randint(jax.random.fold_in(rng, axis), (), 0, length) for axis, length in enumerate(drawn.shape)]
    longest = drawn.shape.index(max(drawn.shape))
    next_to = spot[:longest] + [(spot[longest] + 1) % drawn.shape[longest]] + spot[longest + 1:]
    return drawn.at[tuple(spot)].set(low).at[tuple(next_to)].set(largest)


def shard_levels(key, shape, cuts, smallest, high):
    def one(position, parts):
        draws = jax.random.uniform(jax.random.fold_in(jax.random.fold_in(key, 6), position), (parts,), jnp.float32, smallest / len(cuts), high / len(cuts))
        return jnp.repeat(jnp.exp(draws), shape[position] // parts).reshape((-1,) + (1,) * (len(shape) - position - 1))

    loudness = one(*cuts[0])
    for cut in cuts[1:]:
        loudness = loudness * one(*cut)
    return loudness


def scatter_about(key, extent, width, reach, cuts=(), held_as=jnp.bfloat16):
    values = jax.random.normal(key, extent, jnp.float32) * width
    if len(cuts) > 0:
        values = shard_levels(key, extent, cuts, -0.22, 0.18) * values
    return jnp.clip(values, min=-reach, max=reach).astype(held_as)


def setup_inputs(seed: int = 0) -> dict:
    streams_of = jax.random.split(jax.random.key(seed), 15)
    return {
        "tokens": draw_tokens(jax.random.fold_in(streams_of[14], 71), 0),
        "parent_keys": draw_parent_keys(jax.random.fold_in(streams_of[14], 71), 0),
        "parent_values": scatter_about(streams_of[2], (PARENTS, PLEN, KVH * HD), 4.0, 24.0, ((0, 8), (2, 4))),
        "parent_blocks": plant(jax.random.randint(streams_of[3], (PARENTS,), 1, PLEN // 128 + 1), jax.random.fold_in(streams_of[3], 1), 1, (PLEN // 128 + 1) - 1).astype(jnp.int32),
        "child_parent": draw_child_parent(jax.random.fold_in(streams_of[14], 71), 0),
        "child_count": draw_child_count(jax.random.fold_in(streams_of[14], 71), 0),
        "node_shard": draw_node_shard(jax.random.fold_in(streams_of[14], 71), 0),
        "attn_gain": jnp.clip(1.0 + 0.1 * jax.random.normal(streams_of[7], (D,), jnp.float32), 0.5, 1.5),
        "w_query": draw_w_query(jax.random.fold_in(streams_of[14], 71), 0),
        "w_key": draw_w_key(jax.random.fold_in(streams_of[14], 71), 0),
        "w_value": scatter_about(streams_of[10], (D, KVH * HD), D ** -0.5, 0.078125, ((1, 4),)),
        "w_out": scatter_about(streams_of[11], (HEADS * HD, D), (HEADS * HD) ** -0.5, 0.109375, ((0, 4),)),
        "reward_up": scatter_about(streams_of[12], (N_DP, D, RH), D ** -0.5, 0.078125, ((0, 8), (1, 4))),
        "reward_out": scatter_about(streams_of[13], (N_DP, RH), RH ** -0.5, 0.25, ((0, 8),), jnp.float32),
    }


def slot_ranks(targets, live):
    count = targets.shape[-1]
    index = jnp.arange(count)
    earlier = index[None, :] < index[:, None]
    same = (targets[:, :, None] == targets[:, None, :]) & earlier[None] & live[:, None, :]
    return lax.optimization_barrier(jnp.sum(same.astype(jnp.int32), -1))

def attend_part(query, keys, values, valid):
    scale = HD ** (-0.5)
    scores = jnp.einsum('ckgd,ctkd->ckgt', query.astype(jnp.float32), keys.astype(jnp.float32)) * scale
    scores = jnp.where(valid[:, None, None, :], scores, -jnp.inf)
    top = lax.optimization_barrier(jnp.max(scores, -1))
    weight = jnp.exp(scores - top[..., None])
    total = lax.optimization_barrier(jnp.sum(weight, -1))
    summed = jnp.einsum('ckgt,ctkd->ckgd', weight.astype(jnp.bfloat16).astype(jnp.float32), values.astype(jnp.float32))
    return (top, total, summed)

def reference(tokens, parent_keys, parent_values, parent_blocks, child_parent, child_count, node_shard, attn_gain, w_query, w_key, w_value, w_out, reward_up, reward_out):
    group = HEADS // KVH
    tok_blocks = tokens.reshape(N_DP, CH_DEV, D)
    par_blocks = child_parent.reshape(N_DP, CH_DEV)

    def expand(pair):
        first, parents = pair
        keys = parent_keys[parents].reshape(CH_DEV, PLEN, KVH, HD)
        values = parent_values[parents].reshape(CH_DEV, PLEN, KVH, HD)
        valid = jnp.arange(PLEN)[None, :] < (parent_blocks[parents] * 128)[:, None]
        state = first.astype(jnp.float32)
        new_keys = jnp.zeros((CH_DEV, STEPS, KVH, HD), jnp.bfloat16)
        new_values = jnp.zeros((CH_DEV, STEPS, KVH, HD), jnp.bfloat16)
        rows = []
        for step in range(STEPS):
            normed = (state * lax.rsqrt(lax.optimization_barrier(jnp.mean(state * state, -1, keepdims=True)) + 1e-06) * attn_gain).astype(jnp.bfloat16)
            query = jnp.dot(normed, w_query, preferred_element_type=jnp.float32).astype(jnp.bfloat16).reshape(CH_DEV, KVH, group, HD)
            key_now = jnp.dot(normed, w_key, preferred_element_type=jnp.float32).astype(jnp.bfloat16).reshape(CH_DEV, KVH, HD)
            value_now = jnp.dot(normed, w_value, preferred_element_type=jnp.float32).astype(jnp.bfloat16).reshape(CH_DEV, KVH, HD)
            new_keys = new_keys.at[:, step].set(key_now)
            new_values = new_values.at[:, step].set(value_now)
            top_a, total_a, sum_a = attend_part(query, keys, values, valid)
            recent = jnp.broadcast_to(jnp.arange(STEPS)[None, :] <= step, (CH_DEV, STEPS))
            top_b, total_b, sum_b = attend_part(query, new_keys, new_values, recent)
            both = jnp.maximum(top_a, top_b)
            fac_a = jnp.exp(top_a - both)
            fac_b = jnp.exp(top_b - both)
            attn = ((sum_a * fac_a[..., None] + sum_b * fac_b[..., None]) / (total_a * fac_a + total_b * fac_b)[..., None]).astype(jnp.bfloat16)
            state = state + jnp.dot(attn.reshape(CH_DEV, HEADS * HD), w_out, preferred_element_type=jnp.float32)
            rows.append(state.astype(jnp.bfloat16))
        return jnp.stack(rows, 1)
    rows = lax.map(expand, (tok_blocks, par_blocks))
    shard_blocks = node_shard.reshape(N_DP, CH_DEV)
    live = jnp.arange(CH_DEV)[None, :] < child_count[:, None]
    ranks = slot_ranks(shard_blocks, live)

    def score(shard):
        select = (shard_blocks[:, None, :] == shard) & (ranks[:, None, :] == jnp.arange(RCAP)[None, :, None]) & live[:, None, :]
        which = lax.optimization_barrier(jnp.sum(select.astype(jnp.int32) * jnp.arange(CH_DEV)[None, None, :], -1)).astype(jnp.int32)
        filled = jnp.any(select, -1)
        picked = rows[jnp.arange(N_DP)[:, None], which]
        picked = jnp.where(filled[:, :, None, None], picked, jnp.zeros_like(picked))
        flat = picked.reshape(N_DP * RCAP * STEPS, D)
        lifted = jnp.dot(flat, reward_up[shard], preferred_element_type=jnp.float32)
        wide = flat.astype(jnp.float32)
        lifted = lifted * lax.rsqrt(lax.optimization_barrier(jnp.mean(wide * wide, -1, keepdims=True)) + 1e-06)
        values = lax.optimization_barrier(jnp.sum(jax.nn.silu(lifted) * reward_out[shard], -1))
        return values.reshape(N_DP * RCAP, STEPS).T
    scored = lax.map(score, jnp.arange(N_DP).astype(jnp.int32))
    return jnp.transpose(scored, (1, 0, 2)).reshape(STEPS, N_DP * N_DP * RCAP)
```

```python
import functools

import jax
import jax.numpy as jnp
from jax import lax
from jax.experimental import pallas as pl
from jax.experimental.pallas import tpu as pltpu
from jax.sharding import PartitionSpec as P

D = 5120
HEADS = 24
KVH = 8
HD = 128
STEPS = 8
GROUP = HEADS // KVH
CHUNK = 512
MASKED = -1e30
VMEM = pltpu.VMEM


def slot_ranks(targets, live):
    count = targets.shape[-1]
    index = jnp.arange(count)
    earlier = index[None, :] < index[:, None]
    same = (targets[:, :, None] == targets[:, None, :]) & earlier[None] & live[:, None, :]
    return jnp.sum(same.astype(jnp.int32), -1)


def dot(a, b):
    return jnp.dot(a, b, preferred_element_type=jnp.float32)


def project(attn, w_out, out, first):
    width = out.shape[1]

    @pl.loop(0, width // CHUNK)
    def _(i):
        columns = pl.ds(pl.multiple_of(first + i * CHUNK, CHUNK), CHUNK)
        out[:, pl.ds(pl.multiple_of(i * CHUNK, CHUNK), CHUNK)] = dot(
            attn[...], w_out[:, columns]
        ).astype(out.dtype)


def step_kernel(step, core, own, peer, gain, w_query, w_key, w_value, keys, values, bias, w_out, *rest):
    past_keys, past_values = rest[:step], rest[step : 2 * step]
    part, attn, key_now, value_now, normed, query = rest[2 * step :]
    half = own.shape[1]
    slots = own.shape[0]
    kv_heads = w_key.shape[1] // HD
    first = core[0] == 0
    low = jnp.where(first, own[...], peer[...]).astype(jnp.float32)
    high = jnp.where(first, peer[...], own[...]).astype(jnp.float32)
    squares = jnp.sum(low * low, -1, keepdims=True) + jnp.sum(high * high, -1, keepdims=True)
    factor = lax.rsqrt(squares / D + 1e-06)
    normed[:, :half] = (low * factor * gain[:, :half]).astype(jnp.bfloat16)
    normed[:, half:] = (high * factor * gain[:, half:]).astype(jnp.bfloat16)
    q_cols, kv_cols = w_query.shape[1], w_key.shape[1]
    query[...] = jnp.zeros_like(query)

    @pl.loop(0, D // CHUNK)
    def _(i):
        rows = pl.ds(pl.multiple_of(i * CHUNK, CHUNK), CHUNK)
        block = normed[:, rows]
        query[:, :q_cols] += dot(block, w_query[rows, :])
        query[:, q_cols : q_cols + kv_cols] += dot(block, w_key[rows, :])
        query[:, q_cols + kv_cols :] += dot(block, w_value[rows, :])

    key_now[...] = query[:, q_cols : q_cols + kv_cols].astype(jnp.bfloat16)
    value_now[...] = query[:, q_cols + kv_cols :].astype(jnp.bfloat16)
    recent = slots * (step + 1)
    row = lax.broadcasted_iota(jnp.int32, (GROUP * slots, recent), 0)
    column = lax.broadcasted_iota(jnp.int32, (GROUP * slots, recent), 1)
    same = lax.rem(row, slots) == lax.rem(column, slots)
    for head in range(kv_heads):
        lanes = slice(head * HD, (head + 1) * HD)
        q = jnp.concatenate(
            [query[:, (head * GROUP + g) * HD : (head * GROUP + g + 1) * HD] for g in range(GROUP)], 0
        ).astype(jnp.bfloat16)
        k_new = jnp.concatenate([k[:, lanes] for k in past_keys] + [key_now[:, lanes]], 0)
        v_new = jnp.concatenate([v[:, lanes] for v in past_values] + [value_now[:, lanes]], 0)
        contract = (((1,), (1,)), ((), ()))
        scale = HD ** (-0.5)
        s_old = lax.dot_general(q, keys[:, lanes], contract, preferred_element_type=jnp.float32) * scale
        s_old = s_old + jnp.concatenate([bias[...]] * GROUP, 0)
        s_new = lax.dot_general(q, k_new, contract, preferred_element_type=jnp.float32) * scale
        s_new = jnp.where(same, s_new, MASKED)
        top = jnp.maximum(jnp.max(s_old, -1, keepdims=True), jnp.max(s_new, -1, keepdims=True))
        p_old = jnp.exp(s_old - top)
        p_new = jnp.exp(s_new - top)
        total = jnp.sum(p_old, -1, keepdims=True) + jnp.sum(p_new, -1, keepdims=True)
        summed = dot(p_old.astype(jnp.bfloat16), values[:, lanes]) + dot(p_new.astype(jnp.bfloat16), v_new)
        result = (summed / total).astype(jnp.bfloat16)
        for g in range(GROUP):
            at = (head * GROUP + g) * HD
            attn[:, at : at + HD] = result[g * slots : (g + 1) * slots]
    project(attn, w_out, part, (1 - core[0]) * half)


def expand(step, core, own, peer, gain, w_query, w_key, w_value, keys, values, bias, w_out, past_keys, past_values):
    slots, half = own.shape
    kv_cols = w_key.shape[1]
    q_cols = w_query.shape[1]
    whole = pl.BlockSpec(memory_space=VMEM)
    bf16 = lambda *shape: jax.ShapeDtypeStruct(shape, jnp.bfloat16)
    return pl.pallas_call(
        functools.partial(step_kernel, step),
        out_shape=(bf16(slots, half), bf16(slots, q_cols), bf16(slots, kv_cols), bf16(slots, kv_cols)),
        in_specs=[pl.BlockSpec(memory_space=pltpu.SMEM)] + [whole] * (10 + 2 * step),
        out_specs=[whole] * 4,
        scratch_shapes=[VMEM((slots, D), jnp.bfloat16), VMEM((slots, q_cols + 2 * kv_cols), jnp.float32)],
        compiler_params=pltpu.CompilerParams(vmem_limit_bytes=48 << 20),
        cost_estimate=pl.CostEstimate(
            flops=2 * slots * D * (q_cols + 2 * kv_cols), bytes_accessed=21 << 20, transcendentals=1 << 20
        ),
        name="expand",
    )(core, own, peer, gain, w_query, w_key, w_value, keys, values, bias, w_out, *past_keys, *past_values)


def project_kernel(core, attn, w_out, part):
    project(attn, w_out, part, core[0] * part.shape[1])


def project_own(core, attn, w_out):
    whole = pl.BlockSpec(memory_space=VMEM)
    slots, half = attn.shape[0], w_out.shape[1] // 2
    return pl.pallas_call(
        project_kernel,
        out_shape=jax.ShapeDtypeStruct((slots, half), jnp.float32),
        in_specs=[pl.BlockSpec(memory_space=pltpu.SMEM), whole, whole],
        out_specs=whole,
        compiler_params=pltpu.CompilerParams(vmem_limit_bytes=16 << 20),
        cost_estimate=pl.CostEstimate(
            flops=2 * slots * half * attn.shape[1], bytes_accessed=4 << 20, transcendentals=0
        ),
        name="project_own",
    )(core, attn, w_out)


def shards(
    tokens,
    parent_keys,
    parent_values,
    parent_blocks,
    child_parent,
    child_count,
    node_shard,
    attn_gain,
    w_query,
    w_key,
    w_value,
    w_out,
    reward_up,
    reward_out,
):
    groups = lax.axis_size("dp")
    own = lax.axis_index("dp")
    mp = lax.axis_size("mp")
    me = lax.axis_index("mp")
    core = lax.rem(me, 2)
    core_ref = core.reshape(1).astype(jnp.int32)
    children, width = tokens.shape
    half = width // 2
    held, prefix, kv_cols = parent_keys.shape
    capacity = max(2, 2 * children // groups)
    reward_cap = max(2, 3 * children // (2 * groups))
    slots = groups * capacity
    hidden = reward_out.shape[1] // mp
    swap = [(i, i ^ 1) for i in range(mp)]

    parents_all = child_parent.reshape(groups, children)
    source_all = parents_all // held
    local_all = parents_all % held
    rank_all = slot_ranks(source_all, jnp.ones(source_all.shape, bool))
    slot_ids = jnp.arange(capacity)
    my_source = lax.dynamic_index_in_dim(source_all, own, 0, keepdims=False)
    my_rank = lax.dynamic_index_in_dim(rank_all, own, 0, keepdims=False)
    sending = (my_source[None, None, :] == jnp.arange(groups)[:, None, None]) & (
        my_rank[None, None, :] == slot_ids[None, :, None]
    )
    token_half = lax.dynamic_slice_in_dim(tokens, core * half, half, 1)
    outbound = dot(sending.reshape(slots, children).astype(jnp.bfloat16), token_half).astype(jnp.bfloat16)
    arrived = lax.all_to_all(
        outbound.reshape(groups, capacity, half), "dp", split_axis=0, concat_axis=0, tiled=True
    ).reshape(slots, half)

    taking = (source_all[:, None, :] == own) & (rank_all[:, None, :] == slot_ids[None, :, None])
    pick = lambda table: jnp.sum(jnp.where(taking, table[:, None, :], 0), -1)
    row_parent = pick(local_all).reshape(slots)
    lengths = lax.dynamic_slice_in_dim(parent_blocks, own * held, held, 0) * 128
    valid = jnp.arange(prefix)[None, :] < lengths[:, None]
    usable = (row_parent[:, None, None] == jnp.arange(held)[None, :, None]) & valid[None]
    bias = jnp.where(usable, 0.0, MASKED).astype(jnp.float32).reshape(slots, held * prefix)

    up = reward_up[0].reshape(reward_up.shape[1], mp, hidden)
    pieces = [lax.dynamic_index_in_dim(up, me, 1, keepdims=False)]
    for k in range(1, mp):
        piece = lax.dynamic_index_in_dim(up, lax.rem(me + k, mp), 1, keepdims=False)
        pieces.append(lax.ppermute(piece, "mp", [(i, (i + k) % mp) for i in range(mp)]))
    pieces = jnp.stack(pieces)
    mine = jnp.stack(
        [lax.dynamic_index_in_dim(pieces, lax.rem(me - j + mp, mp), 0, keepdims=False) for j in range(mp)]
    ).reshape(width, hidden)
    up_all = lax.all_gather(mine, "dp", axis=0)
    out_all = lax.all_gather(reward_out[0], "dp", axis=0)
    counts = lax.all_gather(child_count[0], "dp", axis=0)

    keys = parent_keys.reshape(held * prefix, kv_cols)
    values = parent_values.reshape(held * prefix, kv_cols)
    gain = attn_gain.reshape(1, width)
    state = arrived.astype(jnp.float32)
    row_own = arrived
    row_peer = lax.ppermute(row_own, "mp", swap)
    past_keys, past_values, rows_own, rows_peer = [], [], [], []
    for step in range(STEPS):
        part, attn, key_now, value_now = expand(
            step, core_ref, row_own, row_peer, gain, w_query, w_key, w_value, keys, values, bias, w_out,
            past_keys, past_values,
        )
        past_keys.append(key_now)
        past_values.append(value_now)
        from_peer = lax.ppermute(part, "mp", swap)
        chip = project_own(core_ref, attn, w_out) + from_peer.astype(jnp.float32)
        sent = chip.astype(jnp.bfloat16)
        for k in range(2, mp, 2):
            chip = chip + lax.ppermute(sent, "mp", [(i, (i + k) % mp) for i in range(mp)]).astype(jnp.float32)
        state = state + chip
        row_own = state.astype(jnp.bfloat16)
        row_peer = lax.ppermute(row_own, "mp", swap)
        rows_own.append(row_own)
        rows_peer.append(row_peer)

    shard_all = node_shard.reshape(groups, children)
    live_all = jnp.arange(children)[None, :] < counts[:, None]
    reward_rank = slot_ranks(shard_all, live_all)
    row_shard = pick(shard_all).reshape(slots)
    row_rank = pick(reward_rank).reshape(groups, capacity)
    row_live = jnp.any(taking & live_all[:, None, :], -1).reshape(slots)
    flat_own = jnp.concatenate(rows_own, 0)
    flat_peer = jnp.concatenate(rows_peer, 0)
    low = jnp.where(core == 0, flat_own, flat_peer)
    high = jnp.where(core == 0, flat_peer, flat_own)
    flat = jnp.concatenate([low, high], 1)
    wide = flat.astype(jnp.float32)
    squares = jnp.sum(wide * wide, -1, keepdims=True)
    lifted = jnp.einsum("nd,rdh->rnh", flat, up_all, preferred_element_type=jnp.float32)
    chosen = (jnp.tile(row_shard, STEPS)[None, :] == jnp.arange(groups)[:, None])[:, :, None]
    lifted = jnp.sum(jnp.where(chosen, lifted, 0.0), 0) * lax.rsqrt(squares / width + 1e-06)
    out_mine = lax.dynamic_slice_in_dim(out_all, me * hidden, hidden, 1)
    row_out = jnp.sum(jnp.where(chosen, out_mine[:, None, :], 0.0), 0)
    scores = jnp.sum(jax.nn.silu(lifted) * row_out, -1).reshape(STEPS, slots)
    place = (row_shard.reshape(groups, capacity) * groups + jnp.arange(groups)[:, None]) * reward_cap + row_rank
    place = place.reshape(slots)
    put = (place[:, None] == jnp.arange(groups * groups * reward_cap)[None, :]) & row_live[:, None]
    table = jnp.sum(jnp.where(put[None], scores[:, :, None], 0.0), 1)
    table = lax.psum(table, ("dp", "mp"))
    return lax.dynamic_slice_in_dim(table, own * groups * reward_cap, groups * reward_cap, 1)


def solution(mesh):
    placed = (
        P("dp", None),
        P("dp", None, "mp"),
        P("dp", None, "mp"),
        P(),
        P(),
        P("dp"),
        P(),
        P(),
        P(None, "mp"),
        P(None, "mp"),
        P(None, "mp"),
        P("mp", None),
        P("dp", "mp", None),
        P("dp", None),
    )
    return jax.shard_map(
        shards, mesh=mesh, in_specs=placed, out_specs=P(None, "dp"), check_vma=False
    )
```

```python
import functools

import jax
import jax.numpy as jnp
from jax import lax
from jax.experimental import pallas as pl
from jax.experimental.pallas import tpu as pltpu
from jax.sharding import PartitionSpec as P

D = 5120
HEADS = 24
KVH = 8
HD = 128
STEPS = 8
GROUP = HEADS // KVH
CHUNK = 512
MASKED = -1e30
VMEM = pltpu.VMEM


def slot_ranks(targets, live):
    count = targets.shape[-1]
    index = jnp.arange(count)
    earlier = index[None, :] < index[:, None]
    same = (targets[:, :, None] == targets[:, None, :]) & earlier[None] & live[:, None, :]
    return jnp.sum(same.astype(jnp.int32), -1)


def in_parts(x):
    parts = []
    for _ in range(3):
        top = lax.reduce_precision(x, 8, 7)
        parts.append(top.astype(jnp.bfloat16))
        x = x - top
    return jnp.stack(parts)


def dot(a, b):
    return jnp.dot(a, b, preferred_element_type=jnp.float32)


def project(attn, w_out, out, first):
    width = out.shape[1]

    @pl.loop(0, width // CHUNK)
    def _(i):
        columns = pl.ds(pl.multiple_of(first + i * CHUNK, CHUNK), CHUNK)
        out[:, pl.ds(pl.multiple_of(i * CHUNK, CHUNK), CHUNK)] = dot(
            attn[...], w_out[:, columns]
        ).astype(out.dtype)


def step_kernel(step, core, own, peer, gain, w_query, w_key, w_value, keys, values, bias, w_out, *rest):
    past_keys, past_values = rest[:step], rest[step : 2 * step]
    part, attn, key_now, value_now, normed, query = rest[2 * step :]
    half = own.shape[1]
    slots = own.shape[0]
    kv_heads = w_key.shape[1] // HD
    first = core[0] == 0
    low = jnp.where(first, own[...], peer[...]).astype(jnp.float32)
    high = jnp.where(first, peer[...], own[...]).astype(jnp.float32)
    squares = jnp.sum(low * low, -1, keepdims=True) + jnp.sum(high * high, -1, keepdims=True)
    factor = lax.rsqrt(squares / D + 1e-06)
    normed[:, :half] = (low * factor * gain[:, :half]).astype(jnp.bfloat16)
    normed[:, half:] = (high * factor * gain[:, half:]).astype(jnp.bfloat16)
    q_cols, kv_cols = w_query.shape[1], w_key.shape[1]
    query[...] = jnp.zeros_like(query)

    @pl.loop(0, D // CHUNK)
    def _(i):
        rows = pl.ds(pl.multiple_of(i * CHUNK, CHUNK), CHUNK)
        block = normed[:, rows]
        query[:, :q_cols] += dot(block, w_query[rows, :])
        query[:, q_cols : q_cols + kv_cols] += dot(block, w_key[rows, :])
        query[:, q_cols + kv_cols :] += dot(block, w_value[rows, :])

    key_now[...] = query[:, q_cols : q_cols + kv_cols].astype(jnp.bfloat16)
    value_now[...] = query[:, q_cols + kv_cols :].astype(jnp.bfloat16)
    recent = slots * (step + 1)
    row = lax.broadcasted_iota(jnp.int32, (GROUP * slots, recent), 0)
    column = lax.broadcasted_iota(jnp.int32, (GROUP * slots, recent), 1)
    same = lax.rem(row, slots) == lax.rem(column, slots)
    for head in range(kv_heads):
        lanes = slice(head * HD, (head + 1) * HD)
        q = jnp.concatenate(
            [query[:, (head * GROUP + g) * HD : (head * GROUP + g + 1) * HD] for g in range(GROUP)], 0
        ).astype(jnp.bfloat16)
        k_new = jnp.concatenate([k[:, lanes] for k in past_keys] + [key_now[:, lanes]], 0)
        v_new = jnp.concatenate([v[:, lanes] for v in past_values] + [value_now[:, lanes]], 0)
        contract = (((1,), (1,)), ((), ()))
        scale = HD ** (-0.5)
        s_old = lax.dot_general(q, keys[:, lanes], contract, preferred_element_type=jnp.float32) * scale
        s_old = s_old + jnp.concatenate([bias[...]] * GROUP, 0)
        s_new = lax.dot_general(q, k_new, contract, preferred_element_type=jnp.float32) * scale
        s_new = jnp.where(same, s_new, MASKED)
        top = jnp.maximum(jnp.max(s_old, -1, keepdims=True), jnp.max(s_new, -1, keepdims=True))
        p_old = jnp.exp(s_old - top)
        p_new = jnp.exp(s_new - top)
        total = jnp.sum(p_old, -1, keepdims=True) + jnp.sum(p_new, -1, keepdims=True)
        summed = dot(p_old.astype(jnp.bfloat16), values[:, lanes]) + dot(p_new.astype(jnp.bfloat16), v_new)
        result = (summed / total).astype(jnp.bfloat16)
        for g in range(GROUP):
            at = (head * GROUP + g) * HD
            attn[:, at : at + HD] = result[g * slots : (g + 1) * slots]
    project(attn, w_out, part, (1 - core[0]) * half)


def held(x):
    return pltpu.with_memory_space_constraint(x, VMEM)


def expand(step, core, own, peer, gain, w_query, w_key, w_value, keys, values, bias, w_out, past_keys, past_values):
    slots, half = own.shape
    kv_cols = w_key.shape[1]
    q_cols = w_query.shape[1]
    whole = pl.BlockSpec(memory_space=VMEM)
    bf16 = lambda *shape: jax.ShapeDtypeStruct(shape, jnp.bfloat16)
    return pl.pallas_call(
        functools.partial(step_kernel, step),
        out_shape=(bf16(slots, half), bf16(slots, q_cols), bf16(slots, kv_cols), bf16(slots, kv_cols)),
        in_specs=[pl.BlockSpec(memory_space=pltpu.SMEM)] + [whole] * (10 + 2 * step),
        out_specs=[whole] * 4,
        scratch_shapes=[VMEM((slots, D), jnp.bfloat16), VMEM((slots, q_cols + 2 * kv_cols), jnp.float32)],
        compiler_params=pltpu.CompilerParams(vmem_limit_bytes=20 << 20),
        cost_estimate=pl.CostEstimate(
            flops=2 * slots * D * (q_cols + 2 * kv_cols), bytes_accessed=21 << 20, transcendentals=1 << 20
        ),
        name="expand",
    )(core, own, peer, gain, w_query, w_key, w_value, keys, values, bias, w_out, *past_keys, *past_values)


def project_kernel(core, attn, w_out, part):
    project(attn, w_out, part, core[0] * part.shape[1])


def project_own(core, attn, w_out):
    whole = pl.BlockSpec(memory_space=VMEM)
    slots, half = attn.shape[0], w_out.shape[1] // 2
    return pl.pallas_call(
        project_kernel,
        out_shape=jax.ShapeDtypeStruct((slots, half), jnp.float32),
        in_specs=[pl.BlockSpec(memory_space=pltpu.SMEM), whole, whole],
        out_specs=whole,
        compiler_params=pltpu.CompilerParams(vmem_limit_bytes=8 << 20),
        cost_estimate=pl.CostEstimate(
            flops=2 * slots * half * attn.shape[1], bytes_accessed=4 << 20, transcendentals=0
        ),
        name="project_own",
    )(core, attn, w_out)


def shards(
    tokens,
    parent_keys,
    parent_values,
    parent_blocks,
    child_parent,
    child_count,
    node_shard,
    attn_gain,
    w_query,
    w_key,
    w_value,
    w_out,
    reward_up,
    reward_out,
):
    groups = lax.axis_size("dp")
    own = lax.axis_index("dp")
    mp = lax.axis_size("mp")
    me = lax.axis_index("mp")
    core = lax.rem(me, 2)
    core_ref = core.reshape(1).astype(jnp.int32)
    children, width = tokens.shape
    half = width // 2
    parents, prefix, kv_cols = parent_keys.shape
    capacity = max(2, 2 * children // groups)
    reward_cap = max(2, 3 * children // (2 * groups))
    slots = groups * capacity
    hidden = reward_out.shape[1] // mp
    swap = [(i, i ^ 1) for i in range(mp)]

    parents_all = child_parent.reshape(groups, children)
    source_all = parents_all // parents
    local_all = parents_all % parents
    rank_all = slot_ranks(source_all, jnp.ones(source_all.shape, bool))
    slot_ids = jnp.arange(capacity)
    my_source = lax.dynamic_index_in_dim(source_all, own, 0, keepdims=False)
    my_rank = lax.dynamic_index_in_dim(rank_all, own, 0, keepdims=False)
    sending = (my_source[None, None, :] == jnp.arange(groups)[:, None, None]) & (
        my_rank[None, None, :] == slot_ids[None, :, None]
    )
    my_shard = lax.dynamic_index_in_dim(node_shard.reshape(groups, children), own, 0, keepdims=False)
    live = jnp.arange(children) < child_count[0]
    my_reward_rank = slot_ranks(my_shard[None], live[None])[0]
    notes = jnp.stack([live, my_reward_rank], 1).astype(jnp.bfloat16)
    token_half = lax.dynamic_slice_in_dim(tokens, core * half, half, 1)
    rows_out = jnp.concatenate([token_half, notes], 1)
    outbound = dot(sending.reshape(slots, children).astype(jnp.bfloat16), rows_out).astype(jnp.bfloat16)
    outbound = outbound.reshape(groups, capacity, half + 2)
    scales = in_parts(reward_out[0]).reshape(capacity, -1)
    scales = jnp.broadcast_to(scales[None], (groups, *scales.shape))
    spare = -(scales.shape[2] + 2) % 128
    outbound = jnp.pad(jnp.concatenate([outbound, scales], 2), ((0, 0), (0, 0), (0, spare)))
    arrived = lax.all_to_all(outbound, "dp", split_axis=0, concat_axis=0, tiled=True)
    row_live = (arrived[:, :, half] > 0.5).reshape(slots)
    row_rank = arrived[:, :, half + 1].astype(jnp.int32)
    out_all = arrived[:, :, half + 2 : half + 2 + scales.shape[2]].reshape(groups, 3, -1)
    out_all = jnp.sum(out_all.astype(jnp.float32), 1)
    arrived = arrived[:, :, :half].reshape(slots, half)

    taking = (source_all[:, None, :] == own) & (rank_all[:, None, :] == slot_ids[None, :, None])
    pick = lambda table: jnp.sum(jnp.where(taking, table[:, None, :], 0), -1)
    row_parent = pick(local_all).reshape(slots)
    lengths = lax.dynamic_slice_in_dim(parent_blocks, own * parents, parents, 0) * 128
    valid = jnp.arange(prefix)[None, :] < lengths[:, None]
    usable = (row_parent[:, None, None] == jnp.arange(parents)[None, :, None]) & valid[None]
    bias = jnp.where(usable, 0.0, MASKED).astype(jnp.float32).reshape(slots, parents * prefix)

    up = jnp.transpose(reward_up[0].reshape(reward_up.shape[1], mp, hidden), (1, 0, 2))
    up = lax.all_to_all(up, "mp", split_axis=0, concat_axis=0, tiled=True).reshape(width, hidden)
    up_all = lax.all_gather(up, "dp", axis=0)

    keys = held(parent_keys.reshape(parents * prefix, kv_cols))
    values = held(parent_values.reshape(parents * prefix, kv_cols))
    gain = attn_gain.reshape(1, width)
    w_query, w_key, w_value, w_out = held(w_query), held(w_key), held(w_value), held(w_out)
    state = arrived.astype(jnp.float32)
    row_own = arrived
    row_peer = lax.ppermute(row_own, "mp", swap)
    past_keys, past_values, rows_own, rows_peer = [], [], [], []
    for step in range(STEPS):
        part, attn, key_now, value_now = expand(
            step, core_ref, row_own, row_peer, gain, w_query, w_key, w_value, keys, values, bias, w_out,
            past_keys, past_values,
        )
        past_keys.append(key_now)
        past_values.append(value_now)
        from_peer = lax.ppermute(part, "mp", swap)
        chip = project_own(core_ref, attn, w_out) + from_peer.astype(jnp.float32)
        sent = chip.astype(jnp.bfloat16)
        for k in range(2, mp, 2):
            chip = chip + lax.ppermute(sent, "mp", [(i, (i + k) % mp) for i in range(mp)]).astype(jnp.float32)
        state = state + chip
        row_own = state.astype(jnp.bfloat16)
        row_peer = lax.ppermute(row_own, "mp", swap)
        rows_own.append(row_own)
        rows_peer.append(row_peer)

    row_shard = pick(node_shard.reshape(groups, children)).reshape(slots)
    flat_own = jnp.concatenate(rows_own, 0)
    flat_peer = jnp.concatenate(rows_peer, 0)
    low = jnp.where(core == 0, flat_own, flat_peer)
    high = jnp.where(core == 0, flat_peer, flat_own)
    flat = jnp.concatenate([low, high], 1)
    wide = flat.astype(jnp.float32)
    squares = jnp.sum(wide * wide, -1, keepdims=True)
    lifted = jnp.einsum("nd,rdh->rnh", flat, up_all, preferred_element_type=jnp.float32)
    chosen = (jnp.tile(row_shard, STEPS)[None, :] == jnp.arange(groups)[:, None])[:, :, None]
    lifted = jnp.sum(jnp.where(chosen, lifted, 0.0), 0) * lax.rsqrt(squares / width + 1e-06)
    out_mine = lax.dynamic_slice_in_dim(out_all, me * hidden, hidden, 1)
    row_out = jnp.sum(jnp.where(chosen, out_mine[:, None, :], 0.0), 0)
    scores = jnp.sum(jax.nn.silu(lifted) * row_out, -1).reshape(STEPS, slots)
    place = (row_shard.reshape(groups, capacity) * groups + jnp.arange(groups)[:, None]) * reward_cap + row_rank
    place = place.reshape(slots)
    put = (place[:, None] == jnp.arange(groups * groups * reward_cap)[None, :]) & row_live[:, None]
    table = jnp.sum(jnp.where(put[None], scores[:, :, None], 0.0), 1)
    table = table + lax.ppermute(table, "mp", swap)
    total = table
    for k in range(2, mp, 2):
        total = total + lax.ppermute(table, "mp", [(i, (i + k) % mp) for i in range(mp)])
    total = jnp.transpose(total.reshape(STEPS, groups, groups * reward_cap), (1, 0, 2))
    return jnp.sum(lax.all_to_all(total, "dp", split_axis=0, concat_axis=0, tiled=True), 0)


def solution(mesh):
    placed = (
        P("dp", None),
        P("dp", None, "mp"),
        P("dp", None, "mp"),
        P(),
        P(),
        P("dp"),
        P(),
        P(),
        P(None, "mp"),
        P(None, "mp"),
        P(None, "mp"),
        P("mp", None),
        P("dp", "mp", None),
        P("dp", None),
    )
    return jax.shard_map(
        shards, mesh=mesh, in_specs=placed, out_specs=P(None, "dp"), check_vma=False
    )
```

```python
import functools

import jax
import jax.numpy as jnp
from jax import lax
from jax.experimental import pallas as pl
from jax.experimental.pallas import tpu as pltpu
from jax.sharding import PartitionSpec as P

D = 5120
HEADS = 24
KVH = 8
HD = 128
STEPS = 8
GROUP = HEADS // KVH
CHUNK = 512
MASKED = -1e30
VMEM = pltpu.VMEM
NOTES = 128
LIVE, RANK, SHARD, PARENT, SOURCE = range(5)


def dot(a, b):
    return jnp.dot(a, b, preferred_element_type=jnp.float32)


def held(x):
    return pltpu.with_memory_space_constraint(x, VMEM)


def struct(shape, dtype=jnp.bfloat16):
    return jax.ShapeDtypeStruct(shape, dtype)


WHOLE = pl.BlockSpec(memory_space=VMEM)
SCALARS = pl.BlockSpec(memory_space=pltpu.SMEM)


def in_parts(x):
    parts = []
    for _ in range(3):
        top = lax.reduce_precision(x, 8, 7)
        parts.append(top.astype(jnp.bfloat16))
        x = x - top
    return parts


def earlier_alike(targets, live):
    index = jnp.arange(targets.shape[0])
    same = (targets[:, None] == targets[None, :]) & (index[None, :] < index[:, None]) & live[None, :]
    return jnp.sum(same.astype(jnp.int32), -1)


def dispatch_kernel(core, slot, tokens, notes, extra, *blocks):
    children, half = tokens.shape[0], tokens.shape[1] // 2
    capacity = blocks[0].shape[0]
    slots = capacity * len(blocks)
    rows = lax.broadcasted_iota(jnp.int32, (slots, children), 0)
    put = (rows == slot[...]).astype(jnp.bfloat16)
    token_half = tokens[:, pl.ds(pl.multiple_of(core[0] * half, half), half)]
    token_rows = dot(put, token_half)
    note_rows = dot(put, notes[...])
    top = lax.broadcasted_iota(jnp.int32, (capacity, extra.shape[1]), 0) == 0
    shared = jnp.where(top, extra[...].astype(jnp.float32), 0.0)
    for k, block in enumerate(blocks):
        at = slice(k * capacity, (k + 1) * capacity)
        block[...] = jnp.concatenate([token_rows[at], note_rows[at], shared], 1).astype(jnp.bfloat16)


def dispatch(core, slot, tokens, notes, extra, groups, capacity):
    block = struct((capacity, tokens.shape[1] // 2 + NOTES + extra.shape[1]))
    return pl.pallas_call(
        dispatch_kernel,
        out_shape=(block,) * groups,
        in_specs=[SCALARS] + [WHOLE] * 4,
        out_specs=[WHOLE] * groups,
        compiler_params=pltpu.CompilerParams(vmem_limit_bytes=8 << 20),
        name="dispatch",
    )(core, slot, tokens, notes, extra)


def pack_kernel(offset, hidden, prefix, ids, blocks_held, sources, *rest):
    blocks, (row, notes, bias, scale, over) = rest[:-5], rest[-5:]
    own = ids[1]
    groups, capacity = len(blocks), blocks[0].shape[0]
    rows, half = row.shape
    slots = groups * capacity
    arrived = jnp.concatenate([block[...].astype(jnp.float32) for block in blocks], 0)
    live = arrived[:, half + LIVE : half + LIVE + 1]
    first = lax.broadcasted_iota(jnp.int32, (slots, slots), 0)
    second = lax.broadcasted_iota(jnp.int32, (slots, slots), 1)
    place = jnp.sum(jnp.where(first < second, live, 0.0), 0, keepdims=True)
    kept = jnp.sum(jnp.where(first == second, live, 0.0), 0, keepdims=True) > 0.5
    wanted = lax.broadcasted_iota(jnp.int32, (rows, slots), 0) + offset
    take = (wanted == place.astype(jnp.int32)) & kept
    take = take.astype(jnp.float32).astype(jnp.bfloat16)
    row[...] = dot(take, arrived[:, :half].astype(jnp.bfloat16)).astype(jnp.bfloat16)
    note = dot(take, arrived[:, half : half + NOTES].astype(jnp.bfloat16))
    notes[...] = note
    parent = note[:, PARENT : PARENT + 1].astype(jnp.int32)
    parents = bias.shape[1] // prefix
    position = lax.broadcasted_iota(jnp.int32, (rows, prefix), 1)
    for p in range(parents):
        usable = (parent == p) & (position < blocks_held[own * parents + p] * 128)
        bias[:, p * prefix : (p + 1) * prefix] = jnp.where(usable, 0.0, MASKED)
    base = half + NOTES
    load = jnp.zeros((groups, sources.shape[1]), jnp.float32)
    target = lax.broadcasted_iota(jnp.int32, load.shape, 0)
    child = lax.broadcasted_iota(jnp.int32, (1, sources.shape[1]), 1)
    for k in range(groups):
        head = arrived[k * capacity : k * capacity + 1, base:]
        scale[k : k + 1, :] = head[:, :hidden] + head[:, hidden : 2 * hidden] + head[:, 2 * hidden : 3 * hidden]
        count = head[:, 3 * hidden : 3 * hidden + 1].astype(jnp.int32)
        source = sources[pl.ds(lax.rem(own - k + groups, groups), 1), :]
        load = load + jnp.where((source == target) & (child < count), 1.0, 0.0)
    most = jnp.max(jnp.sum(load, -1, keepdims=True), 0, keepdims=True)
    over[...] = jnp.broadcast_to((most > rows).astype(jnp.int32), over.shape)


def pack(offset, rows, hidden, prefix, ids, blocks_held, sources, blocks):
    groups = len(blocks)
    half = D // 2
    parents = blocks_held.shape[0] // groups
    return pl.pallas_call(
        functools.partial(pack_kernel, offset, hidden, prefix),
        out_shape=(
            struct((rows, half)),
            struct((rows, NOTES), jnp.float32),
            struct((rows, parents * prefix), jnp.float32),
            struct((groups, hidden), jnp.float32),
            struct((8, 128), jnp.int32),
        ),
        in_specs=[SCALARS, SCALARS] + [WHOLE] * (1 + groups),
        out_specs=[WHOLE] * 5,
        compiler_params=pltpu.CompilerParams(vmem_limit_bytes=12 << 20),
        name="pack",
    )(ids, blocks_held, sources, *blocks)


def project(attn, w_out, out, first):
    width = out.shape[1]

    @pl.loop(0, width // CHUNK)
    def _(i):
        columns = pl.ds(pl.multiple_of(first + i * CHUNK, CHUNK), CHUNK)
        out[:, pl.ds(pl.multiple_of(i * CHUNK, CHUNK), CHUNK)] = dot(
            attn[...], w_out[:, columns]
        ).astype(out.dtype)


def step_kernel(step, ids, own, peer, gain, w_query, w_key, w_value, keys, values, bias, w_out, *rest):
    past_keys, past_values = rest[:step], rest[step : 2 * step]
    part, attn, key_now, value_now, normed, query = rest[2 * step :]
    half = own.shape[1]
    slots = own.shape[0]
    kv_heads = w_key.shape[1] // HD
    core = ids[0]
    first = core == 0
    low = jnp.where(first, own[...], peer[...]).astype(jnp.float32)
    high = jnp.where(first, peer[...], own[...]).astype(jnp.float32)
    squares = jnp.sum(low * low, -1, keepdims=True) + jnp.sum(high * high, -1, keepdims=True)
    factor = lax.rsqrt(squares / D + 1e-06)
    normed[:, :half] = (low * factor * gain[:, :half]).astype(jnp.bfloat16)
    normed[:, half:] = (high * factor * gain[:, half:]).astype(jnp.bfloat16)
    q_cols, kv_cols = w_query.shape[1], w_key.shape[1]
    query[...] = jnp.zeros_like(query)

    @pl.loop(0, D // CHUNK)
    def _(i):
        rows = pl.ds(pl.multiple_of(i * CHUNK, CHUNK), CHUNK)
        block = normed[:, rows]
        query[:, :q_cols] += dot(block, w_query[rows, :])
        query[:, q_cols : q_cols + kv_cols] += dot(block, w_key[rows, :])
        query[:, q_cols + kv_cols :] += dot(block, w_value[rows, :])

    key_now[...] = query[:, q_cols : q_cols + kv_cols].astype(jnp.bfloat16)
    value_now[...] = query[:, q_cols + kv_cols :].astype(jnp.bfloat16)
    recent = slots * (step + 1)
    row = lax.broadcasted_iota(jnp.int32, (GROUP * slots, recent), 0)
    column = lax.broadcasted_iota(jnp.int32, (GROUP * slots, recent), 1)
    same = lax.rem(row, slots) == lax.rem(column, slots)
    for head in range(kv_heads):
        lanes = slice(head * HD, (head + 1) * HD)
        q = jnp.concatenate(
            [query[:, (head * GROUP + g) * HD : (head * GROUP + g + 1) * HD] for g in range(GROUP)], 0
        ).astype(jnp.bfloat16)
        k_new = jnp.concatenate([k[:, lanes] for k in past_keys] + [key_now[:, lanes]], 0)
        v_new = jnp.concatenate([v[:, lanes] for v in past_values] + [value_now[:, lanes]], 0)
        contract = (((1,), (1,)), ((), ()))
        scale = HD ** (-0.5)
        s_old = lax.dot_general(q, keys[:, lanes], contract, preferred_element_type=jnp.float32) * scale
        s_old = s_old + jnp.concatenate([bias[...]] * GROUP, 0)
        s_new = lax.dot_general(q, k_new, contract, preferred_element_type=jnp.float32) * scale
        s_new = jnp.where(same, s_new, MASKED)
        top = jnp.maximum(jnp.max(s_old, -1, keepdims=True), jnp.max(s_new, -1, keepdims=True))
        p_old = jnp.exp(s_old - top)
        p_new = jnp.exp(s_new - top)
        total = jnp.sum(p_old, -1, keepdims=True) + jnp.sum(p_new, -1, keepdims=True)
        summed = dot(p_old.astype(jnp.bfloat16), values[:, lanes]) + dot(p_new.astype(jnp.bfloat16), v_new)
        result = (summed / total).astype(jnp.bfloat16)
        for g in range(GROUP):
            at = (head * GROUP + g) * HD
            attn[:, at : at + HD] = result[g * slots : (g + 1) * slots]
    project(attn, w_out, part, (1 - core) * half)


def expand(step, ids, own, peer, gain, w_query, w_key, w_value, keys, values, bias, w_out, past_keys, past_values):
    slots, half = own.shape
    kv_cols = w_key.shape[1]
    q_cols = w_query.shape[1]
    return pl.pallas_call(
        functools.partial(step_kernel, step),
        out_shape=(struct((slots, half)), struct((slots, q_cols)), struct((slots, kv_cols)), struct((slots, kv_cols))),
        in_specs=[SCALARS] + [WHOLE] * (10 + 2 * step),
        out_specs=[WHOLE] * 4,
        scratch_shapes=[VMEM((slots, D), jnp.bfloat16), VMEM((slots, q_cols + 2 * kv_cols), jnp.float32)],
        compiler_params=pltpu.CompilerParams(vmem_limit_bytes=16 << 20),
        cost_estimate=pl.CostEstimate(
            flops=2 * slots * D * (q_cols + 2 * kv_cols), bytes_accessed=21 << 20, transcendentals=1 << 20
        ),
        name="expand",
    )(ids, own, peer, gain, w_query, w_key, w_value, keys, values, bias, w_out, *past_keys, *past_values)


def project_kernel(ids, attn, w_out, part):
    project(attn, w_out, part, ids[0] * part.shape[1])


def project_own(ids, attn, w_out):
    slots, half = attn.shape[0], w_out.shape[1] // 2
    return pl.pallas_call(
        project_kernel,
        out_shape=struct((slots, half), jnp.float32),
        in_specs=[SCALARS, WHOLE, WHOLE],
        out_specs=WHOLE,
        compiler_params=pltpu.CompilerParams(vmem_limit_bytes=8 << 20),
        cost_estimate=pl.CostEstimate(
            flops=2 * slots * half * attn.shape[1], bytes_accessed=4 << 20, transcendentals=0
        ),
        name="project_own",
    )(ids, attn, w_out)


def cut_kernel(mp, ids, up, *pieces):
    hidden = up.shape[2] // mp
    for k, piece in enumerate(pieces):
        target = lax.rem(ids[2] + k, mp)
        for m in range(mp):

            @pl.when(target == m)
            def _():
                piece[...] = up[0, :, m * hidden : (m + 1) * hidden]


def cut(mp, ids, up):
    piece = struct((up.shape[1], up.shape[2] // mp))
    return pl.pallas_call(
        functools.partial(cut_kernel, mp),
        out_shape=(piece,) * mp,
        in_specs=[SCALARS, WHOLE],
        out_specs=[WHOLE] * mp,
        compiler_params=pltpu.CompilerParams(vmem_limit_bytes=12 << 20),
        name="cut",
    )(ids, up)


def join_kernel(ids, *refs):
    pieces, whole, sems = refs[:-2], refs[-2], refs[-1]
    mp, rows = len(pieces), pieces[0].shape[0]
    copies = []
    for k, piece in enumerate(pieces):
        source = lax.rem(ids[2] - k + mp, mp)
        copies.append(pltpu.make_async_copy(piece, whole.at[pl.ds(source * rows, rows)], sems.at[k]))
        copies[-1].start()
    for copy in copies:
        copy.wait()


def join(ids, pieces):
    rows, hidden = pieces[0].shape
    anywhere = pl.BlockSpec(memory_space=pl.ANY)
    return pl.pallas_call(
        join_kernel,
        out_shape=struct((rows * len(pieces), hidden)),
        in_specs=[SCALARS] + [anywhere] * len(pieces),
        out_specs=anywhere,
        scratch_shapes=[pltpu.SemaphoreType.DMA((len(pieces),))],
        compiler_params=pltpu.CompilerParams(vmem_limit_bytes=2 << 20),
        name="join",
    )(ids, *pieces)


def score_kernel(steps, groups, ids, notes, scale, *refs):
    own_rows, peer_rows = refs[:steps], refs[steps : 2 * steps]
    ups = refs[2 * steps : 2 * steps + groups]
    out, flat, buffer, sems = refs[2 * steps + groups :]
    rows, half = own_rows[0].shape
    hidden = ups[0].shape[1]

    def fetch(k, slot):
        return pltpu.make_async_copy(ups[k], buffer.at[slot], sems.at[slot])

    fetch(0, 0).start()
    fetch(1, 1).start()
    first = ids[0] == 0
    for t in range(steps):
        at = slice(t * rows, (t + 1) * rows)
        flat[at, :half] = jnp.where(first, own_rows[t][...], peer_rows[t][...])
        flat[at, half:] = jnp.where(first, peer_rows[t][...], own_rows[t][...])
    squares = jnp.zeros((steps * rows, 1), jnp.float32)
    for i in range(0, D, CHUNK):
        wide = flat[:, i : i + CHUNK].astype(jnp.float32)
        squares = squares + jnp.sum(wide * wide, -1, keepdims=True)
    factor = lax.rsqrt(squares / D + 1e-06)
    shard = notes[:, SHARD : SHARD + 1].astype(jnp.int32)
    block = lax.rem(ids[1] - shard + groups, groups)
    block = jnp.concatenate([block] * steps, 0)
    z = jnp.zeros((steps * rows, hidden), jnp.float32)
    gain = jnp.zeros((steps * rows, hidden), jnp.float32)
    for k in range(0, groups, 2):
        slot = (k // 2 % 2) * 2
        if k + 2 < groups:
            fetch(k + 2, 2 - slot).start()
            fetch(k + 3, 3 - slot).start()
        fetch(k, slot).wait()
        fetch(k + 1, slot + 1).wait()

        def body(i, acc):
            at = pl.ds(pl.multiple_of(i * CHUNK, CHUNK), CHUNK)
            pair = jnp.concatenate([buffer[slot, at, :], buffer[slot + 1, at, :]], 1)
            return acc + dot(flat[:, at], pair)

        both = lax.fori_loop(0, D // CHUNK, body, jnp.zeros((steps * rows, 2 * hidden), jnp.float32))
        for j in range(2):
            here = block == k + j
            z = z + jnp.where(here, both[:, j * hidden : (j + 1) * hidden], 0.0)
            gain = gain + jnp.where(here, scale[k + j : k + j + 1, :], 0.0)
    z = z * factor
    total = jnp.sum(z * jax.nn.sigmoid(z) * gain, -1, keepdims=True)
    out[...] = jnp.broadcast_to(total, out.shape)


def score(ids, notes, scale, own_rows, peer_rows, ups):
    steps, groups = len(own_rows), len(ups)
    rows = own_rows[0].shape[0]
    hidden = ups[0].shape[1]
    anywhere = pl.BlockSpec(memory_space=pl.ANY)
    return pl.pallas_call(
        functools.partial(score_kernel, steps, groups),
        out_shape=struct((steps * rows, 128), jnp.float32),
        in_specs=[SCALARS] + [WHOLE] * (2 + 2 * steps) + [anywhere] * groups,
        out_specs=WHOLE,
        scratch_shapes=[
            VMEM((steps * rows, D), jnp.bfloat16),
            VMEM((4, D, hidden), jnp.bfloat16),
            pltpu.SemaphoreType.DMA((4,)),
        ],
        compiler_params=pltpu.CompilerParams(vmem_limit_bytes=20 << 20),
        cost_estimate=pl.CostEstimate(
            flops=2 * steps * rows * D * hidden * groups, bytes_accessed=2 * D * hidden * groups, transcendentals=0
        ),
        name="score",
    )(ids, notes, scale, *own_rows, *peer_rows, *ups)


def place_kernel(groups, cap, ids, notes, *refs):
    scores, table = refs[:-1], refs[-1]
    rows = notes.shape[0]
    number = lambda lane: notes[:, lane : lane + 1].astype(jnp.int32)
    target = lax.rem(number(SHARD) - ids[1] + groups, groups)
    at = number(SOURCE) * cap + number(RANK)
    live = notes[:, LIVE : LIVE + 1] > 0.5
    column = lax.broadcasted_iota(jnp.int32, (rows, groups * cap), 1)
    spots = [(column == at) & (target == k) & live for k in range(groups)]
    t = 0
    for score in scores:
        for i in range(score.shape[0] // rows):
            value = score[i * rows : (i + 1) * rows, : 1]
            for k in range(groups):
                table[k, t : t + 1, :] = jnp.sum(jnp.where(spots[k], value, 0.0), 0, keepdims=True)
            t += 1


def place(groups, cap, ids, notes, scores):
    return pl.pallas_call(
        functools.partial(place_kernel, groups, cap),
        out_shape=struct((groups, STEPS, groups * cap), jnp.float32),
        in_specs=[SCALARS] + [WHOLE] * (1 + len(scores)),
        out_specs=WHOLE,
        compiler_params=pltpu.CompilerParams(vmem_limit_bytes=8 << 20),
        name="place",
    )(ids, notes, *scores)


def shards(
    tokens,
    parent_keys,
    parent_values,
    parent_blocks,
    child_parent,
    child_count,
    node_shard,
    attn_gain,
    w_query,
    w_key,
    w_value,
    w_out,
    reward_up,
    reward_out,
):
    groups = lax.axis_size("dp")
    own = lax.axis_index("dp")
    mp = lax.axis_size("mp")
    me = lax.axis_index("mp")
    core = lax.rem(me, 2)
    ids = jnp.stack([core, own, me]).astype(jnp.int32)
    children, width = tokens.shape
    parents, prefix, kv_cols = parent_keys.shape
    capacity = max(2, 2 * children // groups)
    reward_cap = max(2, 3 * children // (2 * groups))
    slots = groups * capacity
    rows = min(slots, 3 * children // 2)
    hidden = reward_out.shape[1] // mp
    swap = [(i, i ^ 1) for i in range(mp)]
    shift = lambda count, k: [(i, (i + k) % count) for i in range(count)]

    pieces = cut(mp, ids, reward_up)
    pieces = [pieces[0]] + [lax.ppermute(pieces[k], "mp", shift(mp, k)) for k in range(1, mp)]
    up_here = join(ids, pieces)
    ups = [up_here] + [lax.ppermute(up_here, "dp", shift(groups, k)) for k in range(1, groups)]

    here = lambda table: lax.dynamic_slice_in_dim(table, own * children, children, 0)
    my_parents, my_shard = here(child_parent), here(node_shard)
    my_source = my_parents // parents
    live = jnp.arange(children) < child_count[0]
    slot = lax.rem(my_source - own + groups, groups) * capacity + earlier_alike(my_source, live)
    slot = jnp.where(live, slot, -1)
    notes = jnp.stack(
        [live.astype(jnp.int32), earlier_alike(my_shard, live), my_shard, my_parents % parents,
         jnp.full((children,), own, jnp.int32)], 1,
    ).astype(jnp.bfloat16)
    notes = jnp.pad(notes, ((0, 0), (0, NOTES - notes.shape[1])))
    my_scale = lax.dynamic_slice_in_dim(reward_out[0], me * hidden, hidden, 0)
    extra = jnp.concatenate(in_parts(my_scale) + [child_count.astype(jnp.bfloat16)])
    extra = jnp.pad(extra, (0, -extra.shape[0] % 128))[None]
    sources = (child_parent // parents).reshape(groups, children)
    core_ids, slot, tokens, notes, extra, sources = lax.optimization_barrier(
        (ids, slot[None], tokens, notes, extra, sources)
    )
    blocks = dispatch(core_ids, slot, tokens, notes, extra, groups, capacity)
    blocks = [blocks[0]] + [lax.ppermute(blocks[k], "dp", shift(groups, k)) for k in range(1, groups)]

    keys = parent_keys.reshape(parents * prefix, kv_cols)
    values = parent_values.reshape(parents * prefix, kv_cols)
    gain = attn_gain.reshape(1, width)

    def run(offset, blocks, ups, sources, ids, gain, keys, values, w_query, w_key, w_value, w_out, parent_blocks):
        row_own, notes, bias, scale, over = pack(
            offset, rows, hidden, prefix, ids, parent_blocks, sources, blocks
        )
        keys, values = held(keys), held(values)
        w_query, w_key, w_value, w_out = held(w_query), held(w_key), held(w_value), held(w_out)
        state = row_own.astype(jnp.float32)
        row_peer = lax.ppermute(row_own, "mp", swap)
        past_keys, past_values, rows_own, rows_peer, scores = [], [], [], [], []
        for step in range(STEPS):
            part, attn, key_now, value_now = expand(
                step, ids, row_own, row_peer, gain, w_query, w_key, w_value, keys, values, bias, w_out,
                past_keys, past_values,
            )
            past_keys.append(key_now)
            past_values.append(value_now)
            from_peer = lax.ppermute(part, "mp", swap)
            chip = project_own(ids, attn, w_out) + from_peer.astype(jnp.float32)
            sent = chip.astype(jnp.bfloat16)
            for k in range(2, mp, 2):
                chip = chip + lax.ppermute(sent, "mp", shift(mp, k)).astype(jnp.float32)
            state = state + chip
            row_own = state.astype(jnp.bfloat16)
            row_peer = lax.ppermute(row_own, "mp", swap)
            rows_own.append(row_own)
            rows_peer.append(row_peer)
        for first, last in ((0, 4), (4, 7), (7, 8)):
            scores.append(score(ids, notes, scale, rows_own[first:last], rows_peer[first:last], ups))
        return place(groups, reward_cap, ids, notes, scores), over

    operands = (blocks, ups, sources, ids, gain, keys, values, w_query, w_key, w_value, w_out, parent_blocks)
    table, over = run(0, *operands)
    if rows < slots:
        table, over, operands = lax.optimization_barrier((table, over, operands))
        table = lax.cond(
            over[0, 0] > 0, lambda table, *args: table + run(rows, *args)[0], lambda table, *args: table,
            table, *operands,
        )

    total = table[0]
    for k in range(1, groups):
        total = total + lax.ppermute(table[k], "dp", shift(groups, k))
    total = total + lax.ppermute(total, "mp", swap)
    result = total
    for k in range(2, mp, 2):
        result = result + lax.ppermute(total, "mp", shift(mp, k))
    return result


def solution(mesh):
    placed = (
        P("dp", None),
        P("dp", None, "mp"),
        P("dp", None, "mp"),
        P(),
        P(),
        P("dp"),
        P(),
        P(),
        P(None, "mp"),
        P(None, "mp"),
        P(None, "mp"),
        P("mp", None),
        P("dp", "mp", None),
        P("dp", None),
    )
    return jax.shard_map(
        shards, mesh=mesh, in_specs=placed, out_specs=P(None, "dp"), check_vma=False
    )
```

```python
import functools
import math

import jax
import jax.numpy as jnp
from jax import lax
from jax.experimental import pallas as pl
from jax.experimental.pallas import tpu as pltpu
from jax.sharding import PartitionSpec as P

D = 5120
HEADS = 24
KVH = 8
HD = 128
STEPS = 8
GROUP = HEADS // KVH
CHUNK = 512
COLUMNS = 256
MASKED = -1e30
EXPONENT = HD ** (-0.5) * math.log2(math.e)
VMEM = pltpu.VMEM
NOTES = 128
LIVE, RANK, SHARD, PARENT, SOURCE = range(5)


def dot(a, b):
    return jnp.dot(a, b, preferred_element_type=jnp.float32)


def held(x):
    return pltpu.with_memory_space_constraint(x, VMEM)


def struct(shape, dtype=jnp.bfloat16):
    return jax.ShapeDtypeStruct(shape, dtype)


WHOLE = pl.BlockSpec(memory_space=VMEM)
SCALARS = pl.BlockSpec(memory_space=pltpu.SMEM)


def in_parts(x):
    parts = []
    for _ in range(3):
        top = lax.reduce_precision(x, 8, 7)
        parts.append(top.astype(jnp.bfloat16))
        x = x - top
    return parts


def earlier_alike(targets, live):
    index = jnp.arange(targets.shape[0])
    same = (targets[:, None] == targets[None, :]) & (index[None, :] < index[:, None]) & live[None, :]
    return jnp.sum(same.astype(jnp.int32), -1)


def dispatch_kernel(core, slot, tokens, notes, extra, *blocks):
    children, half = tokens.shape[0], tokens.shape[1] // 2
    capacity = blocks[0].shape[0]
    slots = capacity * len(blocks)
    rows = lax.broadcasted_iota(jnp.int32, (slots, children), 0)
    put = (rows == slot[...]).astype(jnp.bfloat16)
    token_half = tokens[:, pl.ds(pl.multiple_of(core[0] * half, half), half)]
    token_rows = dot(put, token_half)
    note_rows = dot(put, notes[...])
    top = lax.broadcasted_iota(jnp.int32, (capacity, extra.shape[1]), 0) == 0
    shared = jnp.where(top, extra[...].astype(jnp.float32), 0.0)
    for k, block in enumerate(blocks):
        at = slice(k * capacity, (k + 1) * capacity)
        block[...] = jnp.concatenate([token_rows[at], note_rows[at], shared], 1).astype(jnp.bfloat16)


def dispatch(core, slot, tokens, notes, extra, groups, capacity):
    block = struct((capacity, tokens.shape[1] // 2 + NOTES + extra.shape[1]))
    return pl.pallas_call(
        dispatch_kernel,
        out_shape=(block,) * groups,
        in_specs=[SCALARS] + [WHOLE] * 4,
        out_specs=[WHOLE] * groups,
        compiler_params=pltpu.CompilerParams(vmem_limit_bytes=8 << 20),
        name="dispatch",
    )(core, slot, tokens, notes, extra)


def pack_kernel(offset, hidden, prefix, ids, blocks_held, sources, *rest):
    blocks, (row, notes, bias, scale, over) = rest[:-5], rest[-5:]
    own = ids[1]
    groups, capacity = len(blocks), blocks[0].shape[0]
    rows, half = row.shape
    slots = groups * capacity
    arrived = jnp.concatenate([block[...].astype(jnp.float32) for block in blocks], 0)
    live = arrived[:, half + LIVE : half + LIVE + 1]
    first = lax.broadcasted_iota(jnp.int32, (slots, slots), 0)
    second = lax.broadcasted_iota(jnp.int32, (slots, slots), 1)
    place = jnp.sum(jnp.where(first < second, live, 0.0), 0, keepdims=True)
    kept = jnp.sum(jnp.where(first == second, live, 0.0), 0, keepdims=True) > 0.5
    wanted = lax.broadcasted_iota(jnp.int32, (rows, slots), 0) + offset
    take = (wanted == place.astype(jnp.int32)) & kept
    take = take.astype(jnp.float32).astype(jnp.bfloat16)
    row[...] = dot(take, arrived[:, :half].astype(jnp.bfloat16)).astype(jnp.bfloat16)
    note = dot(take, arrived[:, half : half + NOTES].astype(jnp.bfloat16))
    notes[...] = note
    parent = note[:, PARENT : PARENT + 1].astype(jnp.int32)
    parents = bias.shape[1] // prefix
    position = lax.broadcasted_iota(jnp.int32, (rows, prefix), 1)
    for p in range(parents):
        usable = (parent == p) & (position < blocks_held[own * parents + p] * 128)
        bias[:, p * prefix : (p + 1) * prefix] = jnp.where(usable, 0.0, MASKED)
    base = half + NOTES
    load = jnp.zeros((groups, sources.shape[1]), jnp.float32)
    target = lax.broadcasted_iota(jnp.int32, load.shape, 0)
    child = lax.broadcasted_iota(jnp.int32, (1, sources.shape[1]), 1)
    for k in range(groups):
        head = arrived[k * capacity : k * capacity + 1, base:]
        scale[k : k + 1, :] = head[:, :hidden] + head[:, hidden : 2 * hidden] + head[:, 2 * hidden : 3 * hidden]
        count = head[:, 3 * hidden : 3 * hidden + 1].astype(jnp.int32)
        source = sources[pl.ds(lax.rem(own - k + groups, groups), 1), :]
        load = load + jnp.where((source == target) & (child < count), 1.0, 0.0)
    most = jnp.max(jnp.sum(load, -1, keepdims=True), 0, keepdims=True)
    over[...] = jnp.broadcast_to((most > rows).astype(jnp.int32), over.shape)


def pack(offset, rows, hidden, prefix, ids, blocks_held, sources, blocks):
    groups = len(blocks)
    half = D // 2
    parents = blocks_held.shape[0] // groups
    return pl.pallas_call(
        functools.partial(pack_kernel, offset, hidden, prefix),
        out_shape=(
            struct((rows, half)),
            struct((rows, NOTES), jnp.float32),
            struct((rows, parents * prefix), jnp.float32),
            struct((groups, hidden), jnp.float32),
            struct((8, 128), jnp.int32),
        ),
        in_specs=[SCALARS, SCALARS] + [WHOLE] * (1 + groups),
        out_specs=[WHOLE] * 5,
        compiler_params=pltpu.CompilerParams(vmem_limit_bytes=12 << 20),
        name="pack",
    )(ids, blocks_held, sources, *blocks)


def load_kernel(*refs):
    count = (len(refs) - 1) // 2
    sems = refs[-1]
    copies = [pltpu.make_async_copy(refs[i], refs[count + i], sems.at[i]) for i in range(count)]
    for copy in copies:
        copy.start()
    for copy in copies:
        copy.wait()


def load(*arrays):
    count = len(arrays)
    return pl.pallas_call(
        load_kernel,
        out_shape=tuple(VMEM(x.shape, x.dtype) for x in arrays),
        in_specs=[pl.BlockSpec(memory_space=pl.ANY)] * count,
        out_specs=(WHOLE,) * count,
        scratch_shapes=[pltpu.SemaphoreType.DMA((count,))],
        compiler_params=pltpu.CompilerParams(vmem_limit_bytes=2 << 20),
        cost_estimate=pl.CostEstimate(flops=0, bytes_accessed=48 << 20, transcendentals=0),
        name="load",
    )(*arrays)


def project(attn, w_out, out, first):
    width = out.shape[1]

    @pl.loop(0, width // CHUNK)
    def _(i):
        columns = pl.ds(pl.multiple_of(first + i * CHUNK, CHUNK), CHUNK)
        out[:, pl.ds(pl.multiple_of(i * CHUNK, CHUNK), CHUNK)] = dot(
            attn[...], w_out[:, columns]
        ).astype(out.dtype)


def step_kernel(step, ids, own, peer, gain, w_query, w_key, w_value, keys, values, bias, w_out, *rest):
    past_keys, past_values = rest[:step], rest[step : 2 * step]
    part, attn, key_now, value_now, normed, query = rest[2 * step :]
    half = own.shape[1]
    slots = own.shape[0]
    kv_heads = w_key.shape[1] // HD
    core = ids[0]
    first = core == 0
    low = jnp.where(first, own[...], peer[...]).astype(jnp.float32)
    high = jnp.where(first, peer[...], own[...]).astype(jnp.float32)
    squares = jnp.sum(low * low, -1, keepdims=True) + jnp.sum(high * high, -1, keepdims=True)
    factor = lax.rsqrt(squares / D + 1e-06)
    normed[:, :half] = (low * factor * gain[:, :half]).astype(jnp.bfloat16)
    normed[:, half:] = (high * factor * gain[:, half:]).astype(jnp.bfloat16)
    q_cols, kv_cols = w_query.shape[1], w_key.shape[1]
    for at in range(0, q_cols, COLUMNS):
        end = min(at + COLUMNS, q_cols)
        query[:, at:end] = dot(normed[...], w_query[:, at:end])
    query[:, q_cols : q_cols + kv_cols] = dot(normed[...], w_key[...])
    query[:, q_cols + kv_cols :] = dot(normed[...], w_value[...])
    key_now[...] = query[:, q_cols : q_cols + kv_cols].astype(jnp.bfloat16)
    value_now[...] = query[:, q_cols + kv_cols :].astype(jnp.bfloat16)
    recent = slots * (step + 1)
    row = lax.broadcasted_iota(jnp.int32, (GROUP * slots, recent), 0)
    column = lax.broadcasted_iota(jnp.int32, (GROUP * slots, recent), 1)
    same = lax.rem(row, slots) == lax.rem(column, slots)
    for head in range(kv_heads):
        lanes = slice(head * HD, (head + 1) * HD)
        q = jnp.concatenate(
            [query[:, (head * GROUP + g) * HD : (head * GROUP + g + 1) * HD] for g in range(GROUP)], 0
        ).astype(jnp.bfloat16)
        k_new = jnp.concatenate([k[:, lanes] for k in past_keys] + [key_now[:, lanes]], 0)
        v_new = jnp.concatenate([v[:, lanes] for v in past_values] + [value_now[:, lanes]], 0)
        contract = (((1,), (1,)), ((), ()))
        s_old = lax.dot_general(q, keys[:, lanes], contract, preferred_element_type=jnp.float32)
        s_old = s_old + jnp.concatenate([bias[...]] * GROUP, 0)
        s_new = lax.dot_general(q, k_new, contract, preferred_element_type=jnp.float32)
        s_new = jnp.where(same, s_new, MASKED)
        top = jnp.maximum(jnp.max(s_old, -1, keepdims=True), jnp.max(s_new, -1, keepdims=True))
        p_old = jnp.exp2(s_old * EXPONENT - top * EXPONENT)
        p_new = jnp.exp2(s_new * EXPONENT - top * EXPONENT)
        total = jnp.sum(p_old, -1, keepdims=True) + jnp.sum(p_new, -1, keepdims=True)
        summed = dot(p_old.astype(jnp.bfloat16), values[:, lanes]) + dot(p_new.astype(jnp.bfloat16), v_new)
        result = (summed / total).astype(jnp.bfloat16)
        for g in range(GROUP):
            at = (head * GROUP + g) * HD
            attn[:, at : at + HD] = result[g * slots : (g + 1) * slots]
    project(attn, w_out, part, (1 - core) * half)


def expand(step, ids, own, peer, gain, w_query, w_key, w_value, keys, values, bias, w_out, past_keys, past_values):
    slots, half = own.shape
    kv_cols = w_key.shape[1]
    q_cols = w_query.shape[1]
    return pl.pallas_call(
        functools.partial(step_kernel, step),
        out_shape=(struct((slots, half)), struct((slots, q_cols)), struct((slots, kv_cols)), struct((slots, kv_cols))),
        in_specs=[SCALARS] + [WHOLE] * (10 + 2 * step),
        out_specs=[WHOLE] * 4,
        scratch_shapes=[VMEM((slots, D), jnp.bfloat16), VMEM((slots, q_cols + 2 * kv_cols), jnp.float32)],
        compiler_params=pltpu.CompilerParams(vmem_limit_bytes=16 << 20),
        cost_estimate=pl.CostEstimate(
            flops=2 * slots * D * (q_cols + 2 * kv_cols), bytes_accessed=21 << 20, transcendentals=1 << 20
        ),
        name="expand",
    )(ids, own, peer, gain, w_query, w_key, w_value, keys, values, bias, w_out, *past_keys, *past_values)


def project_kernel(ids, attn, w_out, part):
    project(attn, w_out, part, ids[0] * part.shape[1])


def project_own(ids, attn, w_out):
    slots, half = attn.shape[0], w_out.shape[1] // 2
    return pl.pallas_call(
        project_kernel,
        out_shape=struct((slots, half), jnp.float32),
        in_specs=[SCALARS, WHOLE, WHOLE],
        out_specs=WHOLE,
        compiler_params=pltpu.CompilerParams(vmem_limit_bytes=8 << 20),
        cost_estimate=pl.CostEstimate(
            flops=2 * slots * half * attn.shape[1], bytes_accessed=4 << 20, transcendentals=0
        ),
        name="project_own",
    )(ids, attn, w_out)


def cut_kernel(mp, ids, up, *pieces):
    hidden = up.shape[2] // mp
    for k, piece in enumerate(pieces):
        target = lax.rem(ids[2] + k, mp)
        for m in range(mp):

            @pl.when(target == m)
            def _():
                piece[...] = up[0, :, m * hidden : (m + 1) * hidden]


def cut(mp, ids, up):
    piece = struct((up.shape[1], up.shape[2] // mp))
    return pl.pallas_call(
        functools.partial(cut_kernel, mp),
        out_shape=(piece,) * mp,
        in_specs=[SCALARS, WHOLE],
        out_specs=[WHOLE] * mp,
        compiler_params=pltpu.CompilerParams(vmem_limit_bytes=12 << 20),
        name="cut",
    )(ids, up)


def join_kernel(ids, *refs):
    pieces, halves = refs[:-2], refs[-2:]
    mp, rows = len(pieces), pieces[0].shape[0]
    for k, piece in enumerate(pieces):
        source = lax.rem(ids[2] - k + mp, mp)
        for m in range(mp):

            @pl.when(source == m)
            def _():
                at = m % (mp // 2) * rows
                halves[m // (mp // 2)][at : at + rows, :] = piece[...]


def join(ids, pieces):
    rows, hidden = pieces[0].shape
    half = struct((rows * len(pieces) // 2, hidden))
    return pl.pallas_call(
        join_kernel,
        out_shape=(half, half),
        in_specs=[SCALARS] + [WHOLE] * len(pieces),
        out_specs=(WHOLE, WHOLE),
        compiler_params=pltpu.CompilerParams(vmem_limit_bytes=12 << 20),
        name="join",
    )(ids, *pieces)


def ring_order(groups):
    return list(range(0, groups, 2)) + list(range(groups - 1, 0, -2))


def ring_place(index, groups):
    return jnp.where(lax.rem(index, 2) == 0, index // 2, groups - 1 - index // 2)


def score_kernel(steps, groups, ids, notes, scale, *refs):
    own_rows, peer_rows = refs[:steps], refs[steps : 2 * steps]
    ups = refs[2 * steps : 2 * steps + 2 * groups]
    out, flat = refs[2 * steps + 2 * groups :]
    rows, half = own_rows[0].shape
    hidden = ups[0].shape[1]
    first = ids[0] == 0
    for t in range(steps):
        at = slice(t * rows, (t + 1) * rows)
        flat[at, :half] = jnp.where(first, own_rows[t][...], peer_rows[t][...])
        flat[at, half:] = jnp.where(first, peer_rows[t][...], own_rows[t][...])
    squares = jnp.zeros((steps * rows, 1), jnp.float32)
    for i in range(0, D, CHUNK):
        wide = flat[:, i : i + CHUNK].astype(jnp.float32)
        squares = squares + jnp.sum(wide * wide, -1, keepdims=True)
    factor = lax.rsqrt(squares / D + 1e-06)
    shard = jnp.concatenate([notes[:, SHARD : SHARD + 1].astype(jnp.int32)] * steps, 0)
    there, here = ring_place(shard, groups), ring_place(ids[1], groups)
    z = jnp.zeros((steps * rows, hidden), jnp.float32)
    for side in range(2):
        hops = lax.rem((here - there if side == 0 else there - here) + groups, groups)
        for k in range(0, groups, 2):
            one, two = ups[side * groups + k], ups[side * groups + k + 1]

            def body(i, acc):
                at = pl.multiple_of(i * CHUNK, CHUNK)
                pair = jnp.concatenate([one[pl.ds(at, CHUNK), :], two[pl.ds(at, CHUNK), :]], 1)
                return acc + dot(flat[:, pl.ds(side * half + at, CHUNK)], pair)

            both = lax.fori_loop(0, half // CHUNK, body, jnp.zeros((steps * rows, 2 * hidden), jnp.float32))
            z = z + jnp.where(hops == k, both[:, :hidden], 0.0) + jnp.where(hops == k + 1, both[:, hidden:], 0.0)
    block = lax.rem(ids[1] - shard + groups, groups)
    gain = jnp.zeros((steps * rows, hidden), jnp.float32)
    for k in range(groups):
        gain = gain + jnp.where(block == k, scale[k : k + 1, :], 0.0)
    z = z * factor
    total = jnp.sum(z * jax.nn.sigmoid(z) * gain, -1, keepdims=True)
    out[...] = jnp.broadcast_to(total, out.shape)


def score(ids, notes, scale, own_rows, peer_rows, tops, bottoms):
    steps, groups = len(own_rows), len(tops)
    rows = own_rows[0].shape[0]
    hidden = tops[0].shape[1]
    return pl.pallas_call(
        functools.partial(score_kernel, steps, groups),
        out_shape=struct((steps * rows, 128), jnp.float32),
        in_specs=[SCALARS] + [WHOLE] * (2 + 2 * steps + 2 * groups),
        out_specs=WHOLE,
        scratch_shapes=[VMEM((steps * rows, D), jnp.bfloat16)],
        compiler_params=pltpu.CompilerParams(vmem_limit_bytes=12 << 20),
        cost_estimate=pl.CostEstimate(
            flops=2 * steps * rows * D * hidden * groups, bytes_accessed=2 * D * hidden * groups, transcendentals=0
        ),
        name="score",
    )(ids, notes, scale, *own_rows, *peer_rows, *[held(x) for x in tops], *[held(x) for x in bottoms])


def place_kernel(groups, cap, count, ids, notes, *refs):
    scores, tables = refs[:count], refs[count:]
    rows = notes.shape[0]
    number = lambda lane: notes[:, lane : lane + 1].astype(jnp.int32)
    target = number(SHARD) ^ ids[1]
    at = number(SOURCE) * cap + number(RANK)
    live = notes[:, LIVE : LIVE + 1] > 0.5
    column = lax.broadcasted_iota(jnp.int32, (rows, groups * cap), 1)
    j = 0
    for table in tables:
        for k in range(table.shape[0]):
            spots = (column == at) & (target == j) & live
            t = 0
            for score in scores:
                for i in range(score.shape[0] // rows):
                    value = score[i * rows : (i + 1) * rows, :1]
                    table[k, t : t + 1, :] = jnp.sum(jnp.where(spots, value, 0.0), 0, keepdims=True)
                    t += 1
            j += 1


def place(groups, cap, ids, notes, scores):
    sizes = [1] + [1 << i for i in range((groups - 1).bit_length())]
    return pl.pallas_call(
        functools.partial(place_kernel, groups, cap, len(scores)),
        out_shape=tuple(struct((size, STEPS, groups * cap), jnp.float32) for size in sizes),
        in_specs=[SCALARS] + [WHOLE] * (1 + len(scores)),
        out_specs=(WHOLE,) * len(sizes),
        compiler_params=pltpu.CompilerParams(vmem_limit_bytes=8 << 20),
        name="place",
    )(ids, notes, *scores)


def shards(
    tokens,
    parent_keys,
    parent_values,
    parent_blocks,
    child_parent,
    child_count,
    node_shard,
    attn_gain,
    w_query,
    w_key,
    w_value,
    w_out,
    reward_up,
    reward_out,
):
    groups = lax.axis_size("dp")
    own = lax.axis_index("dp")
    mp = lax.axis_size("mp")
    me = lax.axis_index("mp")
    core = lax.rem(me, 2)
    ids = jnp.stack([core, own, me]).astype(jnp.int32)
    children, width = tokens.shape
    parents, prefix, kv_cols = parent_keys.shape
    capacity = max(2, 2 * children // groups)
    reward_cap = max(2, 3 * children // (2 * groups))
    slots = groups * capacity
    rows = min(slots, 3 * children // 2)
    hidden = reward_out.shape[1] // mp
    swap = [(i, i ^ 1) for i in range(mp)]
    shift = lambda count, k: [(i, (i + k) % count) for i in range(count)]

    here = lambda table: lax.dynamic_slice_in_dim(table, own * children, children, 0)
    my_parents, my_shard = here(child_parent), here(node_shard)
    my_source = my_parents // parents
    live = jnp.arange(children) < child_count[0]
    slot = lax.rem(my_source - own + groups, groups) * capacity + earlier_alike(my_source, live)
    slot = jnp.where(live, slot, -1)
    notes = jnp.stack(
        [live.astype(jnp.int32), earlier_alike(my_shard, live), my_shard, my_parents % parents,
         jnp.full((children,), own, jnp.int32)], 1,
    ).astype(jnp.bfloat16)
    notes = jnp.pad(notes, ((0, 0), (0, NOTES - notes.shape[1])))
    my_scale = lax.dynamic_slice_in_dim(reward_out[0], me * hidden, hidden, 0)
    extra = jnp.concatenate(in_parts(my_scale) + [child_count.astype(jnp.bfloat16)])
    extra = jnp.pad(extra, (0, -extra.shape[0] % 128))[None]
    sources = (child_parent // parents).reshape(groups, children)
    pieces = cut(mp, ids, reward_up)
    pieces, slot, notes, extra, sources = lax.optimization_barrier((pieces, slot[None], notes, extra, sources))
    pieces = [pieces[0]] + [lax.ppermute(pieces[k], "mp", shift(mp, k)) for k in range(1, mp)]

    blocks = dispatch(ids, slot, tokens, notes, extra, groups, capacity)
    keys = parent_keys.reshape(parents * prefix, kv_cols)
    values = parent_values.reshape(parents * prefix, kv_cols)
    raw = (keys, values, w_query, w_key, w_value, w_out)
    blocks, raw = lax.optimization_barrier((blocks, raw))
    blocks = [blocks[0]] + [lax.ppermute(blocks[k], "dp", shift(groups, k)) for k in range(1, groups)]
    loaded = load(*raw)
    blocks, loaded, pieces = lax.optimization_barrier((blocks, loaded, pieces))
    gain = attn_gain.reshape(1, width)
    order = ring_order(groups)
    onward = [(order[i], order[(i + 1) % groups]) for i in range(groups)]
    backward = [(b, a) for a, b in onward]

    def run(offset, blocks, loaded, tops, bottoms, sources, ids, gain, parent_blocks):
        row_own, notes, bias, scale, over = pack(
            offset, rows, hidden, prefix, ids, parent_blocks, sources, blocks
        )
        keys, values, w_query, w_key, w_value, w_out = [held(x) for x in loaded]
        state = row_own.astype(jnp.float32)
        row_peer = lax.ppermute(row_own, "mp", swap)
        past_keys, past_values, rows_own, rows_peer, scores = [], [], [], [], []
        tops, bottoms = list(tops), list(bottoms)
        hops = -(-(groups - 1) // (STEPS - 1))
        for step in range(STEPS):
            if len(tops) < groups:
                row_own, row_peer, top, bottom = lax.optimization_barrier((row_own, row_peer, tops[-1], bottoms[-1]))
                tops[-1], bottoms[-1] = top, bottom
                for _ in range(min(hops, groups - len(tops))):
                    tops.append(lax.ppermute(tops[-1], "dp", onward))
                    bottoms.append(lax.ppermute(bottoms[-1], "dp", backward))
            part, attn, key_now, value_now = expand(
                step, ids, row_own, row_peer, gain, w_query, w_key, w_value, keys, values, bias, w_out,
                past_keys, past_values,
            )
            past_keys.append(key_now)
            past_values.append(value_now)
            from_peer = lax.ppermute(part, "mp", swap)
            chip = project_own(ids, attn, w_out) + from_peer.astype(jnp.float32)
            sent = chip.astype(jnp.bfloat16)
            for k in range(2, mp, 2):
                chip = chip + lax.ppermute(sent, "mp", shift(mp, k)).astype(jnp.float32)
            state = state + chip
            row_own = state.astype(jnp.bfloat16)
            row_peer = lax.ppermute(row_own, "mp", swap)
            rows_own.append(row_own)
            rows_peer.append(row_peer)
        for first, last in ((0, 4), (4, 7), (7, 8)):
            scores.append(score(ids, notes, scale, rows_own[first:last], rows_peer[first:last], tops, bottoms))
        return place(groups, reward_cap, ids, notes, scores), over, tops, bottoms

    top, bottom = join(ids, pieces)
    others = (sources, ids, gain, parent_blocks)
    tables, over, tops, bottoms = run(0, blocks, loaded, [top], [bottom], *others)
    if rows < slots:
        operands = (blocks, raw, tops, bottoms, others)
        tables, over, operands = lax.optimization_barrier((tables, over, operands))

        def again(tables, operands):
            blocks, raw, tops, bottoms, others = operands
            more = run(rows, blocks, load(*raw), tops, bottoms, *others)[0]
            return tuple(a + b for a, b in zip(tables, more))

        tables = lax.cond(over[0, 0] > 0, again, lambda tables, operands: tables, tables, operands)

    tables = list(tables)
    while len(tables) > 1:
        bit = tables[-1].shape[0]
        arrived = lax.ppermute(tables.pop(), "dp", [(i, i ^ bit) for i in range(groups)])
        at = 0
        for i, table in enumerate(tables):
            tables[i] = table + arrived[at : at + table.shape[0]]
            at += table.shape[0]
    total = tables[0][0]
    total = total + lax.ppermute(total, "mp", swap)
    result = total
    for k in range(2, mp, 2):
        result = result + lax.ppermute(total, "mp", shift(mp, k))
    return result


def solution(mesh):
    placed = (
        P("dp", None),
        P("dp", None, "mp"),
        P("dp", None, "mp"),
        P(),
        P(),
        P("dp"),
        P(),
        P(),
        P(None, "mp"),
        P(None, "mp"),
        P(None, "mp"),
        P("mp", None),
        P("dp", "mp", None),
        P("dp", None),
    )
    return jax.shard_map(
        shards, mesh=mesh, in_specs=placed, out_specs=P(None, "dp"), check_vma=False
    )
```

```python
import functools
import math

import jax
import jax.numpy as jnp
from jax import lax
from jax.experimental import pallas as pl
from jax.experimental.pallas import tpu as pltpu
from jax.sharding import PartitionSpec as P

D = 5120
HEADS = 24
KVH = 8
HD = 128
STEPS = 8
GROUP = HEADS // KVH
CHUNK = 512
COLUMNS = 256
ROWS = 64
MASKED = -1e30
EXPONENT = HD ** (-0.5) * math.log2(math.e)
VMEM = pltpu.VMEM
NOTES = 128
LIVE, RANK, SHARD, PARENT, SOURCE = range(5)


def dot(a, b):
    return jnp.dot(a, b, preferred_element_type=jnp.float32)


def held(x):
    return pltpu.with_memory_space_constraint(x, VMEM)


def struct(shape, dtype=jnp.bfloat16):
    return jax.ShapeDtypeStruct(shape, dtype)


WHOLE = pl.BlockSpec(memory_space=VMEM)
SMALL = pl.CostEstimate(flops=0, bytes_accessed=0, transcendentals=0)
SCALARS = pl.BlockSpec(memory_space=pltpu.SMEM)


def in_parts(x):
    parts = []
    for _ in range(3):
        top = lax.reduce_precision(x, 8, 7)
        parts.append(top.astype(jnp.bfloat16))
        x = x - top
    return parts


def earlier_alike(targets, live):
    index = jnp.arange(targets.shape[0])
    same = (targets[:, None] == targets[None, :]) & (index[None, :] < index[:, None]) & live[None, :]
    return jnp.sum(same.astype(jnp.int32), -1)


def dispatch_kernel(core, slot, tokens, notes, extra, *blocks):
    children, half = tokens.shape[0], tokens.shape[1] // 2
    capacity = blocks[0].shape[0]
    slots = capacity * len(blocks)
    rows = lax.broadcasted_iota(jnp.int32, (slots, children), 0)
    put = (rows == slot[...]).astype(jnp.bfloat16)
    token_half = tokens[:, pl.ds(pl.multiple_of(core[0] * half, half), half)]
    token_rows = dot(put, token_half)
    note_rows = dot(put, notes[...])
    top = lax.broadcasted_iota(jnp.int32, (capacity, extra.shape[1]), 0) == 0
    shared = jnp.where(top, extra[...].astype(jnp.float32), 0.0)
    for k, block in enumerate(blocks):
        at = slice(k * capacity, (k + 1) * capacity)
        block[...] = jnp.concatenate([token_rows[at], note_rows[at], shared], 1).astype(jnp.bfloat16)


def dispatch(core, slot, tokens, notes, extra, groups, capacity):
    block = struct((capacity, tokens.shape[1] // 2 + NOTES + extra.shape[1]))
    return pl.pallas_call(
        dispatch_kernel,
        out_shape=(block,) * groups,
        in_specs=[SCALARS] + [WHOLE] * 4,
        out_specs=[WHOLE] * groups,
        compiler_params=pltpu.CompilerParams(vmem_limit_bytes=8 << 20),
        name="dispatch",
    )(core, slot, tokens, notes, extra)


def pack_kernel(offset, hidden, prefix, ids, blocks_held, sources, *rest):
    blocks, (row, notes, bias, scale, over) = rest[:-5], rest[-5:]
    own = ids[1]
    groups, capacity = len(blocks), blocks[0].shape[0]
    rows, half = row.shape
    slots = groups * capacity
    arrived = jnp.concatenate([block[...].astype(jnp.float32) for block in blocks], 0)
    live = arrived[:, half + LIVE : half + LIVE + 1]
    first = lax.broadcasted_iota(jnp.int32, (slots, slots), 0)
    second = lax.broadcasted_iota(jnp.int32, (slots, slots), 1)
    place = jnp.sum(jnp.where(first < second, live, 0.0), 0, keepdims=True)
    kept = jnp.sum(jnp.where(first == second, live, 0.0), 0, keepdims=True) > 0.5
    wanted = lax.broadcasted_iota(jnp.int32, (rows, slots), 0) + offset
    take = (wanted == place.astype(jnp.int32)) & kept
    take = take.astype(jnp.float32).astype(jnp.bfloat16)
    row[...] = dot(take, arrived[:, :half].astype(jnp.bfloat16)).astype(jnp.bfloat16)
    note = dot(take, arrived[:, half : half + NOTES].astype(jnp.bfloat16))
    notes[...] = note
    parent = note[:, PARENT : PARENT + 1].astype(jnp.int32)
    parents = bias.shape[1] // prefix
    position = lax.broadcasted_iota(jnp.int32, (rows, prefix), 1)
    for p in range(parents):
        usable = (parent == p) & (position < blocks_held[own * parents + p] * 128)
        bias[:, p * prefix : (p + 1) * prefix] = jnp.where(usable, 0.0, MASKED)
    base = half + NOTES
    load = jnp.zeros((groups, sources.shape[1]), jnp.float32)
    target = lax.broadcasted_iota(jnp.int32, load.shape, 0)
    child = lax.broadcasted_iota(jnp.int32, (1, sources.shape[1]), 1)
    for k in range(groups):
        head = arrived[k * capacity : k * capacity + 1, base:]
        scale[k : k + 1, :] = head[:, :hidden] + head[:, hidden : 2 * hidden] + head[:, 2 * hidden : 3 * hidden]
        count = head[:, 3 * hidden : 3 * hidden + 1].astype(jnp.int32)
        source = sources[pl.ds(lax.rem(own - k + groups, groups), 1), :]
        load = load + jnp.where((source == target) & (child < count), 1.0, 0.0)
    most = jnp.max(jnp.sum(load, -1, keepdims=True), 0, keepdims=True)
    over[...] = jnp.broadcast_to((most > rows).astype(jnp.int32), over.shape)


def pack(offset, rows, hidden, prefix, ids, blocks_held, sources, blocks):
    groups = len(blocks)
    half = D // 2
    parents = blocks_held.shape[0] // groups
    return pl.pallas_call(
        functools.partial(pack_kernel, offset, hidden, prefix),
        out_shape=(
            struct((rows, half)),
            struct((rows, NOTES), jnp.float32),
            struct((rows, parents * prefix), jnp.float32),
            struct((groups, hidden), jnp.float32),
            struct((8, 128), jnp.int32),
        ),
        in_specs=[SCALARS, SCALARS] + [WHOLE] * (1 + groups),
        out_specs=[WHOLE] * 5,
        compiler_params=pltpu.CompilerParams(vmem_limit_bytes=12 << 20),
        name="pack",
    )(ids, blocks_held, sources, *blocks)


def project(attn, w_out, out, first):
    width = out.shape[1]

    @pl.loop(0, width // CHUNK)
    def _(i):
        columns = pl.ds(pl.multiple_of(first + i * CHUNK, CHUNK), CHUNK)
        out[:, pl.ds(pl.multiple_of(i * CHUNK, CHUNK), CHUNK)] = dot(
            attn[...], w_out[:, columns]
        )[: out.shape[0]].astype(out.dtype)


def step_kernel(step, ids, own, peer, gain, w_query, w_key, w_value, keys, values, bias, w_out, *rest):
    past_keys, past_values = rest[:step], rest[step : 2 * step]
    rest = rest[2 * step :]
    half = own.shape[1]
    slots = own.shape[0]
    q_cols, kv_cols = w_query.shape[1], w_key.shape[1]
    kv_heads = kv_cols // HD
    ready = {}
    if step == 0:
        part, attn, key_now, value_now, *kept, normed, query, sems = rest
        moves = [(w_query, kept[0], at, min(at + COLUMNS, q_cols)) for at in range(0, q_cols, COLUMNS)]
        moves += [(w, v, 0, w.shape[1]) for w, v in zip((w_key, w_value, keys, values, w_out), kept[1:])]
        for i, (source, target, at, end) in enumerate(moves):
            copy = pltpu.make_async_copy(source.at[:, at:end], target.at[:, at:end], sems.at[i])
            copy.start()
            ready[i] = copy
        w_query, w_key, w_value, keys, values, w_out = kept
    else:
        part, attn, key_now, value_now, normed, query = rest
    arrivals = iter(ready.values())

    def arrive():
        for copy in arrivals:
            copy.wait()
            break

    core = ids[0]
    first = core == 0
    low = jnp.where(first, own[...], peer[...]).astype(jnp.float32)
    high = jnp.where(first, peer[...], own[...]).astype(jnp.float32)
    squares = jnp.sum(low * low, -1, keepdims=True) + jnp.sum(high * high, -1, keepdims=True)
    factor = lax.rsqrt(squares / D + 1e-06)
    normed[:slots, :half] = (low * factor * gain[:, :half]).astype(jnp.bfloat16)
    normed[:slots, half:] = (high * factor * gain[:, half:]).astype(jnp.bfloat16)
    if normed.shape[0] > slots:
        normed[slots:, :] = jnp.zeros((normed.shape[0] - slots, D), jnp.bfloat16)
    for at in range(0, q_cols, COLUMNS):
        end = min(at + COLUMNS, q_cols)
        arrive()
        query[:, at:end] = dot(normed[...], w_query[:, at:end])
    arrive()
    query[:, q_cols : q_cols + kv_cols] = dot(normed[...], w_key[...])
    arrive()
    query[:, q_cols + kv_cols :] = dot(normed[...], w_value[...])
    arrive()
    arrive()
    key_now[...] = query[:slots, q_cols : q_cols + kv_cols].astype(jnp.bfloat16)
    value_now[...] = query[:slots, q_cols + kv_cols :].astype(jnp.bfloat16)
    recent = slots * (step + 1)
    row = lax.broadcasted_iota(jnp.int32, (GROUP * slots, recent), 0)
    column = lax.broadcasted_iota(jnp.int32, (GROUP * slots, recent), 1)
    same = lax.rem(row, slots) == lax.rem(column, slots)
    for head in range(kv_heads):
        lanes = slice(head * HD, (head + 1) * HD)
        q = jnp.concatenate(
            [query[:slots, (head * GROUP + g) * HD : (head * GROUP + g + 1) * HD] for g in range(GROUP)], 0
        ).astype(jnp.bfloat16)
        k_new = jnp.concatenate([k[:, lanes] for k in past_keys] + [key_now[:, lanes]], 0)
        v_new = jnp.concatenate([v[:, lanes] for v in past_values] + [value_now[:, lanes]], 0)
        contract = (((1,), (1,)), ((), ()))
        s_old = lax.dot_general(q, keys[:, lanes], contract, preferred_element_type=jnp.float32)
        s_old = s_old + jnp.concatenate([bias[...]] * GROUP, 0)
        s_new = lax.dot_general(q, k_new, contract, preferred_element_type=jnp.float32)
        s_new = jnp.where(same, s_new, MASKED)
        top = jnp.maximum(jnp.max(s_old, -1, keepdims=True), jnp.max(s_new, -1, keepdims=True))
        p_old = jnp.exp2(s_old * EXPONENT - top * EXPONENT)
        p_new = jnp.exp2(s_new * EXPONENT - top * EXPONENT)
        total = jnp.sum(p_old, -1, keepdims=True) + jnp.sum(p_new, -1, keepdims=True)
        summed = dot(p_old.astype(jnp.bfloat16), values[:, lanes]) + dot(p_new.astype(jnp.bfloat16), v_new)
        result = (summed / total).astype(jnp.bfloat16)
        for g in range(GROUP):
            at = (head * GROUP + g) * HD
            attn[:slots, at : at + HD] = result[g * slots : (g + 1) * slots]
    if attn.shape[0] > slots:
        attn[slots:, :] = jnp.zeros((attn.shape[0] - slots, q_cols), jnp.bfloat16)
    arrive()
    project(attn, w_out, part, (1 - core) * half)


def expand(step, ids, own, peer, gain, w_query, w_key, w_value, keys, values, bias, w_out, past_keys, past_values):
    slots, half = own.shape
    kv_cols = w_key.shape[1]
    q_cols = w_query.shape[1]
    padded = -(-slots // ROWS) * ROWS
    weights = (w_query, w_key, w_value, keys, values, w_out)
    kept, sems = [], []
    place = WHOLE
    if step == 0:
        kept = [VMEM(w.shape, w.dtype) for w in weights]
        sems = [pltpu.SemaphoreType.DMA((-(-q_cols // COLUMNS) + 5,))]
        place = pl.BlockSpec(memory_space=pl.ANY)
    return pl.pallas_call(
        functools.partial(step_kernel, step),
        out_shape=(
            struct((slots, half)), struct((padded, q_cols)), struct((slots, kv_cols)), struct((slots, kv_cols)), *kept
        ),
        in_specs=[SCALARS] + [WHOLE] * 3 + [place] * 5 + [WHOLE, place] + [WHOLE] * (2 * step),
        out_specs=[WHOLE] * (4 + len(kept)),
        scratch_shapes=[VMEM((padded, D), jnp.bfloat16), VMEM((padded, q_cols + 2 * kv_cols), jnp.float32)] + sems,
        compiler_params=pltpu.CompilerParams(vmem_limit_bytes=16 << 20),
        cost_estimate=SMALL,
        name="expand",
    )(ids, own, peer, gain, w_query, w_key, w_value, keys, values, bias, w_out, *past_keys, *past_values)


def project_kernel(ids, attn, w_out, part):
    project(attn, w_out, part, ids[0] * part.shape[1])


def project_own(ids, rows, attn, w_out):
    return pl.pallas_call(
        project_kernel,
        out_shape=struct((rows, w_out.shape[1] // 2), jnp.float32),
        in_specs=[SCALARS, WHOLE, WHOLE],
        out_specs=WHOLE,
        compiler_params=pltpu.CompilerParams(vmem_limit_bytes=8 << 20),
        cost_estimate=SMALL,
        name="project_own",
    )(ids, attn, w_out)


def score_kernel(steps, load, ids, notes, up, *refs):
    own_rows, peer_rows = refs[:steps], refs[steps : 2 * steps]
    blocks, rest = refs[2 * steps : -2 - 2 * load], refs[-2 - 2 * load :]
    flat, total = rest[load : load + 2]
    copies = []
    if load:
        for r in range(up.shape[0]):
            copies.append(pltpu.make_async_copy(up.at[r], rest[0].at[r], rest[-1].at[r]))
            copies[-1].start()
        up = rest[0]
    groups, depth, hidden = up.shape
    mp = len(blocks)
    rows = own_rows[0].shape[0]
    for t in range(steps):
        for m in range(mp):
            rows_from = [own_rows, peer_rows]
            for core in range(2):
                source = rows_from[int(m // (mp // 2) != core)][t]

                @pl.when((ids[2] == m) & (ids[0] == core))
                def _():
                    at = m % (mp // 2) * depth
                    flat[t * rows : (t + 1) * rows, :] = source[:, at : at + depth]

    shard = jnp.concatenate([notes[:, SHARD : SHARD + 1].astype(jnp.int32)] * steps, 0)
    for r in range(groups):
        if load:
            copies[r].wait()
        for at in range(0, hidden, COLUMNS):
            end = min(at + COLUMNS, hidden)
            here = jnp.where(shard == r, dot(flat[...], up[r, :, at:end]), 0.0)
            total[:, at:end] = here if r == 0 else total[:, at:end] + here
    width = hidden // mp
    for j, block in enumerate(blocks):
        for m in range(mp):

            @pl.when(lax.rem(ids[2] + j, mp) == m)
            def _():
                block[...] = total[:, m * width : (m + 1) * width].astype(jnp.bfloat16)


def score(mp, ids, notes, up, own_rows, peer_rows, load):
    steps = len(own_rows)
    groups, depth, hidden = up.shape
    count = steps * own_rows[0].shape[0]
    block = struct((count, hidden // mp))
    return pl.pallas_call(
        functools.partial(score_kernel, steps, load),
        out_shape=(block,) * mp + (VMEM(up.shape, up.dtype),) * load,
        in_specs=[SCALARS, WHOLE, pl.BlockSpec(memory_space=pl.ANY) if load else WHOLE] + [WHOLE] * (2 * steps),
        out_specs=(WHOLE,) * (mp + load),
        scratch_shapes=[VMEM((count, depth), jnp.bfloat16), VMEM((count, hidden), jnp.float32)]
        + [pltpu.SemaphoreType.DMA((groups,))] * load,
        compiler_params=pltpu.CompilerParams(vmem_limit_bytes=16 << 20),
        cost_estimate=SMALL,
        name="score",
    )(ids, notes, up, *own_rows, *peer_rows)


def place_kernel(groups, cap, counts, tables_count, ids, notes, scale, *refs):
    refs = list(refs)
    take = lambda count: [refs.pop(0) for _ in range(count)]
    own_rows, peer_rows = take(STEPS), take(STEPS)
    parts = [take(count) for count in counts]
    tables = take(tables_count)
    rows = notes.shape[0]
    number = lambda lane: notes[:, lane : lane + 1].astype(jnp.int32)
    shard = number(SHARD)
    block = lax.rem(ids[1] - shard + groups, groups)
    gain = jnp.zeros((rows, scale.shape[1]), jnp.float32)
    for k in range(groups):
        gain = gain + jnp.where(block == k, scale[k : k + 1, :], 0.0)
    values = []
    for part in parts:
        total = sum(p[...].astype(jnp.float32) for p in part)
        for i in range(total.shape[0] // rows):
            t = len(values)
            own, peer = own_rows[t][...].astype(jnp.float32), peer_rows[t][...].astype(jnp.float32)
            squares = jnp.sum(own * own, -1, keepdims=True) + jnp.sum(peer * peer, -1, keepdims=True)
            z = total[i * rows : (i + 1) * rows] * lax.rsqrt(squares / D + 1e-06)
            values.append(jnp.sum(z * jax.nn.sigmoid(z) * gain, -1, keepdims=True))
    target = shard ^ ids[1]
    at = number(SOURCE) * cap + number(RANK)
    live = notes[:, LIVE : LIVE + 1] > 0.5
    column = lax.broadcasted_iota(jnp.int32, (rows, groups * cap), 1)
    j = 0
    for table in tables:
        for k in range(table.shape[0]):
            spots = (column == at) & (target == j) & live
            for t, value in enumerate(values):
                table[k, t : t + 1, :] = jnp.sum(jnp.where(spots, value, 0.0), 0, keepdims=True)
            j += 1


def place(groups, cap, ids, notes, scale, own_rows, peer_rows, parts):
    sizes = [1] + [1 << i for i in range((groups - 1).bit_length())]
    counts = [len(part) for part in parts]
    return pl.pallas_call(
        functools.partial(place_kernel, groups, cap, counts, len(sizes)),
        out_shape=tuple(struct((size, STEPS, groups * cap), jnp.float32) for size in sizes),
        in_specs=[SCALARS] + [WHOLE] * (2 + 2 * STEPS + sum(counts)),
        out_specs=(WHOLE,) * len(sizes),
        compiler_params=pltpu.CompilerParams(vmem_limit_bytes=12 << 20),
        cost_estimate=SMALL,
        name="place",
    )(ids, notes, scale, *own_rows, *peer_rows, *[x for part in parts for x in part])


def shards(
    tokens,
    parent_keys,
    parent_values,
    parent_blocks,
    child_parent,
    child_count,
    node_shard,
    attn_gain,
    w_query,
    w_key,
    w_value,
    w_out,
    reward_up,
    reward_out,
):
    groups = lax.axis_size("dp")
    own = lax.axis_index("dp")
    mp = lax.axis_size("mp")
    me = lax.axis_index("mp")
    core = lax.rem(me, 2)
    ids = jnp.stack([core, own, me]).astype(jnp.int32)
    children, width = tokens.shape
    parents, prefix, kv_cols = parent_keys.shape
    capacity = max(2, 2 * children // groups)
    reward_cap = max(2, 3 * children // (2 * groups))
    slots = groups * capacity
    rows = min(slots, 3 * children // 2)
    hidden = reward_out.shape[1] // mp
    swap = [(i, i ^ 1) for i in range(mp)]
    shift = lambda count, k: [(i, (i + k) % count) for i in range(count)]

    up = lax.all_gather(reward_up[0], "dp", axis=0)

    here = lambda table: lax.dynamic_slice_in_dim(table, own * children, children, 0)
    my_parents, my_shard = here(child_parent), here(node_shard)
    my_source = my_parents // parents
    live = jnp.arange(children) < child_count[0]
    slot = lax.rem(my_source - own + groups, groups) * capacity + earlier_alike(my_source, live)
    slot = jnp.where(live, slot, -1)
    notes = jnp.stack(
        [live.astype(jnp.int32), earlier_alike(my_shard, live), my_shard, my_parents % parents,
         jnp.full((children,), own, jnp.int32)], 1,
    ).astype(jnp.bfloat16)
    notes = jnp.pad(notes, ((0, 0), (0, NOTES - notes.shape[1])))
    my_scale = lax.dynamic_slice_in_dim(reward_out[0], me * hidden, hidden, 0)
    extra = jnp.concatenate(in_parts(my_scale) + [child_count.astype(jnp.bfloat16)])
    extra = jnp.pad(extra, (0, -extra.shape[0] % 128))[None]
    sources = (child_parent // parents).reshape(groups, children)
    slot, notes, extra, sources = lax.optimization_barrier((slot[None], notes, extra, sources))
    blocks = dispatch(ids, slot, tokens, notes, extra, groups, capacity)
    blocks = [blocks[0]] + [lax.ppermute(blocks[k], "dp", shift(groups, k)) for k in range(1, groups)]

    keys = parent_keys.reshape(parents * prefix, kv_cols)
    values = parent_values.reshape(parents * prefix, kv_cols)
    raw = (w_query, w_key, w_value, keys, values, w_out)
    gain = attn_gain.reshape(1, width)

    def run(offset, blocks, raw, up, sources, ids, gain, parent_blocks):
        row_own, notes, bias, scale, over = pack(
            offset, rows, hidden, prefix, ids, parent_blocks, sources, blocks
        )
        weights = raw
        state = row_own.astype(jnp.float32)
        row_peer = lax.ppermute(row_own, "mp", swap)
        past_keys, past_values, rows_own, rows_peer, scores = [], [], [], [], []
        for step in range(STEPS):
            w_query, w_key, w_value, keys, values, w_out = weights
            part, attn, key_now, value_now, *kept = expand(
                step, ids, row_own, row_peer, gain, w_query, w_key, w_value, keys, values, bias, w_out,
                past_keys, past_values,
            )
            if step == 0:
                weights = [held(x) for x in kept]
            past_keys.append(key_now)
            past_values.append(value_now)
            from_peer = lax.ppermute(part, "mp", swap)
            chip = project_own(ids, rows, attn, weights[-1]) + from_peer.astype(jnp.float32)
            sent = chip.astype(jnp.bfloat16)
            for k in range(2, mp, 2):
                chip = chip + lax.ppermute(sent, "mp", shift(mp, k)).astype(jnp.float32)
            state = state + chip
            row_own = state.astype(jnp.bfloat16)
            row_peer = lax.ppermute(row_own, "mp", swap)
            rows_own.append(row_own)
            rows_peer.append(row_peer)
        parts = []
        for first, last in ((0, STEPS - 1), (STEPS - 1, STEPS)):
            sums = score(mp, ids, notes, up, rows_own[first:last], rows_peer[first:last], load=first == 0)
            if first == 0:
                up = held(sums[-1])
            parts.append([sums[0]] + [lax.ppermute(sums[k], "mp", shift(mp, k)) for k in range(1, mp)])
        return place(groups, reward_cap, ids, notes, scale, rows_own, rows_peer, parts), over

    others = (sources, ids, gain, parent_blocks)
    tables, over = run(0, blocks, raw, up, *others)
    if rows < slots:
        operands = (blocks, raw, up, others)
        tables, over, operands = lax.optimization_barrier((tables, over, operands))

        def again(tables, operands):
            blocks, raw, up, others = operands
            more = run(rows, blocks, raw, up, *others)[0]
            return tuple(a + b for a, b in zip(tables, more))

        tables = lax.cond(over[0, 0] > 0, again, lambda tables, operands: tables, tables, operands)

    tables = list(tables)
    while len(tables) > 1:
        bit = tables[-1].shape[0]
        arrived = lax.ppermute(tables.pop(), "dp", [(i, i ^ bit) for i in range(groups)])
        at = 0
        for i, table in enumerate(tables):
            tables[i] = table + arrived[at : at + table.shape[0]]
            at += table.shape[0]
    total = tables[0][0]
    total = total + lax.ppermute(total, "mp", swap)
    result = total
    for k in range(2, mp, 2):
        result = result + lax.ppermute(total, "mp", shift(mp, k))
    return result


def solution(mesh):
    placed = (
        P("dp", None),
        P("dp", None, "mp"),
        P("dp", None, "mp"),
        P(),
        P(),
        P("dp"),
        P(),
        P(),
        P(None, "mp"),
        P(None, "mp"),
        P(None, "mp"),
        P("mp", None),
        P("dp", "mp", None),
        P("dp", None),
    )
    return jax.shard_map(
        shards, mesh=mesh, in_specs=placed, out_specs=P(None, "dp"), check_vma=False
    )
```

```python
import functools
import math

import jax
import jax.numpy as jnp
from jax import lax
from jax.experimental import pallas as pl
from jax.experimental.pallas import tpu as pltpu
from jax.sharding import PartitionSpec as P

D = 5120
HEADS = 24
KVH = 8
HD = 128
STEPS = 8
GROUP = HEADS // KVH
CHUNK = 512
COLUMNS = 256
ROWS = 64
MASKED = -1e30
EXPONENT = HD ** (-0.5) * math.log2(math.e)
VMEM = pltpu.VMEM
NOTES = 128
LIVE, RANK, SHARD, PARENT, SOURCE = range(5)


def dot(a, b):
    return jnp.dot(a, b, preferred_element_type=jnp.float32)


def held(x):
    return pltpu.with_memory_space_constraint(x, VMEM)


def struct(shape, dtype=jnp.bfloat16):
    return jax.ShapeDtypeStruct(shape, dtype)


WHOLE = pl.BlockSpec(memory_space=VMEM)
SMALL = pl.CostEstimate(flops=0, bytes_accessed=0, transcendentals=0)
SCALARS = pl.BlockSpec(memory_space=pltpu.SMEM)


def coordinates():
    me = lax.axis_index("mp")
    return lax.rem(me, 2), lax.axis_index("dp"), me


def dispatch_kernel(parents, count, parent_row, shard_row, tokens, reward_out, *blocks):
    core, own, me = coordinates()
    groups, capacity = len(blocks), blocks[0].shape[0]
    children, half = tokens.shape[0], tokens.shape[1] // 2
    everyone = parent_row.shape[1]
    int32, float32, bfloat16 = jnp.int32, jnp.float32, jnp.bfloat16

    mine = lax.broadcasted_iota(int32, (everyone, children), 0) - own * children
    mine = (mine == lax.broadcasted_iota(int32, (everyone, children), 1)).astype(float32).astype(bfloat16)

    def row_and_column(table):
        table = table[...].astype(float32).astype(bfloat16)
        column = lax.dot_general(mine, table, (((0,), (1,)), ((), ())), preferred_element_type=float32)
        return dot(table, mine).astype(int32), column.astype(int32)

    parent, parent_c = row_and_column(parent_row)
    shard, shard_c = row_and_column(shard_row)
    source, source_c = lax.div(parent, parents), lax.div(parent_c, parents)
    first = lax.broadcasted_iota(int32, (children, children), 0)
    second = lax.broadcasted_iota(int32, (children, children), 1)
    live = lax.broadcasted_iota(int32, (1, children), 1) < count[0]
    live_c = lax.broadcasted_iota(int32, (children, 1), 0) < count[0]
    rank = jnp.sum(jnp.where((source_c == source) & (first < second) & live_c, 1, 0), 0, keepdims=True)
    slot = lax.rem(source - own + groups, groups) * capacity + rank
    slot = jnp.where(live, slot, -1)
    reward_rank = jnp.sum(jnp.where((shard_c == shard) & (second < first) & live, 1, 0), 1, keepdims=True)
    lane = lax.broadcasted_iota(int32, (children, NOTES), 1)
    notes = jnp.where(lane == LIVE, live_c.astype(int32), 0)
    for at, value in ((RANK, reward_rank), (SHARD, shard_c), (PARENT, lax.rem(parent_c, parents)), (SOURCE, own)):
        notes = jnp.where(lane == at, value, notes)

    width = blocks[0].shape[1] - half - NOTES
    hidden = (width - 128) // 3
    rest = jnp.zeros((1, hidden), float32)
    for m in range(reward_out.shape[1] // hidden):
        rest = rest + jnp.where(me == m, reward_out[:, m * hidden : (m + 1) * hidden], 0.0)
    parts = []
    for _ in range(3):
        parts.append(rest.astype(bfloat16).astype(float32))
        rest = rest - parts[-1]
    parts.append(jnp.full((1, 128), 1, int32).astype(float32) * count[0].astype(float32))
    top = lax.broadcasted_iota(int32, (capacity, width), 0) == 0
    shared = jnp.where(top, jnp.concatenate(parts, 1), 0.0)

    rows = lax.broadcasted_iota(int32, (groups * capacity, children), 0)
    put = (rows == slot).astype(float32).astype(bfloat16)
    token_rows = dot(put, tokens[:, pl.ds(pl.multiple_of(core * half, half), half)])
    note_rows = dot(put, notes.astype(float32).astype(bfloat16))
    for k, block in enumerate(blocks):
        at = slice(k * capacity, (k + 1) * capacity)
        block[...] = jnp.concatenate([token_rows[at], note_rows[at], shared], 1).astype(bfloat16)


def dispatch(parents, child_count, child_parent, node_shard, tokens, reward_out, groups, capacity, hidden):
    block = struct((capacity, tokens.shape[1] // 2 + NOTES + 3 * hidden + 128))
    return pl.pallas_call(
        functools.partial(dispatch_kernel, parents),
        out_shape=(block,) * groups,
        in_specs=[SCALARS] + [WHOLE] * 4,
        out_specs=[WHOLE] * groups,
        compiler_params=pltpu.CompilerParams(vmem_limit_bytes=8 << 20),
        cost_estimate=SMALL,
        name="dispatch",
    )(child_count, child_parent[None], node_shard[None], tokens, reward_out)


def pack_kernel(offset, hidden, prefix, blocks_held, parent_row, *rest):
    blocks, (row, notes, bias, scale, over) = rest[:-5], rest[-5:]
    _, own, _ = coordinates()
    groups, capacity = len(blocks), blocks[0].shape[0]
    rows, half = row.shape
    slots = groups * capacity
    arrived = jnp.concatenate([block[...].astype(jnp.float32) for block in blocks], 0)
    live = arrived[:, half + LIVE : half + LIVE + 1]
    first = lax.broadcasted_iota(jnp.int32, (slots, slots), 0)
    second = lax.broadcasted_iota(jnp.int32, (slots, slots), 1)
    place = jnp.sum(jnp.where(first < second, live, 0.0), 0, keepdims=True)
    kept = jnp.sum(jnp.where(first == second, live, 0.0), 0, keepdims=True) > 0.5
    wanted = lax.broadcasted_iota(jnp.int32, (rows, slots), 0) + offset
    take = (wanted == place.astype(jnp.int32)) & kept
    take = take.astype(jnp.float32).astype(jnp.bfloat16)
    row[...] = dot(take, arrived[:, :half].astype(jnp.bfloat16)).astype(jnp.bfloat16)
    note = dot(take, arrived[:, half : half + NOTES].astype(jnp.bfloat16))
    notes[...] = note
    parent = note[:, PARENT : PARENT + 1].astype(jnp.int32)
    parents = bias.shape[1] // prefix
    position = lax.broadcasted_iota(jnp.int32, (rows, prefix), 1)
    for p in range(parents):
        usable = (parent == p) & (position < blocks_held[own * parents + p] * 128)
        bias[:, p * prefix : (p + 1) * prefix] = jnp.where(usable, 0.0, MASKED)
    base = half + NOTES
    child = lax.broadcasted_iota(jnp.int32, parent_row.shape, 1)
    children = parent_row.shape[1] // groups
    at, child = lax.div(child, children), lax.rem(child, children)
    count = jnp.zeros(parent_row.shape, jnp.float32)
    for k in range(groups):
        head = arrived[k * capacity : k * capacity + 1, base:]
        scale[k : k + 1, :] = head[:, :hidden] + head[:, hidden : 2 * hidden] + head[:, 2 * hidden : 3 * hidden]
        count = jnp.where(at == lax.rem(own - k + groups, groups), head[:, 3 * hidden : 3 * hidden + 1], count)
    source = lax.div(parent_row[...], parents)
    going = child < count.astype(jnp.int32)
    most = jnp.zeros((1, 1), jnp.float32)
    for d in range(groups):
        load = jnp.sum(jnp.where((source == d) & going, 1.0, 0.0), 1, keepdims=True)
        most = jnp.maximum(most, load)
    over[...] = jnp.broadcast_to((most > rows).astype(jnp.int32), over.shape)


def pack(offset, rows, hidden, prefix, blocks_held, child_parent, blocks):
    groups = len(blocks)
    half = D // 2
    parents = blocks_held.shape[0] // groups
    return pl.pallas_call(
        functools.partial(pack_kernel, offset, hidden, prefix),
        out_shape=(
            struct((rows, half)),
            struct((rows, NOTES), jnp.float32),
            struct((rows, parents * prefix), jnp.float32),
            struct((groups, hidden), jnp.float32),
            struct((8, 128), jnp.int32),
        ),
        in_specs=[SCALARS] + [WHOLE] * (1 + groups),
        out_specs=[WHOLE] * 5,
        compiler_params=pltpu.CompilerParams(vmem_limit_bytes=12 << 20),
        name="pack",
    )(blocks_held, child_parent[None], *blocks)


def project(attn, w_out, out, first):
    width = out.shape[1]

    @pl.loop(0, width // CHUNK)
    def _(i):
        columns = pl.ds(pl.multiple_of(first + i * CHUNK, CHUNK), CHUNK)
        out[:, pl.ds(pl.multiple_of(i * CHUNK, CHUNK), CHUNK)] = dot(
            attn[...], w_out[:, columns]
        )[: out.shape[0]].astype(out.dtype)


def step_kernel(step, own, peer, gain, w_query, w_key, w_value, keys, values, bias, w_out, *rest):
    past_keys, past_values = rest[:step], rest[step : 2 * step]
    rest = rest[2 * step :]
    half = own.shape[1]
    slots = own.shape[0]
    q_cols, kv_cols = w_query.shape[1], w_key.shape[1]
    kv_heads = kv_cols // HD
    ready = {}
    if step == 0:
        part, attn, key_now, value_now, *kept, normed, query, sems = rest
        moves = [(w_query, kept[0], at, min(at + COLUMNS, q_cols)) for at in range(0, q_cols, COLUMNS)]
        moves += [(w, v, 0, w.shape[1]) for w, v in zip((w_key, w_value, keys, values, w_out), kept[1:])]
        for i, (source, target, at, end) in enumerate(moves):
            copy = pltpu.make_async_copy(source.at[:, at:end], target.at[:, at:end], sems.at[i])
            copy.start()
            ready[i] = copy
        w_query, w_key, w_value, keys, values, w_out = kept
    else:
        part, attn, key_now, value_now, normed, query = rest
    arrivals = iter(ready.values())

    def arrive():
        for copy in arrivals:
            copy.wait()
            break

    core, _, _ = coordinates()
    first = core == 0
    low = jnp.where(first, own[...], peer[...]).astype(jnp.float32)
    high = jnp.where(first, peer[...], own[...]).astype(jnp.float32)
    squares = jnp.sum(low * low, -1, keepdims=True) + jnp.sum(high * high, -1, keepdims=True)
    factor = lax.rsqrt(squares / D + 1e-06)
    normed[:slots, :half] = (low * factor * gain[:, :half]).astype(jnp.bfloat16)
    normed[:slots, half:] = (high * factor * gain[:, half:]).astype(jnp.bfloat16)
    if normed.shape[0] > slots:
        normed[slots:, :] = jnp.zeros((normed.shape[0] - slots, D), jnp.bfloat16)
    for at in range(0, q_cols, COLUMNS):
        end = min(at + COLUMNS, q_cols)
        arrive()
        query[:, at:end] = dot(normed[...], w_query[:, at:end])
    arrive()
    query[:, q_cols : q_cols + kv_cols] = dot(normed[...], w_key[...])
    arrive()
    query[:, q_cols + kv_cols :] = dot(normed[...], w_value[...])
    arrive()
    arrive()
    key_now[...] = query[:slots, q_cols : q_cols + kv_cols].astype(jnp.bfloat16)
    value_now[...] = query[:slots, q_cols + kv_cols :].astype(jnp.bfloat16)
    recent = slots * (step + 1)
    row = lax.broadcasted_iota(jnp.int32, (GROUP * slots, recent), 0)
    column = lax.broadcasted_iota(jnp.int32, (GROUP * slots, recent), 1)
    same = lax.rem(row, slots) == lax.rem(column, slots)
    for head in range(kv_heads):
        lanes = slice(head * HD, (head + 1) * HD)
        q = jnp.concatenate(
            [query[:slots, (head * GROUP + g) * HD : (head * GROUP + g + 1) * HD] for g in range(GROUP)], 0
        ).astype(jnp.bfloat16)
        k_new = jnp.concatenate([k[:, lanes] for k in past_keys] + [key_now[:, lanes]], 0)
        v_new = jnp.concatenate([v[:, lanes] for v in past_values] + [value_now[:, lanes]], 0)
        contract = (((1,), (1,)), ((), ()))
        s_old = lax.dot_general(q, keys[:, lanes], contract, preferred_element_type=jnp.float32)
        s_old = s_old + jnp.concatenate([bias[...]] * GROUP, 0)
        s_new = lax.dot_general(q, k_new, contract, preferred_element_type=jnp.float32)
        s_new = jnp.where(same, s_new, MASKED)
        top = jnp.maximum(jnp.max(s_old, -1, keepdims=True), jnp.max(s_new, -1, keepdims=True))
        p_old = jnp.exp2(s_old * EXPONENT - top * EXPONENT)
        p_new = jnp.exp2(s_new * EXPONENT - top * EXPONENT)
        total = jnp.sum(p_old, -1, keepdims=True) + jnp.sum(p_new, -1, keepdims=True)
        summed = dot(p_old.astype(jnp.bfloat16), values[:, lanes]) + dot(p_new.astype(jnp.bfloat16), v_new)
        result = (summed / total).astype(jnp.bfloat16)
        for g in range(GROUP):
            at = (head * GROUP + g) * HD
            attn[:slots, at : at + HD] = result[g * slots : (g + 1) * slots]
    if attn.shape[0] > slots:
        attn[slots:, :] = jnp.zeros((attn.shape[0] - slots, q_cols), jnp.bfloat16)
    arrive()
    project(attn, w_out, part, (1 - core) * half)


def expand(step, own, peer, gain, w_query, w_key, w_value, keys, values, bias, w_out, past_keys, past_values):
    slots, half = own.shape
    kv_cols = w_key.shape[1]
    q_cols = w_query.shape[1]
    padded = -(-slots // ROWS) * ROWS
    weights = (w_query, w_key, w_value, keys, values, w_out)
    kept, sems = [], []
    place = WHOLE
    if step == 0:
        kept = [VMEM(w.shape, w.dtype) for w in weights]
        sems = [pltpu.SemaphoreType.DMA((-(-q_cols // COLUMNS) + 5,))]
        place = pl.BlockSpec(memory_space=pl.ANY)
    return pl.pallas_call(
        functools.partial(step_kernel, step),
        out_shape=(
            struct((slots, half)), struct((padded, q_cols)), struct((slots, kv_cols)), struct((slots, kv_cols)), *kept
        ),
        in_specs=[WHOLE] * 3 + [place] * 5 + [WHOLE, place] + [WHOLE] * (2 * step),
        out_specs=[WHOLE] * (4 + len(kept)),
        scratch_shapes=[VMEM((padded, D), jnp.bfloat16), VMEM((padded, q_cols + 2 * kv_cols), jnp.float32)] + sems,
        compiler_params=pltpu.CompilerParams(vmem_limit_bytes=16 << 20),
        cost_estimate=SMALL,
        name="expand",
    )(own, peer, gain, w_query, w_key, w_value, keys, values, bias, w_out, *past_keys, *past_values)


def project_kernel(attn, w_out, part):
    core, _, _ = coordinates()
    project(attn, w_out, part, core * part.shape[1])


def project_own(rows, attn, w_out):
    return pl.pallas_call(
        project_kernel,
        out_shape=struct((rows, w_out.shape[1] // 2), jnp.float32),
        in_specs=[WHOLE, WHOLE],
        out_specs=WHOLE,
        compiler_params=pltpu.CompilerParams(vmem_limit_bytes=8 << 20),
        cost_estimate=SMALL,
        name="project_own",
    )(attn, w_out)


def score_kernel(steps, load, notes, up, *refs):
    own_rows, peer_rows = refs[:steps], refs[steps : 2 * steps]
    blocks, rest = refs[2 * steps : -2 - 2 * load], refs[-2 - 2 * load :]
    flat, total = rest[load : load + 2]
    copies = []
    if load:
        for r in range(up.shape[0]):
            copies.append(pltpu.make_async_copy(up.at[r], rest[0].at[r], rest[-1].at[r]))
            copies[-1].start()
        up = rest[0]
    groups, depth, hidden = up.shape
    mp = len(blocks)
    rows = own_rows[0].shape[0]
    here_core, _, me = coordinates()
    for t in range(steps):
        for m in range(mp):
            rows_from = [own_rows, peer_rows]
            for core in range(2):
                source = rows_from[int(m // (mp // 2) != core)][t]

                @pl.when((me == m) & (here_core == core))
                def _():
                    at = m % (mp // 2) * depth
                    flat[t * rows : (t + 1) * rows, :] = source[:, at : at + depth]

    shard = jnp.concatenate([notes[:, SHARD : SHARD + 1].astype(jnp.int32)] * steps, 0)
    for r in range(groups):
        if load:
            copies[r].wait()
        for at in range(0, hidden, COLUMNS):
            end = min(at + COLUMNS, hidden)
            here = jnp.where(shard == r, dot(flat[...], up[r, :, at:end]), 0.0)
            total[:, at:end] = here if r == 0 else total[:, at:end] + here
    width = hidden // mp
    for j, block in enumerate(blocks):
        for m in range(mp):

            @pl.when(lax.rem(me + j, mp) == m)
            def _():
                block[...] = total[:, m * width : (m + 1) * width].astype(jnp.bfloat16)


def score(mp, notes, up, own_rows, peer_rows, load):
    steps = len(own_rows)
    groups, depth, hidden = up.shape
    count = steps * own_rows[0].shape[0]
    block = struct((count, hidden // mp))
    return pl.pallas_call(
        functools.partial(score_kernel, steps, load),
        out_shape=(block,) * mp + (VMEM(up.shape, up.dtype),) * load,
        in_specs=[WHOLE, pl.BlockSpec(memory_space=pl.ANY) if load else WHOLE] + [WHOLE] * (2 * steps),
        out_specs=(WHOLE,) * (mp + load),
        scratch_shapes=[VMEM((count, depth), jnp.bfloat16), VMEM((count, hidden), jnp.float32)]
        + [pltpu.SemaphoreType.DMA((groups,))] * load,
        compiler_params=pltpu.CompilerParams(vmem_limit_bytes=16 << 20),
        cost_estimate=SMALL,
        name="score",
    )(notes, up, *own_rows, *peer_rows)


def scores_of(notes, scale, parts, own_rows, peer_rows):
    _, own, _ = coordinates()
    rows = notes.shape[0]
    shard = notes[:, SHARD : SHARD + 1].astype(jnp.int32)
    groups = scale.shape[0]
    block = lax.rem(own - shard + groups, groups)
    gain = jnp.zeros((rows, scale.shape[1]), jnp.float32)
    for k in range(groups):
        gain = gain + jnp.where(block == k, scale[k : k + 1, :], 0.0)
    values = []
    for t in range(len(own_rows)):
        z = sum(part[t * rows : (t + 1) * rows, :].astype(jnp.float32) for part in parts)
        low, high = own_rows[t][...].astype(jnp.float32), peer_rows[t][...].astype(jnp.float32)
        squares = jnp.sum(low * low, -1, keepdims=True) + jnp.sum(high * high, -1, keepdims=True)
        z = z * lax.rsqrt(squares / D + 1e-06)
        values.append(jnp.sum(z * jax.nn.sigmoid(z) * gain, -1, keepdims=True))
    return values


def finish_kernel(steps, notes, scale, *refs):
    own_rows, peer_rows, parts, out = refs[:steps], refs[steps : 2 * steps], refs[2 * steps : -1], refs[-1]
    lane = lax.broadcasted_iota(jnp.int32, out.shape, 1)
    total = jnp.zeros(out.shape, jnp.float32)
    for t, value in enumerate(scores_of(notes, scale, parts, own_rows, peer_rows)):
        total = jnp.where(lane == t, value, total)
    out[...] = total


def finish(notes, scale, own_rows, peer_rows, parts):
    steps = len(own_rows)
    return pl.pallas_call(
        functools.partial(finish_kernel, steps),
        out_shape=struct((notes.shape[0], 128), jnp.float32),
        in_specs=[WHOLE] * (2 + 2 * steps + len(parts)),
        out_specs=WHOLE,
        compiler_params=pltpu.CompilerParams(vmem_limit_bytes=12 << 20),
        cost_estimate=SMALL,
        name="finish",
    )(notes, scale, *own_rows, *peer_rows, *parts)


def place_kernel(groups, cap, before, notes, scale, own_row, peer_row, *refs):
    parts, table = refs[:-1], refs[-1]
    rows = notes.shape[0]
    values = [before[:, t : t + 1] for t in range(STEPS - 1)]
    values += scores_of(notes, scale, parts, [own_row], [peer_row])
    number = lambda lane: notes[:, lane : lane + 1].astype(jnp.int32)
    shard, at = number(SHARD), number(SOURCE) * cap + number(RANK)
    live = notes[:, LIVE : LIVE + 1] > 0.5
    column = lax.broadcasted_iota(jnp.int32, (rows, table.shape[1]), 1)
    for r in range(groups):
        spots = (column == at) & (shard == r) & live
        for t, value in enumerate(values):
            table[r * STEPS + t : r * STEPS + t + 1, :] = jnp.sum(jnp.where(spots, value, 0.0), 0, keepdims=True)


def place(groups, cap, before, notes, scale, own_row, peer_row, parts):
    return pl.pallas_call(
        functools.partial(place_kernel, groups, cap),
        out_shape=struct((groups * STEPS, -(-groups * cap // 128) * 128), jnp.float32),
        in_specs=[WHOLE] * (5 + len(parts)),
        out_specs=WHOLE,
        compiler_params=pltpu.CompilerParams(vmem_limit_bytes=12 << 20),
        cost_estimate=SMALL,
        name="place",
    )(before, notes, scale, own_row, peer_row, *parts)


def shards(
    tokens,
    parent_keys,
    parent_values,
    parent_blocks,
    child_parent,
    child_count,
    node_shard,
    attn_gain,
    w_query,
    w_key,
    w_value,
    w_out,
    reward_up,
    reward_out,
):
    groups, mp = lax.axis_size("dp"), lax.axis_size("mp")
    children, width = tokens.shape
    parents, prefix, kv_cols = parent_keys.shape
    capacity = max(2, 2 * children // groups)
    reward_cap = max(2, 3 * children // (2 * groups))
    slots = groups * capacity
    rows = min(slots, 3 * children // 2)
    hidden = reward_out.shape[1] // mp
    swap = [(i, i ^ 1) for i in range(mp)]
    shift = lambda count, k: [(i, (i + k) % count) for i in range(count)]

    up = lax.all_gather(reward_up[0], "dp", axis=0)

    blocks = dispatch(parents, child_count, child_parent, node_shard, tokens, reward_out, groups, capacity, hidden)
    blocks = [blocks[0]] + [lax.ppermute(blocks[k], "dp", shift(groups, k)) for k in range(1, groups)]

    keys = parent_keys.reshape(parents * prefix, kv_cols)
    values = parent_values.reshape(parents * prefix, kv_cols)
    raw = (w_query, w_key, w_value, keys, values, w_out)
    gain = attn_gain.reshape(1, width)

    def run(offset, blocks, raw, up, gain, child_parent, parent_blocks):
        row_own, notes, bias, scale, over = pack(
            offset, rows, hidden, prefix, parent_blocks, child_parent, blocks
        )
        weights = raw
        state = row_own.astype(jnp.float32)
        row_peer = lax.ppermute(row_own, "mp", swap)
        past_keys, past_values, rows_own, rows_peer = [], [], [], []

        def products(first, last, up, load):
            sums = score(mp, notes, up, rows_own[first:last], rows_peer[first:last], load)
            return sums[:mp], held(sums[-1])

        send = lambda sums: [sums[0]] + [lax.ppermute(sums[k], "mp", shift(mp, k)) for k in range(1, mp)]
        for step in range(STEPS):
            w_query, w_key, w_value, keys, values, w_out = weights
            part, attn, key_now, value_now, *kept = expand(
                step, row_own, row_peer, gain, w_query, w_key, w_value, keys, values, bias, w_out,
                past_keys, past_values,
            )
            if step == 0:
                weights = [held(x) for x in kept]
            past_keys.append(key_now)
            past_values.append(value_now)
            from_peer = lax.ppermute(part, "mp", swap)
            chip = project_own(rows, attn, weights[-1]) + from_peer.astype(jnp.float32)
            sent = chip.astype(jnp.bfloat16)
            others = [lax.ppermute(sent, "mp", shift(mp, k)) for k in range(2, mp, 2)]
            if step + 1 == STEPS:
                _, up = lax.optimization_barrier((sent, up))
                before, up = products(0, step, up, True)
                over = over[0, 0]
                others, before, over = lax.optimization_barrier((others, before, over))
            for other in others:
                chip = chip + other.astype(jnp.float32)
            state = state + chip
            row_own = state.astype(jnp.bfloat16)
            row_peer = lax.ppermute(row_own, "mp", swap)
            rows_own.append(row_own)
            rows_peer.append(row_peer)
        before = send(before)
        last, _ = products(step, STEPS, up, False)
        last = send(last)
        before = finish(notes, scale, rows_own[:step], rows_peer[:step], before)
        return place(groups, reward_cap, before, notes, scale, row_own, row_peer, last), over

    operands = (blocks, raw, up, gain, child_parent, parent_blocks)

    table, over = run(0, *operands)
    if rows < slots:
        table, operands = lax.optimization_barrier((table, operands))
        again = lambda table, operands: table + run(rows, *operands)[0]
        table = lax.cond(over > 0, again, lambda table, operands: table, table, operands)

    table = lax.all_to_all(table, "dp", split_axis=0, concat_axis=0, tiled=True)
    total = jnp.sum(table.reshape(groups, STEPS, -1), 0)[:, : groups * reward_cap]
    total = total + lax.ppermute(total, "mp", swap)
    result = total
    for k in range(2, mp, 2):
        result = result + lax.ppermute(total, "mp", shift(mp, k))
    return result


def solution(mesh):
    placed = (
        P("dp", None),
        P("dp", None, "mp"),
        P("dp", None, "mp"),
        P(),
        P(),
        P("dp"),
        P(),
        P(),
        P(None, "mp"),
        P(None, "mp"),
        P(None, "mp"),
        P("mp", None),
        P("dp", "mp", None),
        P("dp", None),
    )
    return jax.shard_map(
        shards, mesh=mesh, in_specs=placed, out_specs=P(None, "dp"), check_vma=False
    )
```

```python
import functools
import math

import jax
import jax.numpy as jnp
from jax import lax
from jax.experimental import pallas as pl
from jax.experimental.pallas import tpu as pltpu
from jax.sharding import PartitionSpec as P

D = 5120
HEADS = 24
KVH = 8
HD = 128
STEPS = 8
GROUP = HEADS // KVH
CHUNK = 512
COLUMNS = 256
ROWS = 64
MASKED = -1e30
EXPONENT = HD ** (-0.5) * math.log2(math.e)
VMEM = pltpu.VMEM
NOTES = 128
LIVE, RANK, SHARD, PARENT, SOURCE = range(5)


def dot(a, b):
    return jnp.dot(a, b, preferred_element_type=jnp.float32)


def held(x):
    return pltpu.with_memory_space_constraint(x, VMEM)


def struct(shape, dtype=jnp.bfloat16):
    return jax.ShapeDtypeStruct(shape, dtype)


WHOLE = pl.BlockSpec(memory_space=VMEM)
SMALL = pl.CostEstimate(flops=0, bytes_accessed=0, transcendentals=0)
SCALARS = pl.BlockSpec(memory_space=pltpu.SMEM)


def coordinates():
    me = lax.axis_index("mp")
    return lax.rem(me, 2), lax.axis_index("dp"), me


def dispatch_kernel(parents, groups, count, parent_far, shard_far, tokens_far, reward_far, block, *near):
    core, own, me = coordinates()
    parent_row, shard_row, tokens, reward_out, sems = near
    children, half = tokens.shape
    sources = (parent_far, shard_far, tokens_far.at[:, pl.ds(pl.multiple_of(core * half, half), half)], reward_far)
    copies = [pltpu.make_async_copy(a, b, sems.at[i]) for i, (a, b) in enumerate(zip(sources, near))]
    for copy in copies:
        copy.start()
    for copy in copies:
        copy.wait()
    capacity = block.shape[0] // groups
    everyone = parent_row.shape[1]
    int32, float32, bfloat16 = jnp.int32, jnp.float32, jnp.bfloat16

    mine = lax.broadcasted_iota(int32, (everyone, children), 0) - own * children
    mine = (mine == lax.broadcasted_iota(int32, (everyone, children), 1)).astype(float32).astype(bfloat16)

    def row_and_column(table):
        table = table[...].astype(float32).astype(bfloat16)
        column = lax.dot_general(mine, table, (((0,), (1,)), ((), ())), preferred_element_type=float32)
        return dot(table, mine).astype(int32), column.astype(int32)

    parent, parent_c = row_and_column(parent_row)
    shard, shard_c = row_and_column(shard_row)
    source, source_c = lax.div(parent, parents), lax.div(parent_c, parents)
    first = lax.broadcasted_iota(int32, (children, children), 0)
    second = lax.broadcasted_iota(int32, (children, children), 1)
    live = lax.broadcasted_iota(int32, (1, children), 1) < count[0]
    live_c = lax.broadcasted_iota(int32, (children, 1), 0) < count[0]
    rank = jnp.sum(jnp.where((source_c == source) & (first < second) & live_c, 1, 0), 0, keepdims=True)
    slot = source * capacity + rank
    slot = jnp.where(live, slot, -1)
    reward_rank = jnp.sum(jnp.where((shard_c == shard) & (second < first) & live, 1, 0), 1, keepdims=True)
    lane = lax.broadcasted_iota(int32, (children, NOTES), 1)
    notes = jnp.where(lane == LIVE, live_c.astype(int32), 0)
    for at, value in ((RANK, reward_rank), (SHARD, shard_c), (PARENT, lax.rem(parent_c, parents)), (SOURCE, own)):
        notes = jnp.where(lane == at, value, notes)

    width = block.shape[1] - half - NOTES
    hidden = (width - 128) // 3
    rest = jnp.zeros((1, hidden), float32)
    for m in range(reward_out.shape[1] // hidden):
        rest = rest + jnp.where(me == m, reward_out[:, m * hidden : (m + 1) * hidden], 0.0)
    parts = []
    for _ in range(3):
        parts.append(rest.astype(bfloat16).astype(float32))
        rest = rest - parts[-1]
    parts.append(jnp.full((1, 128), 1, int32).astype(float32) * count[0].astype(float32))
    shared = jnp.broadcast_to(jnp.concatenate(parts, 1), (groups * capacity, width))

    rows = lax.broadcasted_iota(int32, (groups * capacity, children), 0)
    put = (rows == slot).astype(float32).astype(bfloat16)
    token_rows = dot(put, tokens[...])
    note_rows = dot(put, notes.astype(float32).astype(bfloat16))
    block[:, :half] = token_rows.astype(bfloat16)
    block[:, half : half + NOTES] = note_rows.astype(bfloat16)
    block[:, half + NOTES :] = shared.astype(bfloat16)


def dispatch(parents, child_count, child_parent, node_shard, tokens, reward_out, groups, capacity, hidden):
    children, half = tokens.shape[0], tokens.shape[1] // 2
    tables = (child_parent[None], node_shard[None])
    anywhere = pl.BlockSpec(memory_space=pl.ANY)
    return pl.pallas_call(
        functools.partial(dispatch_kernel, parents, groups),
        out_shape=struct((groups * capacity, half + NOTES + 3 * hidden + 128)),
        in_specs=[SCALARS] + [anywhere] * 4,
        out_specs=WHOLE,
        scratch_shapes=[VMEM(x.shape, x.dtype) for x in tables]
        + [VMEM((children, half), tokens.dtype), VMEM(reward_out.shape, reward_out.dtype)]
        + [pltpu.SemaphoreType.DMA((4,))],
        compiler_params=pltpu.CompilerParams(vmem_limit_bytes=8 << 20),
        cost_estimate=SMALL,
        name="dispatch",
    )(child_count, *tables, tokens, reward_out)


def pack_kernel(offset, hidden, prefix, blocks_held, parent_row, arrived, row, notes, bias, scale, over):
    _, own, _ = coordinates()
    groups, slots = scale.shape[0], arrived.shape[0]
    capacity = slots // groups
    rows, half = row.shape
    noted = arrived[:, half : half + NOTES].astype(jnp.float32)
    live = noted[:, LIVE : LIVE + 1]
    first = lax.broadcasted_iota(jnp.int32, (slots, slots), 0)
    second = lax.broadcasted_iota(jnp.int32, (slots, slots), 1)
    place = jnp.sum(jnp.where(first < second, live, 0.0), 0, keepdims=True)
    kept = jnp.sum(jnp.where(first == second, live, 0.0), 0, keepdims=True) > 0.5
    wanted = lax.broadcasted_iota(jnp.int32, (rows, slots), 0) + offset
    take = (wanted == place.astype(jnp.int32)) & kept
    take = take.astype(jnp.float32).astype(jnp.bfloat16)
    row[...] = dot(take, arrived[:, :half]).astype(jnp.bfloat16)
    note = dot(take, arrived[:, half : half + NOTES])
    notes[...] = note
    parent = note[:, PARENT : PARENT + 1].astype(jnp.int32)
    parents = bias.shape[1] // prefix
    position = lax.broadcasted_iota(jnp.int32, (rows, prefix), 1)
    for p in range(parents):
        usable = (parent == p) & (position < blocks_held[own * parents + p] * 128)
        bias[:, p * prefix : (p + 1) * prefix] = jnp.where(usable, 0.0, MASKED)
    base = half + NOTES
    child = lax.broadcasted_iota(jnp.int32, parent_row.shape, 1)
    children = parent_row.shape[1] // groups
    at, child = lax.div(child, children), lax.rem(child, children)
    count = jnp.zeros(parent_row.shape, jnp.float32)
    shared = arrived[:, base:].astype(jnp.float32)
    for k in range(groups):
        head = shared[k * capacity : k * capacity + 1]
        scale[k : k + 1, :] = head[:, :hidden] + head[:, hidden : 2 * hidden] + head[:, 2 * hidden : 3 * hidden]
        count = jnp.where(at == k, head[:, 3 * hidden : 3 * hidden + 1], count)
    source = lax.div(parent_row[...], parents)
    going = child < count.astype(jnp.int32)
    most = jnp.zeros((1, 1), jnp.float32)
    for d in range(groups):
        load = jnp.sum(jnp.where((source == d) & going, 1.0, 0.0), 1, keepdims=True)
        most = jnp.maximum(most, load)
    over[...] = jnp.broadcast_to((most > rows).astype(jnp.int32), over.shape)


def pack(offset, rows, hidden, prefix, groups, blocks_held, child_parent, arrived):
    half = D // 2
    parents = blocks_held.shape[0] // groups
    return pl.pallas_call(
        functools.partial(pack_kernel, offset, hidden, prefix),
        out_shape=(
            struct((rows, half)),
            struct((rows, NOTES), jnp.float32),
            struct((rows, parents * prefix), jnp.float32),
            struct((groups, hidden), jnp.float32),
            struct((8, 128), jnp.int32),
        ),
        in_specs=[SCALARS, WHOLE, WHOLE],
        out_specs=[WHOLE] * 5,
        compiler_params=pltpu.CompilerParams(vmem_limit_bytes=12 << 20),
        cost_estimate=SMALL,
        name="pack",
    )(blocks_held, child_parent[None], arrived)


def project(attn, w_out, out, first):
    width = out.shape[1]

    @pl.loop(0, width // CHUNK)
    def _(i):
        columns = pl.ds(pl.multiple_of(first + i * CHUNK, CHUNK), CHUNK)
        out[:, pl.ds(pl.multiple_of(i * CHUNK, CHUNK), CHUNK)] = dot(
            attn[...], w_out[:, columns]
        )[: out.shape[0]].astype(out.dtype)


def step_kernel(step, own, peer, gain, w_query, w_key, w_value, keys, values, bias, w_out, *rest):
    past_keys, past_values = rest[:step], rest[step : 2 * step]
    rest = rest[2 * step :]
    half = own.shape[1]
    slots = own.shape[0]
    q_cols, kv_cols = w_query.shape[1], w_key.shape[1]
    kv_heads = kv_cols // HD
    ready = {}
    if step == 0:
        part, attn, key_now, value_now, norm, *kept, normed, query, sems = rest
        moves = [(w_query, kept[0], at, min(at + COLUMNS, q_cols)) for at in range(0, q_cols, COLUMNS)]
        moves += [(w, v, 0, w.shape[1]) for w, v in zip((w_key, w_value, keys, values, w_out), kept[1:])]
        for i, (source, target, at, end) in enumerate(moves):
            copy = pltpu.make_async_copy(source.at[:, at:end], target.at[:, at:end], sems.at[i])
            copy.start()
            ready[i] = copy
        w_query, w_key, w_value, keys, values, w_out = kept
    else:
        part, attn, key_now, value_now, norm, normed, query = rest
    arrivals = iter(ready.values())

    def arrive():
        for copy in arrivals:
            copy.wait()
            break

    core, _, _ = coordinates()
    first = core == 0
    low = jnp.where(first, own[...], peer[...]).astype(jnp.float32)
    high = jnp.where(first, peer[...], own[...]).astype(jnp.float32)
    squares = jnp.sum(low * low, -1, keepdims=True) + jnp.sum(high * high, -1, keepdims=True)
    factor = lax.rsqrt(squares / D + 1e-06)
    norm[...] = jnp.broadcast_to(factor, norm.shape)
    normed[:slots, :half] = (low * factor * gain[:, :half]).astype(jnp.bfloat16)
    normed[:slots, half:] = (high * factor * gain[:, half:]).astype(jnp.bfloat16)
    if normed.shape[0] > slots:
        normed[slots:, :] = jnp.zeros((normed.shape[0] - slots, D), jnp.bfloat16)
    for at in range(0, q_cols, COLUMNS):
        end = min(at + COLUMNS, q_cols)
        arrive()
        query[:, at:end] = dot(normed[...], w_query[:, at:end])
    arrive()
    query[:, q_cols : q_cols + kv_cols] = dot(normed[...], w_key[...])
    arrive()
    query[:, q_cols + kv_cols :] = dot(normed[...], w_value[...])
    arrive()
    arrive()
    key_now[...] = query[:slots, q_cols : q_cols + kv_cols].astype(jnp.bfloat16)
    value_now[...] = query[:slots, q_cols + kv_cols :].astype(jnp.bfloat16)
    recent = slots * (step + 1)
    row = lax.broadcasted_iota(jnp.int32, (GROUP * slots, recent), 0)
    column = lax.broadcasted_iota(jnp.int32, (GROUP * slots, recent), 1)
    same = lax.rem(row, slots) == lax.rem(column, slots)
    for head in range(kv_heads):
        lanes = slice(head * HD, (head + 1) * HD)
        q = jnp.concatenate(
            [query[:slots, (head * GROUP + g) * HD : (head * GROUP + g + 1) * HD] for g in range(GROUP)], 0
        ).astype(jnp.bfloat16)
        k_new = jnp.concatenate([k[:, lanes] for k in past_keys] + [key_now[:, lanes]], 0)
        v_new = jnp.concatenate([v[:, lanes] for v in past_values] + [value_now[:, lanes]], 0)
        contract = (((1,), (1,)), ((), ()))
        s_old = lax.dot_general(q, keys[:, lanes], contract, preferred_element_type=jnp.float32)
        s_old = s_old + jnp.concatenate([bias[...]] * GROUP, 0)
        s_new = lax.dot_general(q, k_new, contract, preferred_element_type=jnp.float32)
        s_new = jnp.where(same, s_new, MASKED)
        top = jnp.maximum(jnp.max(s_old, -1, keepdims=True), jnp.max(s_new, -1, keepdims=True))
        p_old = jnp.exp2(s_old * EXPONENT - top * EXPONENT)
        p_new = jnp.exp2(s_new * EXPONENT - top * EXPONENT)
        total = jnp.sum(p_old, -1, keepdims=True) + jnp.sum(p_new, -1, keepdims=True)
        summed = dot(p_old.astype(jnp.bfloat16), values[:, lanes]) + dot(p_new.astype(jnp.bfloat16), v_new)
        result = (summed / total).astype(jnp.bfloat16)
        for g in range(GROUP):
            at = (head * GROUP + g) * HD
            attn[:slots, at : at + HD] = result[g * slots : (g + 1) * slots]
    if attn.shape[0] > slots:
        attn[slots:, :] = jnp.zeros((attn.shape[0] - slots, q_cols), jnp.bfloat16)
    arrive()
    project(attn, w_out, part, (1 - core) * half)


def expand(step, own, peer, gain, w_query, w_key, w_value, keys, values, bias, w_out, past_keys, past_values):
    slots, half = own.shape
    kv_cols = w_key.shape[1]
    q_cols = w_query.shape[1]
    padded = -(-slots // ROWS) * ROWS
    weights = (w_query, w_key, w_value, keys, values, w_out)
    kept, sems = [], []
    place = WHOLE
    if step == 0:
        kept = [VMEM(w.shape, w.dtype) for w in weights]
        sems = [pltpu.SemaphoreType.DMA((-(-q_cols // COLUMNS) + 5,))]
        place = pl.BlockSpec(memory_space=pl.ANY)
    return pl.pallas_call(
        functools.partial(step_kernel, step),
        out_shape=(
            struct((slots, half)), struct((padded, q_cols)), struct((slots, kv_cols)), struct((slots, kv_cols)),
            struct((slots, 128), jnp.float32), *kept
        ),
        in_specs=[WHOLE] * 3 + [place] * 5 + [WHOLE, place] + [WHOLE] * (2 * step),
        out_specs=[WHOLE] * (5 + len(kept)),
        scratch_shapes=[VMEM((padded, D), jnp.bfloat16), VMEM((padded, q_cols + 2 * kv_cols), jnp.float32)] + sems,
        compiler_params=pltpu.CompilerParams(vmem_limit_bytes=16 << 20),
        cost_estimate=SMALL,
        name="expand",
    )(own, peer, gain, w_query, w_key, w_value, keys, values, bias, w_out, *past_keys, *past_values)


def project_kernel(attn, w_out, part):
    core, _, _ = coordinates()
    project(attn, w_out, part, core * part.shape[1])


def project_own(rows, attn, w_out):
    return pl.pallas_call(
        project_kernel,
        out_shape=struct((rows, w_out.shape[1] // 2), jnp.float32),
        in_specs=[WHOLE, WHOLE],
        out_specs=WHOLE,
        compiler_params=pltpu.CompilerParams(vmem_limit_bytes=8 << 20),
        cost_estimate=SMALL,
        name="project_own",
    )(attn, w_out)


def score_kernel(steps, load, cuts, mp, notes, *refs):
    take = lambda count: [refs.pop(0) for _ in range(count)]
    refs = list(refs)
    ups, own_rows, peer_rows, blocks = take(cuts), take(steps), take(steps), take(mp)
    kept = take(cuts * load)
    flat, total, *sems = refs
    groups, depth, hidden = ups[0].shape
    rows = own_rows[0].shape[0]
    core, _, me = coordinates()
    for t in range(steps):
        target = flat.at[t * rows : (t + 1) * rows]
        for m in range(mp):
            at = m % (mp // 2) * depth * cuts
            for c in range(2):
                source = (own_rows if m // (mp // 2) == c else peer_rows)[t].at[:, at : at + depth * cuts]

                @pl.when((me == m) & (core == c))
                def _():
                    if load:
                        pltpu.make_async_copy(source, target, sems[0].at[t]).start()
                    else:
                        target[...] = source[...]

    copies = {}
    if load:
        for r in range(groups):
            for i in range(cuts):
                copies[r, i] = pltpu.make_async_copy(ups[i].at[r], kept[i].at[r], sems[1].at[r, i])
                copies[r, i].start()
        ups = kept
        for t in range(steps):
            target = flat.at[t * rows : (t + 1) * rows]
            pltpu.make_async_copy(target, target, sems[0].at[t]).wait()
    shard = jnp.concatenate([notes[:, SHARD : SHARD + 1].astype(jnp.int32)] * steps, 0)
    for r in range(groups):
        for i in range(cuts):
            if load:
                copies[r, i].wait()
        for at in range(0, hidden, COLUMNS):
            end = min(at + COLUMNS, hidden)
            z = sum(dot(flat[:, i * depth : (i + 1) * depth], ups[i][r, :, at:end]) for i in range(cuts))
            here = jnp.where(shard == r, z, 0.0)
            total[:, at:end] = here if r == 0 else total[:, at:end] + here
    width = hidden // mp
    for j, block in enumerate(blocks):
        for m in range(mp):

            @pl.when(lax.rem(me + j, mp) == m)
            def _():
                block[...] = total[:, m * width : (m + 1) * width].astype(jnp.bfloat16)


def score(mp, notes, ups, own_rows, peer_rows, load):
    steps, cuts = len(own_rows), len(ups)
    groups, depth, hidden = ups[0].shape
    count = steps * own_rows[0].shape[0]
    block = struct((count, hidden // mp))
    far = pl.BlockSpec(memory_space=pl.ANY) if load else WHOLE
    return pl.pallas_call(
        functools.partial(score_kernel, steps, load, cuts, mp),
        out_shape=(block,) * mp + tuple(VMEM(up.shape, up.dtype) for up in ups) * load,
        in_specs=[WHOLE] + [far] * (cuts + 2 * steps),
        out_specs=(WHOLE,) * (mp + cuts * load),
        scratch_shapes=[VMEM((count, depth * cuts), jnp.bfloat16), VMEM((count, hidden), jnp.float32)]
        + [pltpu.SemaphoreType.DMA((steps,)), pltpu.SemaphoreType.DMA((groups, cuts))] * load,
        compiler_params=pltpu.CompilerParams(vmem_limit_bytes=16 << 20),
        cost_estimate=SMALL,
        name="score",
    )(notes, *ups, *own_rows, *peer_rows)


def scores_of(notes, scale, parts, factors):
    rows = notes.shape[0]
    shard = notes[:, SHARD : SHARD + 1].astype(jnp.int32)
    gain = jnp.zeros((rows, scale.shape[1]), jnp.float32)
    for r in range(scale.shape[0]):
        gain = gain + jnp.where(shard == r, scale[r : r + 1, :], 0.0)
    values = []
    for t, factor in enumerate(factors):
        z = sum(part[t * rows : (t + 1) * rows, :].astype(jnp.float32) for part in parts) * factor
        values.append(jnp.sum(z * jax.nn.sigmoid(z) * gain, -1, keepdims=True))
    return values


def finish_kernel(steps, notes, scale, *refs):
    norms, parts, out = refs[:steps], refs[steps:-1], refs[-1]
    lane = lax.broadcasted_iota(jnp.int32, out.shape, 1)
    total = jnp.zeros(out.shape, jnp.float32)
    for t, value in enumerate(scores_of(notes, scale, parts, [norm[:, :1] for norm in norms])):
        total = jnp.where(lane == t, value, total)
    out[...] = total


def finish(notes, scale, norms, parts):
    return pl.pallas_call(
        functools.partial(finish_kernel, len(norms)),
        out_shape=struct((notes.shape[0], 128), jnp.float32),
        in_specs=[WHOLE] * (2 + len(norms) + len(parts)),
        out_specs=WHOLE,
        compiler_params=pltpu.CompilerParams(vmem_limit_bytes=12 << 20),
        cost_estimate=SMALL,
        name="finish",
    )(notes, scale, *norms, *parts)


def place_kernel(groups, cap, before, notes, scale, own_row, peer_row, *refs):
    parts, table = refs[:-1], refs[-1]
    rows = notes.shape[0]
    values = [before[:, t : t + 1] for t in range(STEPS - 1)]
    low, high = own_row[...].astype(jnp.float32), peer_row[...].astype(jnp.float32)
    squares = jnp.sum(low * low, -1, keepdims=True) + jnp.sum(high * high, -1, keepdims=True)
    values += scores_of(notes, scale, parts, [lax.rsqrt(squares / D + 1e-06)])
    number = lambda lane: notes[:, lane : lane + 1].astype(jnp.int32)
    shard, at = number(SHARD), number(SOURCE) * cap + number(RANK)
    live = notes[:, LIVE : LIVE + 1] > 0.5
    column = lax.broadcasted_iota(jnp.int32, (rows, table.shape[1]), 1)
    for r in range(groups):
        spots = (column == at) & (shard == r) & live
        for t, value in enumerate(values):
            table[r * STEPS + t : r * STEPS + t + 1, :] = jnp.sum(jnp.where(spots, value, 0.0), 0, keepdims=True)


def place(groups, cap, before, notes, scale, own_row, peer_row, parts):
    return pl.pallas_call(
        functools.partial(place_kernel, groups, cap),
        out_shape=struct((groups * STEPS, -(-groups * cap // 128) * 128), jnp.float32),
        in_specs=[WHOLE] * (5 + len(parts)),
        out_specs=WHOLE,
        compiler_params=pltpu.CompilerParams(vmem_limit_bytes=12 << 20),
        cost_estimate=SMALL,
        name="place",
    )(before, notes, scale, own_row, peer_row, *parts)


def shards(
    tokens,
    parent_keys,
    parent_values,
    parent_blocks,
    child_parent,
    child_count,
    node_shard,
    attn_gain,
    w_query,
    w_key,
    w_value,
    w_out,
    reward_up,
    reward_out,
):
    groups, mp = lax.axis_size("dp"), lax.axis_size("mp")
    children, width = tokens.shape
    parents, prefix, kv_cols = parent_keys.shape
    capacity = max(2, 2 * children // groups)
    reward_cap = max(2, 3 * children // (2 * groups))
    slots = groups * capacity
    rows = min(slots, 3 * children // 2)
    hidden = reward_out.shape[1] // mp
    swap = [(i, i ^ 1) for i in range(mp)]
    shift = lambda count, k: [(i, (i + k) % count) for i in range(count)]

    ups = [lax.all_gather(reward_up[0], "dp", axis=0)]

    blocks = dispatch(parents, child_count, child_parent, node_shard, tokens, reward_out, groups, capacity, hidden)
    blocks = lax.all_to_all(blocks, "dp", split_axis=0, concat_axis=0, tiled=True)

    keys = parent_keys.reshape(parents * prefix, kv_cols)
    values = parent_values.reshape(parents * prefix, kv_cols)
    raw = (w_query, w_key, w_value, keys, values, w_out)
    gain = attn_gain.reshape(1, width)

    def run(offset, blocks, raw, ups, gain, child_parent, parent_blocks):
        row_own, notes, bias, scale, over = pack(
            offset, rows, hidden, prefix, groups, parent_blocks, child_parent, blocks
        )
        weights = raw
        state = row_own.astype(jnp.float32)
        row_peer = lax.ppermute(row_own, "mp", swap)
        past_keys, past_values, rows_own, rows_peer, norms = [], [], [], [], []

        def products(first, last, ups, load):
            sums = score(mp, notes, ups, rows_own[first:last], rows_peer[first:last], load)
            return sums[:mp], [held(up) for up in sums[mp:]]

        send = lambda sums: [sums[0]] + [lax.ppermute(sums[k], "mp", shift(mp, k)) for k in range(1, mp)]
        for step in range(STEPS):
            w_query, w_key, w_value, keys, values, w_out = weights
            part, attn, key_now, value_now, norm, *kept = expand(
                step, row_own, row_peer, gain, w_query, w_key, w_value, keys, values, bias, w_out,
                past_keys, past_values,
            )
            if step == 0:
                weights = [held(x) for x in kept]
            norms.append(norm)
            past_keys.append(key_now)
            past_values.append(value_now)
            from_peer = lax.ppermute(part, "mp", swap)
            chip = project_own(rows, attn, weights[-1]) + from_peer.astype(jnp.float32)
            sent = chip.astype(jnp.bfloat16)
            others = [lax.ppermute(sent, "mp", shift(mp, k)) for k in range(2, mp, 2)]
            if step + 1 == STEPS:
                _, ups = lax.optimization_barrier((sent, ups))
                before, ups = products(0, step, ups, True)
                others, before = lax.optimization_barrier((others, before))
            for other in others:
                chip = chip + other.astype(jnp.float32)
            state = state + chip
            row_own = state.astype(jnp.bfloat16)
            row_peer = lax.ppermute(row_own, "mp", swap)
            rows_own.append(row_own)
            rows_peer.append(row_peer)
        before = send(before)
        last, _ = products(step, STEPS, ups, False)
        last, over = lax.optimization_barrier((send(last), over[0, 0]))
        before = finish(notes, scale, norms[1:], before)
        return place(groups, reward_cap, before, notes, scale, row_own, row_peer, last), over

    operands = (blocks, raw, ups, gain, child_parent, parent_blocks)

    table, over = run(0, *operands)
    if rows < slots:
        table, operands = lax.optimization_barrier((table, operands))
        again = lambda table, operands: table + run(rows, *operands)[0]
        table = lax.cond(over > 0, again, lambda table, operands: table, table, operands)

    table = lax.all_to_all(table, "dp", split_axis=0, concat_axis=0, tiled=True)
    total = jnp.sum(table.reshape(groups, STEPS, -1), 0)[:, : groups * reward_cap]
    total = total + lax.ppermute(total, "mp", swap)
    result = total
    for k in range(2, mp, 2):
        result = result + lax.ppermute(total, "mp", shift(mp, k))
    return result


def solution(mesh):
    placed = (
        P("dp", None),
        P("dp", None, "mp"),
        P("dp", None, "mp"),
        P(),
        P(),
        P("dp"),
        P(),
        P(),
        P(None, "mp"),
        P(None, "mp"),
        P(None, "mp"),
        P("mp", None),
        P("dp", "mp", None),
        P("dp", None),
    )
    return jax.shard_map(
        shards, mesh=mesh, in_specs=placed, out_specs=P(None, "dp"), check_vma=False
    )
```

```python
import functools
import math

import jax
import jax.numpy as jnp
from jax import lax
from jax.experimental import pallas as pl
from jax.experimental.pallas import tpu as pltpu
from jax.sharding import PartitionSpec as P

D = 5120
HEADS = 24
KVH = 8
HD = 128
STEPS = 8
GROUP = HEADS // KVH
CHUNK = 512
COLUMNS = 256
ROWS = 64
MASKED = -1e30
EXPONENT = HD ** (-0.5) * math.log2(math.e)
VMEM = pltpu.VMEM
NOTES = 128
LIVE, RANK, SHARD, PARENT, SOURCE = range(5)


def dot(a, b):
    return jnp.dot(a, b, preferred_element_type=jnp.float32)


def held(x):
    return pltpu.with_memory_space_constraint(x, VMEM)


def far(x):
    return pltpu.with_memory_space_constraint(x, pltpu.HBM)


def struct(shape, dtype=jnp.bfloat16):
    return jax.ShapeDtypeStruct(shape, dtype)


WHOLE = pl.BlockSpec(memory_space=VMEM)
FAR = pl.BlockSpec(memory_space=pltpu.HBM)
SMALL = pl.CostEstimate(flops=0, bytes_accessed=0, transcendentals=0)
SCALARS = pl.BlockSpec(memory_space=pltpu.SMEM)


def coordinates():
    me = lax.axis_index("mp")
    return lax.rem(me, 2), lax.axis_index("dp"), me


def dispatch_kernel(parents, groups, count, parent_far, shard_far, tokens_far, reward_far, *rest):
    core, own, me = coordinates()
    blocks, near = rest[:groups], rest[groups:]
    parent_row, shard_row, tokens, reward_out, sems = near
    children, half = tokens.shape
    sources = (parent_far, shard_far, tokens_far.at[:, pl.ds(pl.multiple_of(core * half, half), half)], reward_far)
    copies = [pltpu.make_async_copy(a, b, sems.at[i]) for i, (a, b) in enumerate(zip(sources, near))]
    for copy in copies:
        copy.start()
    for copy in copies:
        copy.wait()
    capacity = blocks[0].shape[0]
    everyone = parent_row.shape[1]
    int32, float32, bfloat16 = jnp.int32, jnp.float32, jnp.bfloat16

    mine = lax.broadcasted_iota(int32, (everyone, children), 0) - own * children
    mine = (mine == lax.broadcasted_iota(int32, (everyone, children), 1)).astype(float32).astype(bfloat16)

    def row_and_column(table):
        table = table[...].astype(float32).astype(bfloat16)
        column = lax.dot_general(mine, table, (((0,), (1,)), ((), ())), preferred_element_type=float32)
        return dot(table, mine).astype(int32), column.astype(int32)

    parent, parent_c = row_and_column(parent_row)
    shard, shard_c = row_and_column(shard_row)
    source, source_c = lax.div(parent, parents), lax.div(parent_c, parents)
    first = lax.broadcasted_iota(int32, (children, children), 0)
    second = lax.broadcasted_iota(int32, (children, children), 1)
    live = lax.broadcasted_iota(int32, (1, children), 1) < count[0]
    live_c = lax.broadcasted_iota(int32, (children, 1), 0) < count[0]
    rank = jnp.sum(jnp.where((source_c == source) & (first < second) & live_c, 1, 0), 0, keepdims=True)
    slot = (source ^ own) * capacity + rank
    slot = jnp.where(live, slot, -1)
    reward_rank = jnp.sum(jnp.where((shard_c == shard) & (second < first) & live, 1, 0), 1, keepdims=True)
    lane = lax.broadcasted_iota(int32, (children, NOTES), 1)
    notes = jnp.where(lane == LIVE, live_c.astype(int32), 0)
    for at, value in ((RANK, reward_rank), (SHARD, shard_c), (PARENT, lax.rem(parent_c, parents)), (SOURCE, own)):
        notes = jnp.where(lane == at, value, notes)

    width = blocks[0].shape[1] - half - NOTES
    hidden = (width - 128) // 3
    rest = jnp.zeros((1, hidden), float32)
    for m in range(reward_out.shape[1] // hidden):
        rest = rest + jnp.where(me == m, reward_out[:, m * hidden : (m + 1) * hidden], 0.0)
    parts = []
    for _ in range(3):
        parts.append(rest.astype(bfloat16).astype(float32))
        rest = rest - parts[-1]
    parts.append(jnp.full((1, 128), 1, int32).astype(float32) * count[0].astype(float32))
    shared = jnp.broadcast_to(jnp.concatenate(parts, 1), (capacity, width))

    rows = lax.broadcasted_iota(int32, (groups * capacity, children), 0)
    put = (rows == slot).astype(float32).astype(bfloat16)
    token_rows = dot(put, tokens[...])
    note_rows = dot(put, notes.astype(float32).astype(bfloat16))
    for k, block in enumerate(blocks):
        at = slice(k * capacity, (k + 1) * capacity)
        block[...] = jnp.concatenate([token_rows[at], note_rows[at], shared], 1).astype(bfloat16)


def dispatch(parents, child_count, child_parent, node_shard, tokens, reward_out, groups, capacity, hidden):
    children, half = tokens.shape[0], tokens.shape[1] // 2
    tables = (child_parent[None], node_shard[None])
    return pl.pallas_call(
        functools.partial(dispatch_kernel, parents, groups),
        out_shape=(struct((capacity, half + NOTES + 3 * hidden + 128)),) * groups,
        in_specs=[SCALARS] + [FAR] * 4,
        out_specs=(WHOLE,) * groups,
        scratch_shapes=[VMEM(x.shape, x.dtype) for x in tables]
        + [VMEM((children, half), tokens.dtype), VMEM(reward_out.shape, reward_out.dtype)]
        + [pltpu.SemaphoreType.DMA((4,))],
        compiler_params=pltpu.CompilerParams(vmem_limit_bytes=8 << 20),
        cost_estimate=SMALL,
        name="dispatch",
    )(child_count, *map(far, (*tables, tokens, reward_out)))


def pack_kernel(offset, hidden, prefix, blocks_held, parent_row, *rest):
    blocks, (row, notes, bias, scale, over) = rest[:-5], rest[-5:]
    _, own, _ = coordinates()
    groups, capacity = len(blocks), blocks[0].shape[0]
    rows, half = row.shape
    slots = groups * capacity
    arrived = jnp.concatenate([block[...].astype(jnp.float32) for block in blocks], 0)
    live = arrived[:, half + LIVE : half + LIVE + 1]
    first = lax.broadcasted_iota(jnp.int32, (slots, slots), 0)
    second = lax.broadcasted_iota(jnp.int32, (slots, slots), 1)
    place = jnp.sum(jnp.where(first < second, live, 0.0), 0, keepdims=True)
    kept = jnp.sum(jnp.where(first == second, live, 0.0), 0, keepdims=True) > 0.5
    wanted = lax.broadcasted_iota(jnp.int32, (rows, slots), 0) + offset
    take = (wanted == place.astype(jnp.int32)) & kept
    take = take.astype(jnp.float32).astype(jnp.bfloat16)
    row[...] = dot(take, arrived[:, :half].astype(jnp.bfloat16)).astype(jnp.bfloat16)
    note = dot(take, arrived[:, half : half + NOTES].astype(jnp.bfloat16))
    notes[...] = note
    parent = note[:, PARENT : PARENT + 1].astype(jnp.int32)
    parents = bias.shape[1] // prefix
    position = lax.broadcasted_iota(jnp.int32, (rows, prefix), 1)
    for p in range(parents):
        usable = (parent == p) & (position < blocks_held[own * parents + p] * 128)
        bias[:, p * prefix : (p + 1) * prefix] = jnp.where(usable, 0.0, MASKED)
    base = half + NOTES
    child = lax.broadcasted_iota(jnp.int32, parent_row.shape, 1)
    children = parent_row.shape[1] // groups
    at, child = lax.div(child, children), lax.rem(child, children)
    count = jnp.zeros(parent_row.shape, jnp.float32)
    for k in range(groups):
        head = arrived[k * capacity : k * capacity + 1, base:]
        scale[pl.ds(own ^ k, 1), :] = head[:, :hidden] + head[:, hidden : 2 * hidden] + head[:, 2 * hidden : 3 * hidden]
        count = jnp.where(at == (own ^ k), head[:, 3 * hidden : 3 * hidden + 1], count)
    source = lax.div(parent_row[...], parents)
    going = child < count.astype(jnp.int32)
    most = jnp.zeros((1, 1), jnp.float32)
    for d in range(groups):
        load = jnp.sum(jnp.where((source == d) & going, 1.0, 0.0), 1, keepdims=True)
        most = jnp.maximum(most, load)
    over[...] = jnp.broadcast_to((most > rows).astype(jnp.int32), over.shape)


def pack(offset, rows, hidden, prefix, blocks_held, child_parent, blocks):
    half = D // 2
    groups = len(blocks)
    parents = blocks_held.shape[0] // groups
    return pl.pallas_call(
        functools.partial(pack_kernel, offset, hidden, prefix),
        out_shape=(
            struct((rows, half)),
            struct((rows, NOTES), jnp.float32),
            struct((rows, parents * prefix), jnp.float32),
            struct((groups, hidden), jnp.float32),
            struct((8, 128), jnp.int32),
        ),
        in_specs=[SCALARS] + [WHOLE] * (1 + groups),
        out_specs=[WHOLE] * 5,
        compiler_params=pltpu.CompilerParams(vmem_limit_bytes=12 << 20),
        cost_estimate=SMALL,
        name="pack",
    )(blocks_held, child_parent[None], *blocks)


def project(attn, w_out, out, first):
    width = out.shape[1]

    @pl.loop(0, width // CHUNK)
    def _(i):
        columns = pl.ds(pl.multiple_of(first + i * CHUNK, CHUNK), CHUNK)
        out[:, pl.ds(pl.multiple_of(i * CHUNK, CHUNK), CHUNK)] = dot(
            attn[...], w_out[:, columns]
        )[: out.shape[0]].astype(out.dtype)


def step_kernel(step, own, peer, gain, w_query, w_key, w_value, keys, values, bias, w_out, *rest):
    past_keys, past_values = rest[:step], rest[step : 2 * step]
    rest = rest[2 * step :]
    half = own.shape[1]
    slots = own.shape[0]
    q_cols, kv_cols = w_query.shape[1], w_key.shape[1]
    kv_heads = kv_cols // HD
    ready = {}
    if step == 0:
        part, attn, key_now, value_now, norm, *kept, normed, query, sems = rest
        moves = [(w_query, kept[0], at, min(at + COLUMNS, q_cols)) for at in range(0, q_cols, COLUMNS)]
        moves += [(w, v, 0, w.shape[1]) for w, v in zip((w_key, w_value, keys, values, w_out), kept[1:])]
        for i, (source, target, at, end) in enumerate(moves):
            copy = pltpu.make_async_copy(source.at[:, at:end], target.at[:, at:end], sems.at[i])
            copy.start()
            ready[i] = copy
        w_query, w_key, w_value, keys, values, w_out = kept
    else:
        part, attn, key_now, value_now, norm, normed, query = rest
    arrivals = iter(ready.values())

    def arrive():
        for copy in arrivals:
            copy.wait()
            break

    core, _, _ = coordinates()
    first = core == 0
    low = jnp.where(first, own[...], peer[...]).astype(jnp.float32)
    high = jnp.where(first, peer[...], own[...]).astype(jnp.float32)
    squares = jnp.sum(low * low, -1, keepdims=True) + jnp.sum(high * high, -1, keepdims=True)
    factor = lax.rsqrt(squares / D + 1e-06)
    norm[...] = jnp.broadcast_to(factor, norm.shape)
    normed[:slots, :half] = (low * factor * gain[:, :half]).astype(jnp.bfloat16)
    normed[:slots, half:] = (high * factor * gain[:, half:]).astype(jnp.bfloat16)
    if normed.shape[0] > slots:
        normed[slots:, :] = jnp.zeros((normed.shape[0] - slots, D), jnp.bfloat16)
    for at in range(0, q_cols, COLUMNS):
        end = min(at + COLUMNS, q_cols)
        arrive()
        query[:, at:end] = dot(normed[...], w_query[:, at:end])
    arrive()
    query[:, q_cols : q_cols + kv_cols] = dot(normed[...], w_key[...])
    arrive()
    query[:, q_cols + kv_cols :] = dot(normed[...], w_value[...])
    arrive()
    arrive()
    key_now[...] = query[:slots, q_cols : q_cols + kv_cols].astype(jnp.bfloat16)
    value_now[...] = query[:slots, q_cols + kv_cols :].astype(jnp.bfloat16)
    recent = slots * (step + 1)
    row = lax.broadcasted_iota(jnp.int32, (GROUP * slots, recent), 0)
    column = lax.broadcasted_iota(jnp.int32, (GROUP * slots, recent), 1)
    same = lax.rem(row, slots) == lax.rem(column, slots)
    for head in range(kv_heads):
        lanes = slice(head * HD, (head + 1) * HD)
        q = jnp.concatenate(
            [query[:slots, (head * GROUP + g) * HD : (head * GROUP + g + 1) * HD] for g in range(GROUP)], 0
        ).astype(jnp.bfloat16)
        k_new = jnp.concatenate([k[:, lanes] for k in past_keys] + [key_now[:, lanes]], 0)
        v_new = jnp.concatenate([v[:, lanes] for v in past_values] + [value_now[:, lanes]], 0)
        contract = (((1,), (1,)), ((), ()))
        s_old = lax.dot_general(q, keys[:, lanes], contract, preferred_element_type=jnp.float32)
        s_old = s_old + jnp.concatenate([bias[...]] * GROUP, 0)
        s_new = lax.dot_general(q, k_new, contract, preferred_element_type=jnp.float32)
        s_new = jnp.where(same, s_new, MASKED)
        top = jnp.maximum(jnp.max(s_old, -1, keepdims=True), jnp.max(s_new, -1, keepdims=True))
        p_old = jnp.exp2(s_old * EXPONENT - top * EXPONENT)
        p_new = jnp.exp2(s_new * EXPONENT - top * EXPONENT)
        total = jnp.sum(p_old, -1, keepdims=True) + jnp.sum(p_new, -1, keepdims=True)
        summed = dot(p_old.astype(jnp.bfloat16), values[:, lanes]) + dot(p_new.astype(jnp.bfloat16), v_new)
        result = (summed / total).astype(jnp.bfloat16)
        for g in range(GROUP):
            at = (head * GROUP + g) * HD
            attn[:slots, at : at + HD] = result[g * slots : (g + 1) * slots]
    if attn.shape[0] > slots:
        attn[slots:, :] = jnp.zeros((attn.shape[0] - slots, q_cols), jnp.bfloat16)
    arrive()
    project(attn, w_out, part, (1 - core) * half)


def expand(step, own, peer, gain, w_query, w_key, w_value, keys, values, bias, w_out, past_keys, past_values):
    slots, half = own.shape
    kv_cols = w_key.shape[1]
    q_cols = w_query.shape[1]
    padded = -(-slots // ROWS) * ROWS
    weights = (w_query, w_key, w_value, keys, values, w_out)
    kept, sems = [], []
    place = WHOLE
    if step == 0:
        kept = [VMEM(w.shape, w.dtype) for w in weights]
        sems = [pltpu.SemaphoreType.DMA((-(-q_cols // COLUMNS) + 5,))]
        place = pl.BlockSpec(memory_space=pl.ANY)
    return pl.pallas_call(
        functools.partial(step_kernel, step),
        out_shape=(
            struct((slots, half)), struct((padded, q_cols)), struct((slots, kv_cols)), struct((slots, kv_cols)),
            struct((slots, 128), jnp.float32), *kept
        ),
        in_specs=[WHOLE] * 3 + [place] * 5 + [WHOLE, place] + [WHOLE] * (2 * step),
        out_specs=[WHOLE] * (5 + len(kept)),
        scratch_shapes=[VMEM((padded, D), jnp.bfloat16), VMEM((padded, q_cols + 2 * kv_cols), jnp.float32)] + sems,
        compiler_params=pltpu.CompilerParams(vmem_limit_bytes=16 << 20),
        cost_estimate=SMALL,
        name="expand",
    )(own, peer, gain, w_query, w_key, w_value, keys, values, bias, w_out, *past_keys, *past_values)


def project_kernel(attn, w_out, part):
    core, _, _ = coordinates()
    project(attn, w_out, part, core * part.shape[1])


def project_own(rows, attn, w_out):
    return pl.pallas_call(
        project_kernel,
        out_shape=struct((rows, w_out.shape[1] // 2), jnp.float32),
        in_specs=[WHOLE, WHOLE],
        out_specs=WHOLE,
        compiler_params=pltpu.CompilerParams(vmem_limit_bytes=8 << 20),
        cost_estimate=SMALL,
        name="project_own",
    )(attn, w_out)


def score_kernel(steps, load, cuts, mp, notes, *refs):
    take = lambda count: [refs.pop(0) for _ in range(count)]
    refs = list(refs)
    ups, own_rows, peer_rows, blocks = take(cuts), take(steps), take(steps), take(mp)
    kept = take(cuts * load)
    flat, total, *sems = refs
    groups, depth, hidden = ups[0].shape
    rows = own_rows[0].shape[0]
    core, _, me = coordinates()
    for t in range(steps):
        target = flat.at[t * rows : (t + 1) * rows]
        for m in range(mp):
            at = m % (mp // 2) * depth * cuts
            for c in range(2):
                source = (own_rows if m // (mp // 2) == c else peer_rows)[t].at[:, at : at + depth * cuts]

                @pl.when((me == m) & (core == c))
                def _():
                    if load:
                        pltpu.make_async_copy(source, target, sems[0].at[t]).start()
                    else:
                        target[...] = source[...]

    copies = {}
    if load:
        for r in range(groups):
            for i in range(cuts):
                copies[r, i] = pltpu.make_async_copy(ups[i].at[r], kept[i].at[r], sems[1].at[r, i])
                copies[r, i].start()
        ups = kept
        for t in range(steps):
            target = flat.at[t * rows : (t + 1) * rows]
            pltpu.make_async_copy(target, target, sems[0].at[t]).wait()
    shard = jnp.concatenate([notes[:, SHARD : SHARD + 1].astype(jnp.int32)] * steps, 0)
    for r in range(groups):
        for i in range(cuts):
            if load:
                copies[r, i].wait()
        for at in range(0, hidden, COLUMNS):
            end = min(at + COLUMNS, hidden)
            z = sum(dot(flat[:, i * depth : (i + 1) * depth], ups[i][r, :, at:end]) for i in range(cuts))
            here = jnp.where(shard == r, z, 0.0)
            total[:, at:end] = here if r == 0 else total[:, at:end] + here
    width = hidden // mp
    for j, block in enumerate(blocks):
        for m in range(mp):

            @pl.when((me ^ j) == m)
            def _():
                block[...] = total[:, m * width : (m + 1) * width].astype(jnp.bfloat16)


def score(mp, notes, ups, own_rows, peer_rows, load):
    steps, cuts = len(own_rows), len(ups)
    groups, depth, hidden = ups[0].shape
    count = steps * own_rows[0].shape[0]
    block = struct((count, hidden // mp))
    place = FAR if load else WHOLE
    return pl.pallas_call(
        functools.partial(score_kernel, steps, load, cuts, mp),
        out_shape=(block,) * mp + tuple(VMEM(up.shape, up.dtype) for up in ups) * load,
        in_specs=[WHOLE] + [place] * (cuts + 2 * steps),
        out_specs=(WHOLE,) * (mp + cuts * load),
        scratch_shapes=[VMEM((count, depth * cuts), jnp.bfloat16), VMEM((count, hidden), jnp.float32)]
        + [pltpu.SemaphoreType.DMA((steps,)), pltpu.SemaphoreType.DMA((groups, cuts))] * load,
        compiler_params=pltpu.CompilerParams(vmem_limit_bytes=16 << 20),
        cost_estimate=SMALL,
        name="score",
    )(notes, *(map(far, (*ups, *own_rows, *peer_rows)) if load else (*ups, *own_rows, *peer_rows)))


def scores_of(notes, scale, parts, factors):
    rows = notes.shape[0]
    shard = notes[:, SHARD : SHARD + 1].astype(jnp.int32)
    gain = jnp.zeros((rows, scale.shape[1]), jnp.float32)
    for r in range(scale.shape[0]):
        gain = gain + jnp.where(shard == r, scale[r : r + 1, :], 0.0)
    values = []
    for t, factor in enumerate(factors):
        z = sum(part[t * rows : (t + 1) * rows, :].astype(jnp.float32) for part in parts) * factor
        values.append(jnp.sum(z * jax.nn.sigmoid(z) * gain, -1, keepdims=True))
    return values


def finish_kernel(steps, notes, scale, *refs):
    norms, parts, out = refs[:steps], refs[steps:-1], refs[-1]
    lane = lax.broadcasted_iota(jnp.int32, out.shape, 1)
    total = jnp.zeros(out.shape, jnp.float32)
    for t, value in enumerate(scores_of(notes, scale, parts, [norm[:, :1] for norm in norms])):
        total = jnp.where(lane == t, value, total)
    out[...] = total


def finish(notes, scale, norms, parts):
    return pl.pallas_call(
        functools.partial(finish_kernel, len(norms)),
        out_shape=struct((notes.shape[0], 128), jnp.float32),
        in_specs=[WHOLE] * (2 + len(norms) + len(parts)),
        out_specs=WHOLE,
        compiler_params=pltpu.CompilerParams(vmem_limit_bytes=12 << 20),
        cost_estimate=SMALL,
        name="finish",
    )(notes, scale, *norms, *parts)


def place_kernel(groups, cap, before, notes, scale, own_row, peer_row, *refs):
    parts, table = refs[:-1], refs[-1]
    rows = notes.shape[0]
    values = [before[:, t : t + 1] for t in range(STEPS - 1)]
    low, high = own_row[...].astype(jnp.float32), peer_row[...].astype(jnp.float32)
    squares = jnp.sum(low * low, -1, keepdims=True) + jnp.sum(high * high, -1, keepdims=True)
    values += scores_of(notes, scale, parts, [lax.rsqrt(squares / D + 1e-06)])
    number = lambda lane: notes[:, lane : lane + 1].astype(jnp.int32)
    shard, at = number(SHARD), number(SOURCE) * cap + number(RANK)
    live = notes[:, LIVE : LIVE + 1] > 0.5
    column = lax.broadcasted_iota(jnp.int32, (rows, table.shape[1]), 1)
    for r in range(groups):
        spots = (column == at) & (shard == r) & live
        for t, value in enumerate(values):
            table[r * STEPS + t : r * STEPS + t + 1, :] = jnp.sum(jnp.where(spots, value, 0.0), 0, keepdims=True)


def place(groups, cap, before, notes, scale, own_row, peer_row, parts):
    return pl.pallas_call(
        functools.partial(place_kernel, groups, cap),
        out_shape=struct((groups * STEPS, -(-groups * cap // 128) * 128), jnp.float32),
        in_specs=[WHOLE] * (5 + len(parts)),
        out_specs=WHOLE,
        compiler_params=pltpu.CompilerParams(vmem_limit_bytes=12 << 20),
        cost_estimate=SMALL,
        name="place",
    )(before, notes, scale, own_row, peer_row, *parts)


def shards(
    tokens,
    parent_keys,
    parent_values,
    parent_blocks,
    child_parent,
    child_count,
    node_shard,
    attn_gain,
    w_query,
    w_key,
    w_value,
    w_out,
    reward_up,
    reward_out,
):
    groups, mp = lax.axis_size("dp"), lax.axis_size("mp")
    children, width = tokens.shape
    parents, prefix, kv_cols = parent_keys.shape
    capacity = max(2, 2 * children // groups)
    reward_cap = max(2, 3 * children // (2 * groups))
    slots = groups * capacity
    rows = min(slots, 3 * children // 2)
    hidden = reward_out.shape[1] // mp
    pairs = lambda count, k: [(i, i ^ k) for i in range(count)]
    swap = pairs(mp, 1)
    shift = lambda count, k: [(i, (i + k) % count) for i in range(count)]

    ups = [lax.all_gather(reward_up[0], "dp", axis=0)]

    blocks = dispatch(parents, child_count, child_parent, node_shard, tokens, reward_out, groups, capacity, hidden)
    blocks = [blocks[0]] + [lax.ppermute(blocks[k], "dp", pairs(groups, k)) for k in range(1, groups)]

    keys = parent_keys.reshape(parents * prefix, kv_cols)
    values = parent_values.reshape(parents * prefix, kv_cols)
    raw = (w_query, w_key, w_value, keys, values, w_out)
    gain = attn_gain.reshape(1, width)

    def run(offset, blocks, raw, ups, gain, child_parent, parent_blocks):
        row_own, notes, bias, scale, over = pack(
            offset, rows, hidden, prefix, parent_blocks, child_parent, blocks
        )
        weights = raw
        state = row_own.astype(jnp.float32)
        row_peer = lax.ppermute(row_own, "mp", swap)
        past_keys, past_values, rows_own, rows_peer, norms = [], [], [], [], []

        def products(first, last, ups, load):
            sums = score(mp, notes, ups, rows_own[first:last], rows_peer[first:last], load)
            return sums[:mp], [held(up) for up in sums[mp:]]

        send = lambda sums: [sums[0]] + [lax.ppermute(sums[k], "mp", pairs(mp, k)) for k in range(1, mp)]
        for step in range(STEPS):
            w_query, w_key, w_value, keys, values, w_out = weights
            part, attn, key_now, value_now, norm, *kept = expand(
                step, row_own, row_peer, gain, w_query, w_key, w_value, keys, values, bias, w_out,
                past_keys, past_values,
            )
            if step == 0:
                weights = [held(x) for x in kept]
            norms.append(norm)
            past_keys.append(key_now)
            past_values.append(value_now)
            from_peer = lax.ppermute(part, "mp", swap)
            chip = project_own(rows, attn, weights[-1]) + from_peer.astype(jnp.float32)
            sent = chip.astype(jnp.bfloat16)
            others = [lax.ppermute(sent, "mp", shift(mp, k)) for k in range(2, mp, 2)]
            if step + 1 == STEPS:
                _, ups = lax.optimization_barrier((sent, ups))
                before, ups = products(0, step, ups, True)
                others, before = lax.optimization_barrier((others, before))
            for other in others:
                chip = chip + other.astype(jnp.float32)
            state = state + chip
            row_own = state.astype(jnp.bfloat16)
            row_peer = lax.ppermute(row_own, "mp", swap)
            rows_own.append(row_own)
            rows_peer.append(row_peer)
        before = send(before)
        last, _ = products(step, STEPS, ups, False)
        last, over = lax.optimization_barrier((send(last), over[0, 0]))
        before = finish(notes, scale, norms[1:], before)
        return place(groups, reward_cap, before, notes, scale, row_own, row_peer, last), over

    operands = (blocks, raw, ups, gain, child_parent, parent_blocks)

    table, over = run(0, *operands)
    if rows < slots:
        table, operands = lax.optimization_barrier((table, operands))
        again = lambda table, operands: table + run(rows, *operands)[0]
        table = lax.cond(over > 0, again, lambda table, operands: table, table, operands)

    table = lax.all_to_all(table, "dp", split_axis=0, concat_axis=0, tiled=True)
    total = jnp.sum(table.reshape(groups, STEPS, -1), 0)[:, : groups * reward_cap]
    total = total + lax.ppermute(total, "mp", swap)
    result = total
    for k in range(2, mp, 2):
        result = result + lax.ppermute(total, "mp", shift(mp, k))
    return result


def solution(mesh):
    placed = (
        P("dp", None),
        P("dp", None, "mp"),
        P("dp", None, "mp"),
        P(),
        P(),
        P("dp"),
        P(),
        P(),
        P(None, "mp"),
        P(None, "mp"),
        P(None, "mp"),
        P("mp", None),
        P("dp", "mp", None),
        P("dp", None),
    )
    return jax.shard_map(
        shards, mesh=mesh, in_specs=placed, out_specs=P(None, "dp"), check_vma=False
    )
```

```python
import functools
import math

import jax
import jax.numpy as jnp
from jax import lax
from jax.experimental import pallas as pl
from jax.experimental.pallas import tpu as pltpu
from jax.sharding import PartitionSpec as P

D = 5120
HEADS = 24
KVH = 8
HD = 128
STEPS = 8
GROUP = HEADS // KVH
CHUNK = 512
COLUMNS = 256
ROWS = 64
MASKED = -1e30
EXPONENT = HD ** (-0.5) * math.log2(math.e)
VMEM = pltpu.VMEM
NOTES = 128
LIVE, RANK, SHARD, PARENT, SOURCE = range(5)


def dot(a, b):
    return jnp.dot(a, b, preferred_element_type=jnp.float32)


def held(x):
    return pltpu.with_memory_space_constraint(x, VMEM)


def far(x):
    return pltpu.with_memory_space_constraint(x, pltpu.HBM)


def struct(shape, dtype=jnp.bfloat16):
    return jax.ShapeDtypeStruct(shape, dtype)


WHOLE = pl.BlockSpec(memory_space=VMEM)
FAR = pl.BlockSpec(memory_space=pltpu.HBM)
SMALL = pl.CostEstimate(flops=0, bytes_accessed=0, transcendentals=0)
SCALARS = pl.BlockSpec(memory_space=pltpu.SMEM)


def coordinates():
    me = lax.axis_index("mp")
    return lax.rem(me, 2), lax.axis_index("dp"), me


def dispatch_kernel(parents, groups, count, parent_far, shard_far, tokens_far, reward_far, *rest):
    core, own, me = coordinates()
    blocks, near = rest[:groups], rest[groups:]
    parent_row, shard_row, tokens, reward_out, sems = near
    children, half = tokens.shape
    sources = (parent_far, shard_far, tokens_far.at[:, pl.ds(pl.multiple_of(core * half, half), half)], reward_far)
    copies = [pltpu.make_async_copy(a, b, sems.at[i]) for i, (a, b) in enumerate(zip(sources, near))]
    for copy in copies:
        copy.start()
    for copy in copies:
        copy.wait()
    capacity = blocks[0].shape[0]
    everyone = parent_row.shape[1]
    int32, float32, bfloat16 = jnp.int32, jnp.float32, jnp.bfloat16

    mine = lax.broadcasted_iota(int32, (everyone, children), 0) - own * children
    mine = (mine == lax.broadcasted_iota(int32, (everyone, children), 1)).astype(float32).astype(bfloat16)

    def row_and_column(table):
        table = table[...].astype(float32).astype(bfloat16)
        column = lax.dot_general(mine, table, (((0,), (1,)), ((), ())), preferred_element_type=float32)
        return dot(table, mine).astype(int32), column.astype(int32)

    parent, parent_c = row_and_column(parent_row)
    shard, shard_c = row_and_column(shard_row)
    source, source_c = lax.div(parent, parents), lax.div(parent_c, parents)
    first = lax.broadcasted_iota(int32, (children, children), 0)
    second = lax.broadcasted_iota(int32, (children, children), 1)
    live = lax.broadcasted_iota(int32, (1, children), 1) < count[0]
    live_c = lax.broadcasted_iota(int32, (children, 1), 0) < count[0]
    rank = jnp.sum(jnp.where((source_c == source) & (first < second) & live_c, 1, 0), 0, keepdims=True)
    slot = (source ^ own) * capacity + rank
    slot = jnp.where(live, slot, -1)
    reward_rank = jnp.sum(jnp.where((shard_c == shard) & (second < first) & live, 1, 0), 1, keepdims=True)
    lane = lax.broadcasted_iota(int32, (children, NOTES), 1)
    notes = jnp.where(lane == LIVE, live_c.astype(int32), 0)
    for at, value in ((RANK, reward_rank), (SHARD, shard_c), (PARENT, lax.rem(parent_c, parents)), (SOURCE, own)):
        notes = jnp.where(lane == at, value, notes)

    width = blocks[0].shape[1] - half - NOTES
    hidden = (width - 128) // 3
    rest = jnp.zeros((1, hidden), float32)
    for m in range(reward_out.shape[1] // hidden):
        rest = rest + jnp.where(me == m, reward_out[:, m * hidden : (m + 1) * hidden], 0.0)
    parts = []
    for _ in range(3):
        parts.append(rest.astype(bfloat16).astype(float32))
        rest = rest - parts[-1]
    parts.append(jnp.full((1, 128), 1, int32).astype(float32) * count[0].astype(float32))
    shared = jnp.broadcast_to(jnp.concatenate(parts, 1), (capacity, width))

    rows = lax.broadcasted_iota(int32, (groups * capacity, children), 0)
    put = (rows == slot).astype(float32).astype(bfloat16)
    token_rows = dot(put, tokens[...])
    note_rows = dot(put, notes.astype(float32).astype(bfloat16))
    for k, block in enumerate(blocks):
        at = slice(k * capacity, (k + 1) * capacity)
        block[...] = jnp.concatenate([token_rows[at], note_rows[at], shared], 1).astype(bfloat16)


def dispatch(parents, child_count, child_parent, node_shard, tokens, reward_out, groups, capacity, hidden):
    children, half = tokens.shape[0], tokens.shape[1] // 2
    tables = (child_parent[None], node_shard[None])
    return pl.pallas_call(
        functools.partial(dispatch_kernel, parents, groups),
        out_shape=(struct((capacity, half + NOTES + 3 * hidden + 128)),) * groups,
        in_specs=[SCALARS] + [FAR] * 4,
        out_specs=(WHOLE,) * groups,
        scratch_shapes=[VMEM(x.shape, x.dtype) for x in tables]
        + [VMEM((children, half), tokens.dtype), VMEM(reward_out.shape, reward_out.dtype)]
        + [pltpu.SemaphoreType.DMA((4,))],
        compiler_params=pltpu.CompilerParams(vmem_limit_bytes=8 << 20),
        cost_estimate=SMALL,
        name="dispatch",
    )(child_count, *map(far, (*tables, tokens, reward_out)))


def pack_kernel(offset, hidden, prefix, blocks_held, parent_row, *rest):
    blocks, (row, notes, bias, scale, over) = rest[:-5], rest[-5:]
    _, own, _ = coordinates()
    groups, capacity = len(blocks), blocks[0].shape[0]
    rows, half = row.shape
    slots = groups * capacity
    arrived = jnp.concatenate([block[...].astype(jnp.float32) for block in blocks], 0)
    live = arrived[:, half + LIVE : half + LIVE + 1]
    first = lax.broadcasted_iota(jnp.int32, (slots, slots), 0)
    second = lax.broadcasted_iota(jnp.int32, (slots, slots), 1)
    place = jnp.sum(jnp.where(first < second, live, 0.0), 0, keepdims=True)
    kept = jnp.sum(jnp.where(first == second, live, 0.0), 0, keepdims=True) > 0.5
    wanted = lax.broadcasted_iota(jnp.int32, (rows, slots), 0) + offset
    take = (wanted == place.astype(jnp.int32)) & kept
    take = take.astype(jnp.float32).astype(jnp.bfloat16)
    row[...] = dot(take, arrived[:, :half].astype(jnp.bfloat16)).astype(jnp.bfloat16)
    note = dot(take, arrived[:, half : half + NOTES].astype(jnp.bfloat16))
    notes[...] = note
    parent = note[:, PARENT : PARENT + 1].astype(jnp.int32)
    parents = bias.shape[1] // prefix
    position = lax.broadcasted_iota(jnp.int32, (rows, prefix), 1)
    for p in range(parents):
        usable = (parent == p) & (position < blocks_held[own * parents + p] * 128)
        bias[:, p * prefix : (p + 1) * prefix] = jnp.where(usable, 0.0, MASKED)
    base = half + NOTES
    child = lax.broadcasted_iota(jnp.int32, parent_row.shape, 1)
    children = parent_row.shape[1] // groups
    at, child = lax.div(child, children), lax.rem(child, children)
    count = jnp.zeros(parent_row.shape, jnp.float32)
    for k in range(groups):
        head = arrived[k * capacity : k * capacity + 1, base:]
        scale[pl.ds(own ^ k, 1), :] = head[:, :hidden] + head[:, hidden : 2 * hidden] + head[:, 2 * hidden : 3 * hidden]
        count = jnp.where(at == (own ^ k), head[:, 3 * hidden : 3 * hidden + 1], count)
    source = lax.div(parent_row[...], parents)
    going = child < count.astype(jnp.int32)
    most = jnp.zeros((1, 1), jnp.float32)
    for d in range(groups):
        load = jnp.sum(jnp.where((source == d) & going, 1.0, 0.0), 1, keepdims=True)
        most = jnp.maximum(most, load)
    over[...] = jnp.broadcast_to((most > rows).astype(jnp.int32), over.shape)


def pack(offset, rows, hidden, prefix, blocks_held, child_parent, blocks):
    half = D // 2
    groups = len(blocks)
    parents = blocks_held.shape[0] // groups
    return pl.pallas_call(
        functools.partial(pack_kernel, offset, hidden, prefix),
        out_shape=(
            struct((rows, half)),
            struct((rows, NOTES), jnp.float32),
            struct((rows, parents * prefix), jnp.float32),
            struct((groups, hidden), jnp.float32),
            struct((8, 128), jnp.int32),
        ),
        in_specs=[SCALARS] + [WHOLE] * (1 + groups),
        out_specs=[WHOLE] * 5,
        compiler_params=pltpu.CompilerParams(vmem_limit_bytes=12 << 20),
        cost_estimate=SMALL,
        name="pack",
    )(blocks_held, child_parent[None], *blocks)


def load_kernel(*refs):
    count = (len(refs) - 1) // 2
    copies = [pltpu.make_async_copy(refs[i], refs[count + i], refs[-1].at[i]) for i in range(count)]
    for copy in copies:
        copy.start()
    for copy in copies:
        copy.wait()


def load(*arrays):
    count = len(arrays)
    return pl.pallas_call(
        load_kernel,
        out_shape=tuple(VMEM(x.shape, x.dtype) for x in arrays),
        in_specs=[FAR] * count,
        out_specs=(WHOLE,) * count,
        scratch_shapes=[pltpu.SemaphoreType.DMA((count,))],
        compiler_params=pltpu.CompilerParams(vmem_limit_bytes=2 << 20),
        cost_estimate=pl.CostEstimate(flops=0, bytes_accessed=24 << 20, transcendentals=0),
        name="load",
    )(*map(far, arrays))


def project(attn, w_out, out, first):
    width = out.shape[1]

    @pl.loop(0, width // CHUNK)
    def _(i):
        columns = pl.ds(pl.multiple_of(first + i * CHUNK, CHUNK), CHUNK)
        out[:, pl.ds(pl.multiple_of(i * CHUNK, CHUNK), CHUNK)] = dot(
            attn[...], w_out[:, columns]
        )[: out.shape[0]].astype(out.dtype)


def step_kernel(step, own, peer, gain, w_query, w_key, w_value, keys, values, bias, w_out, *rest):
    past_keys, past_values = rest[:step], rest[step : 2 * step]
    rest = rest[2 * step :]
    half = own.shape[1]
    slots = own.shape[0]
    q_cols, kv_cols = w_query.shape[1], w_key.shape[1]
    kv_heads = kv_cols // HD
    part, attn, key_now, value_now, norm, normed, query = rest
    core, _, _ = coordinates()
    first = core == 0
    low = jnp.where(first, own[...], peer[...]).astype(jnp.float32)
    high = jnp.where(first, peer[...], own[...]).astype(jnp.float32)
    squares = jnp.sum(low * low, -1, keepdims=True) + jnp.sum(high * high, -1, keepdims=True)
    factor = lax.rsqrt(squares / D + 1e-06)
    norm[...] = jnp.broadcast_to(factor, norm.shape)
    normed[:slots, :half] = (low * factor * gain[:, :half]).astype(jnp.bfloat16)
    normed[:slots, half:] = (high * factor * gain[:, half:]).astype(jnp.bfloat16)
    if normed.shape[0] > slots:
        normed[slots:, :] = jnp.zeros((normed.shape[0] - slots, D), jnp.bfloat16)
    for at in range(0, q_cols, COLUMNS):
        end = min(at + COLUMNS, q_cols)
        query[:, at:end] = dot(normed[...], w_query[:, at:end])
    query[:, q_cols : q_cols + kv_cols] = dot(normed[...], w_key[...])
    query[:, q_cols + kv_cols :] = dot(normed[...], w_value[...])
    key_now[...] = query[:slots, q_cols : q_cols + kv_cols].astype(jnp.bfloat16)
    value_now[...] = query[:slots, q_cols + kv_cols :].astype(jnp.bfloat16)
    recent = slots * (step + 1)
    row = lax.broadcasted_iota(jnp.int32, (GROUP * slots, recent), 0)
    column = lax.broadcasted_iota(jnp.int32, (GROUP * slots, recent), 1)
    same = lax.rem(row, slots) == lax.rem(column, slots)
    for head in range(kv_heads):
        lanes = slice(head * HD, (head + 1) * HD)
        q = jnp.concatenate(
            [query[:slots, (head * GROUP + g) * HD : (head * GROUP + g + 1) * HD] for g in range(GROUP)], 0
        ).astype(jnp.bfloat16)
        k_new = jnp.concatenate([k[:, lanes] for k in past_keys] + [key_now[:, lanes]], 0)
        v_new = jnp.concatenate([v[:, lanes] for v in past_values] + [value_now[:, lanes]], 0)
        contract = (((1,), (1,)), ((), ()))
        s_old = lax.dot_general(q, keys[:, lanes], contract, preferred_element_type=jnp.float32)
        s_old = s_old + jnp.concatenate([bias[...]] * GROUP, 0)
        s_new = lax.dot_general(q, k_new, contract, preferred_element_type=jnp.float32)
        s_new = jnp.where(same, s_new, MASKED)
        top = jnp.maximum(jnp.max(s_old, -1, keepdims=True), jnp.max(s_new, -1, keepdims=True))
        p_old = jnp.exp2(s_old * EXPONENT - top * EXPONENT)
        p_new = jnp.exp2(s_new * EXPONENT - top * EXPONENT)
        total = jnp.sum(p_old, -1, keepdims=True) + jnp.sum(p_new, -1, keepdims=True)
        summed = dot(p_old.astype(jnp.bfloat16), values[:, lanes]) + dot(p_new.astype(jnp.bfloat16), v_new)
        result = (summed / total).astype(jnp.bfloat16)
        for g in range(GROUP):
            at = (head * GROUP + g) * HD
            attn[:slots, at : at + HD] = result[g * slots : (g + 1) * slots]
    if attn.shape[0] > slots:
        attn[slots:, :] = jnp.zeros((attn.shape[0] - slots, q_cols), jnp.bfloat16)
    project(attn, w_out, part, (1 - core) * half)


def expand(step, own, peer, gain, w_query, w_key, w_value, keys, values, bias, w_out, past_keys, past_values):
    slots, half = own.shape
    kv_cols = w_key.shape[1]
    q_cols = w_query.shape[1]
    padded = -(-slots // ROWS) * ROWS
    return pl.pallas_call(
        functools.partial(step_kernel, step),
        out_shape=(
            struct((slots, half)), struct((padded, q_cols)), struct((slots, kv_cols)), struct((slots, kv_cols)),
            struct((slots, 128), jnp.float32),
        ),
        in_specs=[WHOLE] * (10 + 2 * step),
        out_specs=[WHOLE] * 5,
        scratch_shapes=[VMEM((padded, D), jnp.bfloat16), VMEM((padded, q_cols + 2 * kv_cols), jnp.float32)],
        compiler_params=pltpu.CompilerParams(vmem_limit_bytes=16 << 20),
        cost_estimate=SMALL,
        name="expand",
    )(own, peer, gain, w_query, w_key, w_value, keys, values, bias, w_out, *past_keys, *past_values)


def project_kernel(attn, w_out, part):
    core, _, _ = coordinates()
    project(attn, w_out, part, core * part.shape[1])


def project_own(rows, attn, w_out):
    return pl.pallas_call(
        project_kernel,
        out_shape=struct((rows, w_out.shape[1] // 2), jnp.float32),
        in_specs=[WHOLE, WHOLE],
        out_specs=WHOLE,
        compiler_params=pltpu.CompilerParams(vmem_limit_bytes=8 << 20),
        cost_estimate=SMALL,
        name="project_own",
    )(attn, w_out)


def score_kernel(steps, load, cuts, mp, notes, *refs):
    take = lambda count: [refs.pop(0) for _ in range(count)]
    refs = list(refs)
    ups, own_rows, peer_rows, blocks = take(cuts), take(steps), take(steps), take(mp)
    kept = take(cuts * load)
    flat, total, *sems = refs
    groups, depth, hidden = ups[0].shape
    rows = own_rows[0].shape[0]
    core, _, me = coordinates()
    for t in range(steps):
        target = flat.at[t * rows : (t + 1) * rows]
        for m in range(mp):
            at = m % (mp // 2) * depth * cuts
            for c in range(2):
                source = (own_rows if m // (mp // 2) == c else peer_rows)[t].at[:, at : at + depth * cuts]

                @pl.when((me == m) & (core == c))
                def _():
                    if load:
                        pltpu.make_async_copy(source, target, sems[0].at[t]).start()
                    else:
                        target[...] = source[...]

    copies = {}
    if load:
        for r in range(groups):
            for i in range(cuts):
                copies[r, i] = pltpu.make_async_copy(ups[i].at[r], kept[i].at[r], sems[1].at[r, i])
                copies[r, i].start()
        ups = kept
        for t in range(steps):
            target = flat.at[t * rows : (t + 1) * rows]
            pltpu.make_async_copy(target, target, sems[0].at[t]).wait()
    shard = jnp.concatenate([notes[:, SHARD : SHARD + 1].astype(jnp.int32)] * steps, 0)
    for r in range(groups):
        for i in range(cuts):
            if load:
                copies[r, i].wait()
        for at in range(0, hidden, COLUMNS):
            end = min(at + COLUMNS, hidden)
            z = sum(dot(flat[:, i * depth : (i + 1) * depth], ups[i][r, :, at:end]) for i in range(cuts))
            here = jnp.where(shard == r, z, 0.0)
            total[:, at:end] = here if r == 0 else total[:, at:end] + here
    width = hidden // mp
    for j, block in enumerate(blocks):
        for m in range(mp):

            @pl.when((me ^ j) == m)
            def _():
                block[...] = total[:, m * width : (m + 1) * width].astype(jnp.bfloat16)


def score(mp, notes, ups, own_rows, peer_rows, load):
    steps, cuts = len(own_rows), len(ups)
    groups, depth, hidden = ups[0].shape
    count = steps * own_rows[0].shape[0]
    block = struct((count, hidden // mp))
    place = FAR if load else WHOLE
    return pl.pallas_call(
        functools.partial(score_kernel, steps, load, cuts, mp),
        out_shape=(block,) * mp + tuple(VMEM(up.shape, up.dtype) for up in ups) * load,
        in_specs=[WHOLE] + [place] * (cuts + 2 * steps),
        out_specs=(WHOLE,) * (mp + cuts * load),
        scratch_shapes=[VMEM((count, depth * cuts), jnp.bfloat16), VMEM((count, hidden), jnp.float32)]
        + [pltpu.SemaphoreType.DMA((steps,)), pltpu.SemaphoreType.DMA((groups, cuts))] * load,
        compiler_params=pltpu.CompilerParams(vmem_limit_bytes=16 << 20),
        cost_estimate=SMALL,
        name="score",
    )(notes, *(map(far, (*ups, *own_rows, *peer_rows)) if load else (*ups, *own_rows, *peer_rows)))


def scores_of(notes, scale, parts, factors):
    rows = notes.shape[0]
    shard = notes[:, SHARD : SHARD + 1].astype(jnp.int32)
    gain = jnp.zeros((rows, scale.shape[1]), jnp.float32)
    for r in range(scale.shape[0]):
        gain = gain + jnp.where(shard == r, scale[r : r + 1, :], 0.0)
    values = []
    for t, factor in enumerate(factors):
        z = sum(part[t * rows : (t + 1) * rows, :].astype(jnp.float32) for part in parts) * factor
        values.append(jnp.sum(z * jax.nn.sigmoid(z) * gain, -1, keepdims=True))
    return values


def finish_kernel(steps, notes, scale, *refs):
    norms, parts, out = refs[:steps], refs[steps:-1], refs[-1]
    lane = lax.broadcasted_iota(jnp.int32, out.shape, 1)
    total = jnp.zeros(out.shape, jnp.float32)
    for t, value in enumerate(scores_of(notes, scale, parts, [norm[:, :1] for norm in norms])):
        total = jnp.where(lane == t, value, total)
    out[...] = total


def finish(notes, scale, norms, parts):
    return pl.pallas_call(
        functools.partial(finish_kernel, len(norms)),
        out_shape=struct((notes.shape[0], 128), jnp.float32),
        in_specs=[WHOLE] * (2 + len(norms) + len(parts)),
        out_specs=WHOLE,
        compiler_params=pltpu.CompilerParams(vmem_limit_bytes=12 << 20),
        cost_estimate=SMALL,
        name="finish",
    )(notes, scale, *norms, *parts)


def place_kernel(groups, cap, before, notes, scale, own_row, peer_row, *refs):
    parts, table = refs[:-1], refs[-1]
    rows = notes.shape[0]
    values = [before[:, t : t + 1] for t in range(STEPS - 1)]
    low, high = own_row[...].astype(jnp.float32), peer_row[...].astype(jnp.float32)
    squares = jnp.sum(low * low, -1, keepdims=True) + jnp.sum(high * high, -1, keepdims=True)
    values += scores_of(notes, scale, parts, [lax.rsqrt(squares / D + 1e-06)])
    number = lambda lane: notes[:, lane : lane + 1].astype(jnp.int32)
    shard, at = number(SHARD), number(SOURCE) * cap + number(RANK)
    live = notes[:, LIVE : LIVE + 1] > 0.5
    column = lax.broadcasted_iota(jnp.int32, (rows, table.shape[1]), 1)
    for r in range(groups):
        spots = (column == at) & (shard == r) & live
        for t, value in enumerate(values):
            table[r * STEPS + t : r * STEPS + t + 1, :] = jnp.sum(jnp.where(spots, value, 0.0), 0, keepdims=True)


def place(groups, cap, before, notes, scale, own_row, peer_row, parts):
    return pl.pallas_call(
        functools.partial(place_kernel, groups, cap),
        out_shape=struct((groups * STEPS, -(-groups * cap // 128) * 128), jnp.float32),
        in_specs=[WHOLE] * (5 + len(parts)),
        out_specs=WHOLE,
        compiler_params=pltpu.CompilerParams(vmem_limit_bytes=12 << 20),
        cost_estimate=SMALL,
        name="place",
    )(before, notes, scale, own_row, peer_row, *parts)


def shards(
    tokens,
    parent_keys,
    parent_values,
    parent_blocks,
    child_parent,
    child_count,
    node_shard,
    attn_gain,
    w_query,
    w_key,
    w_value,
    w_out,
    reward_up,
    reward_out,
):
    groups, mp = lax.axis_size("dp"), lax.axis_size("mp")
    children, width = tokens.shape
    parents, prefix, kv_cols = parent_keys.shape
    capacity = max(2, 2 * children // groups)
    reward_cap = max(2, 3 * children // (2 * groups))
    slots = groups * capacity
    rows = min(slots, 3 * children // 2)
    hidden = reward_out.shape[1] // mp
    pairs = lambda count, k: [(i, i ^ k) for i in range(count)]
    swap = pairs(mp, 1)
    shift = lambda count, k: [(i, (i + k) % count) for i in range(count)]

    ups = [lax.all_gather(reward_up[0], "dp", axis=0)]

    blocks = dispatch(parents, child_count, child_parent, node_shard, tokens, reward_out, groups, capacity, hidden)
    keys = parent_keys.reshape(parents * prefix, kv_cols)
    values = parent_values.reshape(parents * prefix, kv_cols)
    raw = (w_query, w_key, w_value, keys, values, w_out)
    blocks, raw = lax.optimization_barrier((blocks, raw))
    blocks = [blocks[0]] + [lax.ppermute(blocks[k], "dp", pairs(groups, k)) for k in range(1, groups)]
    blocks, weights = lax.optimization_barrier((blocks, load(*raw)))
    gain = attn_gain.reshape(1, width)

    def run(offset, weights, blocks, ups, gain, child_parent, parent_blocks):
        row_own, notes, bias, scale, over = pack(
            offset, rows, hidden, prefix, parent_blocks, child_parent, blocks
        )
        w_query, w_key, w_value, keys, values, w_out = [held(w) for w in weights]
        state = row_own.astype(jnp.float32)
        row_peer = lax.ppermute(row_own, "mp", swap)
        past_keys, past_values, rows_own, rows_peer, norms = [], [], [], [], []

        def products(first, last, ups, load):
            sums = score(mp, notes, ups, rows_own[first:last], rows_peer[first:last], load)
            return sums[:mp], [held(up) for up in sums[mp:]]

        send = lambda sums: [sums[0]] + [lax.ppermute(sums[k], "mp", pairs(mp, k)) for k in range(1, mp)]
        for step in range(STEPS):
            part, attn, key_now, value_now, norm = expand(
                step, row_own, row_peer, gain, w_query, w_key, w_value, keys, values, bias, w_out,
                past_keys, past_values,
            )
            norms.append(norm)
            past_keys.append(key_now)
            past_values.append(value_now)
            from_peer = lax.ppermute(part, "mp", swap)
            chip = project_own(rows, attn, w_out) + from_peer.astype(jnp.float32)
            sent = chip.astype(jnp.bfloat16)
            others = [lax.ppermute(sent, "mp", shift(mp, k)) for k in range(2, mp, 2)]
            if step + 1 == STEPS:
                _, ups = lax.optimization_barrier((sent, ups))
                before, ups = products(0, step, ups, True)
                others, before = lax.optimization_barrier((others, before))
            for other in others:
                chip = chip + other.astype(jnp.float32)
            state = state + chip
            row_own = state.astype(jnp.bfloat16)
            row_peer = lax.ppermute(row_own, "mp", swap)
            rows_own.append(row_own)
            rows_peer.append(row_peer)
        before = send(before)
        last, _ = products(step, STEPS, ups, False)
        last, over = lax.optimization_barrier((send(last), over[0, 0]))
        before = finish(notes, scale, norms[1:], before)
        return place(groups, reward_cap, before, notes, scale, row_own, row_peer, last), over

    operands = (blocks, ups, gain, child_parent, parent_blocks)

    table, over = run(0, weights, *operands)
    if rows < slots:
        table, raw, operands = lax.optimization_barrier((table, raw, operands))
        again = lambda table, raw, operands: table + run(rows, load(*raw), *operands)[0]
        table = lax.cond(over > 0, again, lambda table, raw, operands: table, table, raw, operands)

    table = lax.all_to_all(table, "dp", split_axis=0, concat_axis=0, tiled=True)
    total = jnp.sum(table.reshape(groups, STEPS, -1), 0)[:, : groups * reward_cap]
    total = total + lax.ppermute(total, "mp", swap)
    result = total
    for k in range(2, mp, 2):
        result = result + lax.ppermute(total, "mp", shift(mp, k))
    return result


def solution(mesh):
    placed = (
        P("dp", None),
        P("dp", None, "mp"),
        P("dp", None, "mp"),
        P(),
        P(),
        P("dp"),
        P(),
        P(),
        P(None, "mp"),
        P(None, "mp"),
        P(None, "mp"),
        P("mp", None),
        P("dp", "mp", None),
        P("dp", None),
    )
    return jax.shard_map(
        shards, mesh=mesh, in_specs=placed, out_specs=P(None, "dp"), check_vma=False
    )
```

```python
import functools
import math

import jax
import jax.numpy as jnp
from jax import lax
from jax.experimental import pallas as pl
from jax.experimental.pallas import tpu as pltpu
from jax.sharding import PartitionSpec as P

D = 5120
HEADS = 24
KVH = 8
HD = 128
STEPS = 8
GROUP = HEADS // KVH
CHUNK = 512
COLUMNS = 256
ROWS = 64
MASKED = -1e30
EXPONENT = HD ** (-0.5) * math.log2(math.e)
VMEM = pltpu.VMEM
NOTES = 128
LIVE, RANK, SHARD, PARENT, SOURCE, COUNT = range(6)


def dot(a, b):
    return jnp.dot(a, b, preferred_element_type=jnp.float32)


def held(x):
    return pltpu.with_memory_space_constraint(x, VMEM)


def far(x):
    return pltpu.with_memory_space_constraint(x, pltpu.HBM)


def struct(shape, dtype=jnp.bfloat16):
    return jax.ShapeDtypeStruct(shape, dtype)


WHOLE = pl.BlockSpec(memory_space=VMEM)
FAR = pl.BlockSpec(memory_space=pltpu.HBM)
SMALL = pl.CostEstimate(flops=0, bytes_accessed=0, transcendentals=0)
SCALARS = pl.BlockSpec(memory_space=pltpu.SMEM)


def paired_sum(parts):
    while len(parts) > 1:
        parts = [a + b for a, b in zip(parts[::2], parts[1::2])]
    return parts[0]


def coordinates():
    me = lax.axis_index("mp")
    return lax.rem(me, 2), lax.axis_index("dp"), me


def dispatch_kernel(parents, groups, count, parent_far, shard_far, tokens_far, reward_far, *rest):
    core, own, me = coordinates()
    blocks, near = rest[:groups], rest[groups:]
    parent_row, shard_row, tokens, reward_out, sems = near
    children, half = tokens.shape
    sources = (parent_far, shard_far, tokens_far.at[:, pl.ds(pl.multiple_of(core * half, half), half)], reward_far)
    copies = [pltpu.make_async_copy(a, b, sems.at[i]) for i, (a, b) in enumerate(zip(sources, near))]
    for copy in copies:
        copy.start()
    for copy in copies:
        copy.wait()
    capacity = blocks[0].shape[0]
    everyone = parent_row.shape[1]
    int32, float32, bfloat16 = jnp.int32, jnp.float32, jnp.bfloat16

    mine = lax.broadcasted_iota(int32, (everyone, children), 0) - own * children
    mine = (mine == lax.broadcasted_iota(int32, (everyone, children), 1)).astype(float32).astype(bfloat16)

    def row_and_column(table):
        table = table[...].astype(float32).astype(bfloat16)
        column = lax.dot_general(mine, table, (((0,), (1,)), ((), ())), preferred_element_type=float32)
        return dot(table, mine).astype(int32), column.astype(int32)

    parent, parent_c = row_and_column(parent_row)
    shard, shard_c = row_and_column(shard_row)
    source, source_c = lax.div(parent, parents), lax.div(parent_c, parents)
    first = lax.broadcasted_iota(int32, (children, children), 0)
    second = lax.broadcasted_iota(int32, (children, children), 1)
    live = lax.broadcasted_iota(int32, (1, children), 1) < count[0]
    live_c = lax.broadcasted_iota(int32, (children, 1), 0) < count[0]
    rank = jnp.sum(jnp.where((source_c == source) & (first < second) & live_c, 1, 0), 0, keepdims=True)
    slot = (source ^ own) * capacity + rank
    slot = jnp.where(live, slot, -1)
    reward_rank = jnp.sum(jnp.where((shard_c == shard) & (second < first) & live, 1, 0), 1, keepdims=True)
    lane = lax.broadcasted_iota(int32, (children, NOTES), 1)
    notes = jnp.where(lane == LIVE, live_c.astype(int32), 0)
    for at, value in ((RANK, reward_rank), (SHARD, shard_c), (PARENT, lax.rem(parent_c, parents)), (SOURCE, own)):
        notes = jnp.where(lane == at, value, notes)

    width = blocks[0].shape[1] - half - NOTES
    hidden = width // 3
    rest = jnp.zeros((1, hidden), float32)
    for m in range(reward_out.shape[1] // hidden):
        rest = rest + jnp.where(me == m, reward_out[:, m * hidden : (m + 1) * hidden], 0.0)
    parts = []
    for _ in range(3):
        parts.append(rest.astype(bfloat16).astype(float32))
        rest = rest - parts[-1]
    shared = jnp.broadcast_to(jnp.concatenate(parts, 1), (capacity, width))

    rows = lax.broadcasted_iota(int32, (groups * capacity, children), 0)
    put = (rows == slot).astype(float32).astype(bfloat16)
    token_rows = dot(put, tokens[...])
    note_rows = dot(put, notes.astype(float32).astype(bfloat16))
    row = lax.broadcasted_iota(int32, note_rows.shape, 0)
    lane = lax.broadcasted_iota(int32, note_rows.shape, 1)
    note_rows = jnp.where((lax.rem(row, capacity) == 0) & (lane == COUNT), count[0].astype(float32), note_rows)
    for k, block in enumerate(blocks):
        at = slice(k * capacity, (k + 1) * capacity)
        block[...] = jnp.concatenate([token_rows[at], note_rows[at], shared], 1).astype(bfloat16)


def dispatch(parents, child_count, child_parent, node_shard, tokens, reward_out, groups, capacity, hidden):
    children, half = tokens.shape[0], tokens.shape[1] // 2
    tables = (child_parent[None], node_shard[None])
    return pl.pallas_call(
        functools.partial(dispatch_kernel, parents, groups),
        out_shape=(struct((capacity, half + NOTES + 3 * hidden)),) * groups,
        in_specs=[SCALARS] + [FAR] * 4,
        out_specs=(WHOLE,) * groups,
        scratch_shapes=[VMEM(x.shape, x.dtype) for x in tables]
        + [VMEM((children, half), tokens.dtype), VMEM(reward_out.shape, reward_out.dtype)]
        + [pltpu.SemaphoreType.DMA((4,))],
        compiler_params=pltpu.CompilerParams(vmem_limit_bytes=8 << 20),
        cost_estimate=SMALL,
        name="dispatch",
    )(child_count, *map(far, (*tables, tokens, reward_out)))


def pack_kernel(offset, hidden, prefix, blocks_held, parent_row, *rest):
    blocks, (row, notes, bias, scale, over) = rest[:-5], rest[-5:]
    _, own, _ = coordinates()
    groups, capacity = len(blocks), blocks[0].shape[0]
    rows, half = row.shape
    slots = groups * capacity
    arrived = jnp.concatenate([block[...].astype(jnp.float32) for block in blocks], 0)
    live = arrived[:, half + LIVE : half + LIVE + 1]
    first = lax.broadcasted_iota(jnp.int32, (slots, slots), 0)
    second = lax.broadcasted_iota(jnp.int32, (slots, slots), 1)
    place = jnp.sum(jnp.where(first < second, live, 0.0), 0, keepdims=True)
    kept = jnp.sum(jnp.where(first == second, live, 0.0), 0, keepdims=True) > 0.5
    wanted = lax.broadcasted_iota(jnp.int32, (rows, slots), 0) + offset
    take = (wanted == place.astype(jnp.int32)) & kept
    take = take.astype(jnp.float32).astype(jnp.bfloat16)
    row[...] = dot(take, arrived[:, :half].astype(jnp.bfloat16)).astype(jnp.bfloat16)
    note = dot(take, arrived[:, half : half + NOTES].astype(jnp.bfloat16))
    notes[...] = note
    parent = note[:, PARENT : PARENT + 1].astype(jnp.int32)
    parents = bias.shape[1] // prefix
    position = lax.broadcasted_iota(jnp.int32, (rows, prefix), 1)
    for p in range(parents):
        usable = (parent == p) & (position < blocks_held[own * parents + p] * 128)
        bias[:, p * prefix : (p + 1) * prefix] = jnp.where(usable, 0.0, MASKED)
    base = half + NOTES
    child = lax.broadcasted_iota(jnp.int32, parent_row.shape, 1)
    children = parent_row.shape[1] // groups
    at, child = lax.div(child, children), lax.rem(child, children)
    count = jnp.zeros(parent_row.shape, jnp.float32)
    for k in range(groups):
        first_row = arrived[k * capacity : k * capacity + 1]
        head = first_row[:, base:]
        scale[pl.ds(own ^ k, 1), :] = head[:, :hidden] + head[:, hidden : 2 * hidden] + head[:, 2 * hidden : 3 * hidden]
        count = jnp.where(at == (own ^ k), first_row[:, half + COUNT : half + COUNT + 1], count)
    source = lax.div(parent_row[...], parents)
    going = child < count.astype(jnp.int32)
    most = jnp.zeros((1, 1), jnp.float32)
    for d in range(groups):
        load = jnp.sum(jnp.where((source == d) & going, 1.0, 0.0), 1, keepdims=True)
        most = jnp.maximum(most, load)
    over[...] = jnp.broadcast_to((most > rows).astype(jnp.int32), over.shape)


def pack(offset, rows, hidden, prefix, blocks_held, child_parent, blocks):
    half = D // 2
    groups = len(blocks)
    parents = blocks_held.shape[0] // groups
    return pl.pallas_call(
        functools.partial(pack_kernel, offset, hidden, prefix),
        out_shape=(
            struct((rows, half)),
            struct((rows, NOTES), jnp.float32),
            struct((rows, parents * prefix), jnp.float32),
            struct((groups, hidden), jnp.float32),
            struct((8, 128), jnp.int32),
        ),
        in_specs=[SCALARS] + [WHOLE] * (1 + groups),
        out_specs=[WHOLE] * 5,
        compiler_params=pltpu.CompilerParams(vmem_limit_bytes=12 << 20),
        cost_estimate=SMALL,
        name="pack",
    )(blocks_held, child_parent[None], *blocks)


def load_kernel(*refs):
    count = (len(refs) - 1) // 2
    copies = [pltpu.make_async_copy(refs[i], refs[count + i], refs[-1].at[i]) for i in range(count)]
    for copy in copies:
        copy.start()
    for copy in copies:
        copy.wait()


def load(*arrays):
    count = len(arrays)
    return pl.pallas_call(
        load_kernel,
        out_shape=tuple(VMEM(x.shape, x.dtype) for x in arrays),
        in_specs=[FAR] * count,
        out_specs=(WHOLE,) * count,
        scratch_shapes=[pltpu.SemaphoreType.DMA((count,))],
        compiler_params=pltpu.CompilerParams(vmem_limit_bytes=2 << 20),
        cost_estimate=pl.CostEstimate(flops=0, bytes_accessed=24 << 20, transcendentals=0),
        name="load",
    )(*map(far, arrays))


def project(attn, w_out, out, first):
    width = out.shape[1]

    @pl.loop(0, width // CHUNK)
    def _(i):
        columns = pl.ds(pl.multiple_of(first + i * CHUNK, CHUNK), CHUNK)
        out[:, pl.ds(pl.multiple_of(i * CHUNK, CHUNK), CHUNK)] = dot(
            attn[...], w_out[:, columns]
        )[: out.shape[0]].astype(out.dtype)


def step_kernel(step, own, peer, gain, w_query, w_key, w_value, keys, values, bias, w_out, *rest):
    past_keys, past_values = rest[:step], rest[step : 2 * step]
    rest = rest[2 * step :]
    half = own.shape[1]
    slots = own.shape[0]
    q_cols, kv_cols = w_query.shape[1], w_key.shape[1]
    kv_heads = kv_cols // HD
    part, attn, key_now, value_now, norm, normed, query = rest
    core, _, _ = coordinates()
    first = core == 0
    low = jnp.where(first, own[...], peer[...]).astype(jnp.float32)
    high = jnp.where(first, peer[...], own[...]).astype(jnp.float32)
    squares = jnp.sum(low * low, -1, keepdims=True) + jnp.sum(high * high, -1, keepdims=True)
    factor = lax.rsqrt(squares / D + 1e-06)
    norm[...] = jnp.broadcast_to(factor, norm.shape)
    normed[:slots, :half] = (low * factor * gain[:, :half]).astype(jnp.bfloat16)
    normed[:slots, half:] = (high * factor * gain[:, half:]).astype(jnp.bfloat16)
    if normed.shape[0] > slots:
        normed[slots:, :] = jnp.zeros((normed.shape[0] - slots, D), jnp.bfloat16)
    for at in range(0, q_cols, COLUMNS):
        end = min(at + COLUMNS, q_cols)
        query[:, at:end] = dot(normed[...], w_query[:, at:end])
    query[:, q_cols : q_cols + kv_cols] = dot(normed[...], w_key[...])
    query[:, q_cols + kv_cols :] = dot(normed[...], w_value[...])
    key_now[...] = query[:slots, q_cols : q_cols + kv_cols].astype(jnp.bfloat16)
    value_now[...] = query[:slots, q_cols + kv_cols :].astype(jnp.bfloat16)
    recent = slots * (step + 1)
    row = lax.broadcasted_iota(jnp.int32, (GROUP * slots, recent), 0)
    column = lax.broadcasted_iota(jnp.int32, (GROUP * slots, recent), 1)
    same = lax.rem(row, slots) == lax.rem(column, slots)
    for head in range(kv_heads):
        lanes = slice(head * HD, (head + 1) * HD)
        q = jnp.concatenate(
            [query[:slots, (head * GROUP + g) * HD : (head * GROUP + g + 1) * HD] for g in range(GROUP)], 0
        ).astype(jnp.bfloat16)
        k_new = jnp.concatenate([k[:, lanes] for k in past_keys] + [key_now[:, lanes]], 0)
        v_new = jnp.concatenate([v[:, lanes] for v in past_values] + [value_now[:, lanes]], 0)
        contract = (((1,), (1,)), ((), ()))
        s_old = lax.dot_general(q, keys[:, lanes], contract, preferred_element_type=jnp.float32)
        s_old = s_old + jnp.concatenate([bias[...]] * GROUP, 0)
        s_new = lax.dot_general(q, k_new, contract, preferred_element_type=jnp.float32)
        s_new = jnp.where(same, s_new, MASKED)
        top = jnp.maximum(jnp.max(s_old, -1, keepdims=True), jnp.max(s_new, -1, keepdims=True))
        p_old = jnp.exp2(s_old * EXPONENT - top * EXPONENT)
        p_new = jnp.exp2(s_new * EXPONENT - top * EXPONENT)
        total = jnp.sum(p_old, -1, keepdims=True) + jnp.sum(p_new, -1, keepdims=True)
        summed = dot(p_old.astype(jnp.bfloat16), values[:, lanes]) + dot(p_new.astype(jnp.bfloat16), v_new)
        result = (summed / total).astype(jnp.bfloat16)
        for g in range(GROUP):
            at = (head * GROUP + g) * HD
            attn[:slots, at : at + HD] = result[g * slots : (g + 1) * slots]
    if attn.shape[0] > slots:
        attn[slots:, :] = jnp.zeros((attn.shape[0] - slots, q_cols), jnp.bfloat16)
    project(attn, w_out, part, (1 - core) * half)


def expand(step, own, peer, gain, w_query, w_key, w_value, keys, values, bias, w_out, past_keys, past_values):
    slots, half = own.shape
    kv_cols = w_key.shape[1]
    q_cols = w_query.shape[1]
    padded = -(-slots // ROWS) * ROWS
    return pl.pallas_call(
        functools.partial(step_kernel, step),
        out_shape=(
            struct((slots, half)), struct((padded, q_cols)), struct((slots, kv_cols)), struct((slots, kv_cols)),
            struct((slots, 128), jnp.float32),
        ),
        in_specs=[WHOLE] * (10 + 2 * step),
        out_specs=[WHOLE] * 5,
        scratch_shapes=[VMEM((padded, D), jnp.bfloat16), VMEM((padded, q_cols + 2 * kv_cols), jnp.float32)],
        compiler_params=pltpu.CompilerParams(vmem_limit_bytes=16 << 20),
        cost_estimate=SMALL,
        name="expand",
    )(own, peer, gain, w_query, w_key, w_value, keys, values, bias, w_out, *past_keys, *past_values)


def project_kernel(attn, w_out, part):
    core, _, _ = coordinates()
    project(attn, w_out, part, core * part.shape[1])


def project_own(rows, attn, w_out):
    return pl.pallas_call(
        project_kernel,
        out_shape=struct((rows, w_out.shape[1] // 2), jnp.float32),
        in_specs=[WHOLE, WHOLE],
        out_specs=WHOLE,
        compiler_params=pltpu.CompilerParams(vmem_limit_bytes=8 << 20),
        cost_estimate=SMALL,
        name="project_own",
    )(attn, w_out)


def score_kernel(steps, load, cuts, mp, notes, *refs):
    take = lambda count: [refs.pop(0) for _ in range(count)]
    refs = list(refs)
    ups, own_rows, peer_rows, blocks = take(cuts), take(steps), take(steps), take(mp if load else 1)
    kept = take(cuts * load)
    flat, total, *sems = refs
    groups, depth, hidden = ups[0].shape
    rows = own_rows[0].shape[0]
    core, _, me = coordinates()
    for t in range(steps):
        target = flat.at[t * rows : (t + 1) * rows]
        for m in range(mp):
            at = m % (mp // 2) * depth * cuts
            for c in range(2):
                source = (own_rows if m // (mp // 2) == c else peer_rows)[t].at[:, at : at + depth * cuts]

                @pl.when((me == m) & (core == c))
                def _():
                    if load:
                        pltpu.make_async_copy(source, target, sems[0].at[t]).start()
                    else:
                        target[...] = source[...]

    copies = {}
    if load:
        for r in range(groups):
            for i in range(cuts):
                copies[r, i] = pltpu.make_async_copy(ups[i].at[r], kept[i].at[r], sems[1].at[r, i])
                copies[r, i].start()
        ups = kept
        for t in range(steps):
            target = flat.at[t * rows : (t + 1) * rows]
            pltpu.make_async_copy(target, target, sems[0].at[t]).wait()
    shard = jnp.concatenate([notes[:, SHARD : SHARD + 1].astype(jnp.int32)] * steps, 0)
    for r in range(groups):
        for i in range(cuts):
            if load:
                copies[r, i].wait()
        for at in range(0, hidden, COLUMNS):
            end = min(at + COLUMNS, hidden)
            z = sum(dot(flat[:, i * depth : (i + 1) * depth], ups[i][r, :, at:end]) for i in range(cuts))
            here = jnp.where(shard == r, z, 0.0)
            total[:, at:end] = here if r == 0 else total[:, at:end] + here
    if not load:
        blocks[0][...] = total[...].astype(jnp.bfloat16)
        return
    width = hidden // mp
    for j, block in enumerate(blocks):
        for m in range(mp):

            @pl.when((me ^ j) == m)
            def _():
                block[...] = total[:, m * width : (m + 1) * width].astype(jnp.bfloat16)


def score(mp, notes, ups, own_rows, peer_rows, load):
    steps, cuts = len(own_rows), len(ups)
    groups, depth, hidden = ups[0].shape
    count = steps * own_rows[0].shape[0]
    blocks = (struct((count, hidden // mp)),) * mp if load else (struct((count, hidden)),)
    place = FAR if load else WHOLE
    return pl.pallas_call(
        functools.partial(score_kernel, steps, load, cuts, mp),
        out_shape=blocks + tuple(VMEM(up.shape, up.dtype) for up in ups) * load,
        in_specs=[WHOLE] + [place] * (cuts + 2 * steps),
        out_specs=(WHOLE,) * (len(blocks) + cuts * load),
        scratch_shapes=[VMEM((count, depth * cuts), jnp.bfloat16), VMEM((count, hidden), jnp.float32)]
        + [pltpu.SemaphoreType.DMA((steps,)), pltpu.SemaphoreType.DMA((groups, cuts))] * load,
        compiler_params=pltpu.CompilerParams(vmem_limit_bytes=16 << 20),
        cost_estimate=SMALL,
        name="score",
    )(notes, *(map(far, (*ups, *own_rows, *peer_rows)) if load else (*ups, *own_rows, *peer_rows)))


def scores_of(notes, scale, parts, factors):
    rows = notes.shape[0]
    shard = notes[:, SHARD : SHARD + 1].astype(jnp.int32)
    gain = jnp.zeros((rows, scale.shape[1]), jnp.float32)
    for r in range(scale.shape[0]):
        gain = gain + jnp.where(shard == r, scale[r : r + 1, :], 0.0)
    values = []
    for t, factor in enumerate(factors):
        z = paired_sum([part[t * rows : (t + 1) * rows, :].astype(jnp.float32) for part in parts]) * factor
        values.append(jnp.sum(z * jax.nn.sigmoid(z) * gain, -1, keepdims=True))
    return values


def finish_kernel(steps, notes, scale, *refs):
    norms, parts, out = refs[:steps], refs[steps:-1], refs[-1]
    lane = lax.broadcasted_iota(jnp.int32, out.shape, 1)
    total = jnp.zeros(out.shape, jnp.float32)
    for t, value in enumerate(scores_of(notes, scale, parts, [norm[:, :1] for norm in norms])):
        total = jnp.where(lane == t, value, total)
    out[...] = total


def finish(notes, scale, norms, parts):
    return pl.pallas_call(
        functools.partial(finish_kernel, len(norms)),
        out_shape=struct((notes.shape[0], 128), jnp.float32),
        in_specs=[WHOLE] * (2 + len(norms) + len(parts)),
        out_specs=WHOLE,
        compiler_params=pltpu.CompilerParams(vmem_limit_bytes=12 << 20),
        cost_estimate=SMALL,
        name="finish",
    )(notes, scale, *norms, *parts)


def place_kernel(groups, cap, mp, notes, own_row, peer_row, *refs):
    befores, scales, parts, table = refs[:mp], refs[mp : 2 * mp], refs[2 * mp : 3 * mp], refs[3 * mp]
    rows = notes.shape[0]
    _, _, me = coordinates()
    before = paired_sum([x[...] for x in befores])
    values = [before[:, t : t + 1] for t in range(STEPS - 1)]
    scale = [sum(jnp.where((me ^ j) == m, scales[j][...], 0.0) for j in range(mp)) for m in range(mp)]
    low, high = own_row[...].astype(jnp.float32), peer_row[...].astype(jnp.float32)
    squares = jnp.sum(low * low, -1, keepdims=True) + jnp.sum(high * high, -1, keepdims=True)
    values += scores_of(notes, jnp.concatenate(scale, 1), parts, [lax.rsqrt(squares / D + 1e-06)])
    number = lambda lane: notes[:, lane : lane + 1].astype(jnp.int32)
    shard, at = number(SHARD), number(SOURCE) * cap + number(RANK)
    live = notes[:, LIVE : LIVE + 1] > 0.5
    column = lax.broadcasted_iota(jnp.int32, (rows, table.shape[1]), 1)
    for r in range(groups):
        spots = (column == at) & (shard == r) & live
        for t, value in enumerate(values):
            table[r * STEPS + t : r * STEPS + t + 1, :] = jnp.sum(jnp.where(spots, value, 0.0), 0, keepdims=True)


def place(groups, cap, notes, own_row, peer_row, befores, scales, parts):
    mp = len(parts)
    return pl.pallas_call(
        functools.partial(place_kernel, groups, cap, mp),
        out_shape=struct((groups * STEPS, -(-groups * cap // 128) * 128), jnp.float32),
        in_specs=[WHOLE] * (3 + 3 * mp),
        out_specs=WHOLE,
        compiler_params=pltpu.CompilerParams(vmem_limit_bytes=12 << 20),
        cost_estimate=SMALL,
        name="place",
    )(notes, own_row, peer_row, *befores, *scales, *parts)


def shards(
    tokens,
    parent_keys,
    parent_values,
    parent_blocks,
    child_parent,
    child_count,
    node_shard,
    attn_gain,
    w_query,
    w_key,
    w_value,
    w_out,
    reward_up,
    reward_out,
):
    groups, mp = lax.axis_size("dp"), lax.axis_size("mp")
    children, width = tokens.shape
    parents, prefix, kv_cols = parent_keys.shape
    capacity = max(2, 2 * children // groups)
    reward_cap = max(2, 3 * children // (2 * groups))
    slots = groups * capacity
    rows = min(slots, 3 * children // 2)
    hidden = reward_out.shape[1] // mp
    pairs = lambda count, k: [(i, i ^ k) for i in range(count)]
    swap = pairs(mp, 1)

    ups = [lax.all_gather(reward_up[0], "dp", axis=0)]

    blocks = dispatch(parents, child_count, child_parent, node_shard, tokens, reward_out, groups, capacity, hidden)
    keys = parent_keys.reshape(parents * prefix, kv_cols)
    values = parent_values.reshape(parents * prefix, kv_cols)
    raw = (w_query, w_key, w_value, keys, values, w_out)
    blocks, raw = lax.optimization_barrier((blocks, raw))
    arrived = {0: blocks[0]}
    for k in sorted(range(1, groups), key=lambda k: -(k ^ (k & 1))):
        arrived[k] = lax.ppermute(blocks[k], "dp", pairs(groups, k))
    blocks = [arrived[k] for k in range(groups)]
    blocks, weights = lax.optimization_barrier((blocks, load(*raw)))
    gain = attn_gain.reshape(1, width)

    def run(offset, weights, blocks, ups, gain, child_parent, parent_blocks):
        row_own, notes, bias, scale, over = pack(
            offset, rows, hidden, prefix, parent_blocks, child_parent, blocks
        )
        w_query, w_key, w_value, keys, values, w_out = [held(w) for w in weights]
        state = row_own.astype(jnp.float32)
        row_peer = lax.ppermute(row_own, "mp", swap)
        past_keys, past_values, rows_own, rows_peer, norms = [], [], [], [], []

        def products(first, last, ups, load):
            sums = score(mp, notes, ups, rows_own[first:last], rows_peer[first:last], load)
            count = mp if load else 1
            return list(sums[:count]), [held(up) for up in sums[count:]]

        send = lambda sums: [sums[0]] + [lax.ppermute(sums[k], "mp", pairs(mp, k)) for k in range(1, mp)]
        scales = send([scale] * mp)
        for step in range(STEPS):
            part, attn, key_now, value_now, norm = expand(
                step, row_own, row_peer, gain, w_query, w_key, w_value, keys, values, bias, w_out,
                past_keys, past_values,
            )
            norms.append(norm)
            past_keys.append(key_now)
            past_values.append(value_now)
            from_peer = lax.ppermute(part, "mp", swap)
            chip = project_own(rows, attn, w_out) + from_peer.astype(jnp.float32)
            sent = chip.astype(jnp.bfloat16)
            others = [sent] + [lax.ppermute(sent, "mp", pairs(mp, k)) for k in range(2, mp, 2)]
            if step == 0:
                others, scales = lax.optimization_barrier((others, scales))
            if step + 1 == STEPS:
                _, ups = lax.optimization_barrier((sent, ups))
                before, ups = products(0, step, ups, True)
                others, before = lax.optimization_barrier((others, before))
            state = state + paired_sum([other.astype(jnp.float32) for other in others])
            row_own = state.astype(jnp.bfloat16)
            row_peer = lax.ppermute(row_own, "mp", swap)
            rows_own.append(row_own)
            rows_peer.append(row_peer)
        before = send(before)
        last, _ = products(step, STEPS, ups, False)
        last, over = lax.optimization_barrier((send(last * mp), over[0, 0]))
        before = send([finish(notes, scale, norms[1:], before)] * mp)
        return place(groups, reward_cap, notes, row_own, row_peer, before, scales, last), over

    operands = (blocks, ups, gain, child_parent, parent_blocks)

    table, over = run(0, weights, *operands)
    if rows < slots:
        table, raw, operands = lax.optimization_barrier((table, raw, operands))
        again = lambda table, raw, operands: table + run(rows, load(*raw), *operands)[0]
        table = lax.cond(over > 0, again, lambda table, raw, operands: table, table, raw, operands)

    table = lax.all_to_all(table, "dp", split_axis=0, concat_axis=0, tiled=True)
    return jnp.sum(table.reshape(groups, STEPS, -1), 0)[:, : groups * reward_cap]


def solution(mesh):
    placed = (
        P("dp", None),
        P("dp", None, "mp"),
        P("dp", None, "mp"),
        P(),
        P(),
        P("dp"),
        P(),
        P(),
        P(None, "mp"),
        P(None, "mp"),
        P(None, "mp"),
        P("mp", None),
        P("dp", "mp", None),
        P("dp", None),
    )
    return jax.shard_map(
        shards, mesh=mesh, in_specs=placed, out_specs=P(None, "dp"), check_vma=False
    )
```

```python
import functools
import math

import jax
import jax.numpy as jnp
from jax import lax
from jax.experimental import pallas as pl
from jax.experimental.pallas import tpu as pltpu
from jax.sharding import PartitionSpec as P

D = 5120
HEADS = 24
KVH = 8
HD = 128
STEPS = 8
GROUP = HEADS // KVH
CHUNK = 512
COLUMNS = 256
ROWS = 64
MASKED = -1e30
EXPONENT = HD ** (-0.5) * math.log2(math.e)
VMEM = pltpu.VMEM
NOTES = 128
LIVE, RANK, SHARD, PARENT, SOURCE, COUNT = range(6)


def dot(a, b):
    return jnp.dot(a, b, preferred_element_type=jnp.float32)


def held(x):
    return pltpu.with_memory_space_constraint(x, VMEM)


def far(x):
    return pltpu.with_memory_space_constraint(x, pltpu.HBM)


def struct(shape, dtype=jnp.bfloat16):
    return jax.ShapeDtypeStruct(shape, dtype)


WHOLE = pl.BlockSpec(memory_space=VMEM)
FAR = pl.BlockSpec(memory_space=pltpu.HBM)
SMALL = pl.CostEstimate(flops=0, bytes_accessed=0, transcendentals=0)
SCALARS = pl.BlockSpec(memory_space=pltpu.SMEM)


def paired_sum(parts):
    while len(parts) > 1:
        parts = [a + b for a, b in zip(parts[::2], parts[1::2])]
    return parts[0]


def coordinates():
    me = lax.axis_index("mp")
    return lax.rem(me, 2), lax.axis_index("dp"), me


def dispatch_kernel(parents, groups, count, parent_far, shard_far, tokens_far, reward_far, *rest):
    core, own, me = coordinates()
    blocks, near = rest[:groups], rest[groups:]
    parent_row, shard_row, tokens, reward_out, sems = near
    children, half = tokens.shape
    sources = (parent_far, shard_far, tokens_far.at[:, pl.ds(pl.multiple_of(core * half, half), half)], reward_far)
    copies = [pltpu.make_async_copy(a, b, sems.at[i]) for i, (a, b) in enumerate(zip(sources, near))]
    for copy in copies:
        copy.start()
    for copy in copies:
        copy.wait()
    capacity = blocks[0].shape[0]
    everyone = parent_row.shape[1]
    int32, float32, bfloat16 = jnp.int32, jnp.float32, jnp.bfloat16

    mine = lax.broadcasted_iota(int32, (everyone, children), 0) - own * children
    mine = (mine == lax.broadcasted_iota(int32, (everyone, children), 1)).astype(float32).astype(bfloat16)

    def row_and_column(table):
        table = table[...].astype(float32).astype(bfloat16)
        column = lax.dot_general(mine, table, (((0,), (1,)), ((), ())), preferred_element_type=float32)
        return dot(table, mine).astype(int32), column.astype(int32)

    parent, parent_c = row_and_column(parent_row)
    shard, shard_c = row_and_column(shard_row)
    source, source_c = lax.div(parent, parents), lax.div(parent_c, parents)
    first = lax.broadcasted_iota(int32, (children, children), 0)
    second = lax.broadcasted_iota(int32, (children, children), 1)
    live = lax.broadcasted_iota(int32, (1, children), 1) < count[0]
    live_c = lax.broadcasted_iota(int32, (children, 1), 0) < count[0]
    rank = jnp.sum(jnp.where((source_c == source) & (first < second) & live_c, 1, 0), 0, keepdims=True)
    slot = (source ^ own) * capacity + rank
    slot = jnp.where(live, slot, -1)
    reward_rank = jnp.sum(jnp.where((shard_c == shard) & (second < first) & live, 1, 0), 1, keepdims=True)
    lane = lax.broadcasted_iota(int32, (children, NOTES), 1)
    notes = jnp.where(lane == LIVE, live_c.astype(int32), 0)
    for at, value in ((RANK, reward_rank), (SHARD, shard_c), (PARENT, lax.rem(parent_c, parents)), (SOURCE, own)):
        notes = jnp.where(lane == at, value, notes)

    width = blocks[0].shape[1] - half - NOTES
    hidden = width // 3
    rest = jnp.zeros((1, hidden), float32)
    for m in range(reward_out.shape[1] // hidden):
        rest = rest + jnp.where(me == m, reward_out[:, m * hidden : (m + 1) * hidden], 0.0)
    parts = []
    for _ in range(3):
        parts.append(rest.astype(bfloat16).astype(float32))
        rest = rest - parts[-1]
    shared = jnp.broadcast_to(jnp.concatenate(parts, 1), (capacity, width))

    rows = lax.broadcasted_iota(int32, (groups * capacity, children), 0)
    put = (rows == slot).astype(float32).astype(bfloat16)
    token_rows = dot(put, tokens[...])
    note_rows = dot(put, notes.astype(float32).astype(bfloat16))
    row = lax.broadcasted_iota(int32, note_rows.shape, 0)
    lane = lax.broadcasted_iota(int32, note_rows.shape, 1)
    note_rows = jnp.where((lax.rem(row, capacity) == 0) & (lane == COUNT), count[0].astype(float32), note_rows)
    for k, block in enumerate(blocks):
        at = slice(k * capacity, (k + 1) * capacity)
        block[...] = jnp.concatenate([token_rows[at], note_rows[at], shared], 1).astype(bfloat16)


def dispatch(parents, child_count, child_parent, node_shard, tokens, reward_out, groups, capacity, hidden):
    children, half = tokens.shape[0], tokens.shape[1] // 2
    tables = (child_parent[None], node_shard[None])
    return pl.pallas_call(
        functools.partial(dispatch_kernel, parents, groups),
        out_shape=(struct((capacity, half + NOTES + 3 * hidden)),) * groups,
        in_specs=[SCALARS] + [FAR] * 4,
        out_specs=(WHOLE,) * groups,
        scratch_shapes=[VMEM(x.shape, x.dtype) for x in tables]
        + [VMEM((children, half), tokens.dtype), VMEM(reward_out.shape, reward_out.dtype)]
        + [pltpu.SemaphoreType.DMA((4,))],
        compiler_params=pltpu.CompilerParams(vmem_limit_bytes=8 << 20),
        cost_estimate=SMALL,
        name="dispatch",
    )(child_count, *map(far, (*tables, tokens, reward_out)))


def crossing_first(groups):
    return sorted(range(groups), key=lambda k: -(k ^ (k & 1)))


def pack_kernel(offset, hidden, prefix, blocks_held, parent_row, *rest):
    blocks, (row, notes, bias, scale, over) = rest[:-5], rest[-5:]
    blocks = [block for _, block in sorted(zip(crossing_first(len(blocks)), blocks), key=lambda pair: pair[0])]
    _, own, _ = coordinates()
    groups, capacity = len(blocks), blocks[0].shape[0]
    rows, half = row.shape
    slots = groups * capacity
    arrived = jnp.concatenate([block[...].astype(jnp.float32) for block in blocks], 0)
    live = arrived[:, half + LIVE : half + LIVE + 1]
    first = lax.broadcasted_iota(jnp.int32, (slots, slots), 0)
    second = lax.broadcasted_iota(jnp.int32, (slots, slots), 1)
    place = jnp.sum(jnp.where(first < second, live, 0.0), 0, keepdims=True)
    kept = jnp.sum(jnp.where(first == second, live, 0.0), 0, keepdims=True) > 0.5
    wanted = lax.broadcasted_iota(jnp.int32, (rows, slots), 0) + offset
    take = (wanted == place.astype(jnp.int32)) & kept
    take = take.astype(jnp.float32).astype(jnp.bfloat16)
    row[...] = dot(take, arrived[:, :half].astype(jnp.bfloat16)).astype(jnp.bfloat16)
    note = dot(take, arrived[:, half : half + NOTES].astype(jnp.bfloat16))
    notes[...] = note
    parent = note[:, PARENT : PARENT + 1].astype(jnp.int32)
    parents = bias.shape[1] // prefix
    position = lax.broadcasted_iota(jnp.int32, (rows, prefix), 1)
    for p in range(parents):
        usable = (parent == p) & (position < blocks_held[own * parents + p] * 128)
        bias[:, p * prefix : (p + 1) * prefix] = jnp.where(usable, 0.0, MASKED)
    base = half + NOTES
    child = lax.broadcasted_iota(jnp.int32, parent_row.shape, 1)
    children = parent_row.shape[1] // groups
    at, child = lax.div(child, children), lax.rem(child, children)
    count = jnp.zeros(parent_row.shape, jnp.float32)
    for k in range(groups):
        first_row = arrived[k * capacity : k * capacity + 1]
        head = first_row[:, base:]
        scale[pl.ds(own ^ k, 1), :] = head[:, :hidden] + head[:, hidden : 2 * hidden] + head[:, 2 * hidden : 3 * hidden]
        count = jnp.where(at == (own ^ k), first_row[:, half + COUNT : half + COUNT + 1], count)
    source = lax.div(parent_row[...], parents)
    going = child < count.astype(jnp.int32)
    most = jnp.zeros((1, 1), jnp.float32)
    for d in range(groups):
        load = jnp.sum(jnp.where((source == d) & going, 1.0, 0.0), 1, keepdims=True)
        most = jnp.maximum(most, load)
    over[...] = jnp.broadcast_to((most > rows).astype(jnp.int32), over.shape)


def pack(offset, rows, hidden, prefix, blocks_held, child_parent, blocks):
    half = D // 2
    groups = len(blocks)
    parents = blocks_held.shape[0] // groups
    return pl.pallas_call(
        functools.partial(pack_kernel, offset, hidden, prefix),
        out_shape=(
            struct((rows, half)),
            struct((rows, NOTES), jnp.float32),
            struct((rows, parents * prefix), jnp.float32),
            struct((groups, hidden), jnp.float32),
            struct((8, 128), jnp.int32),
        ),
        in_specs=[SCALARS] + [WHOLE] * (1 + groups),
        out_specs=[WHOLE] * 5,
        compiler_params=pltpu.CompilerParams(vmem_limit_bytes=12 << 20),
        cost_estimate=SMALL,
        name="pack",
    )(blocks_held, child_parent[None], *[blocks[k] for k in crossing_first(groups)])


def load_kernel(*refs):
    count = (len(refs) - 1) // 2
    copies = [pltpu.make_async_copy(refs[i], refs[count + i], refs[-1].at[i]) for i in range(count)]
    for copy in copies:
        copy.start()
    for copy in copies:
        copy.wait()


def load(*arrays):
    count = len(arrays)
    return pl.pallas_call(
        load_kernel,
        out_shape=tuple(VMEM(x.shape, x.dtype) for x in arrays),
        in_specs=[FAR] * count,
        out_specs=(WHOLE,) * count,
        scratch_shapes=[pltpu.SemaphoreType.DMA((count,))],
        compiler_params=pltpu.CompilerParams(vmem_limit_bytes=2 << 20),
        cost_estimate=pl.CostEstimate(flops=0, bytes_accessed=24 << 20, transcendentals=0),
        name="load",
    )(*map(far, arrays))


def project(attn, w_out, out, first):
    width = out.shape[1]

    @pl.loop(0, width // CHUNK)
    def _(i):
        columns = pl.ds(pl.multiple_of(first + i * CHUNK, CHUNK), CHUNK)
        out[:, pl.ds(pl.multiple_of(i * CHUNK, CHUNK), CHUNK)] = dot(
            attn[...], w_out[:, columns]
        )[: out.shape[0]].astype(out.dtype)


def products_of(row, first, half, gain, weights, normed):
    at = pl.ds(pl.multiple_of(first, half), half)
    slots = row.shape[0]
    normed[:slots, :] = (row[...].astype(jnp.float32) * gain[:, at]).astype(jnp.bfloat16)
    if normed.shape[0] > slots:
        normed[slots:, :] = jnp.zeros((normed.shape[0] - slots, half), jnp.bfloat16)
    column = 0
    for w in weights:
        for start in range(0, w.shape[1], COLUMNS):
            end = min(start + COLUMNS, w.shape[1])
            yield slice(column + start, column + end), dot(normed[...], w[at, start:end])[:slots]
        column += w.shape[1]


def begin_kernel(own, gain, w_query, w_key, w_value, out, normed):
    core, _, _ = coordinates()
    half = own.shape[1]
    for columns, value in products_of(own, core * half, half, gain, (w_query, w_key, w_value), normed):
        out[:, columns] = value


def begin(own, gain, w_query, w_key, w_value):
    slots, half = own.shape
    padded = -(-slots // ROWS) * ROWS
    return pl.pallas_call(
        begin_kernel,
        out_shape=struct((slots, w_query.shape[1] + 2 * w_key.shape[1]), jnp.float32),
        in_specs=[WHOLE] * 5,
        out_specs=WHOLE,
        scratch_shapes=[VMEM((padded, half), jnp.bfloat16)],
        compiler_params=pltpu.CompilerParams(vmem_limit_bytes=8 << 20),
        cost_estimate=SMALL,
        name="begin",
    )(own, gain, w_query, w_key, w_value)


def step_kernel(step, own, peer, begun, gain, w_query, w_key, w_value, keys, values, bias, w_out, *rest):
    past_keys, past_values = rest[:step], rest[step : 2 * step]
    rest = rest[2 * step :]
    half = own.shape[1]
    slots = own.shape[0]
    q_cols, kv_cols = w_query.shape[1], w_key.shape[1]
    kv_heads = kv_cols // HD
    part, attn, key_now, value_now, norm, normed, query = rest
    core, _, _ = coordinates()
    here, there = own[...].astype(jnp.float32), peer[...].astype(jnp.float32)
    squares = jnp.sum(here * here, -1, keepdims=True) + jnp.sum(there * there, -1, keepdims=True)
    factor = lax.rsqrt(squares / D + 1e-06)
    norm[...] = jnp.broadcast_to(factor, norm.shape)
    for columns, value in products_of(peer, (1 - core) * half, half, gain, (w_query, w_key, w_value), normed):
        query[:, columns] = (begun[:, columns] + value) * factor
    key_now[...] = query[:slots, q_cols : q_cols + kv_cols].astype(jnp.bfloat16)
    value_now[...] = query[:slots, q_cols + kv_cols :].astype(jnp.bfloat16)
    recent = slots * (step + 1)
    row = lax.broadcasted_iota(jnp.int32, (GROUP * slots, recent), 0)
    column = lax.broadcasted_iota(jnp.int32, (GROUP * slots, recent), 1)
    same = lax.rem(row, slots) == lax.rem(column, slots)
    for head in range(kv_heads):
        lanes = slice(head * HD, (head + 1) * HD)
        q = jnp.concatenate(
            [query[:slots, (head * GROUP + g) * HD : (head * GROUP + g + 1) * HD] for g in range(GROUP)], 0
        ).astype(jnp.bfloat16)
        k_new = jnp.concatenate([k[:, lanes] for k in past_keys] + [key_now[:, lanes]], 0)
        v_new = jnp.concatenate([v[:, lanes] for v in past_values] + [value_now[:, lanes]], 0)
        contract = (((1,), (1,)), ((), ()))
        s_old = lax.dot_general(q, keys[:, lanes], contract, preferred_element_type=jnp.float32)
        s_old = s_old + jnp.concatenate([bias[...]] * GROUP, 0)
        s_new = lax.dot_general(q, k_new, contract, preferred_element_type=jnp.float32)
        s_new = jnp.where(same, s_new, MASKED)
        top = jnp.maximum(jnp.max(s_old, -1, keepdims=True), jnp.max(s_new, -1, keepdims=True))
        p_old = jnp.exp2(s_old * EXPONENT - top * EXPONENT)
        p_new = jnp.exp2(s_new * EXPONENT - top * EXPONENT)
        total = jnp.sum(p_old, -1, keepdims=True) + jnp.sum(p_new, -1, keepdims=True)
        summed = dot(p_old.astype(jnp.bfloat16), values[:, lanes]) + dot(p_new.astype(jnp.bfloat16), v_new)
        result = (summed / total).astype(jnp.bfloat16)
        for g in range(GROUP):
            at = (head * GROUP + g) * HD
            attn[:slots, at : at + HD] = result[g * slots : (g + 1) * slots]
    if attn.shape[0] > slots:
        attn[slots:, :] = jnp.zeros((attn.shape[0] - slots, q_cols), jnp.bfloat16)
    project(attn, w_out, part, (1 - core) * half)


def expand(step, own, peer, begun, gain, w_query, w_key, w_value, keys, values, bias, w_out, past_keys, past_values):
    slots, half = own.shape
    kv_cols = w_key.shape[1]
    q_cols = w_query.shape[1]
    padded = -(-slots // ROWS) * ROWS
    return pl.pallas_call(
        functools.partial(step_kernel, step),
        out_shape=(
            struct((slots, half)), struct((padded, q_cols)), struct((slots, kv_cols)), struct((slots, kv_cols)),
            struct((slots, 128), jnp.float32),
        ),
        in_specs=[WHOLE] * (11 + 2 * step),
        out_specs=[WHOLE] * 5,
        scratch_shapes=[VMEM((padded, half), jnp.bfloat16), VMEM((slots, q_cols + 2 * kv_cols), jnp.float32)],
        compiler_params=pltpu.CompilerParams(vmem_limit_bytes=16 << 20),
        cost_estimate=SMALL,
        name="expand",
    )(own, peer, begun, gain, w_query, w_key, w_value, keys, values, bias, w_out, *past_keys, *past_values)


def project_kernel(attn, w_out, part):
    core, _, _ = coordinates()
    project(attn, w_out, part, core * part.shape[1])


def project_own(rows, attn, w_out):
    return pl.pallas_call(
        project_kernel,
        out_shape=struct((rows, w_out.shape[1] // 2), jnp.float32),
        in_specs=[WHOLE, WHOLE],
        out_specs=WHOLE,
        compiler_params=pltpu.CompilerParams(vmem_limit_bytes=8 << 20),
        cost_estimate=SMALL,
        name="project_own",
    )(attn, w_out)


def score_kernel(steps, load, groups, mp, notes, *refs):
    take = lambda count: [refs.pop(0) for _ in range(count)]
    refs = list(refs)
    ups, own_rows, peer_rows, blocks = take(1 + groups if load else 2), take(steps), take(steps), take(mp if load else 1)
    kept = take(2 * load)
    flat, total, *sems = refs
    _, cut, hidden = ups[0].shape
    depth = flat.shape[1]
    rows = own_rows[0].shape[0]
    core, own, me = coordinates()
    for t in range(steps):
        target = flat.at[t * rows : (t + 1) * rows]
        for m in range(mp):
            at = m % (mp // 2) * depth
            for c in range(2):
                source = (own_rows if m // (mp // 2) == c else peer_rows)[t].at[:, at : at + depth]

                @pl.when((me == m) & (core == c))
                def _():
                    if load:
                        pltpu.make_async_copy(source, target, sems[0].at[t]).start()
                    else:
                        target[...] = source[...]

    if load:
        for r in range(groups):
            pltpu.make_async_copy(ups[0].at[r], kept[0].at[r], sems[1].at[r]).start()
        for k in range(groups):
            pltpu.make_async_copy(ups[1 + k], kept[1].at[own ^ k], sems[2].at[own ^ k]).start()
        ups = kept
        for t in range(steps):
            target = flat.at[t * rows : (t + 1) * rows]
            pltpu.make_async_copy(target, target, sems[0].at[t]).wait()
    shard = jnp.concatenate([notes[:, SHARD : SHARD + 1].astype(jnp.int32)] * steps, 0)
    for r in range(groups):
        if load:
            for i, up in enumerate(ups):
                pltpu.make_async_copy(up.at[r], up.at[r], sems[1 + i].at[r]).wait()
        for at in range(0, hidden, COLUMNS):
            end = min(at + COLUMNS, hidden)
            z = dot(flat[:, :cut], ups[0][r, :, at:end]) + dot(flat[:, cut:], ups[1][r, :, at:end])
            here = jnp.where(shard == r, z, 0.0)
            total[:, at:end] = here if r == 0 else total[:, at:end] + here
    if not load:
        blocks[0][...] = total[...].astype(jnp.bfloat16)
        return
    width = hidden // mp
    for j, block in enumerate(blocks):
        for m in range(mp):

            @pl.when((me ^ j) == m)
            def _():
                block[...] = total[:, m * width : (m + 1) * width].astype(jnp.bfloat16)


def score(mp, notes, ups, own_rows, peer_rows, load):
    steps = len(own_rows)
    groups, cut, hidden = ups[0].shape
    rest = ups[1].shape[-2]
    count = steps * own_rows[0].shape[0]
    blocks = (struct((count, hidden // mp)),) * mp if load else (struct((count, hidden)),)
    kept = (VMEM((groups, cut, hidden), jnp.bfloat16), VMEM((groups, rest, hidden), jnp.bfloat16)) * load
    place = FAR if load else WHOLE
    sems = [pltpu.SemaphoreType.DMA((steps,))] + [pltpu.SemaphoreType.DMA((groups,))] * 2
    return pl.pallas_call(
        functools.partial(score_kernel, steps, load, groups, mp),
        out_shape=blocks + kept,
        in_specs=[WHOLE] + [place] * (len(ups) + 2 * steps),
        out_specs=(WHOLE,) * (len(blocks) + len(kept)),
        scratch_shapes=[VMEM((count, cut + rest), jnp.bfloat16), VMEM((count, hidden), jnp.float32)] + sems * load,
        compiler_params=pltpu.CompilerParams(vmem_limit_bytes=16 << 20),
        cost_estimate=SMALL,
        name="score",
    )(notes, *(map(far, (*ups, *own_rows, *peer_rows)) if load else (*ups, *own_rows, *peer_rows)))


def scores_of(notes, scale, parts, factors):
    rows = notes.shape[0]
    shard = notes[:, SHARD : SHARD + 1].astype(jnp.int32)
    gain = jnp.zeros((rows, scale.shape[1]), jnp.float32)
    for r in range(scale.shape[0]):
        gain = gain + jnp.where(shard == r, scale[r : r + 1, :], 0.0)
    values = []
    for t, factor in enumerate(factors):
        z = paired_sum([part[t * rows : (t + 1) * rows, :].astype(jnp.float32) for part in parts]) * factor
        values.append(jnp.sum(z * jax.nn.sigmoid(z) * gain, -1, keepdims=True))
    return values


def finish_kernel(steps, notes, scale, *refs):
    norms, parts, out = refs[:steps], refs[steps:-1], refs[-1]
    lane = lax.broadcasted_iota(jnp.int32, out.shape, 1)
    total = jnp.zeros(out.shape, jnp.float32)
    for t, value in enumerate(scores_of(notes, scale, parts, [norm[:, :1] for norm in norms])):
        total = jnp.where(lane == t, value, total)
    out[...] = total


def finish(notes, scale, norms, parts):
    return pl.pallas_call(
        functools.partial(finish_kernel, len(norms)),
        out_shape=struct((notes.shape[0], 128), jnp.float32),
        in_specs=[WHOLE] * (2 + len(norms) + len(parts)),
        out_specs=WHOLE,
        compiler_params=pltpu.CompilerParams(vmem_limit_bytes=12 << 20),
        cost_estimate=SMALL,
        name="finish",
    )(notes, scale, *norms, *parts)


def place_kernel(groups, cap, mp, notes, own_row, peer_row, *refs):
    befores, scales, parts, table = refs[:mp], refs[mp : 2 * mp], refs[2 * mp : 3 * mp], refs[3 * mp]
    rows = notes.shape[0]
    _, _, me = coordinates()
    before = paired_sum([x[...] for x in befores])
    values = [before[:, t : t + 1] for t in range(STEPS - 1)]
    scale = [sum(jnp.where((me ^ j) == m, scales[j][...], 0.0) for j in range(mp)) for m in range(mp)]
    low, high = own_row[...].astype(jnp.float32), peer_row[...].astype(jnp.float32)
    squares = jnp.sum(low * low, -1, keepdims=True) + jnp.sum(high * high, -1, keepdims=True)
    values += scores_of(notes, jnp.concatenate(scale, 1), parts, [lax.rsqrt(squares / D + 1e-06)])
    number = lambda lane: notes[:, lane : lane + 1].astype(jnp.int32)
    shard, at = number(SHARD), number(SOURCE) * cap + number(RANK)
    live = notes[:, LIVE : LIVE + 1] > 0.5
    column = lax.broadcasted_iota(jnp.int32, (rows, table.shape[1]), 1)
    for r in range(groups):
        spots = (column == at) & (shard == r) & live
        for t, value in enumerate(values):
            table[r * STEPS + t : r * STEPS + t + 1, :] = jnp.sum(jnp.where(spots, value, 0.0), 0, keepdims=True)


def place(groups, cap, notes, own_row, peer_row, befores, scales, parts):
    mp = len(parts)
    return pl.pallas_call(
        functools.partial(place_kernel, groups, cap, mp),
        out_shape=struct((groups * STEPS, -(-groups * cap // 128) * 128), jnp.float32),
        in_specs=[WHOLE] * (3 + 3 * mp),
        out_specs=WHOLE,
        compiler_params=pltpu.CompilerParams(vmem_limit_bytes=12 << 20),
        cost_estimate=SMALL,
        name="place",
    )(notes, own_row, peer_row, *befores, *scales, *parts)


def shards(
    tokens,
    parent_keys,
    parent_values,
    parent_blocks,
    child_parent,
    child_count,
    node_shard,
    attn_gain,
    w_query,
    w_key,
    w_value,
    w_out,
    reward_up,
    reward_out,
):
    groups, mp = lax.axis_size("dp"), lax.axis_size("mp")
    children, width = tokens.shape
    parents, prefix, kv_cols = parent_keys.shape
    capacity = max(2, 2 * children // groups)
    reward_cap = max(2, 3 * children // (2 * groups))
    slots = groups * capacity
    rows = min(slots, 3 * children // 2)
    hidden = reward_out.shape[1] // mp
    pairs = lambda count, k: [(i, i ^ k) for i in range(count)]
    swap = pairs(mp, 1)

    cut = reward_up.shape[1] * 4 // 5
    rest = reward_up[0, cut:]
    ups = [lax.all_gather(reward_up[0, :cut], "dp", axis=0)]

    blocks = dispatch(parents, child_count, child_parent, node_shard, tokens, reward_out, groups, capacity, hidden)
    keys = parent_keys.reshape(parents * prefix, kv_cols)
    values = parent_values.reshape(parents * prefix, kv_cols)
    raw = (w_query, w_key, w_value, keys, values, w_out)
    blocks, raw = lax.optimization_barrier((blocks, raw))
    blocks = [blocks[0]] + [lax.ppermute(blocks[k], "dp", pairs(groups, k)) for k in range(1, groups)]
    blocks, weights = lax.optimization_barrier((blocks, load(*raw)))
    gain = attn_gain.reshape(1, width)

    def run(offset, weights, blocks, ups, rests, gain, child_parent, parent_blocks):
        rests = list(rests)
        row_own, notes, bias, scale, over = pack(
            offset, rows, hidden, prefix, parent_blocks, child_parent, blocks
        )
        w_query, w_key, w_value, keys, values, w_out = [held(w) for w in weights]
        state = row_own.astype(jnp.float32)
        row_peer = lax.ppermute(row_own, "mp", swap)
        past_keys, past_values, rows_own, rows_peer, norms = [], [], [], [], []

        def products(first, last, ups, load):
            sums = score(mp, notes, ups, rows_own[first:last], rows_peer[first:last], load)
            count = mp if load else 1
            return list(sums[:count]), [held(up) for up in sums[count:]]

        send = lambda sums: [sums[0]] + [lax.ppermute(sums[k], "mp", pairs(mp, k)) for k in range(1, mp)]
        scales = send([scale] * mp)
        for step in range(STEPS):
            part, attn, key_now, value_now, norm = expand(
                step, row_own, row_peer, begin(row_own, gain, w_query, w_key, w_value), gain, w_query, w_key, w_value, keys, values, bias, w_out,
                past_keys, past_values,
            )
            norms.append(norm)
            past_keys.append(key_now)
            past_values.append(value_now)
            from_peer = lax.ppermute(part, "mp", swap)
            chip = project_own(rows, attn, w_out) + from_peer.astype(jnp.float32)
            sent = chip.astype(jnp.bfloat16)
            others = [sent] + [lax.ppermute(sent, "mp", pairs(mp, k)) for k in range(2, mp, 2)]
            if len(rests) < groups:
                more = range(len(rests), min(groups, len(rests) - (1 - groups) // (STEPS - 1)))
                more = [lax.ppermute(rests[0], "dp", pairs(groups, k)) for k in more]
                others, more = lax.optimization_barrier((others, more))
                rests += more
            if step == 0:
                others, scales = lax.optimization_barrier((others, scales))
            if step + 1 == STEPS:
                _, ups = lax.optimization_barrier((sent, ups))
                before, ups = products(0, step, [*ups, *rests], True)
                others, before = lax.optimization_barrier((others, before))
            state = state + paired_sum([other.astype(jnp.float32) for other in others])
            row_own = state.astype(jnp.bfloat16)
            row_peer = lax.ppermute(row_own, "mp", swap)
            rows_own.append(row_own)
            rows_peer.append(row_peer)
        before = send(before)
        last, _ = products(step, STEPS, ups, False)
        last, over = lax.optimization_barrier((send(last * mp), over[0, 0]))
        before = send([finish(notes, scale, norms[1:], before)] * mp)
        return place(groups, reward_cap, notes, row_own, row_peer, before, scales, last), over, rests

    others = (gain, child_parent, parent_blocks)
    table, over, rests = run(0, weights, blocks, ups, [rest], *others)
    operands = (blocks, ups, rests, *others)
    if rows < slots:
        table, raw, operands = lax.optimization_barrier((table, raw, operands))
        again = lambda table, raw, operands: table + run(rows, load(*raw), *operands)[0]
        table = lax.cond(over > 0, again, lambda table, raw, operands: table, table, raw, operands)

    table = lax.all_to_all(table, "dp", split_axis=0, concat_axis=0, tiled=True)
    return jnp.sum(table.reshape(groups, STEPS, -1), 0)[:, : groups * reward_cap]


def solution(mesh):
    placed = (
        P("dp", None),
        P("dp", None, "mp"),
        P("dp", None, "mp"),
        P(),
        P(),
        P("dp"),
        P(),
        P(),
        P(None, "mp"),
        P(None, "mp"),
        P(None, "mp"),
        P("mp", None),
        P("dp", "mp", None),
        P("dp", None),
    )
    return jax.shard_map(
        shards, mesh=mesh, in_specs=placed, out_specs=P(None, "dp"), check_vma=False
    )
```

```python
import functools
import math

import jax
import jax.numpy as jnp
from jax import lax
from jax.experimental import pallas as pl
from jax.experimental.pallas import tpu as pltpu
from jax.sharding import PartitionSpec as P

D = 5120
HEADS = 24
KVH = 8
HD = 128
STEPS = 8
GROUP = HEADS // KVH
CHUNK = 512
COLUMNS = 256
ROWS = 64
MASKED = -1e30
EXPONENT = HD ** (-0.5) * math.log2(math.e)
VMEM = pltpu.VMEM
NOTES = 128
LIVE, RANK, SHARD, PARENT, SOURCE, COUNT = range(6)


def dot(a, b):
    return jnp.dot(a, b, preferred_element_type=jnp.float32)


def held(x):
    return pltpu.with_memory_space_constraint(x, VMEM)


def far(x):
    return pltpu.with_memory_space_constraint(x, pltpu.HBM)


def struct(shape, dtype=jnp.bfloat16):
    return jax.ShapeDtypeStruct(shape, dtype)


WHOLE = pl.BlockSpec(memory_space=VMEM)
FAR = pl.BlockSpec(memory_space=pltpu.HBM)
SMALL = pl.CostEstimate(flops=0, bytes_accessed=0, transcendentals=0)
SCALARS = pl.BlockSpec(memory_space=pltpu.SMEM)


def paired_sum(parts):
    while len(parts) > 1:
        parts = [a + b for a, b in zip(parts[::2], parts[1::2])]
    return parts[0]


def ring_order(groups):
    return list(range(0, groups, 2)) + list(range(groups - 1, 0, -2))


def coordinates():
    me = lax.axis_index("mp")
    return lax.rem(me, 2), lax.axis_index("dp"), me


def dispatch_kernel(parents, groups, count, parent_far, shard_far, tokens_far, reward_far, *rest):
    core, own, me = coordinates()
    blocks, near = rest[:groups], rest[groups:]
    parent_row, shard_row, tokens, reward_out, sems = near
    children, half = tokens.shape
    sources = (parent_far, shard_far, tokens_far.at[:, pl.ds(pl.multiple_of(core * half, half), half)], reward_far)
    copies = [pltpu.make_async_copy(a, b, sems.at[i]) for i, (a, b) in enumerate(zip(sources, near))]
    for copy in copies:
        copy.start()
    for copy in copies:
        copy.wait()
    capacity = blocks[0].shape[0]
    everyone = parent_row.shape[1]
    int32, float32, bfloat16 = jnp.int32, jnp.float32, jnp.bfloat16

    mine = lax.broadcasted_iota(int32, (everyone, children), 0) - own * children
    mine = (mine == lax.broadcasted_iota(int32, (everyone, children), 1)).astype(float32).astype(bfloat16)

    def row_and_column(table):
        table = table[...].astype(float32).astype(bfloat16)
        column = lax.dot_general(mine, table, (((0,), (1,)), ((), ())), preferred_element_type=float32)
        return dot(table, mine).astype(int32), column.astype(int32)

    parent, parent_c = row_and_column(parent_row)
    shard, shard_c = row_and_column(shard_row)
    source, source_c = lax.div(parent, parents), lax.div(parent_c, parents)
    first = lax.broadcasted_iota(int32, (children, children), 0)
    second = lax.broadcasted_iota(int32, (children, children), 1)
    live = lax.broadcasted_iota(int32, (1, children), 1) < count[0]
    live_c = lax.broadcasted_iota(int32, (children, 1), 0) < count[0]
    rank = jnp.sum(jnp.where((source_c == source) & (first < second) & live_c, 1, 0), 0, keepdims=True)
    slot = (source ^ own) * capacity + rank
    slot = jnp.where(live, slot, -1)
    reward_rank = jnp.sum(jnp.where((shard_c == shard) & (second < first) & live, 1, 0), 1, keepdims=True)
    lane = lax.broadcasted_iota(int32, (children, NOTES), 1)
    notes = jnp.where(lane == LIVE, live_c.astype(int32), 0)
    for at, value in ((RANK, reward_rank), (SHARD, shard_c), (PARENT, lax.rem(parent_c, parents)), (SOURCE, own)):
        notes = jnp.where(lane == at, value, notes)

    width = blocks[0].shape[1] - half - NOTES
    hidden = width // 3
    rest = jnp.zeros((1, hidden), float32)
    for m in range(reward_out.shape[1] // hidden):
        rest = rest + jnp.where(me == m, reward_out[:, m * hidden : (m + 1) * hidden], 0.0)
    parts = []
    for _ in range(3):
        parts.append(rest.astype(bfloat16).astype(float32))
        rest = rest - parts[-1]
    shared = jnp.broadcast_to(jnp.concatenate(parts, 1), (capacity, width))

    rows = lax.broadcasted_iota(int32, (groups * capacity, children), 0)
    put = (rows == slot).astype(float32).astype(bfloat16)
    token_rows = dot(put, tokens[...])
    note_rows = dot(put, notes.astype(float32).astype(bfloat16))
    row = lax.broadcasted_iota(int32, note_rows.shape, 0)
    lane = lax.broadcasted_iota(int32, note_rows.shape, 1)
    note_rows = jnp.where((lax.rem(row, capacity) == 0) & (lane == COUNT), count[0].astype(float32), note_rows)
    for k, block in enumerate(blocks):
        at = slice(k * capacity, (k + 1) * capacity)
        block[...] = jnp.concatenate([token_rows[at], note_rows[at], shared], 1).astype(bfloat16)


def dispatch(parents, child_count, child_parent, node_shard, tokens, reward_out, groups, capacity, hidden):
    children, half = tokens.shape[0], tokens.shape[1] // 2
    tables = (child_parent[None], node_shard[None])
    return pl.pallas_call(
        functools.partial(dispatch_kernel, parents, groups),
        out_shape=(struct((capacity, half + NOTES + 3 * hidden)),) * groups,
        in_specs=[SCALARS] + [FAR] * 4,
        out_specs=(WHOLE,) * groups,
        scratch_shapes=[VMEM(x.shape, x.dtype) for x in tables]
        + [VMEM((children, half), tokens.dtype), VMEM(reward_out.shape, reward_out.dtype)]
        + [pltpu.SemaphoreType.DMA((4,))],
        compiler_params=pltpu.CompilerParams(vmem_limit_bytes=8 << 20),
        cost_estimate=SMALL,
        name="dispatch",
    )(child_count, *map(far, (*tables, tokens, reward_out)))


def crossing_first(groups):
    return sorted(range(groups), key=lambda k: -(k ^ (k & 1)))


def pack_kernel(offset, hidden, prefix, blocks_held, parent_row, *rest):
    blocks, (row, notes, bias, scale, over) = rest[:-5], rest[-5:]
    blocks = [block for _, block in sorted(zip(crossing_first(len(blocks)), blocks), key=lambda pair: pair[0])]
    _, own, _ = coordinates()
    groups, capacity = len(blocks), blocks[0].shape[0]
    rows, half = row.shape
    slots = groups * capacity
    arrived = jnp.concatenate([block[...].astype(jnp.float32) for block in blocks], 0)
    live = arrived[:, half + LIVE : half + LIVE + 1]
    first = lax.broadcasted_iota(jnp.int32, (slots, slots), 0)
    second = lax.broadcasted_iota(jnp.int32, (slots, slots), 1)
    place = jnp.sum(jnp.where(first < second, live, 0.0), 0, keepdims=True)
    kept = jnp.sum(jnp.where(first == second, live, 0.0), 0, keepdims=True) > 0.5
    wanted = lax.broadcasted_iota(jnp.int32, (rows, slots), 0) + offset
    take = (wanted == place.astype(jnp.int32)) & kept
    take = take.astype(jnp.float32).astype(jnp.bfloat16)
    row[...] = dot(take, arrived[:, :half].astype(jnp.bfloat16)).astype(jnp.bfloat16)
    note = dot(take, arrived[:, half : half + NOTES].astype(jnp.bfloat16))
    notes[...] = note
    parent = note[:, PARENT : PARENT + 1].astype(jnp.int32)
    parents = bias.shape[1] // prefix
    position = lax.broadcasted_iota(jnp.int32, (rows, prefix), 1)
    for p in range(parents):
        usable = (parent == p) & (position < blocks_held[own * parents + p] * 128)
        bias[:, p * prefix : (p + 1) * prefix] = jnp.where(usable, 0.0, MASKED)
    base = half + NOTES
    child = lax.broadcasted_iota(jnp.int32, parent_row.shape, 1)
    children = parent_row.shape[1] // groups
    at, child = lax.div(child, children), lax.rem(child, children)
    count = jnp.zeros(parent_row.shape, jnp.float32)
    for k in range(groups):
        first_row = arrived[k * capacity : k * capacity + 1]
        head = first_row[:, base:]
        scale[pl.ds(own ^ k, 1), :] = head[:, :hidden] + head[:, hidden : 2 * hidden] + head[:, 2 * hidden : 3 * hidden]
        count = jnp.where(at == (own ^ k), first_row[:, half + COUNT : half + COUNT + 1], count)
    source = lax.div(parent_row[...], parents)
    going = child < count.astype(jnp.int32)
    most = jnp.zeros((1, 1), jnp.float32)
    for d in range(groups):
        load = jnp.sum(jnp.where((source == d) & going, 1.0, 0.0), 1, keepdims=True)
        most = jnp.maximum(most, load)
    over[...] = jnp.broadcast_to((most > rows).astype(jnp.int32), over.shape)


def pack(offset, rows, hidden, prefix, blocks_held, child_parent, blocks):
    half = D // 2
    groups = len(blocks)
    parents = blocks_held.shape[0] // groups
    return pl.pallas_call(
        functools.partial(pack_kernel, offset, hidden, prefix),
        out_shape=(
            struct((rows, half)),
            struct((rows, NOTES), jnp.float32),
            struct((rows, parents * prefix), jnp.float32),
            struct((groups, hidden), jnp.float32),
            struct((8, 128), jnp.int32),
        ),
        in_specs=[SCALARS] + [WHOLE] * (1 + groups),
        out_specs=[WHOLE] * 5,
        compiler_params=pltpu.CompilerParams(vmem_limit_bytes=12 << 20),
        cost_estimate=SMALL,
        name="pack",
    )(blocks_held, child_parent[None], *[blocks[k] for k in crossing_first(groups)])


def load_kernel(*refs):
    count = (len(refs) - 1) // 2
    copies = [pltpu.make_async_copy(refs[i], refs[count + i], refs[-1].at[i]) for i in range(count)]
    for copy in copies:
        copy.start()
    for copy in copies:
        copy.wait()


def load(*arrays):
    count = len(arrays)
    return pl.pallas_call(
        load_kernel,
        out_shape=tuple(VMEM(x.shape, x.dtype) for x in arrays),
        in_specs=[FAR] * count,
        out_specs=(WHOLE,) * count,
        scratch_shapes=[pltpu.SemaphoreType.DMA((count,))],
        compiler_params=pltpu.CompilerParams(vmem_limit_bytes=2 << 20),
        cost_estimate=pl.CostEstimate(flops=0, bytes_accessed=24 << 20, transcendentals=0),
        name="load",
    )(*map(far, arrays))


def project(attn, w_out, out, first):
    width = out.shape[1]

    @pl.loop(0, width // CHUNK)
    def _(i):
        columns = pl.ds(pl.multiple_of(first + i * CHUNK, CHUNK), CHUNK)
        out[:, pl.ds(pl.multiple_of(i * CHUNK, CHUNK), CHUNK)] = dot(
            attn[...], w_out[:, columns]
        )[: out.shape[0]].astype(out.dtype)


def products_of(row, first, half, gain, weights, normed):
    at = pl.ds(pl.multiple_of(first, half), half)
    slots = row.shape[0]
    normed[:slots, :] = (row[...].astype(jnp.float32) * gain[:, at]).astype(jnp.bfloat16)
    if normed.shape[0] > slots:
        normed[slots:, :] = jnp.zeros((normed.shape[0] - slots, half), jnp.bfloat16)
    column = 0
    for w in weights:
        for start in range(0, w.shape[1], COLUMNS):
            end = min(start + COLUMNS, w.shape[1])
            yield slice(column + start, column + end), dot(normed[...], w[at, start:end])[:slots]
        column += w.shape[1]


def begin_kernel(own, gain, w_query, w_key, w_value, out, normed):
    core, _, _ = coordinates()
    half = own.shape[1]
    for columns, value in products_of(own, core * half, half, gain, (w_query, w_key, w_value), normed):
        out[:, columns] = value


def begin(own, gain, w_query, w_key, w_value):
    slots, half = own.shape
    padded = -(-slots // ROWS) * ROWS
    return pl.pallas_call(
        begin_kernel,
        out_shape=struct((slots, w_query.shape[1] + 2 * w_key.shape[1]), jnp.float32),
        in_specs=[WHOLE] * 5,
        out_specs=WHOLE,
        scratch_shapes=[VMEM((padded, half), jnp.bfloat16)],
        compiler_params=pltpu.CompilerParams(vmem_limit_bytes=8 << 20),
        cost_estimate=SMALL,
        name="begin",
    )(own, gain, w_query, w_key, w_value)


def step_kernel(step, own, peer, begun, gain, w_query, w_key, w_value, keys, values, bias, w_out, *rest):
    past_keys, past_values = rest[:step], rest[step : 2 * step]
    rest = rest[2 * step :]
    half = own.shape[1]
    slots = own.shape[0]
    q_cols, kv_cols = w_query.shape[1], w_key.shape[1]
    kv_heads = kv_cols // HD
    part, attn, key_now, value_now, norm, normed, query = rest
    core, _, _ = coordinates()
    here, there = own[...].astype(jnp.float32), peer[...].astype(jnp.float32)
    squares = jnp.sum(here * here, -1, keepdims=True) + jnp.sum(there * there, -1, keepdims=True)
    factor = lax.rsqrt(squares / D + 1e-06)
    norm[...] = jnp.broadcast_to(factor, norm.shape)
    for columns, value in products_of(peer, (1 - core) * half, half, gain, (w_query, w_key, w_value), normed):
        query[:, columns] = (begun[:, columns] + value) * factor
    key_now[...] = query[:slots, q_cols : q_cols + kv_cols].astype(jnp.bfloat16)
    value_now[...] = query[:slots, q_cols + kv_cols :].astype(jnp.bfloat16)
    recent = slots * (step + 1)
    row = lax.broadcasted_iota(jnp.int32, (GROUP * slots, recent), 0)
    column = lax.broadcasted_iota(jnp.int32, (GROUP * slots, recent), 1)
    same = lax.rem(row, slots) == lax.rem(column, slots)
    for head in range(kv_heads):
        lanes = slice(head * HD, (head + 1) * HD)
        q = jnp.concatenate(
            [query[:slots, (head * GROUP + g) * HD : (head * GROUP + g + 1) * HD] for g in range(GROUP)], 0
        ).astype(jnp.bfloat16)
        k_new = jnp.concatenate([k[:, lanes] for k in past_keys] + [key_now[:, lanes]], 0)
        v_new = jnp.concatenate([v[:, lanes] for v in past_values] + [value_now[:, lanes]], 0)
        contract = (((1,), (1,)), ((), ()))
        s_old = lax.dot_general(q, keys[:, lanes], contract, preferred_element_type=jnp.float32)
        s_old = s_old + jnp.concatenate([bias[...]] * GROUP, 0)
        s_new = lax.dot_general(q, k_new, contract, preferred_element_type=jnp.float32)
        s_new = jnp.where(same, s_new, MASKED)
        top = jnp.maximum(jnp.max(s_old, -1, keepdims=True), jnp.max(s_new, -1, keepdims=True))
        p_old = jnp.exp2(s_old * EXPONENT - top * EXPONENT)
        p_new = jnp.exp2(s_new * EXPONENT - top * EXPONENT)
        total = jnp.sum(p_old, -1, keepdims=True) + jnp.sum(p_new, -1, keepdims=True)
        summed = dot(p_old.astype(jnp.bfloat16), values[:, lanes]) + dot(p_new.astype(jnp.bfloat16), v_new)
        result = (summed / total).astype(jnp.bfloat16)
        for g in range(GROUP):
            at = (head * GROUP + g) * HD
            attn[:slots, at : at + HD] = result[g * slots : (g + 1) * slots]
    if attn.shape[0] > slots:
        attn[slots:, :] = jnp.zeros((attn.shape[0] - slots, q_cols), jnp.bfloat16)
    project(attn, w_out, part, (1 - core) * half)


def expand(step, own, peer, begun, gain, w_query, w_key, w_value, keys, values, bias, w_out, past_keys, past_values):
    slots, half = own.shape
    kv_cols = w_key.shape[1]
    q_cols = w_query.shape[1]
    padded = -(-slots // ROWS) * ROWS
    return pl.pallas_call(
        functools.partial(step_kernel, step),
        out_shape=(
            struct((slots, half)), struct((padded, q_cols)), struct((slots, kv_cols)), struct((slots, kv_cols)),
            struct((slots, 128), jnp.float32),
        ),
        in_specs=[WHOLE] * (11 + 2 * step),
        out_specs=[WHOLE] * 5,
        scratch_shapes=[VMEM((padded, half), jnp.bfloat16), VMEM((slots, q_cols + 2 * kv_cols), jnp.float32)],
        compiler_params=pltpu.CompilerParams(vmem_limit_bytes=16 << 20),
        cost_estimate=SMALL,
        name="expand",
    )(own, peer, begun, gain, w_query, w_key, w_value, keys, values, bias, w_out, *past_keys, *past_values)


def project_kernel(attn, w_out, part):
    core, _, _ = coordinates()
    project(attn, w_out, part, core * part.shape[1])


def project_own(rows, attn, w_out):
    return pl.pallas_call(
        project_kernel,
        out_shape=struct((rows, w_out.shape[1] // 2), jnp.float32),
        in_specs=[WHOLE, WHOLE],
        out_specs=WHOLE,
        compiler_params=pltpu.CompilerParams(vmem_limit_bytes=8 << 20),
        cost_estimate=SMALL,
        name="project_own",
    )(attn, w_out)


def score_kernel(steps, load, mp, notes, up, *refs):
    take = lambda count: [refs.pop(0) for _ in range(count)]
    refs = list(refs)
    own_rows, peer_rows, blocks, kept = take(steps), take(steps), take(mp if load else 1), take(1 * load)
    flat, total, *sems = refs
    groups, depth, hidden = up.shape
    rows = own_rows[0].shape[0]
    core, _, me = coordinates()
    for t in range(steps):
        target = flat.at[t * rows : (t + 1) * rows]
        for m in range(mp):
            at = m % (mp // 2) * depth
            for c in range(2):
                source = (own_rows if m // (mp // 2) == c else peer_rows)[t].at[:, at : at + depth]

                @pl.when((me == m) & (core == c))
                def _():
                    if load:
                        pltpu.make_async_copy(source, target, sems[0].at[t]).start()
                    else:
                        target[...] = source[...]

    if load:
        for i, r in enumerate(ring_order(groups)):
            pltpu.make_async_copy(up.at[i], kept[0].at[r], sems[1].at[r]).start()
        up = kept[0]
        for t in range(steps):
            target = flat.at[t * rows : (t + 1) * rows]
            pltpu.make_async_copy(target, target, sems[0].at[t]).wait()
    shard = jnp.concatenate([notes[:, SHARD : SHARD + 1].astype(jnp.int32)] * steps, 0)
    for r in range(groups):
        if load:
            pltpu.make_async_copy(up.at[r], up.at[r], sems[1].at[r]).wait()
        for at in range(0, hidden, COLUMNS):
            end = min(at + COLUMNS, hidden)
            here = jnp.where(shard == r, dot(flat[...], up[r, :, at:end]), 0.0)
            total[:, at:end] = here if r == 0 else total[:, at:end] + here
    if not load:
        blocks[0][...] = total[...].astype(jnp.bfloat16)
        return
    width = hidden // mp
    for j, block in enumerate(blocks):
        for m in range(mp):

            @pl.when((me ^ j) == m)
            def _():
                block[...] = total[:, m * width : (m + 1) * width].astype(jnp.bfloat16)


def score(mp, notes, up, own_rows, peer_rows, load):
    steps = len(own_rows)
    groups, depth, hidden = up.shape
    count = steps * own_rows[0].shape[0]
    blocks = (struct((count, hidden // mp)),) * mp if load else (struct((count, hidden)),)
    kept = (VMEM(up.shape, up.dtype),) * load
    place = FAR if load else WHOLE
    sems = [pltpu.SemaphoreType.DMA((steps,)), pltpu.SemaphoreType.DMA((groups,))]
    return pl.pallas_call(
        functools.partial(score_kernel, steps, load, mp),
        out_shape=blocks + kept,
        in_specs=[WHOLE] + [place] * (1 + 2 * steps),
        out_specs=(WHOLE,) * (len(blocks) + len(kept)),
        scratch_shapes=[VMEM((count, depth), jnp.bfloat16), VMEM((count, hidden), jnp.float32)] + sems * load,
        compiler_params=pltpu.CompilerParams(vmem_limit_bytes=16 << 20),
        cost_estimate=SMALL,
        name="score",
    )(notes, *(map(far, (up, *own_rows, *peer_rows)) if load else (up, *own_rows, *peer_rows)))


def scores_of(notes, scale, parts, factors):
    rows = notes.shape[0]
    shard = notes[:, SHARD : SHARD + 1].astype(jnp.int32)
    gain = jnp.zeros((rows, scale.shape[1]), jnp.float32)
    for r in range(scale.shape[0]):
        gain = gain + jnp.where(shard == r, scale[r : r + 1, :], 0.0)
    values = []
    for t, factor in enumerate(factors):
        z = paired_sum([part[t * rows : (t + 1) * rows, :].astype(jnp.float32) for part in parts]) * factor
        values.append(jnp.sum(z * jax.nn.sigmoid(z) * gain, -1, keepdims=True))
    return values


def finish_kernel(steps, notes, scale, *refs):
    norms, parts, out = refs[:steps], refs[steps:-1], refs[-1]
    lane = lax.broadcasted_iota(jnp.int32, out.shape, 1)
    total = jnp.zeros(out.shape, jnp.float32)
    for t, value in enumerate(scores_of(notes, scale, parts, [norm[:, :1] for norm in norms])):
        total = jnp.where(lane == t, value, total)
    out[...] = total


def finish(notes, scale, norms, parts):
    return pl.pallas_call(
        functools.partial(finish_kernel, len(norms)),
        out_shape=struct((notes.shape[0], 128), jnp.float32),
        in_specs=[WHOLE] * (2 + len(norms) + len(parts)),
        out_specs=WHOLE,
        compiler_params=pltpu.CompilerParams(vmem_limit_bytes=12 << 20),
        cost_estimate=SMALL,
        name="finish",
    )(notes, scale, *norms, *parts)


def place_kernel(groups, cap, mp, notes, own_row, peer_row, *refs):
    befores, scales, parts, table = refs[:mp], refs[mp : 2 * mp], refs[2 * mp : 3 * mp], refs[3 * mp]
    rows = notes.shape[0]
    _, _, me = coordinates()
    before = paired_sum([x[...] for x in befores])
    values = [before[:, t : t + 1] for t in range(STEPS - 1)]
    scale = [sum(jnp.where((me ^ j) == m, scales[j][...], 0.0) for j in range(mp)) for m in range(mp)]
    low, high = own_row[...].astype(jnp.float32), peer_row[...].astype(jnp.float32)
    squares = jnp.sum(low * low, -1, keepdims=True) + jnp.sum(high * high, -1, keepdims=True)
    values += scores_of(notes, jnp.concatenate(scale, 1), parts, [lax.rsqrt(squares / D + 1e-06)])
    number = lambda lane: notes[:, lane : lane + 1].astype(jnp.int32)
    shard, at = number(SHARD), number(SOURCE) * cap + number(RANK)
    live = notes[:, LIVE : LIVE + 1] > 0.5
    column = lax.broadcasted_iota(jnp.int32, (rows, table.shape[1]), 1)
    for r in range(groups):
        spots = (column == at) & (shard == r) & live
        for t, value in enumerate(values):
            table[r * STEPS + t : r * STEPS + t + 1, :] = jnp.sum(jnp.where(spots, value, 0.0), 0, keepdims=True)


def place(groups, cap, notes, own_row, peer_row, befores, scales, parts):
    mp = len(parts)
    return pl.pallas_call(
        functools.partial(place_kernel, groups, cap, mp),
        out_shape=struct((groups * STEPS, -(-groups * cap // 128) * 128), jnp.float32),
        in_specs=[WHOLE] * (3 + 3 * mp),
        out_specs=WHOLE,
        compiler_params=pltpu.CompilerParams(vmem_limit_bytes=12 << 20),
        cost_estimate=SMALL,
        name="place",
    )(notes, own_row, peer_row, *befores, *scales, *parts)


def shards(
    tokens,
    parent_keys,
    parent_values,
    parent_blocks,
    child_parent,
    child_count,
    node_shard,
    attn_gain,
    w_query,
    w_key,
    w_value,
    w_out,
    reward_up,
    reward_out,
):
    groups, mp = lax.axis_size("dp"), lax.axis_size("mp")
    children, width = tokens.shape
    parents, prefix, kv_cols = parent_keys.shape
    capacity = max(2, 2 * children // groups)
    reward_cap = max(2, 3 * children // (2 * groups))
    slots = groups * capacity
    rows = min(slots, 3 * children // 2)
    hidden = reward_out.shape[1] // mp
    pairs = lambda count, k: [(i, i ^ k) for i in range(count)]
    swap = pairs(mp, 1)

    up = lax.all_gather(reward_up[0], "dp", axis=0, axis_index_groups=[ring_order(groups)])

    blocks = dispatch(parents, child_count, child_parent, node_shard, tokens, reward_out, groups, capacity, hidden)
    keys = parent_keys.reshape(parents * prefix, kv_cols)
    values = parent_values.reshape(parents * prefix, kv_cols)
    raw = (w_query, w_key, w_value, keys, values, w_out)
    blocks, raw = lax.optimization_barrier((blocks, raw))
    blocks = [blocks[0]] + [lax.ppermute(blocks[k], "dp", pairs(groups, k)) for k in range(1, groups)]
    blocks, weights = lax.optimization_barrier((blocks, load(*raw)))
    gain = attn_gain.reshape(1, width)

    def run(offset, weights, blocks, up, gain, child_parent, parent_blocks):
        row_own, notes, bias, scale, over = pack(
            offset, rows, hidden, prefix, parent_blocks, child_parent, blocks
        )
        w_query, w_key, w_value, keys, values, w_out = [held(w) for w in weights]
        state = row_own.astype(jnp.float32)
        row_peer = lax.ppermute(row_own, "mp", swap)
        past_keys, past_values, rows_own, rows_peer, norms = [], [], [], [], []

        def products(first, last, up, load):
            sums = score(mp, notes, up, rows_own[first:last], rows_peer[first:last], load)
            count = mp if load else 1
            return list(sums[:count]), held(sums[-1]) if load else None

        send = lambda sums: [sums[0]] + [lax.ppermute(sums[k], "mp", pairs(mp, k)) for k in range(1, mp)]
        scales = send([scale] * mp)
        for step in range(STEPS):
            part, attn, key_now, value_now, norm = expand(
                step, row_own, row_peer, begin(row_own, gain, w_query, w_key, w_value), gain, w_query, w_key, w_value, keys, values, bias, w_out,
                past_keys, past_values,
            )
            norms.append(norm)
            past_keys.append(key_now)
            past_values.append(value_now)
            from_peer = lax.ppermute(part, "mp", swap)
            chip = project_own(rows, attn, w_out) + from_peer.astype(jnp.float32)
            sent = chip.astype(jnp.bfloat16)
            others = [sent] + [lax.ppermute(sent, "mp", pairs(mp, k)) for k in range(2, mp, 2)]
            if step == 0:
                others, scales = lax.optimization_barrier((others, scales))
            if step + 1 == STEPS:
                _, up = lax.optimization_barrier((sent, up))
                before, up = products(0, step, up, True)
                others, before = lax.optimization_barrier((others, before))
            state = state + paired_sum([other.astype(jnp.float32) for other in others])
            row_own = state.astype(jnp.bfloat16)
            row_peer = lax.ppermute(row_own, "mp", swap)
            rows_own.append(row_own)
            rows_peer.append(row_peer)
        before = send(before)
        last, _ = products(step, STEPS, up, False)
        last, over = lax.optimization_barrier((send(last * mp), over[0, 0]))
        before = send([finish(notes, scale, norms[1:], before)] * mp)
        return place(groups, reward_cap, notes, row_own, row_peer, before, scales, last), over

    operands = (blocks, up, gain, child_parent, parent_blocks)
    table, over = run(0, weights, *operands)
    if rows < slots:
        table, raw, operands = lax.optimization_barrier((table, raw, operands))
        again = lambda table, raw, operands: table + run(rows, load(*raw), *operands)[0]
        table = lax.cond(over > 0, again, lambda table, raw, operands: table, table, raw, operands)

    table = lax.all_to_all(table, "dp", split_axis=0, concat_axis=0, tiled=True)
    return jnp.sum(table.reshape(groups, STEPS, -1), 0)[:, : groups * reward_cap]


def solution(mesh):
    placed = (
        P("dp", None),
        P("dp", None, "mp"),
        P("dp", None, "mp"),
        P(),
        P(),
        P("dp"),
        P(),
        P(),
        P(None, "mp"),
        P(None, "mp"),
        P(None, "mp"),
        P("mp", None),
        P("dp", "mp", None),
        P("dp", None),
    )
    return jax.shard_map(
        shards, mesh=mesh, in_specs=placed, out_specs=P(None, "dp"), check_vma=False
    )
```

```python
import functools
import math

import jax
import jax.numpy as jnp
from jax import lax
from jax.experimental import pallas as pl
from jax.experimental.pallas import tpu as pltpu
from jax.sharding import PartitionSpec as P

D = 5120
HEADS = 24
KVH = 8
HD = 128
STEPS = 8
GROUP = HEADS // KVH
CHUNK = 512
COLUMNS = 256
ROWS = 64
MASKED = -1e30
EXPONENT = HD ** (-0.5) * math.log2(math.e)
VMEM = pltpu.VMEM
NOTES = 128
LIVE, RANK, SHARD, PARENT, SOURCE, COUNT = range(6)


def dot(a, b):
    return jnp.dot(a, b, preferred_element_type=jnp.float32)


def held(x):
    return pltpu.with_memory_space_constraint(x, VMEM)


def far(x):
    return pltpu.with_memory_space_constraint(x, pltpu.HBM)


def struct(shape, dtype=jnp.bfloat16):
    return jax.ShapeDtypeStruct(shape, dtype)


WHOLE = pl.BlockSpec(memory_space=VMEM)
FAR = pl.BlockSpec(memory_space=pltpu.HBM)
SMALL = pl.CostEstimate(flops=0, bytes_accessed=0, transcendentals=0)
SCALARS = pl.BlockSpec(memory_space=pltpu.SMEM)


def paired_sum(parts):
    while len(parts) > 1:
        parts = [a + b for a, b in zip(parts[::2], parts[1::2])]
    return parts[0]


def ring_order(groups):
    return list(range(0, groups, 2)) + list(range(groups - 1, 0, -2))


def coordinates():
    me = lax.axis_index("mp")
    return lax.rem(me, 2), lax.axis_index("dp"), me


def dispatch_kernel(parents, groups, count, parent_far, shard_far, tokens_far, reward_far, *rest):
    core, own, me = coordinates()
    blocks, near = rest[:groups], rest[groups:]
    parent_row, shard_row, tokens, reward_out, sems = near
    children, half = tokens.shape
    sources = (parent_far, shard_far, tokens_far.at[:, pl.ds(pl.multiple_of(core * half, half), half)], reward_far)
    copies = [pltpu.make_async_copy(a, b, sems.at[i]) for i, (a, b) in enumerate(zip(sources, near))]
    for copy in copies:
        copy.start()
    for copy in copies:
        copy.wait()
    capacity = blocks[0].shape[0]
    everyone = parent_row.shape[1]
    int32, float32, bfloat16 = jnp.int32, jnp.float32, jnp.bfloat16

    mine = lax.broadcasted_iota(int32, (everyone, children), 0) - own * children
    mine = (mine == lax.broadcasted_iota(int32, (everyone, children), 1)).astype(float32).astype(bfloat16)

    def row_and_column(table):
        table = table[...].astype(float32).astype(bfloat16)
        column = lax.dot_general(mine, table, (((0,), (1,)), ((), ())), preferred_element_type=float32)
        return dot(table, mine).astype(int32), column.astype(int32)

    parent, parent_c = row_and_column(parent_row)
    shard, shard_c = row_and_column(shard_row)
    source, source_c = lax.div(parent, parents), lax.div(parent_c, parents)
    first = lax.broadcasted_iota(int32, (children, children), 0)
    second = lax.broadcasted_iota(int32, (children, children), 1)
    live = lax.broadcasted_iota(int32, (1, children), 1) < count[0]
    live_c = lax.broadcasted_iota(int32, (children, 1), 0) < count[0]
    rank = jnp.sum(jnp.where((source_c == source) & (first < second) & live_c, 1, 0), 0, keepdims=True)
    slot = (source ^ own) * capacity + rank
    slot = jnp.where(live, slot, -1)
    reward_rank = jnp.sum(jnp.where((shard_c == shard) & (second < first) & live, 1, 0), 1, keepdims=True)
    lane = lax.broadcasted_iota(int32, (children, NOTES), 1)
    notes = jnp.where(lane == LIVE, live_c.astype(int32), 0)
    for at, value in ((RANK, reward_rank), (SHARD, shard_c), (PARENT, lax.rem(parent_c, parents)), (SOURCE, own)):
        notes = jnp.where(lane == at, value, notes)

    width = blocks[0].shape[1] - half - NOTES
    hidden = width // 3
    rest = jnp.zeros((1, hidden), float32)
    for m in range(reward_out.shape[1] // hidden):
        rest = rest + jnp.where(me == m, reward_out[:, m * hidden : (m + 1) * hidden], 0.0)
    parts = []
    for _ in range(3):
        parts.append(rest.astype(bfloat16).astype(float32))
        rest = rest - parts[-1]
    shared = jnp.broadcast_to(jnp.concatenate(parts, 1), (capacity, width))

    rows = lax.broadcasted_iota(int32, (groups * capacity, children), 0)
    put = (rows == slot).astype(float32).astype(bfloat16)
    token_rows = dot(put, tokens[...])
    note_rows = dot(put, notes.astype(float32).astype(bfloat16))
    row = lax.broadcasted_iota(int32, note_rows.shape, 0)
    lane = lax.broadcasted_iota(int32, note_rows.shape, 1)
    note_rows = jnp.where((lax.rem(row, capacity) == 0) & (lane == COUNT), count[0].astype(float32), note_rows)
    for k, block in enumerate(blocks):
        at = slice(k * capacity, (k + 1) * capacity)
        block[...] = jnp.concatenate([token_rows[at], note_rows[at], shared], 1).astype(bfloat16)


def dispatch(parents, child_count, child_parent, node_shard, tokens, reward_out, groups, capacity, hidden):
    children, half = tokens.shape[0], tokens.shape[1] // 2
    tables = (child_parent[None], node_shard[None])
    return pl.pallas_call(
        functools.partial(dispatch_kernel, parents, groups),
        out_shape=(struct((capacity, half + NOTES + 3 * hidden)),) * groups,
        in_specs=[SCALARS] + [FAR] * 4,
        out_specs=(WHOLE,) * groups,
        scratch_shapes=[VMEM(x.shape, x.dtype) for x in tables]
        + [VMEM((children, half), tokens.dtype), VMEM(reward_out.shape, reward_out.dtype)]
        + [pltpu.SemaphoreType.DMA((4,))],
        compiler_params=pltpu.CompilerParams(vmem_limit_bytes=8 << 20),
        cost_estimate=SMALL,
        name="dispatch",
    )(child_count, *map(far, (*tables, tokens, reward_out)))


def crossing_first(groups):
    return sorted(range(groups), key=lambda k: -(k ^ (k & 1)))


def pack_kernel(offset, hidden, prefix, blocks_held, parent_row, *rest):
    blocks, (row, notes, bias, scale, over) = rest[:-5], rest[-5:]
    blocks = [block for _, block in sorted(zip(crossing_first(len(blocks)), blocks), key=lambda pair: pair[0])]
    _, own, _ = coordinates()
    groups, capacity = len(blocks), blocks[0].shape[0]
    rows, half = row.shape
    slots = groups * capacity
    arrived = jnp.concatenate([block[...].astype(jnp.float32) for block in blocks], 0)
    live = arrived[:, half + LIVE : half + LIVE + 1]
    first = lax.broadcasted_iota(jnp.int32, (slots, slots), 0)
    second = lax.broadcasted_iota(jnp.int32, (slots, slots), 1)
    place = jnp.sum(jnp.where(first < second, live, 0.0), 0, keepdims=True)
    kept = jnp.sum(jnp.where(first == second, live, 0.0), 0, keepdims=True) > 0.5
    wanted = lax.broadcasted_iota(jnp.int32, (rows, slots), 0) + offset
    take = (wanted == place.astype(jnp.int32)) & kept
    take = take.astype(jnp.float32).astype(jnp.bfloat16)
    row[...] = dot(take, arrived[:, :half].astype(jnp.bfloat16)).astype(jnp.bfloat16)
    note = dot(take, arrived[:, half : half + NOTES].astype(jnp.bfloat16))
    notes[...] = note
    parent = note[:, PARENT : PARENT + 1].astype(jnp.int32)
    parents = bias.shape[1] // prefix
    position = lax.broadcasted_iota(jnp.int32, (rows, prefix), 1)
    for p in range(parents):
        usable = (parent == p) & (position < blocks_held[own * parents + p] * 128)
        bias[:, p * prefix : (p + 1) * prefix] = jnp.where(usable, 0.0, MASKED)
    base = half + NOTES
    child = lax.broadcasted_iota(jnp.int32, parent_row.shape, 1)
    children = parent_row.shape[1] // groups
    at, child = lax.div(child, children), lax.rem(child, children)
    count = jnp.zeros(parent_row.shape, jnp.float32)
    for k in range(groups):
        first_row = arrived[k * capacity : k * capacity + 1]
        head = first_row[:, base:]
        scale[pl.ds(own ^ k, 1), :] = head[:, :hidden] + head[:, hidden : 2 * hidden] + head[:, 2 * hidden : 3 * hidden]
        count = jnp.where(at == (own ^ k), first_row[:, half + COUNT : half + COUNT + 1], count)
    source = lax.div(parent_row[...], parents)
    going = child < count.astype(jnp.int32)
    most = jnp.zeros((1, 1), jnp.float32)
    for d in range(groups):
        load = jnp.sum(jnp.where((source == d) & going, 1.0, 0.0), 1, keepdims=True)
        most = jnp.maximum(most, load)
    over[...] = jnp.broadcast_to((most > rows).astype(jnp.int32), over.shape)


def pack(offset, rows, hidden, prefix, blocks_held, child_parent, blocks):
    half = D // 2
    groups = len(blocks)
    parents = blocks_held.shape[0] // groups
    return pl.pallas_call(
        functools.partial(pack_kernel, offset, hidden, prefix),
        out_shape=(
            struct((rows, half)),
            struct((rows, NOTES), jnp.float32),
            struct((rows, parents * prefix), jnp.float32),
            struct((groups, hidden), jnp.float32),
            struct((8, 128), jnp.int32),
        ),
        in_specs=[SCALARS] + [WHOLE] * (1 + groups),
        out_specs=[WHOLE] * 5,
        compiler_params=pltpu.CompilerParams(vmem_limit_bytes=12 << 20),
        cost_estimate=SMALL,
        name="pack",
    )(blocks_held, child_parent[None], *[blocks[k] for k in crossing_first(groups)])


def load_kernel(*refs):
    count = (len(refs) - 1) // 2
    copies = [pltpu.make_async_copy(refs[i], refs[count + i], refs[-1].at[i]) for i in range(count)]
    for copy in copies:
        copy.start()
    for copy in copies:
        copy.wait()


def load(*arrays):
    count = len(arrays)
    return pl.pallas_call(
        load_kernel,
        out_shape=tuple(VMEM(x.shape, x.dtype) for x in arrays),
        in_specs=[FAR] * count,
        out_specs=(WHOLE,) * count,
        scratch_shapes=[pltpu.SemaphoreType.DMA((count,))],
        compiler_params=pltpu.CompilerParams(vmem_limit_bytes=2 << 20),
        cost_estimate=pl.CostEstimate(flops=0, bytes_accessed=24 << 20, transcendentals=0),
        name="load",
    )(*map(far, arrays))


def project(attn, w_out, out, first):
    width = out.shape[1]

    @pl.loop(0, width // CHUNK)
    def _(i):
        columns = pl.ds(pl.multiple_of(first + i * CHUNK, CHUNK), CHUNK)
        out[:, pl.ds(pl.multiple_of(i * CHUNK, CHUNK), CHUNK)] = dot(
            attn[...], w_out[:, columns]
        )[: out.shape[0]].astype(out.dtype)


def products_of(row, first, half, gain, weights, normed):
    at = pl.ds(pl.multiple_of(first, half), half)
    slots = row.shape[0]
    normed[:slots, :] = (row[...].astype(jnp.float32) * gain[:, at]).astype(jnp.bfloat16)
    if normed.shape[0] > slots:
        normed[slots:, :] = jnp.zeros((normed.shape[0] - slots, half), jnp.bfloat16)
    column = 0
    for w in weights:
        for start in range(0, w.shape[1], COLUMNS):
            end = min(start + COLUMNS, w.shape[1])
            yield slice(column + start, column + end), dot(normed[...], w[at, start:end])[:slots]
        column += w.shape[1]


def begin_kernel(own, gain, w_query, w_key, w_value, out, normed):
    core, _, _ = coordinates()
    half = own.shape[1]
    for columns, value in products_of(own, core * half, half, gain, (w_query, w_key, w_value), normed):
        out[:, columns] = value


def begin(own, gain, w_query, w_key, w_value):
    slots, half = own.shape
    padded = -(-slots // ROWS) * ROWS
    return pl.pallas_call(
        begin_kernel,
        out_shape=struct((slots, w_query.shape[1] + 2 * w_key.shape[1]), jnp.float32),
        in_specs=[WHOLE] * 5,
        out_specs=WHOLE,
        scratch_shapes=[VMEM((padded, half), jnp.bfloat16)],
        compiler_params=pltpu.CompilerParams(vmem_limit_bytes=8 << 20),
        cost_estimate=SMALL,
        name="begin",
    )(own, gain, w_query, w_key, w_value)


def step_kernel(step, own, peer, begun, gain, w_query, w_key, w_value, keys, values, bias, w_out, *rest):
    past_keys, past_values = rest[:step], rest[step : 2 * step]
    rest = rest[2 * step :]
    half = own.shape[1]
    slots = own.shape[0]
    q_cols, kv_cols = w_query.shape[1], w_key.shape[1]
    kv_heads = kv_cols // HD
    part, attn, key_now, value_now, norm, normed, query = rest
    core, _, _ = coordinates()
    here, there = own[...].astype(jnp.float32), peer[...].astype(jnp.float32)
    squares = jnp.sum(here * here, -1, keepdims=True) + jnp.sum(there * there, -1, keepdims=True)
    factor = lax.rsqrt(squares / D + 1e-06)
    norm[...] = jnp.broadcast_to(factor, norm.shape)
    for columns, value in products_of(peer, (1 - core) * half, half, gain, (w_query, w_key, w_value), normed):
        query[:, columns] = (begun[:, columns] + value) * factor
    key_now[...] = query[:slots, q_cols : q_cols + kv_cols].astype(jnp.bfloat16)
    value_now[...] = query[:slots, q_cols + kv_cols :].astype(jnp.bfloat16)
    recent = slots * (step + 1)
    row = lax.broadcasted_iota(jnp.int32, (GROUP * slots, recent), 0)
    column = lax.broadcasted_iota(jnp.int32, (GROUP * slots, recent), 1)
    same = lax.rem(row, slots) == lax.rem(column, slots)
    for head in range(kv_heads):
        lanes = slice(head * HD, (head + 1) * HD)
        q = jnp.concatenate(
            [query[:slots, (head * GROUP + g) * HD : (head * GROUP + g + 1) * HD] for g in range(GROUP)], 0
        ).astype(jnp.bfloat16)
        k_new = jnp.concatenate([k[:, lanes] for k in past_keys] + [key_now[:, lanes]], 0)
        v_new = jnp.concatenate([v[:, lanes] for v in past_values] + [value_now[:, lanes]], 0)
        contract = (((1,), (1,)), ((), ()))
        s_old = lax.dot_general(q, keys[:, lanes], contract, preferred_element_type=jnp.float32)
        s_old = s_old + jnp.concatenate([bias[...]] * GROUP, 0)
        s_new = lax.dot_general(q, k_new, contract, preferred_element_type=jnp.float32)
        s_new = jnp.where(same, s_new, MASKED)
        top = jnp.maximum(jnp.max(s_old, -1, keepdims=True), jnp.max(s_new, -1, keepdims=True))
        p_old = jnp.exp2(s_old * EXPONENT - top * EXPONENT)
        p_new = jnp.exp2(s_new * EXPONENT - top * EXPONENT)
        total = jnp.sum(p_old, -1, keepdims=True) + jnp.sum(p_new, -1, keepdims=True)
        summed = dot(p_old.astype(jnp.bfloat16), values[:, lanes]) + dot(p_new.astype(jnp.bfloat16), v_new)
        result = (summed / total).astype(jnp.bfloat16)
        for g in range(GROUP):
            at = (head * GROUP + g) * HD
            attn[:slots, at : at + HD] = result[g * slots : (g + 1) * slots]
    if attn.shape[0] > slots:
        attn[slots:, :] = jnp.zeros((attn.shape[0] - slots, q_cols), jnp.bfloat16)
    project(attn, w_out, part, (1 - core) * half)


def expand(step, own, peer, begun, gain, w_query, w_key, w_value, keys, values, bias, w_out, past_keys, past_values):
    slots, half = own.shape
    kv_cols = w_key.shape[1]
    q_cols = w_query.shape[1]
    padded = -(-slots // ROWS) * ROWS
    return pl.pallas_call(
        functools.partial(step_kernel, step),
        out_shape=(
            struct((slots, half)), struct((padded, q_cols)), struct((slots, kv_cols)), struct((slots, kv_cols)),
            struct((slots, 128), jnp.float32),
        ),
        in_specs=[WHOLE] * (11 + 2 * step),
        out_specs=[WHOLE] * 5,
        scratch_shapes=[VMEM((padded, half), jnp.bfloat16), VMEM((slots, q_cols + 2 * kv_cols), jnp.float32)],
        compiler_params=pltpu.CompilerParams(vmem_limit_bytes=16 << 20),
        cost_estimate=SMALL,
        name="expand",
    )(own, peer, begun, gain, w_query, w_key, w_value, keys, values, bias, w_out, *past_keys, *past_values)


def project_kernel(attn, w_out, part):
    core, _, _ = coordinates()
    project(attn, w_out, part, core * part.shape[1])


def project_own(rows, attn, w_out):
    return pl.pallas_call(
        project_kernel,
        out_shape=struct((rows, w_out.shape[1] // 2), jnp.float32),
        in_specs=[WHOLE, WHOLE],
        out_specs=WHOLE,
        compiler_params=pltpu.CompilerParams(vmem_limit_bytes=8 << 20),
        cost_estimate=SMALL,
        name="project_own",
    )(attn, w_out)


def score_kernel(steps, load, mp, notes, up, *refs):
    take = lambda count: [refs.pop(0) for _ in range(count)]
    refs = list(refs)
    own_rows, peer_rows, blocks, kept = take(steps), take(steps), take(mp if load else 1), take(1 * load)
    flat, total, *sems = refs
    groups, depth, hidden = up.shape
    rows = own_rows[0].shape[0]
    core, _, me = coordinates()
    for t in range(steps):
        target = flat.at[t * rows : (t + 1) * rows]
        for m in range(mp):
            at = m % (mp // 2) * depth
            for c in range(2):
                source = (own_rows if m // (mp // 2) == c else peer_rows)[t].at[:, at : at + depth]

                @pl.when((me == m) & (core == c))
                def _():
                    if load:
                        pltpu.make_async_copy(source, target, sems[0].at[t]).start()
                    else:
                        target[...] = source[...]

    if load:
        order = ring_order(groups)
        fetch = lambda r: pltpu.make_async_copy(arrived.at[order.index(r)], kept[0].at[r], sems[1].at[r])
        arrived, up = up, kept[0]
        for r in range(3):
            fetch(r).start()
        for t in range(steps):
            target = flat.at[t * rows : (t + 1) * rows]
            pltpu.make_async_copy(target, target, sems[0].at[t]).wait()
    shard = jnp.concatenate([notes[:, SHARD : SHARD + 1].astype(jnp.int32)] * steps, 0)
    for r in range(groups):
        if load:
            fetch(r).wait()
            if r + 3 < groups:
                fetch(r + 3).start()
        for at in range(0, hidden, COLUMNS):
            end = min(at + COLUMNS, hidden)
            here = jnp.where(shard == r, dot(flat[...], up[r, :, at:end]), 0.0)
            total[:, at:end] = here if r == 0 else total[:, at:end] + here
    if not load:
        blocks[0][...] = total[...].astype(jnp.bfloat16)
        return
    width = hidden // mp
    for j, block in enumerate(blocks):
        for m in range(mp):

            @pl.when((me ^ j) == m)
            def _():
                block[...] = total[:, m * width : (m + 1) * width].astype(jnp.bfloat16)


def score(mp, notes, up, own_rows, peer_rows, load):
    steps = len(own_rows)
    groups, depth, hidden = up.shape
    count = steps * own_rows[0].shape[0]
    blocks = (struct((count, hidden // mp)),) * mp if load else (struct((count, hidden)),)
    kept = (VMEM(up.shape, up.dtype),) * load
    place = FAR if load else WHOLE
    sems = [pltpu.SemaphoreType.DMA((steps,)), pltpu.SemaphoreType.DMA((groups,))]
    return pl.pallas_call(
        functools.partial(score_kernel, steps, load, mp),
        out_shape=blocks + kept,
        in_specs=[WHOLE] + [place] * (1 + 2 * steps),
        out_specs=(WHOLE,) * (len(blocks) + len(kept)),
        scratch_shapes=[VMEM((count, depth), jnp.bfloat16), VMEM((count, hidden), jnp.float32)] + sems * load,
        compiler_params=pltpu.CompilerParams(vmem_limit_bytes=16 << 20),
        cost_estimate=SMALL,
        name="score",
    )(notes, *(map(far, (up, *own_rows, *peer_rows)) if load else (up, *own_rows, *peer_rows)))


def scores_of(notes, scale, parts, factors):
    rows = notes.shape[0]
    shard = notes[:, SHARD : SHARD + 1].astype(jnp.int32)
    gain = jnp.zeros((rows, scale.shape[1]), jnp.float32)
    for r in range(scale.shape[0]):
        gain = gain + jnp.where(shard == r, scale[r : r + 1, :], 0.0)
    values = []
    for t, factor in enumerate(factors):
        z = paired_sum([part[t * rows : (t + 1) * rows, :].astype(jnp.float32) for part in parts]) * factor
        values.append(jnp.sum(z * jax.nn.sigmoid(z) * gain, -1, keepdims=True))
    return values


def finish_kernel(steps, notes, scale, *refs):
    norms, parts, out = refs[:steps], refs[steps:-1], refs[-1]
    lane = lax.broadcasted_iota(jnp.int32, out.shape, 1)
    total = jnp.zeros(out.shape, jnp.float32)
    for t, value in enumerate(scores_of(notes, scale, parts, [norm[:, :1] for norm in norms])):
        total = jnp.where(lane == t, value, total)
    out[...] = total


def finish(notes, scale, norms, parts):
    return pl.pallas_call(
        functools.partial(finish_kernel, len(norms)),
        out_shape=struct((notes.shape[0], 128), jnp.float32),
        in_specs=[WHOLE] * (2 + len(norms) + len(parts)),
        out_specs=WHOLE,
        compiler_params=pltpu.CompilerParams(vmem_limit_bytes=12 << 20),
        cost_estimate=SMALL,
        name="finish",
    )(notes, scale, *norms, *parts)


def place_kernel(groups, cap, mp, notes, own_row, peer_row, *refs):
    befores, scales, parts, table = refs[:mp], refs[mp : 2 * mp], refs[2 * mp : 3 * mp], refs[3 * mp]
    rows = notes.shape[0]
    _, _, me = coordinates()
    before = paired_sum([x[...] for x in befores])
    values = [before[:, t : t + 1] for t in range(STEPS - 1)]
    scale = [sum(jnp.where((me ^ j) == m, scales[j][...], 0.0) for j in range(mp)) for m in range(mp)]
    low, high = own_row[...].astype(jnp.float32), peer_row[...].astype(jnp.float32)
    squares = jnp.sum(low * low, -1, keepdims=True) + jnp.sum(high * high, -1, keepdims=True)
    values += scores_of(notes, jnp.concatenate(scale, 1), parts, [lax.rsqrt(squares / D + 1e-06)])
    number = lambda lane: notes[:, lane : lane + 1].astype(jnp.int32)
    shard, at = number(SHARD), number(SOURCE) * cap + number(RANK)
    live = notes[:, LIVE : LIVE + 1] > 0.5
    column = lax.broadcasted_iota(jnp.int32, (rows, table.shape[1]), 1)
    for r in range(groups):
        spots = (column == at) & (shard == r) & live
        for t, value in enumerate(values):
            table[r * STEPS + t : r * STEPS + t + 1, :] = jnp.sum(jnp.where(spots, value, 0.0), 0, keepdims=True)


def place(groups, cap, notes, own_row, peer_row, befores, scales, parts):
    mp = len(parts)
    return pl.pallas_call(
        functools.partial(place_kernel, groups, cap, mp),
        out_shape=struct((groups * STEPS, -(-groups * cap // 128) * 128), jnp.float32),
        in_specs=[WHOLE] * (3 + 3 * mp),
        out_specs=WHOLE,
        compiler_params=pltpu.CompilerParams(vmem_limit_bytes=12 << 20),
        cost_estimate=SMALL,
        name="place",
    )(notes, own_row, peer_row, *befores, *scales, *parts)


def shards(
    tokens,
    parent_keys,
    parent_values,
    parent_blocks,
    child_parent,
    child_count,
    node_shard,
    attn_gain,
    w_query,
    w_key,
    w_value,
    w_out,
    reward_up,
    reward_out,
):
    groups, mp = lax.axis_size("dp"), lax.axis_size("mp")
    children, width = tokens.shape
    parents, prefix, kv_cols = parent_keys.shape
    capacity = max(2, 2 * children // groups)
    reward_cap = max(2, 3 * children // (2 * groups))
    slots = groups * capacity
    rows = min(slots, 3 * children // 2)
    hidden = reward_out.shape[1] // mp
    pairs = lambda count, k: [(i, i ^ k) for i in range(count)]
    swap = pairs(mp, 1)

    up = lax.all_gather(reward_up[0], "dp", axis=0, axis_index_groups=[ring_order(groups)])

    blocks = dispatch(parents, child_count, child_parent, node_shard, tokens, reward_out, groups, capacity, hidden)
    keys = parent_keys.reshape(parents * prefix, kv_cols)
    values = parent_values.reshape(parents * prefix, kv_cols)
    raw = (w_query, w_key, w_value, keys, values, w_out)
    blocks, raw = lax.optimization_barrier((blocks, raw))
    blocks = [blocks[0]] + [lax.ppermute(blocks[k], "dp", pairs(groups, k)) for k in range(1, groups)]
    blocks, weights = lax.optimization_barrier((blocks, load(*raw)))
    gain = attn_gain.reshape(1, width)

    def run(offset, weights, blocks, up, gain, child_parent, parent_blocks):
        row_own, notes, bias, scale, over = pack(
            offset, rows, hidden, prefix, parent_blocks, child_parent, blocks
        )
        w_query, w_key, w_value, keys, values, w_out = [held(w) for w in weights]
        state = row_own.astype(jnp.float32)
        row_peer = lax.ppermute(row_own, "mp", swap)
        past_keys, past_values, rows_own, rows_peer, norms = [], [], [], [], []

        def products(first, last, up, load):
            sums = score(mp, notes, up, rows_own[first:last], rows_peer[first:last], load)
            count = mp if load else 1
            return list(sums[:count]), held(sums[-1]) if load else None

        send = lambda sums: [sums[0]] + [lax.ppermute(sums[k], "mp", pairs(mp, k)) for k in range(1, mp)]
        scales = send([scale] * mp)
        for step in range(STEPS):
            part, attn, key_now, value_now, norm = expand(
                step, row_own, row_peer, begin(row_own, gain, w_query, w_key, w_value), gain, w_query, w_key, w_value, keys, values, bias, w_out,
                past_keys, past_values,
            )
            norms.append(norm)
            past_keys.append(key_now)
            past_values.append(value_now)
            from_peer = lax.ppermute(part, "mp", swap)
            chip = project_own(rows, attn, w_out) + from_peer.astype(jnp.float32)
            sent = chip.astype(jnp.bfloat16)
            others = [sent] + [lax.ppermute(sent, "mp", pairs(mp, k)) for k in range(2, mp, 2)]
            if step == 0:
                others, scales = lax.optimization_barrier((others, scales))
            if step + 1 == STEPS:
                _, up = lax.optimization_barrier((sent, up))
                before, up = products(0, step, up, True)
                others, before = lax.optimization_barrier((others, before))
            state = state + paired_sum([other.astype(jnp.float32) for other in others])
            row_own = state.astype(jnp.bfloat16)
            row_peer = lax.ppermute(row_own, "mp", swap)
            rows_own.append(row_own)
            rows_peer.append(row_peer)
        before = send(before)
        last, _ = products(step, STEPS, up, False)
        last, over = lax.optimization_barrier((send(last * mp), over[0, 0]))
        before = send([finish(notes, scale, norms[1:], before)] * mp)
        return place(groups, reward_cap, notes, row_own, row_peer, before, scales, last), over

    operands = (blocks, up, gain, child_parent, parent_blocks)
    table, over = run(0, weights, *operands)
    if rows < slots:
        table, raw, operands = lax.optimization_barrier((table, raw, operands))
        again = lambda table, raw, operands: table + run(rows, load(*raw), *operands)[0]
        table = lax.cond(over > 0, again, lambda table, raw, operands: table, table, raw, operands)

    table = lax.all_to_all(table, "dp", split_axis=0, concat_axis=0, tiled=True)
    return jnp.sum(table.reshape(groups, STEPS, -1), 0)[:, : groups * reward_cap]


def solution(mesh):
    placed = (
        P("dp", None),
        P("dp", None, "mp"),
        P("dp", None, "mp"),
        P(),
        P(),
        P("dp"),
        P(),
        P(),
        P(None, "mp"),
        P(None, "mp"),
        P(None, "mp"),
        P("mp", None),
        P("dp", "mp", None),
        P("dp", None),
    )
    return jax.shard_map(
        shards, mesh=mesh, in_specs=placed, out_specs=P(None, "dp"), check_vma=False
    )
```

```python
import functools
import math

import jax
import jax.numpy as jnp
from jax import lax
from jax.experimental import pallas as pl
from jax.experimental.pallas import tpu as pltpu
from jax.sharding import PartitionSpec as P

D = 5120
HEADS = 24
KVH = 8
HD = 128
STEPS = 8
GROUP = HEADS // KVH
CHUNK = 512
COLUMNS = 256
ROWS = 64
MASKED = -1e30
EXPONENT = HD ** (-0.5) * math.log2(math.e)
VMEM = pltpu.VMEM
NOTES = 128
LIVE, RANK, SHARD, PARENT, SOURCE, COUNT = range(6)


def dot(a, b):
    return jnp.dot(a, b, preferred_element_type=jnp.float32)


def held(x):
    return pltpu.with_memory_space_constraint(x, VMEM)


def far(x):
    return pltpu.with_memory_space_constraint(x, pltpu.HBM)


def struct(shape, dtype=jnp.bfloat16):
    return jax.ShapeDtypeStruct(shape, dtype)


WHOLE = pl.BlockSpec(memory_space=VMEM)
FAR = pl.BlockSpec(memory_space=pltpu.HBM)
SMALL = pl.CostEstimate(flops=0, bytes_accessed=0, transcendentals=0)
SCALARS = pl.BlockSpec(memory_space=pltpu.SMEM)


def paired_sum(parts):
    while len(parts) > 1:
        parts = [a + b for a, b in zip(parts[::2], parts[1::2])]
    return parts[0]


def ring_order(groups):
    return list(range(0, groups, 2)) + list(range(groups - 1, 0, -2))


def coordinates():
    me = lax.axis_index("mp")
    return lax.rem(me, 2), lax.axis_index("dp"), me


def dispatch_kernel(parents, groups, count, parent_far, shard_far, tokens_far, reward_far, *rest):
    core, own, me = coordinates()
    stay, cross, near = rest[: groups // 2], rest[groups // 2], rest[groups // 2 + 1 :]
    parent_row, shard_row, tokens, reward_out, sems = near
    children, half = tokens.shape
    sources = (parent_far, shard_far, tokens_far.at[:, pl.ds(pl.multiple_of(core * half, half), half)], reward_far)
    copies = [pltpu.make_async_copy(a, b, sems.at[i]) for i, (a, b) in enumerate(zip(sources, near))]
    for copy in copies:
        copy.start()
    for copy in copies:
        copy.wait()
    capacity = stay[0].shape[0]
    everyone = parent_row.shape[1]
    int32, float32, bfloat16 = jnp.int32, jnp.float32, jnp.bfloat16

    mine = lax.broadcasted_iota(int32, (everyone, children), 0) - own * children
    mine = (mine == lax.broadcasted_iota(int32, (everyone, children), 1)).astype(float32).astype(bfloat16)

    def row_and_column(table):
        table = table[...].astype(float32).astype(bfloat16)
        column = lax.dot_general(mine, table, (((0,), (1,)), ((), ())), preferred_element_type=float32)
        return dot(table, mine).astype(int32), column.astype(int32)

    parent, parent_c = row_and_column(parent_row)
    shard, shard_c = row_and_column(shard_row)
    source, source_c = lax.div(parent, parents), lax.div(parent_c, parents)
    first = lax.broadcasted_iota(int32, (children, children), 0)
    second = lax.broadcasted_iota(int32, (children, children), 1)
    live = lax.broadcasted_iota(int32, (1, children), 1) < count[0]
    live_c = lax.broadcasted_iota(int32, (children, 1), 0) < count[0]
    rank = jnp.sum(jnp.where((source_c == source) & (first < second) & live_c, 1, 0), 0, keepdims=True)
    slot = (source ^ own) * capacity + rank
    slot = jnp.where(live, slot, -1)
    reward_rank = jnp.sum(jnp.where((shard_c == shard) & (second < first) & live, 1, 0), 1, keepdims=True)
    lane = lax.broadcasted_iota(int32, (children, NOTES), 1)
    notes = jnp.where(lane == LIVE, live_c.astype(int32), 0)
    for at, value in ((RANK, reward_rank), (SHARD, shard_c), (PARENT, lax.rem(parent_c, parents)), (SOURCE, own)):
        notes = jnp.where(lane == at, value, notes)

    width = cross.shape[1] - half - NOTES
    hidden = width // 3
    rest = jnp.zeros((1, hidden), float32)
    for m in range(reward_out.shape[1] // hidden):
        rest = rest + jnp.where(me == m, reward_out[:, m * hidden : (m + 1) * hidden], 0.0)
    parts = []
    for _ in range(3):
        parts.append(rest.astype(bfloat16).astype(float32))
        rest = rest - parts[-1]
    shared = jnp.broadcast_to(jnp.concatenate(parts, 1), (capacity, width))

    rows = lax.broadcasted_iota(int32, (groups * capacity, children), 0)
    put = (rows == slot).astype(float32).astype(bfloat16)
    token_rows = dot(put, tokens[...])
    note_rows = dot(put, notes.astype(float32).astype(bfloat16))
    row = lax.broadcasted_iota(int32, note_rows.shape, 0)
    lane = lax.broadcasted_iota(int32, note_rows.shape, 1)
    note_rows = jnp.where((lax.rem(row, capacity) == 0) & (lane == COUNT), count[0].astype(float32), note_rows)
    every = []
    for k in range(groups):
        at = slice(k * capacity, (k + 1) * capacity)
        every.append(jnp.concatenate([token_rows[at], note_rows[at], shared], 1))
    for j, block in enumerate(stay):
        block[...] = every[2 * j].astype(bfloat16)
    cross[...] = jnp.concatenate(every[1::2], 0).astype(bfloat16)


def dispatch(parents, child_count, child_parent, node_shard, tokens, reward_out, groups, capacity, hidden):
    children, half = tokens.shape[0], tokens.shape[1] // 2
    width = half + NOTES + 3 * hidden
    tables = (child_parent[None], node_shard[None])
    return pl.pallas_call(
        functools.partial(dispatch_kernel, parents, groups),
        out_shape=(struct((capacity, width)),) * (groups // 2) + (struct((groups // 2 * capacity, width)),),
        in_specs=[SCALARS] + [FAR] * 4,
        out_specs=(WHOLE,) * (groups // 2 + 1),
        scratch_shapes=[VMEM(x.shape, x.dtype) for x in tables]
        + [VMEM((children, half), tokens.dtype), VMEM(reward_out.shape, reward_out.dtype)]
        + [pltpu.SemaphoreType.DMA((4,))],
        compiler_params=pltpu.CompilerParams(vmem_limit_bytes=8 << 20),
        cost_estimate=SMALL,
        name="dispatch",
    )(child_count, *map(far, (*tables, tokens, reward_out)))


def regroup_kernel(*refs):
    count = len(refs) // 2
    stay, cross, pairs = refs[:count], refs[count], refs[count + 1 :]
    capacity = stay[0].shape[0]
    for j, (block, pair) in enumerate(zip(stay, pairs)):
        mine = block[...].astype(jnp.float32)
        other = cross[...].astype(jnp.float32)[j * capacity : (j + 1) * capacity]
        pair[...] = jnp.concatenate([mine, other], 0).astype(jnp.bfloat16)


def regroup(stay, cross):
    capacity, width = stay[0].shape
    return pl.pallas_call(
        regroup_kernel,
        out_shape=(struct((2 * capacity, width)),) * len(stay),
        in_specs=[WHOLE] * (len(stay) + 1),
        out_specs=(WHOLE,) * len(stay),
        compiler_params=pltpu.CompilerParams(vmem_limit_bytes=8 << 20),
        cost_estimate=SMALL,
        name="regroup",
    )(*stay, cross)


def crossing_first(groups):
    return sorted(range(groups), key=lambda k: -(k ^ (k & 1)))


def pack_kernel(offset, hidden, prefix, blocks_held, parent_row, *rest):
    blocks, (row, notes, bias, scale, over) = rest[:-5], rest[-5:]
    blocks = [block for _, block in sorted(zip(crossing_first(len(blocks)), blocks), key=lambda pair: pair[0])]
    _, own, _ = coordinates()
    groups, capacity = 2 * len(blocks), blocks[0].shape[0] // 2
    rows, half = row.shape
    slots = groups * capacity
    arrived = jnp.concatenate([block[...].astype(jnp.float32) for block in blocks], 0)
    live = arrived[:, half + LIVE : half + LIVE + 1]
    first = lax.broadcasted_iota(jnp.int32, (slots, slots), 0)
    second = lax.broadcasted_iota(jnp.int32, (slots, slots), 1)
    place = jnp.sum(jnp.where(first < second, live, 0.0), 0, keepdims=True)
    kept = jnp.sum(jnp.where(first == second, live, 0.0), 0, keepdims=True) > 0.5
    wanted = lax.broadcasted_iota(jnp.int32, (rows, slots), 0) + offset
    take = (wanted == place.astype(jnp.int32)) & kept
    take = take.astype(jnp.float32).astype(jnp.bfloat16)
    row[...] = dot(take, arrived[:, :half].astype(jnp.bfloat16)).astype(jnp.bfloat16)
    note = dot(take, arrived[:, half : half + NOTES].astype(jnp.bfloat16))
    notes[...] = note
    parent = note[:, PARENT : PARENT + 1].astype(jnp.int32)
    parents = bias.shape[1] // prefix
    position = lax.broadcasted_iota(jnp.int32, (rows, prefix), 1)
    for p in range(parents):
        usable = (parent == p) & (position < blocks_held[own * parents + p] * 128)
        bias[:, p * prefix : (p + 1) * prefix] = jnp.where(usable, 0.0, MASKED)
    base = half + NOTES
    child = lax.broadcasted_iota(jnp.int32, parent_row.shape, 1)
    children = parent_row.shape[1] // groups
    at, child = lax.div(child, children), lax.rem(child, children)
    count = jnp.zeros(parent_row.shape, jnp.float32)
    for k in range(groups):
        first_row = arrived[k * capacity : k * capacity + 1]
        head = first_row[:, base:]
        scale[pl.ds(own ^ k, 1), :] = head[:, :hidden] + head[:, hidden : 2 * hidden] + head[:, 2 * hidden : 3 * hidden]
        count = jnp.where(at == (own ^ k), first_row[:, half + COUNT : half + COUNT + 1], count)
    source = lax.div(parent_row[...], parents)
    going = child < count.astype(jnp.int32)
    most = jnp.zeros((1, 1), jnp.float32)
    for d in range(groups):
        load = jnp.sum(jnp.where((source == d) & going, 1.0, 0.0), 1, keepdims=True)
        most = jnp.maximum(most, load)
    over[...] = jnp.broadcast_to((most > rows).astype(jnp.int32), over.shape)


def pack(offset, rows, hidden, prefix, blocks_held, child_parent, blocks):
    half = D // 2
    groups = 2 * len(blocks)
    parents = blocks_held.shape[0] // groups
    return pl.pallas_call(
        functools.partial(pack_kernel, offset, hidden, prefix),
        out_shape=(
            struct((rows, half)),
            struct((rows, NOTES), jnp.float32),
            struct((rows, parents * prefix), jnp.float32),
            struct((groups, hidden), jnp.float32),
            struct((8, 128), jnp.int32),
        ),
        in_specs=[SCALARS] + [WHOLE] * (1 + len(blocks)),
        out_specs=[WHOLE] * 5,
        compiler_params=pltpu.CompilerParams(vmem_limit_bytes=12 << 20),
        cost_estimate=SMALL,
        name="pack",
    )(blocks_held, child_parent[None], *[blocks[k] for k in crossing_first(len(blocks))])


def load_kernel(*refs):
    count = (len(refs) - 1) // 2
    copies = [pltpu.make_async_copy(refs[i], refs[count + i], refs[-1].at[i]) for i in range(count)]
    for copy in copies:
        copy.start()
    for copy in copies:
        copy.wait()


def load(*arrays):
    count = len(arrays)
    return pl.pallas_call(
        load_kernel,
        out_shape=tuple(VMEM(x.shape, x.dtype) for x in arrays),
        in_specs=[FAR] * count,
        out_specs=(WHOLE,) * count,
        scratch_shapes=[pltpu.SemaphoreType.DMA((count,))],
        compiler_params=pltpu.CompilerParams(vmem_limit_bytes=2 << 20),
        cost_estimate=pl.CostEstimate(flops=0, bytes_accessed=24 << 20, transcendentals=0),
        name="load",
    )(*map(far, arrays))


def project(attn, w_out, out, first):
    width = out.shape[1]

    @pl.loop(0, width // CHUNK)
    def _(i):
        columns = pl.ds(pl.multiple_of(first + i * CHUNK, CHUNK), CHUNK)
        out[:, pl.ds(pl.multiple_of(i * CHUNK, CHUNK), CHUNK)] = dot(
            attn[...], w_out[:, columns]
        )[: out.shape[0]].astype(out.dtype)


def products_of(row, first, half, gain, weights, normed):
    at = pl.ds(pl.multiple_of(first, half), half)
    slots = row.shape[0]
    normed[:slots, :] = (row[...].astype(jnp.float32) * gain[:, at]).astype(jnp.bfloat16)
    if normed.shape[0] > slots:
        normed[slots:, :] = jnp.zeros((normed.shape[0] - slots, half), jnp.bfloat16)
    column = 0
    for w in weights:
        for start in range(0, w.shape[1], COLUMNS):
            end = min(start + COLUMNS, w.shape[1])
            yield slice(column + start, column + end), dot(normed[...], w[at, start:end])[:slots]
        column += w.shape[1]


def begin_kernel(own, gain, w_query, w_key, w_value, out, normed):
    core, _, _ = coordinates()
    half = own.shape[1]
    for columns, value in products_of(own, core * half, half, gain, (w_query, w_key, w_value), normed):
        out[:, columns] = value


def begin(own, gain, w_query, w_key, w_value):
    slots, half = own.shape
    padded = -(-slots // ROWS) * ROWS
    return pl.pallas_call(
        begin_kernel,
        out_shape=struct((slots, w_query.shape[1] + 2 * w_key.shape[1]), jnp.float32),
        in_specs=[WHOLE] * 5,
        out_specs=WHOLE,
        scratch_shapes=[VMEM((padded, half), jnp.bfloat16)],
        compiler_params=pltpu.CompilerParams(vmem_limit_bytes=8 << 20),
        cost_estimate=SMALL,
        name="begin",
    )(own, gain, w_query, w_key, w_value)


def step_kernel(step, own, peer, begun, gain, w_query, w_key, w_value, keys, values, bias, w_out, *rest):
    past_keys, past_values = rest[:step], rest[step : 2 * step]
    rest = rest[2 * step :]
    half = own.shape[1]
    slots = own.shape[0]
    q_cols, kv_cols = w_query.shape[1], w_key.shape[1]
    kv_heads = kv_cols // HD
    part, attn, key_now, value_now, norm, normed, query = rest
    core, _, _ = coordinates()
    here, there = own[...].astype(jnp.float32), peer[...].astype(jnp.float32)
    squares = jnp.sum(here * here, -1, keepdims=True) + jnp.sum(there * there, -1, keepdims=True)
    factor = lax.rsqrt(squares / D + 1e-06)
    norm[...] = jnp.broadcast_to(factor, norm.shape)
    for columns, value in products_of(peer, (1 - core) * half, half, gain, (w_query, w_key, w_value), normed):
        query[:, columns] = (begun[:, columns] + value) * factor
    key_now[...] = query[:slots, q_cols : q_cols + kv_cols].astype(jnp.bfloat16)
    value_now[...] = query[:slots, q_cols + kv_cols :].astype(jnp.bfloat16)
    recent = slots * (step + 1)
    row = lax.broadcasted_iota(jnp.int32, (GROUP * slots, recent), 0)
    column = lax.broadcasted_iota(jnp.int32, (GROUP * slots, recent), 1)
    same = lax.rem(row, slots) == lax.rem(column, slots)
    for head in range(kv_heads):
        lanes = slice(head * HD, (head + 1) * HD)
        q = jnp.concatenate(
            [query[:slots, (head * GROUP + g) * HD : (head * GROUP + g + 1) * HD] for g in range(GROUP)], 0
        ).astype(jnp.bfloat16)
        k_new = jnp.concatenate([k[:, lanes] for k in past_keys] + [key_now[:, lanes]], 0)
        v_new = jnp.concatenate([v[:, lanes] for v in past_values] + [value_now[:, lanes]], 0)
        contract = (((1,), (1,)), ((), ()))
        s_old = lax.dot_general(q, keys[:, lanes], contract, preferred_element_type=jnp.float32)
        s_old = s_old + jnp.concatenate([bias[...]] * GROUP, 0)
        s_new = lax.dot_general(q, k_new, contract, preferred_element_type=jnp.float32)
        s_new = jnp.where(same, s_new, MASKED)
        top = jnp.maximum(jnp.max(s_old, -1, keepdims=True), jnp.max(s_new, -1, keepdims=True))
        p_old = jnp.exp2(s_old * EXPONENT - top * EXPONENT)
        p_new = jnp.exp2(s_new * EXPONENT - top * EXPONENT)
        total = jnp.sum(p_old, -1, keepdims=True) + jnp.sum(p_new, -1, keepdims=True)
        summed = dot(p_old.astype(jnp.bfloat16), values[:, lanes]) + dot(p_new.astype(jnp.bfloat16), v_new)
        result = (summed / total).astype(jnp.bfloat16)
        for g in range(GROUP):
            at = (head * GROUP + g) * HD
            attn[:slots, at : at + HD] = result[g * slots : (g + 1) * slots]
    if attn.shape[0] > slots:
        attn[slots:, :] = jnp.zeros((attn.shape[0] - slots, q_cols), jnp.bfloat16)
    project(attn, w_out, part, (1 - core) * half)


def expand(step, own, peer, begun, gain, w_query, w_key, w_value, keys, values, bias, w_out, past_keys, past_values):
    slots, half = own.shape
    kv_cols = w_key.shape[1]
    q_cols = w_query.shape[1]
    padded = -(-slots // ROWS) * ROWS
    return pl.pallas_call(
        functools.partial(step_kernel, step),
        out_shape=(
            struct((slots, half)), struct((padded, q_cols)), struct((slots, kv_cols)), struct((slots, kv_cols)),
            struct((slots, 128), jnp.float32),
        ),
        in_specs=[WHOLE] * (11 + 2 * step),
        out_specs=[WHOLE] * 5,
        scratch_shapes=[VMEM((padded, half), jnp.bfloat16), VMEM((slots, q_cols + 2 * kv_cols), jnp.float32)],
        compiler_params=pltpu.CompilerParams(vmem_limit_bytes=16 << 20),
        cost_estimate=SMALL,
        name="expand",
    )(own, peer, begun, gain, w_query, w_key, w_value, keys, values, bias, w_out, *past_keys, *past_values)


def project_kernel(attn, w_out, part):
    core, _, _ = coordinates()
    project(attn, w_out, part, core * part.shape[1])


def project_own(rows, attn, w_out):
    return pl.pallas_call(
        project_kernel,
        out_shape=struct((rows, w_out.shape[1] // 2), jnp.float32),
        in_specs=[WHOLE, WHOLE],
        out_specs=WHOLE,
        compiler_params=pltpu.CompilerParams(vmem_limit_bytes=8 << 20),
        cost_estimate=SMALL,
        name="project_own",
    )(attn, w_out)


def score_kernel(steps, load, mp, notes, up, *refs):
    take = lambda count: [refs.pop(0) for _ in range(count)]
    refs = list(refs)
    own_rows, peer_rows, blocks, kept = take(steps), take(steps), take(mp if load else 1), take(1 * load)
    flat, total, *sems = refs
    groups, depth, hidden = up.shape
    rows = own_rows[0].shape[0]
    core, _, me = coordinates()
    for t in range(steps):
        target = flat.at[t * rows : (t + 1) * rows]
        for m in range(mp):
            at = m % (mp // 2) * depth
            for c in range(2):
                source = (own_rows if m // (mp // 2) == c else peer_rows)[t].at[:, at : at + depth]

                @pl.when((me == m) & (core == c))
                def _():
                    if load:
                        pltpu.make_async_copy(source, target, sems[0].at[t]).start()
                    else:
                        target[...] = source[...]

    if load:
        order = ring_order(groups)
        fetch = lambda r: pltpu.make_async_copy(arrived.at[order.index(r)], kept[0].at[r], sems[1].at[r])
        arrived, up = up, kept[0]
        for r in range(3):
            fetch(r).start()
        for t in range(steps):
            target = flat.at[t * rows : (t + 1) * rows]
            pltpu.make_async_copy(target, target, sems[0].at[t]).wait()
    shard = jnp.concatenate([notes[:, SHARD : SHARD + 1].astype(jnp.int32)] * steps, 0)
    for r in range(groups):
        if load:
            fetch(r).wait()
            if r + 3 < groups:
                fetch(r + 3).start()
        for at in range(0, hidden, COLUMNS):
            end = min(at + COLUMNS, hidden)
            here = jnp.where(shard == r, dot(flat[...], up[r, :, at:end]), 0.0)
            total[:, at:end] = here if r == 0 else total[:, at:end] + here
    if not load:
        blocks[0][...] = total[...].astype(jnp.bfloat16)
        return
    width = hidden // mp
    for j, block in enumerate(blocks):
        for m in range(mp):

            @pl.when((me ^ j) == m)
            def _():
                block[...] = total[:, m * width : (m + 1) * width].astype(jnp.bfloat16)


def score(mp, notes, up, own_rows, peer_rows, load):
    steps = len(own_rows)
    groups, depth, hidden = up.shape
    count = steps * own_rows[0].shape[0]
    blocks = (struct((count, hidden // mp)),) * mp if load else (struct((count, hidden)),)
    kept = (VMEM(up.shape, up.dtype),) * load
    place = FAR if load else WHOLE
    sems = [pltpu.SemaphoreType.DMA((steps,)), pltpu.SemaphoreType.DMA((groups,))]
    return pl.pallas_call(
        functools.partial(score_kernel, steps, load, mp),
        out_shape=blocks + kept,
        in_specs=[WHOLE] + [place] * (1 + 2 * steps),
        out_specs=(WHOLE,) * (len(blocks) + len(kept)),
        scratch_shapes=[VMEM((count, depth), jnp.bfloat16), VMEM((count, hidden), jnp.float32)] + sems * load,
        compiler_params=pltpu.CompilerParams(vmem_limit_bytes=16 << 20),
        cost_estimate=SMALL,
        name="score",
    )(notes, *(map(far, (up, *own_rows, *peer_rows)) if load else (up, *own_rows, *peer_rows)))


def scores_of(notes, scale, parts, factors):
    rows = notes.shape[0]
    shard = notes[:, SHARD : SHARD + 1].astype(jnp.int32)
    gain = jnp.zeros((rows, scale.shape[1]), jnp.float32)
    for r in range(scale.shape[0]):
        gain = gain + jnp.where(shard == r, scale[r : r + 1, :], 0.0)
    values = []
    for t, factor in enumerate(factors):
        z = paired_sum([part[t * rows : (t + 1) * rows, :].astype(jnp.float32) for part in parts]) * factor
        values.append(jnp.sum(z * jax.nn.sigmoid(z) * gain, -1, keepdims=True))
    return values


def finish_kernel(steps, notes, scale, *refs):
    norms, parts, out = refs[:steps], refs[steps:-1], refs[-1]
    lane = lax.broadcasted_iota(jnp.int32, out.shape, 1)
    total = jnp.zeros(out.shape, jnp.float32)
    for t, value in enumerate(scores_of(notes, scale, parts, [norm[:, :1] for norm in norms])):
        total = jnp.where(lane == t, value, total)
    out[...] = total


def finish(notes, scale, norms, parts):
    return pl.pallas_call(
        functools.partial(finish_kernel, len(norms)),
        out_shape=struct((notes.shape[0], 128), jnp.float32),
        in_specs=[WHOLE] * (2 + len(norms) + len(parts)),
        out_specs=WHOLE,
        compiler_params=pltpu.CompilerParams(vmem_limit_bytes=12 << 20),
        cost_estimate=SMALL,
        name="finish",
    )(notes, scale, *norms, *parts)


def place_kernel(groups, cap, mp, notes, own_row, peer_row, *refs):
    befores, scales, parts, table = refs[:mp], refs[mp : 2 * mp], refs[2 * mp : 3 * mp], refs[3 * mp]
    rows = notes.shape[0]
    _, _, me = coordinates()
    before = paired_sum([x[...] for x in befores])
    values = [before[:, t : t + 1] for t in range(STEPS - 1)]
    scale = [sum(jnp.where((me ^ j) == m, scales[j][...], 0.0) for j in range(mp)) for m in range(mp)]
    low, high = own_row[...].astype(jnp.float32), peer_row[...].astype(jnp.float32)
    squares = jnp.sum(low * low, -1, keepdims=True) + jnp.sum(high * high, -1, keepdims=True)
    values += scores_of(notes, jnp.concatenate(scale, 1), parts, [lax.rsqrt(squares / D + 1e-06)])
    number = lambda lane: notes[:, lane : lane + 1].astype(jnp.int32)
    shard, at = number(SHARD), number(SOURCE) * cap + number(RANK)
    live = notes[:, LIVE : LIVE + 1] > 0.5
    column = lax.broadcasted_iota(jnp.int32, (rows, table.shape[1]), 1)
    for r in range(groups):
        spots = (column == at) & (shard == r) & live
        for t, value in enumerate(values):
            table[r * STEPS + t : r * STEPS + t + 1, :] = jnp.sum(jnp.where(spots, value, 0.0), 0, keepdims=True)


def place(groups, cap, notes, own_row, peer_row, befores, scales, parts):
    mp = len(parts)
    return pl.pallas_call(
        functools.partial(place_kernel, groups, cap, mp),
        out_shape=struct((groups * STEPS, -(-groups * cap // 128) * 128), jnp.float32),
        in_specs=[WHOLE] * (3 + 3 * mp),
        out_specs=WHOLE,
        compiler_params=pltpu.CompilerParams(vmem_limit_bytes=12 << 20),
        cost_estimate=SMALL,
        name="place",
    )(notes, own_row, peer_row, *befores, *scales, *parts)


def shards(
    tokens,
    parent_keys,
    parent_values,
    parent_blocks,
    child_parent,
    child_count,
    node_shard,
    attn_gain,
    w_query,
    w_key,
    w_value,
    w_out,
    reward_up,
    reward_out,
):
    groups, mp = lax.axis_size("dp"), lax.axis_size("mp")
    children, width = tokens.shape
    parents, prefix, kv_cols = parent_keys.shape
    capacity = max(2, 2 * children // groups)
    reward_cap = max(2, 3 * children // (2 * groups))
    slots = groups * capacity
    rows = min(slots, 3 * children // 2)
    hidden = reward_out.shape[1] // mp
    pairs = lambda count, k: [(i, i ^ k) for i in range(count)]
    swap = pairs(mp, 1)

    up = lax.all_gather(reward_up[0], "dp", axis=0, axis_index_groups=[ring_order(groups)])

    *stay, cross = dispatch(
        parents, child_count, child_parent, node_shard, tokens, reward_out, groups, capacity, hidden
    )
    keys = parent_keys.reshape(parents * prefix, kv_cols)
    values = parent_values.reshape(parents * prefix, kv_cols)
    raw = (w_query, w_key, w_value, keys, values, w_out)
    cross, raw = lax.optimization_barrier((cross, raw))
    cross = lax.ppermute(cross, "dp", pairs(groups, 1))
    stay, cross, early, late = lax.optimization_barrier((stay, cross, load(*raw[:2]), raw[2:]))
    blocks, late = lax.optimization_barrier((regroup(stay, cross), late))
    blocks = [blocks[0]] + [lax.ppermute(blocks[j], "dp", pairs(groups, 2 * j)) for j in range(1, groups // 2)]
    blocks, weights = lax.optimization_barrier((blocks, (*early, *load(*late))))
    gain = attn_gain.reshape(1, width)

    def run(offset, weights, blocks, up, gain, child_parent, parent_blocks):
        row_own, notes, bias, scale, over = pack(
            offset, rows, hidden, prefix, parent_blocks, child_parent, blocks
        )
        w_query, w_key, w_value, keys, values, w_out = [held(w) for w in weights]
        state = row_own.astype(jnp.float32)
        row_peer = lax.ppermute(row_own, "mp", swap)
        past_keys, past_values, rows_own, rows_peer, norms = [], [], [], [], []

        def products(first, last, up, load):
            sums = score(mp, notes, up, rows_own[first:last], rows_peer[first:last], load)
            count = mp if load else 1
            return list(sums[:count]), held(sums[-1]) if load else None

        send = lambda sums: [sums[0]] + [lax.ppermute(sums[k], "mp", pairs(mp, k)) for k in range(1, mp)]
        scales = send([scale] * mp)
        for step in range(STEPS):
            part, attn, key_now, value_now, norm = expand(
                step, row_own, row_peer, begin(row_own, gain, w_query, w_key, w_value), gain, w_query, w_key, w_value, keys, values, bias, w_out,
                past_keys, past_values,
            )
            norms.append(norm)
            past_keys.append(key_now)
            past_values.append(value_now)
            from_peer = lax.ppermute(part, "mp", swap)
            chip = project_own(rows, attn, w_out) + from_peer.astype(jnp.float32)
            sent = chip.astype(jnp.bfloat16)
            others = [sent] + [lax.ppermute(sent, "mp", pairs(mp, k)) for k in range(2, mp, 2)]
            if step == 0:
                others, scales = lax.optimization_barrier((others, scales))
            if step + 1 == STEPS:
                _, up = lax.optimization_barrier((sent, up))
                before, up = products(0, step, up, True)
                others, before = lax.optimization_barrier((others, before))
            state = state + paired_sum([other.astype(jnp.float32) for other in others])
            row_own = state.astype(jnp.bfloat16)
            row_peer = lax.ppermute(row_own, "mp", swap)
            rows_own.append(row_own)
            rows_peer.append(row_peer)
        before = send(before)
        last, _ = products(step, STEPS, up, False)
        last, over = lax.optimization_barrier((send(last * mp), over[0, 0]))
        before = send([finish(notes, scale, norms[1:], before)] * mp)
        return place(groups, reward_cap, notes, row_own, row_peer, before, scales, last), over

    operands = (blocks, up, gain, child_parent, parent_blocks)
    table, over = run(0, weights, *operands)
    if rows < slots:
        table, raw, operands = lax.optimization_barrier((table, raw, operands))
        again = lambda table, raw, operands: table + run(rows, load(*raw), *operands)[0]
        table = lax.cond(over > 0, again, lambda table, raw, operands: table, table, raw, operands)

    table = lax.all_to_all(table, "dp", split_axis=0, concat_axis=0, tiled=True)
    return jnp.sum(table.reshape(groups, STEPS, -1), 0)[:, : groups * reward_cap]


def solution(mesh):
    placed = (
        P("dp", None),
        P("dp", None, "mp"),
        P("dp", None, "mp"),
        P(),
        P(),
        P("dp"),
        P(),
        P(),
        P(None, "mp"),
        P(None, "mp"),
        P(None, "mp"),
        P("mp", None),
        P("dp", "mp", None),
        P("dp", None),
    )
    return jax.shard_map(
        shards, mesh=mesh, in_specs=placed, out_specs=P(None, "dp"), check_vma=False
    )
```

```python
import functools
import math

import jax
import jax.numpy as jnp
from jax import lax
from jax.experimental import pallas as pl
from jax.experimental.pallas import tpu as pltpu
from jax.sharding import PartitionSpec as P

D = 5120
HEADS = 24
KVH = 8
HD = 128
STEPS = 8
GROUP = HEADS // KVH
CHUNK = 512
COLUMNS = 256
ROWS = 64
MASKED = -1e30
EXPONENT = HD ** (-0.5) * math.log2(math.e)
VMEM = pltpu.VMEM
NOTES = 128
LIVE, RANK, SHARD, PARENT, SOURCE, COUNT = range(6)


def dot(a, b):
    return jnp.dot(a, b, preferred_element_type=jnp.float32)


def held(x):
    return pltpu.with_memory_space_constraint(x, VMEM)


def far(x):
    return pltpu.with_memory_space_constraint(x, pltpu.HBM)


def struct(shape, dtype=jnp.bfloat16):
    return jax.ShapeDtypeStruct(shape, dtype)


WHOLE = pl.BlockSpec(memory_space=VMEM)
FAR = pl.BlockSpec(memory_space=pltpu.HBM)
SMALL = pl.CostEstimate(flops=0, bytes_accessed=0, transcendentals=0)
SCALARS = pl.BlockSpec(memory_space=pltpu.SMEM)


def paired_sum(parts):
    while len(parts) > 1:
        parts = [a + b for a, b in zip(parts[::2], parts[1::2])]
    return parts[0]


def ring_order(groups):
    return list(range(0, groups, 2)) + list(range(groups - 1, 0, -2))


def coordinates():
    me = lax.axis_index("mp")
    return lax.rem(me, 2), lax.axis_index("dp"), me


def dispatch_kernel(parents, groups, count, parent_far, shard_far, tokens_far, reward_far, *rest):
    core, own, me = coordinates()
    blocks, near = rest[:groups], rest[groups:]
    parent_row, shard_row, tokens, reward_out, sems = near
    children, half = tokens.shape
    sources = (parent_far, shard_far, tokens_far.at[:, pl.ds(pl.multiple_of(core * half, half), half)], reward_far)
    copies = [pltpu.make_async_copy(a, b, sems.at[i]) for i, (a, b) in enumerate(zip(sources, near))]
    for copy in copies:
        copy.start()
    for copy in copies:
        copy.wait()
    capacity = blocks[0].shape[0]
    everyone = parent_row.shape[1]
    int32, float32, bfloat16 = jnp.int32, jnp.float32, jnp.bfloat16

    mine = lax.broadcasted_iota(int32, (everyone, children), 0) - own * children
    mine = (mine == lax.broadcasted_iota(int32, (everyone, children), 1)).astype(float32).astype(bfloat16)

    def row_and_column(table):
        table = table[...].astype(float32).astype(bfloat16)
        column = lax.dot_general(mine, table, (((0,), (1,)), ((), ())), preferred_element_type=float32)
        return dot(table, mine).astype(int32), column.astype(int32)

    parent, parent_c = row_and_column(parent_row)
    shard, shard_c = row_and_column(shard_row)
    source, source_c = lax.div(parent, parents), lax.div(parent_c, parents)
    first = lax.broadcasted_iota(int32, (children, children), 0)
    second = lax.broadcasted_iota(int32, (children, children), 1)
    live = lax.broadcasted_iota(int32, (1, children), 1) < count[0]
    live_c = lax.broadcasted_iota(int32, (children, 1), 0) < count[0]
    rank = jnp.sum(jnp.where((source_c == source) & (first < second) & live_c, 1, 0), 0, keepdims=True)
    slot = (source ^ own) * capacity + rank
    slot = jnp.where(live, slot, -1)
    reward_rank = jnp.sum(jnp.where((shard_c == shard) & (second < first) & live, 1, 0), 1, keepdims=True)
    lane = lax.broadcasted_iota(int32, (children, NOTES), 1)
    notes = jnp.where(lane == LIVE, live_c.astype(int32), 0)
    for at, value in ((RANK, reward_rank), (SHARD, shard_c), (PARENT, lax.rem(parent_c, parents)), (SOURCE, own)):
        notes = jnp.where(lane == at, value, notes)

    width = blocks[0].shape[1] - half - NOTES
    hidden = width // 3
    rest = jnp.zeros((1, hidden), float32)
    for m in range(reward_out.shape[1] // hidden):
        rest = rest + jnp.where(me == m, reward_out[:, m * hidden : (m + 1) * hidden], 0.0)
    parts = []
    for _ in range(3):
        parts.append(rest.astype(bfloat16).astype(float32))
        rest = rest - parts[-1]
    shared = jnp.broadcast_to(jnp.concatenate(parts, 1), (capacity, width))

    rows = lax.broadcasted_iota(int32, (groups * capacity, children), 0)
    put = (rows == slot).astype(float32).astype(bfloat16)
    token_rows = dot(put, tokens[...])
    note_rows = dot(put, notes.astype(float32).astype(bfloat16))
    row = lax.broadcasted_iota(int32, note_rows.shape, 0)
    lane = lax.broadcasted_iota(int32, note_rows.shape, 1)
    note_rows = jnp.where((lax.rem(row, capacity) == 0) & (lane == COUNT), count[0].astype(float32), note_rows)
    for k, block in enumerate(blocks):
        at = slice(k * capacity, (k + 1) * capacity)
        block[...] = jnp.concatenate([token_rows[at], note_rows[at], shared], 1).astype(bfloat16)


def dispatch(parents, child_count, child_parent, node_shard, tokens, reward_out, groups, capacity, hidden):
    children, half = tokens.shape[0], tokens.shape[1] // 2
    tables = (child_parent[None], node_shard[None])
    return pl.pallas_call(
        functools.partial(dispatch_kernel, parents, groups),
        out_shape=(struct((capacity, half + NOTES + 3 * hidden)),) * groups,
        in_specs=[SCALARS] + [FAR] * 4,
        out_specs=(WHOLE,) * groups,
        scratch_shapes=[VMEM(x.shape, x.dtype) for x in tables]
        + [VMEM((children, half), tokens.dtype), VMEM(reward_out.shape, reward_out.dtype)]
        + [pltpu.SemaphoreType.DMA((4,))],
        compiler_params=pltpu.CompilerParams(vmem_limit_bytes=8 << 20),
        cost_estimate=SMALL,
        name="dispatch",
    )(child_count, *map(far, (*tables, tokens, reward_out)))


def crossing_first(groups):
    return sorted(range(groups), key=lambda k: -(k ^ (k & 1)))


def pack_kernel(offset, hidden, prefix, blocks_held, parent_row, *rest):
    blocks, (row, notes, bias, scale, over) = rest[:-5], rest[-5:]
    blocks = [block for _, block in sorted(zip(crossing_first(len(blocks)), blocks), key=lambda pair: pair[0])]
    _, own, _ = coordinates()
    groups, capacity = len(blocks), blocks[0].shape[0]
    rows, half = row.shape
    slots = groups * capacity
    arrived = jnp.concatenate([block[...].astype(jnp.float32) for block in blocks], 0)
    live = arrived[:, half + LIVE : half + LIVE + 1]
    first = lax.broadcasted_iota(jnp.int32, (slots, slots), 0)
    second = lax.broadcasted_iota(jnp.int32, (slots, slots), 1)
    place = jnp.sum(jnp.where(first < second, live, 0.0), 0, keepdims=True)
    kept = jnp.sum(jnp.where(first == second, live, 0.0), 0, keepdims=True) > 0.5
    wanted = lax.broadcasted_iota(jnp.int32, (rows, slots), 0) + offset
    take = (wanted == place.astype(jnp.int32)) & kept
    take = take.astype(jnp.float32).astype(jnp.bfloat16)
    row[...] = dot(take, arrived[:, :half].astype(jnp.bfloat16)).astype(jnp.bfloat16)
    note = dot(take, arrived[:, half : half + NOTES].astype(jnp.bfloat16))
    notes[...] = note
    parent = note[:, PARENT : PARENT + 1].astype(jnp.int32)
    parents = bias.shape[1] // prefix
    position = lax.broadcasted_iota(jnp.int32, (rows, prefix), 1)
    for p in range(parents):
        usable = (parent == p) & (position < blocks_held[own * parents + p] * 128)
        bias[:, p * prefix : (p + 1) * prefix] = jnp.where(usable, 0.0, MASKED)
    base = half + NOTES
    child = lax.broadcasted_iota(jnp.int32, parent_row.shape, 1)
    children = parent_row.shape[1] // groups
    at, child = lax.div(child, children), lax.rem(child, children)
    count = jnp.zeros(parent_row.shape, jnp.float32)
    for k in range(groups):
        first_row = arrived[k * capacity : k * capacity + 1]
        head = first_row[:, base:]
        scale[pl.ds(own ^ k, 1), :] = head[:, :hidden] + head[:, hidden : 2 * hidden] + head[:, 2 * hidden : 3 * hidden]
        count = jnp.where(at == (own ^ k), first_row[:, half + COUNT : half + COUNT + 1], count)
    source = lax.div(parent_row[...], parents)
    going = child < count.astype(jnp.int32)
    most = jnp.zeros((1, 1), jnp.float32)
    for d in range(groups):
        load = jnp.sum(jnp.where((source == d) & going, 1.0, 0.0), 1, keepdims=True)
        most = jnp.maximum(most, load)
    over[...] = jnp.broadcast_to((most > rows).astype(jnp.int32), over.shape)


def pack(offset, rows, hidden, prefix, blocks_held, child_parent, blocks):
    half = D // 2
    groups = len(blocks)
    parents = blocks_held.shape[0] // groups
    return pl.pallas_call(
        functools.partial(pack_kernel, offset, hidden, prefix),
        out_shape=(
            struct((rows, half)),
            struct((rows, NOTES), jnp.float32),
            struct((rows, parents * prefix), jnp.float32),
            struct((groups, hidden), jnp.float32),
            struct((8, 128), jnp.int32),
        ),
        in_specs=[SCALARS] + [WHOLE] * (1 + groups),
        out_specs=[WHOLE] * 5,
        compiler_params=pltpu.CompilerParams(vmem_limit_bytes=12 << 20),
        cost_estimate=SMALL,
        name="pack",
    )(blocks_held, child_parent[None], *[blocks[k] for k in crossing_first(groups)])


def load_kernel(*refs):
    count = (len(refs) - 1) // 2
    copies = [pltpu.make_async_copy(refs[i], refs[count + i], refs[-1].at[i]) for i in range(count)]
    for copy in copies:
        copy.start()
    for copy in copies:
        copy.wait()


def load(*arrays):
    count = len(arrays)
    return pl.pallas_call(
        load_kernel,
        out_shape=tuple(VMEM(x.shape, x.dtype) for x in arrays),
        in_specs=[FAR] * count,
        out_specs=(WHOLE,) * count,
        scratch_shapes=[pltpu.SemaphoreType.DMA((count,))],
        compiler_params=pltpu.CompilerParams(vmem_limit_bytes=2 << 20),
        cost_estimate=pl.CostEstimate(flops=0, bytes_accessed=24 << 20, transcendentals=0),
        name="load",
    )(*map(far, arrays))


def project(attn, w_out, out, first):
    width = out.shape[1]

    @pl.loop(0, width // CHUNK)
    def _(i):
        columns = pl.ds(pl.multiple_of(first + i * CHUNK, CHUNK), CHUNK)
        out[:, pl.ds(pl.multiple_of(i * CHUNK, CHUNK), CHUNK)] = dot(
            attn[...], w_out[:, columns]
        )[: out.shape[0]].astype(out.dtype)


def products_of(row, first, half, gain, weights, normed):
    at = pl.ds(pl.multiple_of(first, half), half)
    slots = row.shape[0]
    normed[:slots, :] = (row[...].astype(jnp.float32) * gain[:, at]).astype(jnp.bfloat16)
    if normed.shape[0] > slots:
        normed[slots:, :] = jnp.zeros((normed.shape[0] - slots, half), jnp.bfloat16)
    column = 0
    for w in weights:
        for start in range(0, w.shape[1], COLUMNS):
            end = min(start + COLUMNS, w.shape[1])
            yield slice(column + start, column + end), dot(normed[...], w[at, start:end])[:slots]
        column += w.shape[1]


def begin_kernel(own, gain, w_query, w_key, w_value, out, normed):
    core, _, _ = coordinates()
    half = own.shape[1]
    for columns, value in products_of(own, core * half, half, gain, (w_query, w_key, w_value), normed):
        out[:, columns] = value


def begin(own, gain, w_query, w_key, w_value):
    slots, half = own.shape
    padded = -(-slots // ROWS) * ROWS
    return pl.pallas_call(
        begin_kernel,
        out_shape=struct((slots, w_query.shape[1] + 2 * w_key.shape[1]), jnp.float32),
        in_specs=[WHOLE] * 5,
        out_specs=WHOLE,
        scratch_shapes=[VMEM((padded, half), jnp.bfloat16)],
        compiler_params=pltpu.CompilerParams(vmem_limit_bytes=8 << 20),
        cost_estimate=SMALL,
        name="begin",
    )(own, gain, w_query, w_key, w_value)


def step_kernel(step, own, peer, begun, gain, w_query, w_key, w_value, keys, values, bias, w_out, *rest):
    past_keys, past_values = rest[:step], rest[step : 2 * step]
    rest = rest[2 * step :]
    half = own.shape[1]
    slots = own.shape[0]
    q_cols, kv_cols = w_query.shape[1], w_key.shape[1]
    kv_heads = kv_cols // HD
    part, attn, key_now, value_now, norm, *kept, normed, query = rest[:5] + rest[5 : len(rest) - (step == 0)]
    copies = []
    if step == 0:
        for i, (source, target) in enumerate(zip((keys, values, w_out), kept)):
            copies.append(pltpu.make_async_copy(source, target, rest[-1].at[i]))
            copies[-1].start()
        keys, values, w_out = kept
    core, _, _ = coordinates()
    here, there = own[...].astype(jnp.float32), peer[...].astype(jnp.float32)
    squares = jnp.sum(here * here, -1, keepdims=True) + jnp.sum(there * there, -1, keepdims=True)
    factor = lax.rsqrt(squares / D + 1e-06)
    norm[...] = jnp.broadcast_to(factor, norm.shape)
    for columns, value in products_of(peer, (1 - core) * half, half, gain, (w_query, w_key, w_value), normed):
        query[:, columns] = (begun[:, columns] + value) * factor
    key_now[...] = query[:slots, q_cols : q_cols + kv_cols].astype(jnp.bfloat16)
    value_now[...] = query[:slots, q_cols + kv_cols :].astype(jnp.bfloat16)
    for copy in copies[:2]:
        copy.wait()
    recent = slots * (step + 1)
    row = lax.broadcasted_iota(jnp.int32, (GROUP * slots, recent), 0)
    column = lax.broadcasted_iota(jnp.int32, (GROUP * slots, recent), 1)
    same = lax.rem(row, slots) == lax.rem(column, slots)
    for head in range(kv_heads):
        lanes = slice(head * HD, (head + 1) * HD)
        q = jnp.concatenate(
            [query[:slots, (head * GROUP + g) * HD : (head * GROUP + g + 1) * HD] for g in range(GROUP)], 0
        ).astype(jnp.bfloat16)
        k_new = jnp.concatenate([k[:, lanes] for k in past_keys] + [key_now[:, lanes]], 0)
        v_new = jnp.concatenate([v[:, lanes] for v in past_values] + [value_now[:, lanes]], 0)
        contract = (((1,), (1,)), ((), ()))
        s_old = lax.dot_general(q, keys[:, lanes], contract, preferred_element_type=jnp.float32)
        s_old = s_old + jnp.concatenate([bias[...]] * GROUP, 0)
        s_new = lax.dot_general(q, k_new, contract, preferred_element_type=jnp.float32)
        s_new = jnp.where(same, s_new, MASKED)
        top = jnp.maximum(jnp.max(s_old, -1, keepdims=True), jnp.max(s_new, -1, keepdims=True))
        p_old = jnp.exp2(s_old * EXPONENT - top * EXPONENT)
        p_new = jnp.exp2(s_new * EXPONENT - top * EXPONENT)
        total = jnp.sum(p_old, -1, keepdims=True) + jnp.sum(p_new, -1, keepdims=True)
        summed = dot(p_old.astype(jnp.bfloat16), values[:, lanes]) + dot(p_new.astype(jnp.bfloat16), v_new)
        result = (summed / total).astype(jnp.bfloat16)
        for g in range(GROUP):
            at = (head * GROUP + g) * HD
            attn[:slots, at : at + HD] = result[g * slots : (g + 1) * slots]
    if attn.shape[0] > slots:
        attn[slots:, :] = jnp.zeros((attn.shape[0] - slots, q_cols), jnp.bfloat16)
    for copy in copies[2:]:
        copy.wait()
    project(attn, w_out, part, (1 - core) * half)


def expand(step, own, peer, begun, gain, w_query, w_key, w_value, keys, values, bias, w_out, past_keys, past_values):
    slots, half = own.shape
    kv_cols = w_key.shape[1]
    q_cols = w_query.shape[1]
    padded = -(-slots // ROWS) * ROWS
    kept, sems, place = [], [], WHOLE
    if step == 0:
        kept = [VMEM(x.shape, x.dtype) for x in (keys, values, w_out)]
        keys, values, w_out = far(keys), far(values), far(w_out)
        sems, place = [pltpu.SemaphoreType.DMA((3,))], FAR
    return pl.pallas_call(
        functools.partial(step_kernel, step),
        out_shape=(
            struct((slots, half)), struct((padded, q_cols)), struct((slots, kv_cols)), struct((slots, kv_cols)),
            struct((slots, 128), jnp.float32), *kept,
        ),
        in_specs=[WHOLE] * 7 + [place] * 2 + [WHOLE, place] + [WHOLE] * (2 * step),
        out_specs=[WHOLE] * (5 + len(kept)),
        scratch_shapes=[VMEM((padded, half), jnp.bfloat16), VMEM((slots, q_cols + 2 * kv_cols), jnp.float32)] + sems,
        compiler_params=pltpu.CompilerParams(vmem_limit_bytes=16 << 20),
        cost_estimate=SMALL,
        name="expand",
    )(own, peer, begun, gain, w_query, w_key, w_value, keys, values, bias, w_out, *past_keys, *past_values)


def project_kernel(attn, w_out, part):
    core, _, _ = coordinates()
    project(attn, w_out, part, core * part.shape[1])


def project_own(rows, attn, w_out):
    return pl.pallas_call(
        project_kernel,
        out_shape=struct((rows, w_out.shape[1] // 2), jnp.float32),
        in_specs=[WHOLE, WHOLE],
        out_specs=WHOLE,
        compiler_params=pltpu.CompilerParams(vmem_limit_bytes=8 << 20),
        cost_estimate=SMALL,
        name="project_own",
    )(attn, w_out)


def score_kernel(steps, load, mp, notes, up, *refs):
    take = lambda count: [refs.pop(0) for _ in range(count)]
    refs = list(refs)
    own_rows, peer_rows, blocks, kept = take(steps), take(steps), take(mp if load else 1), take(1 * load)
    flat, total, *sems = refs
    groups, depth, hidden = up.shape
    rows = own_rows[0].shape[0]
    core, _, me = coordinates()
    for t in range(steps):
        target = flat.at[t * rows : (t + 1) * rows]
        for m in range(mp):
            at = m % (mp // 2) * depth
            for c in range(2):
                source = (own_rows if m // (mp // 2) == c else peer_rows)[t].at[:, at : at + depth]

                @pl.when((me == m) & (core == c))
                def _():
                    if load:
                        pltpu.make_async_copy(source, target, sems[0].at[t]).start()
                    else:
                        target[...] = source[...]

    if load:
        order = ring_order(groups)
        fetch = lambda r: pltpu.make_async_copy(arrived.at[order.index(r)], kept[0].at[r], sems[1].at[r])
        arrived, up = up, kept[0]
        for r in range(3):
            fetch(r).start()
        for t in range(steps):
            target = flat.at[t * rows : (t + 1) * rows]
            pltpu.make_async_copy(target, target, sems[0].at[t]).wait()
    shard = jnp.concatenate([notes[:, SHARD : SHARD + 1].astype(jnp.int32)] * steps, 0)
    for r in range(groups):
        if load:
            fetch(r).wait()
            if r + 3 < groups:
                fetch(r + 3).start()
        for at in range(0, hidden, COLUMNS):
            end = min(at + COLUMNS, hidden)
            here = jnp.where(shard == r, dot(flat[...], up[r, :, at:end]), 0.0)
            total[:, at:end] = here if r == 0 else total[:, at:end] + here
    if not load:
        blocks[0][...] = total[...].astype(jnp.bfloat16)
        return
    width = hidden // mp
    for j, block in enumerate(blocks):
        for m in range(mp):

            @pl.when((me ^ j) == m)
            def _():
                block[...] = total[:, m * width : (m + 1) * width].astype(jnp.bfloat16)


def score(mp, notes, up, own_rows, peer_rows, load):
    steps = len(own_rows)
    groups, depth, hidden = up.shape
    count = steps * own_rows[0].shape[0]
    blocks = (struct((count, hidden // mp)),) * mp if load else (struct((count, hidden)),)
    kept = (VMEM(up.shape, up.dtype),) * load
    place = FAR if load else WHOLE
    sems = [pltpu.SemaphoreType.DMA((steps,)), pltpu.SemaphoreType.DMA((groups,))]
    return pl.pallas_call(
        functools.partial(score_kernel, steps, load, mp),
        out_shape=blocks + kept,
        in_specs=[WHOLE] + [place] * (1 + 2 * steps),
        out_specs=(WHOLE,) * (len(blocks) + len(kept)),
        scratch_shapes=[VMEM((count, depth), jnp.bfloat16), VMEM((count, hidden), jnp.float32)] + sems * load,
        compiler_params=pltpu.CompilerParams(vmem_limit_bytes=16 << 20),
        cost_estimate=SMALL,
        name="score",
    )(notes, *(map(far, (up, *own_rows, *peer_rows)) if load else (up, *own_rows, *peer_rows)))


def scores_of(notes, scale, parts, factors):
    rows = notes.shape[0]
    shard = notes[:, SHARD : SHARD + 1].astype(jnp.int32)
    gain = jnp.zeros((rows, scale.shape[1]), jnp.float32)
    for r in range(scale.shape[0]):
        gain = gain + jnp.where(shard == r, scale[r : r + 1, :], 0.0)
    values = []
    for t, factor in enumerate(factors):
        z = paired_sum([part[t * rows : (t + 1) * rows, :].astype(jnp.float32) for part in parts]) * factor
        values.append(jnp.sum(z * jax.nn.sigmoid(z) * gain, -1, keepdims=True))
    return values


def finish_kernel(steps, notes, scale, *refs):
    norms, parts, out = refs[:steps], refs[steps:-1], refs[-1]
    lane = lax.broadcasted_iota(jnp.int32, out.shape, 1)
    total = jnp.zeros(out.shape, jnp.float32)
    for t, value in enumerate(scores_of(notes, scale, parts, [norm[:, :1] for norm in norms])):
        total = jnp.where(lane == t, value, total)
    out[...] = total


def finish(notes, scale, norms, parts):
    return pl.pallas_call(
        functools.partial(finish_kernel, len(norms)),
        out_shape=struct((notes.shape[0], 128), jnp.float32),
        in_specs=[WHOLE] * (2 + len(norms) + len(parts)),
        out_specs=WHOLE,
        compiler_params=pltpu.CompilerParams(vmem_limit_bytes=12 << 20),
        cost_estimate=SMALL,
        name="finish",
    )(notes, scale, *norms, *parts)


def place_kernel(groups, cap, mp, notes, own_row, peer_row, *refs):
    befores, scales, parts, table = refs[:mp], refs[mp : 2 * mp], refs[2 * mp : 3 * mp], refs[3 * mp]
    rows = notes.shape[0]
    _, _, me = coordinates()
    before = paired_sum([x[...] for x in befores])
    values = [before[:, t : t + 1] for t in range(STEPS - 1)]
    scale = [sum(jnp.where((me ^ j) == m, scales[j][...], 0.0) for j in range(mp)) for m in range(mp)]
    low, high = own_row[...].astype(jnp.float32), peer_row[...].astype(jnp.float32)
    squares = jnp.sum(low * low, -1, keepdims=True) + jnp.sum(high * high, -1, keepdims=True)
    values += scores_of(notes, jnp.concatenate(scale, 1), parts, [lax.rsqrt(squares / D + 1e-06)])
    number = lambda lane: notes[:, lane : lane + 1].astype(jnp.int32)
    shard, at = number(SHARD), number(SOURCE) * cap + number(RANK)
    live = notes[:, LIVE : LIVE + 1] > 0.5
    column = lax.broadcasted_iota(jnp.int32, (rows, table.shape[1]), 1)
    for r in range(groups):
        spots = (column == at) & (shard == r) & live
        for t, value in enumerate(values):
            table[r * STEPS + t : r * STEPS + t + 1, :] = jnp.sum(jnp.where(spots, value, 0.0), 0, keepdims=True)


def place(groups, cap, notes, own_row, peer_row, befores, scales, parts):
    mp = len(parts)
    return pl.pallas_call(
        functools.partial(place_kernel, groups, cap, mp),
        out_shape=struct((groups * STEPS, -(-groups * cap // 128) * 128), jnp.float32),
        in_specs=[WHOLE] * (3 + 3 * mp),
        out_specs=WHOLE,
        compiler_params=pltpu.CompilerParams(vmem_limit_bytes=12 << 20),
        cost_estimate=SMALL,
        name="place",
    )(notes, own_row, peer_row, *befores, *scales, *parts)


def shards(
    tokens,
    parent_keys,
    parent_values,
    parent_blocks,
    child_parent,
    child_count,
    node_shard,
    attn_gain,
    w_query,
    w_key,
    w_value,
    w_out,
    reward_up,
    reward_out,
):
    groups, mp = lax.axis_size("dp"), lax.axis_size("mp")
    children, width = tokens.shape
    parents, prefix, kv_cols = parent_keys.shape
    capacity = max(2, 2 * children // groups)
    reward_cap = max(2, 3 * children // (2 * groups))
    slots = groups * capacity
    rows = min(slots, 3 * children // 2)
    hidden = reward_out.shape[1] // mp
    pairs = lambda count, k: [(i, i ^ k) for i in range(count)]
    swap = pairs(mp, 1)

    up = lax.all_gather(reward_up[0], "dp", axis=0, axis_index_groups=[ring_order(groups)])

    blocks = dispatch(parents, child_count, child_parent, node_shard, tokens, reward_out, groups, capacity, hidden)
    keys = parent_keys.reshape(parents * prefix, kv_cols)
    values = parent_values.reshape(parents * prefix, kv_cols)
    raw = (w_query, w_key, w_value, keys, values, w_out)
    blocks, raw = lax.optimization_barrier((blocks, raw))
    blocks = [blocks[0]] + [lax.ppermute(blocks[k], "dp", pairs(groups, k)) for k in range(1, groups)]
    blocks, ready = lax.optimization_barrier((blocks, load(*raw[:3])))
    weights = (*ready, *raw[3:])
    gain = attn_gain.reshape(1, width)

    def run(offset, weights, blocks, up, gain, child_parent, parent_blocks):
        row_own, notes, bias, scale, over = pack(
            offset, rows, hidden, prefix, parent_blocks, child_parent, blocks
        )
        w_query, w_key, w_value = [held(w) for w in weights[:3]]
        keys, values, w_out = weights[3:]
        state = row_own.astype(jnp.float32)
        row_peer = lax.ppermute(row_own, "mp", swap)
        past_keys, past_values, rows_own, rows_peer, norms = [], [], [], [], []

        def products(first, last, up, load):
            sums = score(mp, notes, up, rows_own[first:last], rows_peer[first:last], load)
            count = mp if load else 1
            return list(sums[:count]), held(sums[-1]) if load else None

        send = lambda sums: [sums[0]] + [lax.ppermute(sums[k], "mp", pairs(mp, k)) for k in range(1, mp)]
        scales = send([scale] * mp)
        for step in range(STEPS):
            part, attn, key_now, value_now, norm, *kept = expand(
                step, row_own, row_peer, begin(row_own, gain, w_query, w_key, w_value), gain, w_query, w_key, w_value, keys, values, bias, w_out,
                past_keys, past_values,
            )
            if step == 0:
                keys, values, w_out = [held(x) for x in kept]
            norms.append(norm)
            past_keys.append(key_now)
            past_values.append(value_now)
            from_peer = lax.ppermute(part, "mp", swap)
            chip = project_own(rows, attn, w_out) + from_peer.astype(jnp.float32)
            sent = chip.astype(jnp.bfloat16)
            others = [sent] + [lax.ppermute(sent, "mp", pairs(mp, k)) for k in range(2, mp, 2)]
            if step == 0:
                others, scales = lax.optimization_barrier((others, scales))
            if step + 1 == STEPS:
                _, up = lax.optimization_barrier((sent, up))
                before, up = products(0, step, up, True)
                others, before = lax.optimization_barrier((others, before))
            state = state + paired_sum([other.astype(jnp.float32) for other in others])
            row_own = state.astype(jnp.bfloat16)
            row_peer = lax.ppermute(row_own, "mp", swap)
            rows_own.append(row_own)
            rows_peer.append(row_peer)
        before = send(before)
        last, _ = products(step, STEPS, up, False)
        last, over = lax.optimization_barrier((send(last * mp), over[0, 0]))
        before = send([finish(notes, scale, norms[1:], before)] * mp)
        return place(groups, reward_cap, notes, row_own, row_peer, before, scales, last), over

    operands = (blocks, up, gain, child_parent, parent_blocks)
    table, over = run(0, weights, *operands)
    if rows < slots:
        table, raw, operands = lax.optimization_barrier((table, raw, operands))
        again = lambda table, raw, operands: table + run(rows, (*load(*raw[:3]), *raw[3:]), *operands)[0]
        table = lax.cond(over > 0, again, lambda table, raw, operands: table, table, raw, operands)

    table = lax.all_to_all(table, "dp", split_axis=0, concat_axis=0, tiled=True)
    return jnp.sum(table.reshape(groups, STEPS, -1), 0)[:, : groups * reward_cap]


def solution(mesh):
    placed = (
        P("dp", None),
        P("dp", None, "mp"),
        P("dp", None, "mp"),
        P(),
        P(),
        P("dp"),
        P(),
        P(),
        P(None, "mp"),
        P(None, "mp"),
        P(None, "mp"),
        P("mp", None),
        P("dp", "mp", None),
        P("dp", None),
    )
    return jax.shard_map(
        shards, mesh=mesh, in_specs=placed, out_specs=P(None, "dp"), check_vma=False
    )
```

```python
import functools
import math

import jax
import jax.numpy as jnp
from jax import lax
from jax.experimental import pallas as pl
from jax.experimental.pallas import tpu as pltpu
from jax.sharding import PartitionSpec as P

D = 5120
HEADS = 24
KVH = 8
HD = 128
STEPS = 8
GROUP = HEADS // KVH
CHUNK = 512
COLUMNS = 256
ROWS = 16
MASKED = -1e30
EXPONENT = HD ** (-0.5) * math.log2(math.e)
VMEM = pltpu.VMEM
NOTES = 128
LIVE, RANK, SHARD, PARENT, SOURCE, COUNT = range(6)


def dot(a, b):
    return jnp.dot(a, b, preferred_element_type=jnp.float32)


def held(x):
    return pltpu.with_memory_space_constraint(x, VMEM)


def far(x):
    return pltpu.with_memory_space_constraint(x, pltpu.HBM)


def struct(shape, dtype=jnp.bfloat16):
    return jax.ShapeDtypeStruct(shape, dtype)


WHOLE = pl.BlockSpec(memory_space=VMEM)
FAR = pl.BlockSpec(memory_space=pltpu.HBM)
SMALL = pl.CostEstimate(flops=0, bytes_accessed=0, transcendentals=0)
SCALARS = pl.BlockSpec(memory_space=pltpu.SMEM)


def paired_sum(parts):
    while len(parts) > 1:
        parts = [a + b for a, b in zip(parts[::2], parts[1::2])]
    return parts[0]


def ring_order(groups):
    return list(range(0, groups, 2)) + list(range(groups - 1, 0, -2))


def coordinates():
    me = lax.axis_index("mp")
    return lax.rem(me, 2), lax.axis_index("dp"), me


def dispatch_kernel(parents, groups, count, parent_far, shard_far, tokens_far, reward_far, *rest):
    core, own, me = coordinates()
    blocks, near = rest[:groups], rest[groups:]
    parent_row, shard_row, tokens, reward_out, sems = near
    children, half = tokens.shape
    sources = (parent_far, shard_far, tokens_far.at[:, pl.ds(pl.multiple_of(core * half, half), half)], reward_far)
    copies = [pltpu.make_async_copy(a, b, sems.at[i]) for i, (a, b) in enumerate(zip(sources, near))]
    for copy in copies:
        copy.start()
    for copy in copies:
        copy.wait()
    capacity = blocks[0].shape[0]
    everyone = parent_row.shape[1]
    int32, float32, bfloat16 = jnp.int32, jnp.float32, jnp.bfloat16

    mine = lax.broadcasted_iota(int32, (everyone, children), 0) - own * children
    mine = (mine == lax.broadcasted_iota(int32, (everyone, children), 1)).astype(float32).astype(bfloat16)

    def row_and_column(table):
        table = table[...].astype(float32).astype(bfloat16)
        column = lax.dot_general(mine, table, (((0,), (1,)), ((), ())), preferred_element_type=float32)
        return dot(table, mine).astype(int32), column.astype(int32)

    parent, parent_c = row_and_column(parent_row)
    shard, shard_c = row_and_column(shard_row)
    source, source_c = lax.div(parent, parents), lax.div(parent_c, parents)
    first = lax.broadcasted_iota(int32, (children, children), 0)
    second = lax.broadcasted_iota(int32, (children, children), 1)
    live = lax.broadcasted_iota(int32, (1, children), 1) < count[0]
    live_c = lax.broadcasted_iota(int32, (children, 1), 0) < count[0]
    rank = jnp.sum(jnp.where((source_c == source) & (first < second) & live_c, 1, 0), 0, keepdims=True)
    slot = (source ^ own) * capacity + rank
    slot = jnp.where(live, slot, -1)
    reward_rank = jnp.sum(jnp.where((shard_c == shard) & (second < first) & live, 1, 0), 1, keepdims=True)
    lane = lax.broadcasted_iota(int32, (children, NOTES), 1)
    notes = jnp.where(lane == LIVE, live_c.astype(int32), 0)
    for at, value in ((RANK, reward_rank), (SHARD, shard_c), (PARENT, lax.rem(parent_c, parents)), (SOURCE, own)):
        notes = jnp.where(lane == at, value, notes)

    width = blocks[0].shape[1] - half - NOTES
    hidden = width // 3
    rest = jnp.zeros((1, hidden), float32)
    for m in range(reward_out.shape[1] // hidden):
        rest = rest + jnp.where(me == m, reward_out[:, m * hidden : (m + 1) * hidden], 0.0)
    parts = []
    for _ in range(3):
        parts.append(rest.astype(bfloat16).astype(float32))
        rest = rest - parts[-1]
    shared = jnp.broadcast_to(jnp.concatenate(parts, 1), (capacity, width))

    rows = lax.broadcasted_iota(int32, (groups * capacity, children), 0)
    put = (rows == slot).astype(float32).astype(bfloat16)
    token_rows = dot(put, tokens[...])
    note_rows = dot(put, notes.astype(float32).astype(bfloat16))
    row = lax.broadcasted_iota(int32, note_rows.shape, 0)
    lane = lax.broadcasted_iota(int32, note_rows.shape, 1)
    note_rows = jnp.where((lax.rem(row, capacity) == 0) & (lane == COUNT), count[0].astype(float32), note_rows)
    for k, block in enumerate(blocks):
        at = slice(k * capacity, (k + 1) * capacity)
        block[...] = jnp.concatenate([token_rows[at], note_rows[at], shared], 1).astype(bfloat16)


def dispatch(parents, child_count, child_parent, node_shard, tokens, reward_out, groups, capacity, hidden):
    children, half = tokens.shape[0], tokens.shape[1] // 2
    tables = (child_parent[None], node_shard[None])
    return pl.pallas_call(
        functools.partial(dispatch_kernel, parents, groups),
        out_shape=(struct((capacity, half + NOTES + 3 * hidden)),) * groups,
        in_specs=[SCALARS] + [FAR] * 4,
        out_specs=(WHOLE,) * groups,
        scratch_shapes=[VMEM(x.shape, x.dtype) for x in tables]
        + [VMEM((children, half), tokens.dtype), VMEM(reward_out.shape, reward_out.dtype)]
        + [pltpu.SemaphoreType.DMA((4,))],
        compiler_params=pltpu.CompilerParams(vmem_limit_bytes=8 << 20),
        cost_estimate=SMALL,
        name="dispatch",
    )(child_count, *map(far, (*tables, tokens, reward_out)))


def crossing_first(groups):
    return sorted(range(groups), key=lambda k: -(k ^ (k & 1)))


def pack_kernel(offset, hidden, prefix, blocks_held, parent_row, *rest):
    blocks, (row, notes, bias, scale, over) = rest[:-5], rest[-5:]
    blocks = [block for _, block in sorted(zip(crossing_first(len(blocks)), blocks), key=lambda pair: pair[0])]
    _, own, _ = coordinates()
    groups, capacity = len(blocks), blocks[0].shape[0]
    rows, half = row.shape
    slots = groups * capacity
    arrived = jnp.concatenate([block[...].astype(jnp.float32) for block in blocks], 0)
    live = arrived[:, half + LIVE : half + LIVE + 1]
    first = lax.broadcasted_iota(jnp.int32, (slots, slots), 0)
    second = lax.broadcasted_iota(jnp.int32, (slots, slots), 1)
    place = jnp.sum(jnp.where(first < second, live, 0.0), 0, keepdims=True)
    kept = jnp.sum(jnp.where(first == second, live, 0.0), 0, keepdims=True) > 0.5
    wanted = lax.broadcasted_iota(jnp.int32, (rows, slots), 0) + offset
    take = (wanted == place.astype(jnp.int32)) & kept
    take = take.astype(jnp.float32).astype(jnp.bfloat16)
    row[...] = dot(take, arrived[:, :half].astype(jnp.bfloat16)).astype(jnp.bfloat16)
    note = dot(take, arrived[:, half : half + NOTES].astype(jnp.bfloat16))
    notes[...] = note
    parent = note[:, PARENT : PARENT + 1].astype(jnp.int32)
    parents = bias.shape[1] // prefix
    position = lax.broadcasted_iota(jnp.int32, (rows, prefix), 1)
    for p in range(parents):
        usable = (parent == p) & (position < blocks_held[own * parents + p] * 128)
        bias[:, p * prefix : (p + 1) * prefix] = jnp.where(usable, 0.0, MASKED)
    base = half + NOTES
    child = lax.broadcasted_iota(jnp.int32, parent_row.shape, 1)
    children = parent_row.shape[1] // groups
    at, child = lax.div(child, children), lax.rem(child, children)
    count = jnp.zeros(parent_row.shape, jnp.float32)
    for k in range(groups):
        first_row = arrived[k * capacity : k * capacity + 1]
        head = first_row[:, base:]
        scale[pl.ds(own ^ k, 1), :] = head[:, :hidden] + head[:, hidden : 2 * hidden] + head[:, 2 * hidden : 3 * hidden]
        count = jnp.where(at == (own ^ k), first_row[:, half + COUNT : half + COUNT + 1], count)
    source = lax.div(parent_row[...], parents)
    going = child < count.astype(jnp.int32)
    most = jnp.zeros((1, 1), jnp.float32)
    for d in range(groups):
        load = jnp.sum(jnp.where((source == d) & going, 1.0, 0.0), 1, keepdims=True)
        most = jnp.maximum(most, load)
    over[...] = jnp.broadcast_to((most > rows).astype(jnp.int32), over.shape)


def pack(offset, rows, hidden, prefix, blocks_held, child_parent, blocks):
    half = D // 2
    groups = len(blocks)
    parents = blocks_held.shape[0] // groups
    return pl.pallas_call(
        functools.partial(pack_kernel, offset, hidden, prefix),
        out_shape=(
            struct((rows, half)),
            struct((rows, NOTES), jnp.float32),
            struct((rows, parents * prefix), jnp.float32),
            struct((groups, hidden), jnp.float32),
            struct((8, 128), jnp.int32),
        ),
        in_specs=[SCALARS] + [WHOLE] * (1 + groups),
        out_specs=[WHOLE] * 5,
        compiler_params=pltpu.CompilerParams(vmem_limit_bytes=12 << 20),
        cost_estimate=SMALL,
        name="pack",
    )(blocks_held, child_parent[None], *[blocks[k] for k in crossing_first(groups)])


def load_kernel(*refs):
    count = (len(refs) - 1) // 2
    copies = [pltpu.make_async_copy(refs[i], refs[count + i], refs[-1].at[i]) for i in range(count)]
    for copy in copies:
        copy.start()
    for copy in copies:
        copy.wait()


def load(*arrays):
    count = len(arrays)
    return pl.pallas_call(
        load_kernel,
        out_shape=tuple(VMEM(x.shape, x.dtype) for x in arrays),
        in_specs=[FAR] * count,
        out_specs=(WHOLE,) * count,
        scratch_shapes=[pltpu.SemaphoreType.DMA((count,))],
        compiler_params=pltpu.CompilerParams(vmem_limit_bytes=2 << 20),
        cost_estimate=pl.CostEstimate(flops=0, bytes_accessed=24 << 20, transcendentals=0),
        name="load",
    )(*map(far, arrays))


def project(attn, w_out, out, first):
    width = out.shape[1]

    @pl.loop(0, width // CHUNK)
    def _(i):
        columns = pl.ds(pl.multiple_of(first + i * CHUNK, CHUNK), CHUNK)
        out[:, pl.ds(pl.multiple_of(i * CHUNK, CHUNK), CHUNK)] = dot(
            attn[...], w_out[:, columns]
        )[: out.shape[0]].astype(out.dtype)


def products_of(row, first, half, gain, weights, normed):
    at = pl.ds(pl.multiple_of(first, half), half)
    slots = row.shape[0]
    normed[:slots, :] = (row[...].astype(jnp.float32) * gain[:, at]).astype(jnp.bfloat16)
    if normed.shape[0] > slots:
        normed[slots:, :] = jnp.zeros((normed.shape[0] - slots, half), jnp.bfloat16)
    column = 0
    for w in weights:
        for start in range(0, w.shape[1], COLUMNS):
            end = min(start + COLUMNS, w.shape[1])
            yield slice(column + start, column + end), dot(normed[...], w[at, start:end])[:slots]
        column += w.shape[1]


def begin_kernel(own, gain, w_query, w_key, w_value, out, normed):
    core, _, _ = coordinates()
    half = own.shape[1]
    for columns, value in products_of(own, core * half, half, gain, (w_query, w_key, w_value), normed):
        out[:, columns] = value


def begin(own, gain, w_query, w_key, w_value):
    slots, half = own.shape
    padded = -(-slots // ROWS) * ROWS
    return pl.pallas_call(
        begin_kernel,
        out_shape=struct((slots, w_query.shape[1] + 2 * w_key.shape[1]), jnp.float32),
        in_specs=[WHOLE] * 5,
        out_specs=WHOLE,
        scratch_shapes=[VMEM((padded, half), jnp.bfloat16)],
        compiler_params=pltpu.CompilerParams(vmem_limit_bytes=8 << 20),
        cost_estimate=SMALL,
        name="begin",
    )(own, gain, w_query, w_key, w_value)


def step_kernel(step, own, peer, begun, gain, w_query, w_key, w_value, keys, values, bias, w_out, *rest):
    past_keys, past_values = rest[:step], rest[step : 2 * step]
    rest = rest[2 * step :]
    half = own.shape[1]
    slots = own.shape[0]
    q_cols, kv_cols = w_query.shape[1], w_key.shape[1]
    kv_heads = kv_cols // HD
    part, attn, key_now, value_now, norm, normed, query = rest
    core, _, _ = coordinates()
    here, there = own[...].astype(jnp.float32), peer[...].astype(jnp.float32)
    squares = jnp.sum(here * here, -1, keepdims=True) + jnp.sum(there * there, -1, keepdims=True)
    factor = lax.rsqrt(squares / D + 1e-06)
    norm[...] = jnp.broadcast_to(factor, norm.shape)
    for columns, value in products_of(peer, (1 - core) * half, half, gain, (w_query, w_key, w_value), normed):
        query[:, columns] = (begun[:, columns] + value) * factor
    key_now[...] = query[:slots, q_cols : q_cols + kv_cols].astype(jnp.bfloat16)
    value_now[...] = query[:slots, q_cols + kv_cols :].astype(jnp.bfloat16)
    recent = slots * (step + 1)
    row = lax.broadcasted_iota(jnp.int32, (GROUP * slots, recent), 0)
    column = lax.broadcasted_iota(jnp.int32, (GROUP * slots, recent), 1)
    same = lax.rem(row, slots) == lax.rem(column, slots)
    for head in range(kv_heads):
        lanes = slice(head * HD, (head + 1) * HD)
        q = jnp.concatenate(
            [query[:slots, (head * GROUP + g) * HD : (head * GROUP + g + 1) * HD] for g in range(GROUP)], 0
        ).astype(jnp.bfloat16)
        k_new = jnp.concatenate([k[:, lanes] for k in past_keys] + [key_now[:, lanes]], 0)
        v_new = jnp.concatenate([v[:, lanes] for v in past_values] + [value_now[:, lanes]], 0)
        contract = (((1,), (1,)), ((), ()))
        s_old = lax.dot_general(q, keys[:, lanes], contract, preferred_element_type=jnp.float32)
        s_old = s_old + jnp.concatenate([bias[...]] * GROUP, 0)
        s_new = lax.dot_general(q, k_new, contract, preferred_element_type=jnp.float32)
        s_new = jnp.where(same, s_new, MASKED)
        top = jnp.maximum(jnp.max(s_old, -1, keepdims=True), jnp.max(s_new, -1, keepdims=True))
        p_old = jnp.exp2(s_old * EXPONENT - top * EXPONENT)
        p_new = jnp.exp2(s_new * EXPONENT - top * EXPONENT)
        total = jnp.sum(p_old, -1, keepdims=True) + jnp.sum(p_new, -1, keepdims=True)
        summed = dot(p_old.astype(jnp.bfloat16), values[:, lanes]) + dot(p_new.astype(jnp.bfloat16), v_new)
        result = (summed / total).astype(jnp.bfloat16)
        for g in range(GROUP):
            at = (head * GROUP + g) * HD
            attn[:slots, at : at + HD] = result[g * slots : (g + 1) * slots]
    if attn.shape[0] > slots:
        attn[slots:, :] = jnp.zeros((attn.shape[0] - slots, q_cols), jnp.bfloat16)
    project(attn, w_out, part, (1 - core) * half)


def expand(step, own, peer, begun, gain, w_query, w_key, w_value, keys, values, bias, w_out, past_keys, past_values):
    slots, half = own.shape
    kv_cols = w_key.shape[1]
    q_cols = w_query.shape[1]
    padded = -(-slots // ROWS) * ROWS
    return pl.pallas_call(
        functools.partial(step_kernel, step),
        out_shape=(
            struct((slots, half)), struct((padded, q_cols)), struct((slots, kv_cols)), struct((slots, kv_cols)),
            struct((slots, 128), jnp.float32),
        ),
        in_specs=[WHOLE] * (11 + 2 * step),
        out_specs=[WHOLE] * 5,
        scratch_shapes=[VMEM((padded, half), jnp.bfloat16), VMEM((slots, q_cols + 2 * kv_cols), jnp.float32)],
        compiler_params=pltpu.CompilerParams(vmem_limit_bytes=16 << 20),
        cost_estimate=SMALL,
        name="expand",
    )(own, peer, begun, gain, w_query, w_key, w_value, keys, values, bias, w_out, *past_keys, *past_values)


def project_kernel(attn, w_out, part):
    core, _, _ = coordinates()
    project(attn, w_out, part, core * part.shape[1])


def project_own(rows, attn, w_out):
    return pl.pallas_call(
        project_kernel,
        out_shape=struct((rows, w_out.shape[1] // 2), jnp.float32),
        in_specs=[WHOLE, WHOLE],
        out_specs=WHOLE,
        compiler_params=pltpu.CompilerParams(vmem_limit_bytes=8 << 20),
        cost_estimate=SMALL,
        name="project_own",
    )(attn, w_out)


def score_kernel(steps, load, mp, notes, up, *refs):
    take = lambda count: [refs.pop(0) for _ in range(count)]
    refs = list(refs)
    own_rows, peer_rows, blocks, kept = take(steps), take(steps), take(mp if load else 1), take(1 * load)
    flat, total, *sems = refs
    groups, depth, hidden = up.shape
    rows = own_rows[0].shape[0]
    core, _, me = coordinates()
    for t in range(steps):
        target = flat.at[t * rows : (t + 1) * rows]
        for m in range(mp):
            at = m % (mp // 2) * depth
            for c in range(2):
                source = (own_rows if m // (mp // 2) == c else peer_rows)[t].at[:, at : at + depth]

                @pl.when((me == m) & (core == c))
                def _():
                    if load:
                        pltpu.make_async_copy(source, target, sems[0].at[t]).start()
                    else:
                        target[...] = source[...]

    if load:
        order = ring_order(groups)
        fetch = lambda r: pltpu.make_async_copy(arrived.at[order.index(r)], kept[0].at[r], sems[1].at[r])
        arrived, up = up, kept[0]
        for r in range(3):
            fetch(r).start()
        for t in range(steps):
            target = flat.at[t * rows : (t + 1) * rows]
            pltpu.make_async_copy(target, target, sems[0].at[t]).wait()
    shard = jnp.concatenate([notes[:, SHARD : SHARD + 1].astype(jnp.int32)] * steps, 0)
    for r in range(groups):
        if load:
            fetch(r).wait()
            if r + 3 < groups:
                fetch(r + 3).start()
        for at in range(0, hidden, COLUMNS):
            end = min(at + COLUMNS, hidden)
            here = jnp.where(shard == r, dot(flat[...], up[r, :, at:end]), 0.0)
            total[:, at:end] = here if r == 0 else total[:, at:end] + here
    if not load:
        blocks[0][...] = total[...].astype(jnp.bfloat16)
        return
    width = hidden // mp
    for j, block in enumerate(blocks):
        for m in range(mp):

            @pl.when((me ^ j) == m)
            def _():
                block[...] = total[:, m * width : (m + 1) * width].astype(jnp.bfloat16)


def score(mp, notes, up, own_rows, peer_rows, load):
    steps = len(own_rows)
    groups, depth, hidden = up.shape
    count = steps * own_rows[0].shape[0]
    blocks = (struct((count, hidden // mp)),) * mp if load else (struct((count, hidden)),)
    kept = (VMEM(up.shape, up.dtype),) * load
    place = FAR if load else WHOLE
    sems = [pltpu.SemaphoreType.DMA((steps,)), pltpu.SemaphoreType.DMA((groups,))]
    return pl.pallas_call(
        functools.partial(score_kernel, steps, load, mp),
        out_shape=blocks + kept,
        in_specs=[WHOLE] + [place] * (1 + 2 * steps),
        out_specs=(WHOLE,) * (len(blocks) + len(kept)),
        scratch_shapes=[VMEM((count, depth), jnp.bfloat16), VMEM((count, hidden), jnp.float32)] + sems * load,
        compiler_params=pltpu.CompilerParams(vmem_limit_bytes=16 << 20),
        cost_estimate=SMALL,
        name="score",
    )(notes, *(map(far, (up, *own_rows, *peer_rows)) if load else (up, *own_rows, *peer_rows)))


def scores_of(notes, scale, parts, factors):
    rows = notes.shape[0]
    shard = notes[:, SHARD : SHARD + 1].astype(jnp.int32)
    gain = jnp.zeros((rows, scale.shape[1]), jnp.float32)
    for r in range(scale.shape[0]):
        gain = gain + jnp.where(shard == r, scale[r : r + 1, :], 0.0)
    values = []
    for t, factor in enumerate(factors):
        z = paired_sum([part[t * rows : (t + 1) * rows, :].astype(jnp.float32) for part in parts]) * factor
        values.append(jnp.sum(z * jax.nn.sigmoid(z) * gain, -1, keepdims=True))
    return values


def finish_kernel(steps, notes, scale, *refs):
    norms, parts, out = refs[:steps], refs[steps:-1], refs[-1]
    lane = lax.broadcasted_iota(jnp.int32, out.shape, 1)
    total = jnp.zeros(out.shape, jnp.float32)
    for t, value in enumerate(scores_of(notes, scale, parts, [norm[:, :1] for norm in norms])):
        total = jnp.where(lane == t, value, total)
    out[...] = total


def finish(notes, scale, norms, parts):
    return pl.pallas_call(
        functools.partial(finish_kernel, len(norms)),
        out_shape=struct((notes.shape[0], 128), jnp.float32),
        in_specs=[WHOLE] * (2 + len(norms) + len(parts)),
        out_specs=WHOLE,
        compiler_params=pltpu.CompilerParams(vmem_limit_bytes=12 << 20),
        cost_estimate=SMALL,
        name="finish",
    )(notes, scale, *norms, *parts)


def place_kernel(groups, cap, mp, notes, own_row, peer_row, *refs):
    befores, scales, parts, table = refs[:mp], refs[mp : 2 * mp], refs[2 * mp : 3 * mp], refs[3 * mp]
    rows = notes.shape[0]
    _, _, me = coordinates()
    before = paired_sum([x[...] for x in befores])
    values = [before[:, t : t + 1] for t in range(STEPS - 1)]
    scale = [sum(jnp.where((me ^ j) == m, scales[j][...], 0.0) for j in range(mp)) for m in range(mp)]
    low, high = own_row[...].astype(jnp.float32), peer_row[...].astype(jnp.float32)
    squares = jnp.sum(low * low, -1, keepdims=True) + jnp.sum(high * high, -1, keepdims=True)
    values += scores_of(notes, jnp.concatenate(scale, 1), parts, [lax.rsqrt(squares / D + 1e-06)])
    number = lambda lane: notes[:, lane : lane + 1].astype(jnp.int32)
    shard, at = number(SHARD), number(SOURCE) * cap + number(RANK)
    live = notes[:, LIVE : LIVE + 1] > 0.5
    column = lax.broadcasted_iota(jnp.int32, (rows, table.shape[1]), 1)
    for r in range(groups):
        spots = (column == at) & (shard == r) & live
        for t, value in enumerate(values):
            table[r * STEPS + t : r * STEPS + t + 1, :] = jnp.sum(jnp.where(spots, value, 0.0), 0, keepdims=True)


def place(groups, cap, notes, own_row, peer_row, befores, scales, parts):
    mp = len(parts)
    return pl.pallas_call(
        functools.partial(place_kernel, groups, cap, mp),
        out_shape=struct((groups * STEPS, -(-groups * cap // 128) * 128), jnp.float32),
        in_specs=[WHOLE] * (3 + 3 * mp),
        out_specs=WHOLE,
        compiler_params=pltpu.CompilerParams(vmem_limit_bytes=12 << 20),
        cost_estimate=SMALL,
        name="place",
    )(notes, own_row, peer_row, *befores, *scales, *parts)


def shards(
    tokens,
    parent_keys,
    parent_values,
    parent_blocks,
    child_parent,
    child_count,
    node_shard,
    attn_gain,
    w_query,
    w_key,
    w_value,
    w_out,
    reward_up,
    reward_out,
):
    groups, mp = lax.axis_size("dp"), lax.axis_size("mp")
    children, width = tokens.shape
    parents, prefix, kv_cols = parent_keys.shape
    capacity = max(2, 2 * children // groups)
    reward_cap = max(2, 3 * children // (2 * groups))
    slots = groups * capacity
    rows = min(slots, 3 * children // 2)
    hidden = reward_out.shape[1] // mp
    pairs = lambda count, k: [(i, i ^ k) for i in range(count)]
    swap = pairs(mp, 1)

    up = lax.all_gather(reward_up[0], "dp", axis=0, axis_index_groups=[ring_order(groups)])

    blocks = dispatch(parents, child_count, child_parent, node_shard, tokens, reward_out, groups, capacity, hidden)
    keys = parent_keys.reshape(parents * prefix, kv_cols)
    values = parent_values.reshape(parents * prefix, kv_cols)
    raw = (w_query, w_key, w_value, keys, values, w_out)
    blocks, raw = lax.optimization_barrier((blocks, raw))
    blocks = [blocks[0]] + [lax.ppermute(blocks[k], "dp", pairs(groups, k)) for k in range(1, groups)]
    blocks, weights = lax.optimization_barrier((blocks, load(*raw)))
    gain = attn_gain.reshape(1, width)

    def run(offset, weights, blocks, up, gain, child_parent, parent_blocks):
        row_own, notes, bias, scale, over = pack(
            offset, rows, hidden, prefix, parent_blocks, child_parent, blocks
        )
        w_query, w_key, w_value, keys, values, w_out = [held(w) for w in weights]
        state = row_own.astype(jnp.float32)
        row_peer = lax.ppermute(row_own, "mp", swap)
        past_keys, past_values, rows_own, rows_peer, norms = [], [], [], [], []

        def products(first, last, up, load):
            sums = score(mp, notes, up, rows_own[first:last], rows_peer[first:last], load)
            count = mp if load else 1
            return list(sums[:count]), held(sums[-1]) if load else None

        send = lambda sums: [sums[0]] + [lax.ppermute(sums[k], "mp", pairs(mp, k)) for k in range(1, mp)]
        scales = send([scale] * mp)
        for step in range(STEPS):
            part, attn, key_now, value_now, norm = expand(
                step, row_own, row_peer, begin(row_own, gain, w_query, w_key, w_value), gain, w_query, w_key, w_value, keys, values, bias, w_out,
                past_keys, past_values,
            )
            norms.append(norm)
            past_keys.append(key_now)
            past_values.append(value_now)
            from_peer = lax.ppermute(part, "mp", swap)
            chip = project_own(rows, attn, w_out) + from_peer.astype(jnp.float32)
            sent = chip.astype(jnp.bfloat16)
            others = [sent] + [lax.ppermute(sent, "mp", pairs(mp, k)) for k in range(2, mp, 2)]
            if step == 0:
                others, scales = lax.optimization_barrier((others, scales))
            if step + 1 == STEPS:
                _, up = lax.optimization_barrier((sent, up))
                before, up = products(0, step, up, True)
                others, before = lax.optimization_barrier((others, before))
            state = state + paired_sum([other.astype(jnp.float32) for other in others])
            row_own = state.astype(jnp.bfloat16)
            row_peer = lax.ppermute(row_own, "mp", swap)
            rows_own.append(row_own)
            rows_peer.append(row_peer)
        before = send(before)
        last, _ = products(step, STEPS, up, False)
        last, over = lax.optimization_barrier((send(last * mp), over[0, 0]))
        before = send([finish(notes, scale, norms[1:], before)] * mp)
        return place(groups, reward_cap, notes, row_own, row_peer, before, scales, last), over

    operands = (blocks, up, gain, child_parent, parent_blocks)
    table, over = run(0, weights, *operands)
    if rows < slots:
        table, raw, operands = lax.optimization_barrier((table, raw, operands))
        again = lambda table, raw, operands: table + run(rows, load(*raw), *operands)[0]
        table = lax.cond(over > 0, again, lambda table, raw, operands: table, table, raw, operands)

    table = lax.all_to_all(table, "dp", split_axis=0, concat_axis=0, tiled=True)
    return jnp.sum(table.reshape(groups, STEPS, -1), 0)[:, : groups * reward_cap]


def solution(mesh):
    placed = (
        P("dp", None),
        P("dp", None, "mp"),
        P("dp", None, "mp"),
        P(),
        P(),
        P("dp"),
        P(),
        P(),
        P(None, "mp"),
        P(None, "mp"),
        P(None, "mp"),
        P("mp", None),
        P("dp", "mp", None),
        P("dp", None),
    )
    return jax.shard_map(
        shards, mesh=mesh, in_specs=placed, out_specs=P(None, "dp"), check_vma=False
    )
```

```python
import functools
import math

import jax
import jax.numpy as jnp
from jax import lax
from jax.experimental import pallas as pl
from jax.experimental.pallas import tpu as pltpu
from jax.sharding import PartitionSpec as P

D = 5120
HEADS = 24
KVH = 8
HD = 128
STEPS = 8
GROUP = HEADS // KVH
CHUNK = 1280
COLUMNS = 256
ROWS = 16
MASKED = -1e30
EXPONENT = HD ** (-0.5) * math.log2(math.e)
VMEM = pltpu.VMEM
NOTES = 128
LIVE, RANK, SHARD, PARENT, SOURCE, COUNT = range(6)


def dot(a, b):
    return jnp.dot(a, b, preferred_element_type=jnp.float32)


def held(x):
    return pltpu.with_memory_space_constraint(x, VMEM)


def far(x):
    return pltpu.with_memory_space_constraint(x, pltpu.HBM)


def struct(shape, dtype=jnp.bfloat16):
    return jax.ShapeDtypeStruct(shape, dtype)


WHOLE = pl.BlockSpec(memory_space=VMEM)
FAR = pl.BlockSpec(memory_space=pltpu.HBM)
SMALL = pl.CostEstimate(flops=0, bytes_accessed=0, transcendentals=0)
SCALARS = pl.BlockSpec(memory_space=pltpu.SMEM)


def paired_sum(parts):
    while len(parts) > 1:
        parts = [a + b for a, b in zip(parts[::2], parts[1::2])]
    return parts[0]


def ring_order(groups):
    return list(range(0, groups, 2)) + list(range(groups - 1, 0, -2))


def coordinates():
    me = lax.axis_index("mp")
    return lax.rem(me, 2), lax.axis_index("dp"), me


def dispatch_kernel(parents, groups, count, parent_far, shard_far, tokens_far, reward_far, *rest):
    core, own, me = coordinates()
    blocks, near = rest[:groups], rest[groups:]
    parent_row, shard_row, tokens, reward_out, sems = near
    children, half = tokens.shape
    sources = (parent_far, shard_far, tokens_far.at[:, pl.ds(pl.multiple_of(core * half, half), half)], reward_far)
    copies = [pltpu.make_async_copy(a, b, sems.at[i]) for i, (a, b) in enumerate(zip(sources, near))]
    for copy in copies:
        copy.start()
    for copy in copies:
        copy.wait()
    capacity = blocks[0].shape[0]
    everyone = parent_row.shape[1]
    int32, float32, bfloat16 = jnp.int32, jnp.float32, jnp.bfloat16

    mine = lax.broadcasted_iota(int32, (everyone, children), 0) - own * children
    mine = (mine == lax.broadcasted_iota(int32, (everyone, children), 1)).astype(float32).astype(bfloat16)

    def row_and_column(table):
        table = table[...].astype(float32).astype(bfloat16)
        column = lax.dot_general(mine, table, (((0,), (1,)), ((), ())), preferred_element_type=float32)
        return dot(table, mine).astype(int32), column.astype(int32)

    parent, parent_c = row_and_column(parent_row)
    shard, shard_c = row_and_column(shard_row)
    source, source_c = lax.div(parent, parents), lax.div(parent_c, parents)
    first = lax.broadcasted_iota(int32, (children, children), 0)
    second = lax.broadcasted_iota(int32, (children, children), 1)
    live = lax.broadcasted_iota(int32, (1, children), 1) < count[0]
    live_c = lax.broadcasted_iota(int32, (children, 1), 0) < count[0]
    rank = jnp.sum(jnp.where((source_c == source) & (first < second) & live_c, 1, 0), 0, keepdims=True)
    slot = (source ^ own) * capacity + rank
    slot = jnp.where(live, slot, -1)
    reward_rank = jnp.sum(jnp.where((shard_c == shard) & (second < first) & live, 1, 0), 1, keepdims=True)
    lane = lax.broadcasted_iota(int32, (children, NOTES), 1)
    notes = jnp.where(lane == LIVE, live_c.astype(int32), 0)
    for at, value in ((RANK, reward_rank), (SHARD, shard_c), (PARENT, lax.rem(parent_c, parents)), (SOURCE, own)):
        notes = jnp.where(lane == at, value, notes)

    width = blocks[0].shape[1] - half - NOTES
    hidden = width // 3
    rest = jnp.zeros((1, hidden), float32)
    for m in range(reward_out.shape[1] // hidden):
        rest = rest + jnp.where(me == m, reward_out[:, m * hidden : (m + 1) * hidden], 0.0)
    parts = []
    for _ in range(3):
        parts.append(rest.astype(bfloat16).astype(float32))
        rest = rest - parts[-1]
    shared = jnp.broadcast_to(jnp.concatenate(parts, 1), (capacity, width))

    rows = lax.broadcasted_iota(int32, (groups * capacity, children), 0)
    put = (rows == slot).astype(float32).astype(bfloat16)
    token_rows = dot(put, tokens[...])
    note_rows = dot(put, notes.astype(float32).astype(bfloat16))
    row = lax.broadcasted_iota(int32, note_rows.shape, 0)
    lane = lax.broadcasted_iota(int32, note_rows.shape, 1)
    note_rows = jnp.where((lax.rem(row, capacity) == 0) & (lane == COUNT), count[0].astype(float32), note_rows)
    for k, block in enumerate(blocks):
        at = slice(k * capacity, (k + 1) * capacity)
        block[...] = jnp.concatenate([token_rows[at], note_rows[at], shared], 1).astype(bfloat16)


def dispatch(parents, child_count, child_parent, node_shard, tokens, reward_out, groups, capacity, hidden):
    children, half = tokens.shape[0], tokens.shape[1] // 2
    tables = (child_parent[None], node_shard[None])
    return pl.pallas_call(
        functools.partial(dispatch_kernel, parents, groups),
        out_shape=(struct((capacity, half + NOTES + 3 * hidden)),) * groups,
        in_specs=[SCALARS] + [FAR] * 4,
        out_specs=(WHOLE,) * groups,
        scratch_shapes=[VMEM(x.shape, x.dtype) for x in tables]
        + [VMEM((children, half), tokens.dtype), VMEM(reward_out.shape, reward_out.dtype)]
        + [pltpu.SemaphoreType.DMA((4,))],
        compiler_params=pltpu.CompilerParams(vmem_limit_bytes=8 << 20),
        cost_estimate=SMALL,
        name="dispatch",
    )(child_count, *map(far, (*tables, tokens, reward_out)))


def crossing_first(groups):
    return sorted(range(groups), key=lambda k: -(k ^ (k & 1)))


def pack_kernel(offset, hidden, prefix, blocks_held, parent_row, *rest):
    blocks, (row, notes, bias, scale, over) = rest[:-5], rest[-5:]
    blocks = [block for _, block in sorted(zip(crossing_first(len(blocks)), blocks), key=lambda pair: pair[0])]
    _, own, _ = coordinates()
    groups, capacity = len(blocks), blocks[0].shape[0]
    rows, half = row.shape
    slots = groups * capacity
    arrived = jnp.concatenate([block[...].astype(jnp.float32) for block in blocks], 0)
    live = arrived[:, half + LIVE : half + LIVE + 1]
    first = lax.broadcasted_iota(jnp.int32, (slots, slots), 0)
    second = lax.broadcasted_iota(jnp.int32, (slots, slots), 1)
    place = jnp.sum(jnp.where(first < second, live, 0.0), 0, keepdims=True)
    kept = jnp.sum(jnp.where(first == second, live, 0.0), 0, keepdims=True) > 0.5
    wanted = lax.broadcasted_iota(jnp.int32, (rows, slots), 0) + offset
    take = (wanted == place.astype(jnp.int32)) & kept
    take = take.astype(jnp.float32).astype(jnp.bfloat16)
    row[...] = dot(take, arrived[:, :half].astype(jnp.bfloat16)).astype(jnp.bfloat16)
    note = dot(take, arrived[:, half : half + NOTES].astype(jnp.bfloat16))
    notes[...] = note
    parent = note[:, PARENT : PARENT + 1].astype(jnp.int32)
    parents = bias.shape[1] // prefix
    position = lax.broadcasted_iota(jnp.int32, (rows, prefix), 1)
    for p in range(parents):
        usable = (parent == p) & (position < blocks_held[own * parents + p] * 128)
        bias[:, p * prefix : (p + 1) * prefix] = jnp.where(usable, 0.0, MASKED)
    base = half + NOTES
    child = lax.broadcasted_iota(jnp.int32, parent_row.shape, 1)
    children = parent_row.shape[1] // groups
    at, child = lax.div(child, children), lax.rem(child, children)
    count = jnp.zeros(parent_row.shape, jnp.float32)
    for k in range(groups):
        first_row = arrived[k * capacity : k * capacity + 1]
        head = first_row[:, base:]
        scale[pl.ds(own ^ k, 1), :] = head[:, :hidden] + head[:, hidden : 2 * hidden] + head[:, 2 * hidden : 3 * hidden]
        count = jnp.where(at == (own ^ k), first_row[:, half + COUNT : half + COUNT + 1], count)
    source = lax.div(parent_row[...], parents)
    going = child < count.astype(jnp.int32)
    most = jnp.zeros((1, 1), jnp.float32)
    for d in range(groups):
        load = jnp.sum(jnp.where((source == d) & going, 1.0, 0.0), 1, keepdims=True)
        most = jnp.maximum(most, load)
    over[...] = jnp.broadcast_to((most > rows).astype(jnp.int32), over.shape)


def pack(offset, rows, hidden, prefix, blocks_held, child_parent, blocks):
    half = D // 2
    groups = len(blocks)
    parents = blocks_held.shape[0] // groups
    return pl.pallas_call(
        functools.partial(pack_kernel, offset, hidden, prefix),
        out_shape=(
            struct((rows, half)),
            struct((rows, NOTES), jnp.float32),
            struct((rows, parents * prefix), jnp.float32),
            struct((groups, hidden), jnp.float32),
            struct((8, 128), jnp.int32),
        ),
        in_specs=[SCALARS] + [WHOLE] * (1 + groups),
        out_specs=[WHOLE] * 5,
        compiler_params=pltpu.CompilerParams(vmem_limit_bytes=12 << 20),
        cost_estimate=SMALL,
        name="pack",
    )(blocks_held, child_parent[None], *[blocks[k] for k in crossing_first(groups)])


def load_kernel(*refs):
    count = (len(refs) - 1) // 2
    copies = [pltpu.make_async_copy(refs[i], refs[count + i], refs[-1].at[i]) for i in range(count)]
    for copy in copies:
        copy.start()
    for copy in copies:
        copy.wait()


def load(*arrays):
    count = len(arrays)
    return pl.pallas_call(
        load_kernel,
        out_shape=tuple(VMEM(x.shape, x.dtype) for x in arrays),
        in_specs=[FAR] * count,
        out_specs=(WHOLE,) * count,
        scratch_shapes=[pltpu.SemaphoreType.DMA((count,))],
        compiler_params=pltpu.CompilerParams(vmem_limit_bytes=2 << 20),
        cost_estimate=pl.CostEstimate(flops=0, bytes_accessed=24 << 20, transcendentals=0),
        name="load",
    )(*map(far, arrays))


def project(attn, w_out, out, first):
    width = out.shape[1]

    @pl.loop(0, width // CHUNK)
    def _(i):
        columns = pl.ds(pl.multiple_of(first + i * CHUNK, CHUNK), CHUNK)
        out[:, pl.ds(pl.multiple_of(i * CHUNK, CHUNK), CHUNK)] = dot(
            attn[...], w_out[:, columns]
        )[: out.shape[0]].astype(out.dtype)


def products_of(row, first, half, gain, weights, normed):
    at = pl.ds(pl.multiple_of(first, half), half)
    slots = row.shape[0]
    normed[:slots, :] = (row[...].astype(jnp.float32) * gain[:, at]).astype(jnp.bfloat16)
    if normed.shape[0] > slots:
        normed[slots:, :] = jnp.zeros((normed.shape[0] - slots, half), jnp.bfloat16)
    column = 0
    for w in weights:
        for start in range(0, w.shape[1], COLUMNS):
            end = min(start + COLUMNS, w.shape[1])
            yield slice(column + start, column + end), dot(normed[...], w[at, start:end])[:slots]
        column += w.shape[1]


def begin_kernel(own, gain, w_query, w_key, w_value, out, normed):
    core, _, _ = coordinates()
    half = own.shape[1]
    for columns, value in products_of(own, core * half, half, gain, (w_query, w_key, w_value), normed):
        out[:, columns] = value


def begin(own, gain, w_query, w_key, w_value):
    slots, half = own.shape
    padded = -(-slots // ROWS) * ROWS
    return pl.pallas_call(
        begin_kernel,
        out_shape=struct((slots, w_query.shape[1] + 2 * w_key.shape[1]), jnp.float32),
        in_specs=[WHOLE] * 5,
        out_specs=WHOLE,
        scratch_shapes=[VMEM((padded, half), jnp.bfloat16)],
        compiler_params=pltpu.CompilerParams(vmem_limit_bytes=8 << 20),
        cost_estimate=SMALL,
        name="begin",
    )(own, gain, w_query, w_key, w_value)


def step_kernel(step, own, peer, begun, gain, w_query, w_key, w_value, keys, values, bias, w_out, *rest):
    past_keys, past_values = rest[:step], rest[step : 2 * step]
    rest = rest[2 * step :]
    half = own.shape[1]
    slots = own.shape[0]
    q_cols, kv_cols = w_query.shape[1], w_key.shape[1]
    kv_heads = kv_cols // HD
    part, attn, key_now, value_now, norm, normed, query = rest
    core, _, _ = coordinates()
    here, there = own[...].astype(jnp.float32), peer[...].astype(jnp.float32)
    squares = jnp.sum(here * here, -1, keepdims=True) + jnp.sum(there * there, -1, keepdims=True)
    factor = lax.rsqrt(squares / D + 1e-06)
    norm[...] = jnp.broadcast_to(factor, norm.shape)
    for columns, value in products_of(peer, (1 - core) * half, half, gain, (w_query, w_key, w_value), normed):
        query[:, columns] = (begun[:, columns] + value) * factor
    key_now[...] = query[:slots, q_cols : q_cols + kv_cols].astype(jnp.bfloat16)
    value_now[...] = query[:slots, q_cols + kv_cols :].astype(jnp.bfloat16)
    recent = slots * (step + 1)
    row = lax.broadcasted_iota(jnp.int32, (GROUP * slots, recent), 0)
    column = lax.broadcasted_iota(jnp.int32, (GROUP * slots, recent), 1)
    same = lax.rem(row, slots) == lax.rem(column, slots)
    for head in range(kv_heads):
        lanes = slice(head * HD, (head + 1) * HD)
        q = jnp.concatenate(
            [query[:slots, (head * GROUP + g) * HD : (head * GROUP + g + 1) * HD] for g in range(GROUP)], 0
        ).astype(jnp.bfloat16)
        k_new = jnp.concatenate([k[:, lanes] for k in past_keys] + [key_now[:, lanes]], 0)
        v_new = jnp.concatenate([v[:, lanes] for v in past_values] + [value_now[:, lanes]], 0)
        contract = (((1,), (1,)), ((), ()))
        s_old = lax.dot_general(q, keys[:, lanes], contract, preferred_element_type=jnp.float32)
        s_old = s_old + jnp.concatenate([bias[...]] * GROUP, 0)
        s_new = lax.dot_general(q, k_new, contract, preferred_element_type=jnp.float32)
        s_new = jnp.where(same, s_new, MASKED)
        top = jnp.maximum(jnp.max(s_old, -1, keepdims=True), jnp.max(s_new, -1, keepdims=True))
        p_old = jnp.exp2(s_old * EXPONENT - top * EXPONENT)
        p_new = jnp.exp2(s_new * EXPONENT - top * EXPONENT)
        total = jnp.sum(p_old, -1, keepdims=True) + jnp.sum(p_new, -1, keepdims=True)
        summed = dot(p_old.astype(jnp.bfloat16), values[:, lanes]) + dot(p_new.astype(jnp.bfloat16), v_new)
        result = (summed / total).astype(jnp.bfloat16)
        for g in range(GROUP):
            at = (head * GROUP + g) * HD
            attn[:slots, at : at + HD] = result[g * slots : (g + 1) * slots]
    if attn.shape[0] > slots:
        attn[slots:, :] = jnp.zeros((attn.shape[0] - slots, q_cols), jnp.bfloat16)
    project(attn, w_out, part, (1 - core) * half)


def expand(step, own, peer, begun, gain, w_query, w_key, w_value, keys, values, bias, w_out, past_keys, past_values):
    slots, half = own.shape
    kv_cols = w_key.shape[1]
    q_cols = w_query.shape[1]
    padded = -(-slots // ROWS) * ROWS
    return pl.pallas_call(
        functools.partial(step_kernel, step),
        out_shape=(
            struct((slots, half)), struct((padded, q_cols)), struct((slots, kv_cols)), struct((slots, kv_cols)),
            struct((slots, 128), jnp.float32),
        ),
        in_specs=[WHOLE] * (11 + 2 * step),
        out_specs=[WHOLE] * 5,
        scratch_shapes=[VMEM((padded, half), jnp.bfloat16), VMEM((slots, q_cols + 2 * kv_cols), jnp.float32)],
        compiler_params=pltpu.CompilerParams(vmem_limit_bytes=16 << 20),
        cost_estimate=SMALL,
        name="expand",
    )(own, peer, begun, gain, w_query, w_key, w_value, keys, values, bias, w_out, *past_keys, *past_values)


def project_kernel(attn, w_out, part):
    core, _, _ = coordinates()
    project(attn, w_out, part, core * part.shape[1])


def project_own(rows, attn, w_out):
    return pl.pallas_call(
        project_kernel,
        out_shape=struct((rows, w_out.shape[1] // 2), jnp.float32),
        in_specs=[WHOLE, WHOLE],
        out_specs=WHOLE,
        compiler_params=pltpu.CompilerParams(vmem_limit_bytes=8 << 20),
        cost_estimate=SMALL,
        name="project_own",
    )(attn, w_out)


def score_kernel(steps, load, mp, notes, up, *refs):
    take = lambda count: [refs.pop(0) for _ in range(count)]
    refs = list(refs)
    own_rows, peer_rows, blocks, kept = take(steps), take(steps), take(mp if load else 1), take(1 * load)
    flat, total, *sems = refs
    groups, depth, hidden = up.shape
    rows = own_rows[0].shape[0]
    core, _, me = coordinates()
    for t in range(steps):
        target = flat.at[t * rows : (t + 1) * rows]
        for m in range(mp):
            at = m % (mp // 2) * depth
            for c in range(2):
                source = (own_rows if m // (mp // 2) == c else peer_rows)[t].at[:, at : at + depth]

                @pl.when((me == m) & (core == c))
                def _():
                    if load:
                        pltpu.make_async_copy(source, target, sems[0].at[t]).start()
                    else:
                        target[...] = source[...]

    if load:
        order = ring_order(groups)
        fetch = lambda r: pltpu.make_async_copy(arrived.at[order.index(r)], kept[0].at[r], sems[1].at[r])
        arrived, up = up, kept[0]
        for r in range(3):
            fetch(r).start()
        for t in range(steps):
            target = flat.at[t * rows : (t + 1) * rows]
            pltpu.make_async_copy(target, target, sems[0].at[t]).wait()
    shard = jnp.concatenate([notes[:, SHARD : SHARD + 1].astype(jnp.int32)] * steps, 0)
    for r in range(groups):
        if load:
            fetch(r).wait()
            if r + 3 < groups:
                fetch(r + 3).start()
        for at in range(0, hidden, COLUMNS):
            end = min(at + COLUMNS, hidden)
            here = jnp.where(shard == r, dot(flat[...], up[r, :, at:end]), 0.0)
            total[:, at:end] = here if r == 0 else total[:, at:end] + here
    if not load:
        blocks[0][...] = total[...].astype(jnp.bfloat16)
        return
    width = hidden // mp
    for j, block in enumerate(blocks):
        for m in range(mp):

            @pl.when((me ^ j) == m)
            def _():
                block[...] = total[:, m * width : (m + 1) * width].astype(jnp.bfloat16)


def score(mp, notes, up, own_rows, peer_rows, load):
    steps = len(own_rows)
    groups, depth, hidden = up.shape
    count = steps * own_rows[0].shape[0]
    blocks = (struct((count, hidden // mp)),) * mp if load else (struct((count, hidden)),)
    kept = (VMEM(up.shape, up.dtype),) * load
    place = FAR if load else WHOLE
    sems = [pltpu.SemaphoreType.DMA((steps,)), pltpu.SemaphoreType.DMA((groups,))]
    return pl.pallas_call(
        functools.partial(score_kernel, steps, load, mp),
        out_shape=blocks + kept,
        in_specs=[WHOLE] + [place] * (1 + 2 * steps),
        out_specs=(WHOLE,) * (len(blocks) + len(kept)),
        scratch_shapes=[VMEM((count, depth), jnp.bfloat16), VMEM((count, hidden), jnp.float32)] + sems * load,
        compiler_params=pltpu.CompilerParams(vmem_limit_bytes=16 << 20),
        cost_estimate=SMALL,
        name="score",
    )(notes, *(map(far, (up, *own_rows, *peer_rows)) if load else (up, *own_rows, *peer_rows)))


def scores_of(notes, scale, parts, factors):
    rows = notes.shape[0]
    shard = notes[:, SHARD : SHARD + 1].astype(jnp.int32)
    gain = jnp.zeros((rows, scale.shape[1]), jnp.float32)
    for r in range(scale.shape[0]):
        gain = gain + jnp.where(shard == r, scale[r : r + 1, :], 0.0)
    values = []
    for t, factor in enumerate(factors):
        z = paired_sum([part[t * rows : (t + 1) * rows, :].astype(jnp.float32) for part in parts]) * factor
        values.append(jnp.sum(z * jax.nn.sigmoid(z) * gain, -1, keepdims=True))
    return values


def finish_kernel(steps, notes, scale, *refs):
    norms, parts, out = refs[:steps], refs[steps:-1], refs[-1]
    lane = lax.broadcasted_iota(jnp.int32, out.shape, 1)
    total = jnp.zeros(out.shape, jnp.float32)
    for t, value in enumerate(scores_of(notes, scale, parts, [norm[:, :1] for norm in norms])):
        total = jnp.where(lane == t, value, total)
    out[...] = total


def finish(notes, scale, norms, parts):
    return pl.pallas_call(
        functools.partial(finish_kernel, len(norms)),
        out_shape=struct((notes.shape[0], 128), jnp.float32),
        in_specs=[WHOLE] * (2 + len(norms) + len(parts)),
        out_specs=WHOLE,
        compiler_params=pltpu.CompilerParams(vmem_limit_bytes=12 << 20),
        cost_estimate=SMALL,
        name="finish",
    )(notes, scale, *norms, *parts)


def place_kernel(groups, cap, mp, notes, own_row, peer_row, *refs):
    befores, scales, parts, table = refs[:mp], refs[mp : 2 * mp], refs[2 * mp : 3 * mp], refs[3 * mp]
    rows = notes.shape[0]
    _, _, me = coordinates()
    before = paired_sum([x[...] for x in befores])
    values = [before[:, t : t + 1] for t in range(STEPS - 1)]
    scale = [sum(jnp.where((me ^ j) == m, scales[j][...], 0.0) for j in range(mp)) for m in range(mp)]
    low, high = own_row[...].astype(jnp.float32), peer_row[...].astype(jnp.float32)
    squares = jnp.sum(low * low, -1, keepdims=True) + jnp.sum(high * high, -1, keepdims=True)
    values += scores_of(notes, jnp.concatenate(scale, 1), parts, [lax.rsqrt(squares / D + 1e-06)])
    number = lambda lane: notes[:, lane : lane + 1].astype(jnp.int32)
    shard, at = number(SHARD), number(SOURCE) * cap + number(RANK)
    live = notes[:, LIVE : LIVE + 1] > 0.5
    column = lax.broadcasted_iota(jnp.int32, (rows, table.shape[1]), 1)
    for r in range(groups):
        spots = (column == at) & (shard == r) & live
        for t, value in enumerate(values):
            table[r * STEPS + t : r * STEPS + t + 1, :] = jnp.sum(jnp.where(spots, value, 0.0), 0, keepdims=True)


def place(groups, cap, notes, own_row, peer_row, befores, scales, parts):
    mp = len(parts)
    return pl.pallas_call(
        functools.partial(place_kernel, groups, cap, mp),
        out_shape=struct((groups * STEPS, -(-groups * cap // 128) * 128), jnp.float32),
        in_specs=[WHOLE] * (3 + 3 * mp),
        out_specs=WHOLE,
        compiler_params=pltpu.CompilerParams(vmem_limit_bytes=12 << 20),
        cost_estimate=SMALL,
        name="place",
    )(notes, own_row, peer_row, *befores, *scales, *parts)


def shards(
    tokens,
    parent_keys,
    parent_values,
    parent_blocks,
    child_parent,
    child_count,
    node_shard,
    attn_gain,
    w_query,
    w_key,
    w_value,
    w_out,
    reward_up,
    reward_out,
):
    groups, mp = lax.axis_size("dp"), lax.axis_size("mp")
    children, width = tokens.shape
    parents, prefix, kv_cols = parent_keys.shape
    capacity = max(2, 2 * children // groups)
    reward_cap = max(2, 3 * children // (2 * groups))
    slots = groups * capacity
    rows = min(slots, 3 * children // 2)
    hidden = reward_out.shape[1] // mp
    pairs = lambda count, k: [(i, i ^ k) for i in range(count)]
    swap = pairs(mp, 1)

    up = lax.all_gather(reward_up[0], "dp", axis=0, axis_index_groups=[ring_order(groups)])

    blocks = dispatch(parents, child_count, child_parent, node_shard, tokens, reward_out, groups, capacity, hidden)
    keys = parent_keys.reshape(parents * prefix, kv_cols)
    values = parent_values.reshape(parents * prefix, kv_cols)
    raw = (w_query, w_key, w_value, keys, values, w_out)
    blocks, raw = lax.optimization_barrier((blocks, raw))
    blocks = [blocks[0]] + [lax.ppermute(blocks[k], "dp", pairs(groups, k)) for k in range(1, groups)]
    blocks, weights = lax.optimization_barrier((blocks, load(*raw)))
    gain = attn_gain.reshape(1, width)

    def run(offset, weights, blocks, up, gain, child_parent, parent_blocks):
        row_own, notes, bias, scale, over = pack(
            offset, rows, hidden, prefix, parent_blocks, child_parent, blocks
        )
        w_query, w_key, w_value, keys, values, w_out = [held(w) for w in weights]
        state = row_own.astype(jnp.float32)
        row_peer = lax.ppermute(row_own, "mp", swap)
        past_keys, past_values, rows_own, rows_peer, norms = [], [], [], [], []

        def products(first, last, up, load):
            sums = score(mp, notes, up, rows_own[first:last], rows_peer[first:last], load)
            count = mp if load else 1
            return list(sums[:count]), held(sums[-1]) if load else None

        send = lambda sums: [sums[0]] + [lax.ppermute(sums[k], "mp", pairs(mp, k)) for k in range(1, mp)]
        scales = send([scale] * mp)
        for step in range(STEPS):
            part, attn, key_now, value_now, norm = expand(
                step, row_own, row_peer, begin(row_own, gain, w_query, w_key, w_value), gain, w_query, w_key, w_value, keys, values, bias, w_out,
                past_keys, past_values,
            )
            norms.append(norm)
            past_keys.append(key_now)
            past_values.append(value_now)
            from_peer = lax.ppermute(part, "mp", swap)
            chip = project_own(rows, attn, w_out) + from_peer.astype(jnp.float32)
            sent = chip.astype(jnp.bfloat16)
            others = [sent] + [lax.ppermute(sent, "mp", pairs(mp, k)) for k in range(2, mp, 2)]
            if step == 0:
                others, scales = lax.optimization_barrier((others, scales))
            if step + 1 == STEPS:
                _, up = lax.optimization_barrier((sent, up))
                before, up = products(0, step, up, True)
                others, before = lax.optimization_barrier((others, before))
            state = state + paired_sum([other.astype(jnp.float32) for other in others])
            row_own = state.astype(jnp.bfloat16)
            row_peer = lax.ppermute(row_own, "mp", swap)
            rows_own.append(row_own)
            rows_peer.append(row_peer)
        before = send(before)
        last, _ = products(step, STEPS, up, False)
        last, over = lax.optimization_barrier((send(last * mp), over[0, 0]))
        before = send([finish(notes, scale, norms[1:], before)] * mp)
        return place(groups, reward_cap, notes, row_own, row_peer, before, scales, last), over

    operands = (blocks, up, gain, child_parent, parent_blocks)
    table, over = run(0, weights, *operands)
    if rows < slots:
        table, raw, operands = lax.optimization_barrier((table, raw, operands))
        again = lambda table, raw, operands: table + run(rows, load(*raw), *operands)[0]
        table = lax.cond(over > 0, again, lambda table, raw, operands: table, table, raw, operands)

    table = lax.all_to_all(table, "dp", split_axis=0, concat_axis=0, tiled=True)
    return jnp.sum(table.reshape(groups, STEPS, -1), 0)[:, : groups * reward_cap]


def solution(mesh):
    placed = (
        P("dp", None),
        P("dp", None, "mp"),
        P("dp", None, "mp"),
        P(),
        P(),
        P("dp"),
        P(),
        P(),
        P(None, "mp"),
        P(None, "mp"),
        P(None, "mp"),
        P("mp", None),
        P("dp", "mp", None),
        P("dp", None),
    )
    return jax.shard_map(
        shards, mesh=mesh, in_specs=placed, out_specs=P(None, "dp"), check_vma=False
    )
```
